32 devices in a mesh: gy: 8 (over y, x, core), gx: 4 (over z).
Axes of the slice: x: 2, y: 2, z: 4, core: 2. Of those that a mesh axis runs over, the one named last changes fastest.
Arguments:
- frames: bfloat16 [384, 256, 512], P('gy', 'gx'), may hold values from -2.390625 to 2.390625
- hidden_state: bfloat16 [384, 256, 128], P('gy', 'gx'), may hold values from -0.8984375 to 0.8984375
- cell_state: float32 [384, 256, 128], P('gy', 'gx'), may hold values from -4 to 4
- w_gates: bfloat16 [3, 3, 384, 512], replicated, may hold values from -0.3125 to 0.3125
- gate_bias: float32 [512], replicated, may hold values from -3 to 3
- w_qkv: bfloat16 [128, 768], replicated, may hold values from -0.5 to 0.5
- w_out: bfloat16 [256, 128], replicated, may hold values from -0.375 to 0.375
- w_up: bfloat16 [128, 512], replicated, may hold values from -0.5 to 0.5
- w_down: bfloat16 [512, 128], replicated, may hold values from -0.25 to 0.25
Outputs:
- block_out: bfloat16 [384, 256, 128], P('gy', 'gx')
- cell_out: float32 [384, 256, 128], P('gy', 'gx')
The draws below stay inside these ranges and needn't reach their ends.
All inputs are finite; a program needn't handle non-finite values.
Results may differ from the reference program's by a relative error of at most 0.014.
Values may be sent and summed in bfloat16 or wider, within the bound.
No kernel may reach another device: no remote copies, remote signals or barrier semaphores. Data moves between devices by JAX's collectives and lax.ppermute only.
A program may use at most 192 MiB of HBM per device.

```python
import jax
import jax.numpy as jnp
from jax import lax

LAT = 256
HID = 128
HEADS = 8
HDIM = 32
MLPW = 512
GRID = 8
ROWS = 384
COLS = 256
EMBED = 256


def shard_levels(rng, shape, shards, least, largest):
    level = 1.0
    for position, shards_of in shards:
        draws = jax.random.uniform(jax.random.fold_in(jax.random.fold_in(rng, 6), position), (shards_of,), jnp.float32, least / len(shards), largest / len(shards))
        level = level * jnp.repeat(jnp.exp(draws), shape[position] // shards_of).reshape((-1,) + (1,) * (len(shape) - 1 - position))
    return level


def centred(rng, extent, scale, limit, split=(), held_as=jnp.bfloat16):
    gain = shard_levels(rng, extent, split, -0.22, 0.18) if split else 1.0
    drawn = jax.random.normal(rng, extent, jnp.float32) * scale * gain
    return jnp.minimum(jnp.maximum(drawn, -limit), limit).astype(held_as)


def setup_inputs(seed: int = 0) -> dict:
    key_of = jax.random.split(jax.random.key(seed), 10)
    return {
        "frames": centred(key_of[0], (ROWS, COLS, 2 * LAT), 0.3, 2.390625, ((0, 8), (1, 4))),
        "hidden_state": jnp.clip(jax.random.uniform(key_of[1], (ROWS, COLS, HID), jnp.float32, -0.8984375, 0.8984375) * shard_levels(key_of[1], (ROWS, COLS, HID), ((0, 8), (1, 4)), -0.4, 0.0), -0.8984375, 0.8984375).astype(jnp.bfloat16),
        "cell_state": centred(key_of[2], (ROWS, COLS, HID), 1.0, 4.0, ((0, 8), (1, 4)), jnp.float32),
        "w_gates": centred(key_of[3], (3, 3, LAT + HID, 4 * HID), (LAT + HID) ** -0.5, 0.3125),
        "gate_bias": centred(key_of[4], (4 * HID,), 0.5, 3.0, (), jnp.float32),
        "w_qkv": centred(key_of[5], (HID, 3 * EMBED), HID ** -0.5, 0.5),
        "w_out": centred(key_of[6], (EMBED, HID), EMBED ** -0.5, 0.375),
        "w_up": centred(key_of[7], (HID, MLPW), HID ** -0.5, 0.5),
        "w_down": centred(key_of[8], (MLPW, HID), MLPW ** -0.5, 0.25),
    }


def layer_norm(values):
    center = values - lax.optimization_barrier(jnp.mean(values, axis=-1, keepdims=True))
    spread = lax.optimization_barrier(jnp.mean(center * center, axis=-1, keepdims=True))
    return center * lax.rsqrt(spread + 1e-05)

def conv_gates(joined, w_gates, gate_bias, out_rows, out_cols):
    channels = joined.shape[2]
    total = jnp.zeros((out_rows * out_cols, w_gates.shape[3]), jnp.float32)
    for row_off in range(3):
        for col_off in range(3):
            window = joined[row_off:row_off + out_rows, col_off:col_off + out_cols].reshape(-1, channels)
            total = total + jnp.dot(window, w_gates[row_off, col_off], preferred_element_type=jnp.float32)
    return total + gate_bias

def lstm_cell(gate_sums, cell_prev):
    width = cell_prev.shape[1]
    in_gate = jax.nn.sigmoid(gate_sums[:, 0:width])
    forget_gate = jax.nn.sigmoid(gate_sums[:, width:2 * width])
    candidate = jnp.tanh(gate_sums[:, 2 * width:3 * width])
    out_gate = jax.nn.sigmoid(gate_sums[:, 3 * width:4 * width])
    new_cell = forget_gate * cell_prev + in_gate * candidate
    new_hidden = (out_gate * jnp.tanh(new_cell)).astype(jnp.bfloat16)
    return (new_cell, new_hidden)

def attend(tokens, w_qkv):
    group_count, length, feature = tokens.shape
    mixed_qkv = jnp.dot(tokens.reshape(-1, feature), w_qkv, preferred_element_type=jnp.float32).astype(jnp.bfloat16)
    mixed_qkv = mixed_qkv.reshape(group_count, length, 3, HEADS, HDIM).astype(jnp.float32)
    queries = mixed_qkv[:, :, 0]
    key_rows = mixed_qkv[:, :, 1]
    values = mixed_qkv[:, :, 2]
    scores = jnp.einsum('gqhd,gkhd->ghqk', queries, key_rows) * HDIM ** (-0.5)
    raised = jnp.exp(scores)
    weights = (raised / lax.optimization_barrier(jnp.sum(raised, axis=-1, keepdims=True))).astype(jnp.bfloat16)
    head_out = jnp.einsum('ghqk,gkhd->gqhd', weights.astype(jnp.float32), values).astype(jnp.bfloat16)
    return head_out.reshape(group_count, length, HEADS * HDIM)

def reference(frames, hidden_state, cell_state, w_gates, gate_bias, w_qkv, w_out, w_up, w_down):
    total_rows, total_cols, width = hidden_state.shape
    latent = frames.shape[2] // 2
    first_in = jnp.pad(jnp.concatenate([frames[:, :, :latent], hidden_state], axis=2), ((1, 1), (1, 1), (0, 0)))
    cell_one, hidden_one = lstm_cell(conv_gates(first_in, w_gates, gate_bias, total_rows, total_cols), cell_state.reshape(-1, width))
    second_in = jnp.concatenate([frames[:, :, latent:], hidden_one.reshape(total_rows, total_cols, width)], axis=2)
    second_in = jnp.pad(second_in, ((1, 1), (1, 1), (0, 0)))
    cell_two, hidden_two = lstm_cell(conv_gates(second_in, w_gates, gate_bias, total_rows, total_cols), cell_one)
    normed = layer_norm(hidden_two.astype(jnp.float32)).astype(jnp.bfloat16)
    stride_y = total_rows // GRID
    stride_x = total_cols // GRID
    grouped = normed.reshape(GRID, stride_y, GRID, stride_x, width).transpose(1, 3, 0, 2, 4)
    grouped = grouped.reshape(stride_y, stride_x, GRID * GRID, width)
    head_out = lax.map(lambda block: attend(block, w_qkv), grouped)
    embed = head_out.shape[-1]
    attended = jnp.dot(head_out.reshape(-1, embed), w_out, preferred_element_type=jnp.float32).astype(jnp.bfloat16)
    attended = attended.reshape(stride_y, stride_x, GRID, GRID, width).transpose(2, 0, 3, 1, 4).reshape(-1, width)
    mixed = hidden_two.astype(jnp.float32) + attended.astype(jnp.float32)
    normed_two = layer_norm(mixed).astype(jnp.bfloat16)
    expanded = jax.nn.gelu(jnp.dot(normed_two, w_up, preferred_element_type=jnp.float32), approximate=True).astype(jnp.bfloat16)
    block_out = (mixed + jnp.dot(expanded, w_down, preferred_element_type=jnp.float32)).astype(jnp.bfloat16)
    return (block_out.reshape(total_rows, total_cols, width), cell_two.reshape(total_rows, total_cols, width))
```

```python
import functools

import jax
import jax.numpy as jnp
from jax import lax
from jax.experimental import pallas as pl
from jax.experimental.pallas import tpu as pltpu
from jax.sharding import PartitionSpec as P

HEADS = 8
HDIM = 32
GRID = 8
STEP = 8
SUB = 4
BF = jnp.bfloat16
F32 = jnp.float32
BF_MAX = 3.3895313892515355e38
VMEM_LIMIT = 40 * 1024 * 1024


def sigmoid(x):
    return 0.5 * jnp.tanh(0.5 * x) + 0.5


def lstm(gates, cell_prev):
    width = cell_prev.shape[-1]
    in_gate = sigmoid(gates[:, 0:width])
    forget_gate = sigmoid(gates[:, width : 2 * width])
    candidate = jnp.tanh(gates[:, 2 * width : 3 * width])
    out_gate = sigmoid(gates[:, 3 * width :])
    cell = forget_gate * cell_prev + in_gate * candidate
    return cell, out_gate * jnp.tanh(cell)


def layer_norm(values):
    center = values - jnp.mean(values, axis=-1, keepdims=True)
    spread = jnp.mean(center * center, axis=-1, keepdims=True)
    return center * lax.rsqrt(spread + 1e-05)


def three_columns(cells, left, right):
    count = cells.shape[1]
    wide = cells.astype(F32)
    place = lax.broadcasted_iota(jnp.int32, wide.shape, 1)
    before = jnp.where(place == 0, left, pltpu.roll(wide, 1, axis=1))
    after = jnp.where(place == count - 1, right, pltpu.roll(wide, count - 1, axis=1))
    return before.astype(BF), cells, after.astype(BF)


def conv_kernel(
    first_block,
    last_block,
    frame, frame_prev, frame_next, frame_top, frame_bot,
    hid, hid_prev, hid_next, hid_top, hid_bot,
    left, right, cell, weights, bias,
    *rest,
    packed,
):
    hid_out, cell_out, spread = rest[-3:]
    block = first_block + pl.program_id(0)
    latent = frame.shape[2]
    chans = latent + hid.shape[2]
    cols = hid.shape[1]

    def place(at, count, lead, x, h):
        low = left[pl.ds(lead, count)]
        high = right[pl.ds(lead, count)]
        for part, start, width in ((x, 0, latent), (h, latent, chans - latent)):
            pieces = three_columns(part, low[:, :, start : start + width], high[:, :, start : start + width])
            for tap in range(3):
                begin = tap * chans + start
                spread[pl.ds(at, count), :, begin : begin + width] = pieces[tap]

    base = block * STEP

    @pl.when(block == 0)
    def _():
        place(0, 1, base, frame_top[...], hid_top[...])

    @pl.when(block != 0)
    def _():
        place(0, 1, base, frame_prev[...], hid_prev[...])

    @pl.when(block == last_block)
    def _():
        place(STEP + 1, 1, base + STEP + 1, frame_bot[...], hid_bot[...])

    @pl.when(block != last_block)
    def _():
        place(STEP + 1, 1, base + STEP + 1, frame_next[...], hid_next[...])

    for at in range(0, STEP, SUB):
        place(1 + at, SUB, base + 1 + at, frame[at : at + SUB], hid[at : at + SUB])

    width = hid.shape[2]
    for at in range(0, STEP, SUB):
        lhs = jnp.concatenate(
            [spread[at + tap : at + tap + SUB].reshape(SUB * cols, 3 * chans) for tap in range(3)], axis=1
        )
        gates = jnp.dot(lhs, weights[...], preferred_element_type=F32) + bias[...]
        new_cell, new_hidden = lstm(gates, cell[at : at + SUB].reshape(SUB * cols, width))
        cell_out[at : at + SUB] = new_cell.reshape(SUB, cols, width)
        new_hidden = new_hidden.reshape(SUB, cols, width)
        if not packed:
            hid_out[at : at + SUB] = new_hidden.astype(BF)
            continue
        owners_x, piece_y = hid_out.shape[1:3]
        local_m, piece_x = packed
        for owner in range(owners_x):
            picked = jnp.concatenate(
                [
                    new_hidden[:, (m * owners_x + owner) * piece_x : (m * owners_x + owner + 1) * piece_x]
                    for m in range(local_m)
                ],
                axis=1,
            ).astype(BF)
            for row in range(SUB):
                line = at + row
                hid_out[line // piece_y, owner, line % piece_y] = picked[row]


def conv_step(
    frames, part, hid, cell, tops, bots, left, right, weights, bias, blocks, out_shapes, out_specs, packed, carry
):
    rows, cols, width = hid.shape
    latent = weights.shape[0] // 9 - width
    first, count = blocks
    last = rows // STEP - 1

    def rowed(depth, channels, channel, index):
        return pl.BlockSpec((depth, cols, channels), lambda i: (index(first + i), 0, channel))

    def whole(array):
        return pl.BlockSpec(array.shape, lambda i: (0,) * array.ndim)

    before = lambda b: jnp.maximum(b * STEP - 1, 0)
    after = lambda b: jnp.minimum(b * STEP + STEP, rows - 1)
    here = lambda b: b
    in_specs = [
        rowed(STEP, latent, part, here), rowed(1, latent, part, before), rowed(1, latent, part, after),
        whole(tops[0]), whole(bots[0]),
        rowed(STEP, width, 0, here), rowed(1, width, 0, before), rowed(1, width, 0, after),
        whole(tops[1]), whole(bots[1]),
        whole(left), whole(right), rowed(STEP, width, 0, here), whole(weights), whole(bias),
    ]
    operands = [
        frames, frames, frames, tops[0], bots[0], hid, hid, hid, tops[1], bots[1], left, right, cell, weights, bias,
    ]
    aliases = {}
    if carry is not None:
        aliases = {len(operands): 1}
        in_specs.append(pl.BlockSpec(memory_space=pl.ANY))
        operands.append(carry)
    cells = count * STEP * cols
    return pl.pallas_call(
        functools.partial(conv_kernel, first, last, packed=packed),
        grid=(count,),
        in_specs=in_specs,
        out_specs=out_specs,
        out_shape=out_shapes,
        scratch_shapes=[pltpu.VMEM((STEP + 2, cols, 3 * (latent + width)), BF)],
        input_output_aliases=aliases,
        compiler_params=pltpu.CompilerParams(vmem_limit_bytes=VMEM_LIMIT),
        cost_estimate=pl.CostEstimate(
            flops=2 * cells * weights.size, bytes_accessed=2 * weights.size + cells * 2048, transcendentals=cells * width * 5
        ),
    )(*operands)


def halo_kernel(lines, strips, left, right, weights, bias, out):
    chans = left.shape[2]
    extent = lines.shape[2]
    rows = left.shape[0] - 4
    parts = []
    for side in range(2):
        lead = side * (rows + 1)
        pieces = three_columns(lines[side, :, :, :chans], left[lead : lead + 3], right[lead : lead + 3])
        parts.append(jnp.concatenate([pieces[tap][row] for row in range(3) for tap in range(3)], axis=1))
    length = strips.shape[2]
    for side in range(2):
        rolled = []
        for col in range(3):
            wide = strips[side, col, :, :chans].astype(F32)
            rolled.append((pltpu.roll(wide, 1, axis=0), wide, pltpu.roll(wide, length - 1, axis=0)))
        parts.append(jnp.concatenate([rolled[col][row].astype(BF) for row in range(3) for col in range(3)], axis=1))
    lhs = jnp.concatenate(parts, axis=0)
    gates = jnp.dot(lhs, weights[...], preferred_element_type=F32) + bias[...]
    cell = jnp.concatenate(
        [lines[0, 1, :, chans:], lines[1, 1, :, chans:], strips[0, 1, :, chans:], strips[1, 1, :, chans:]], axis=0
    ).astype(F32)
    _, hidden = lstm(gates, cell)
    hidden = hidden.astype(BF).astype(F32)
    row, rows_of = lax.axis_index("gy"), lax.axis_size("gy")
    col, cols_of = lax.axis_index("gx"), lax.axis_size("gx")
    above, below = (row > 0).astype(F32), (row < rows_of - 1).astype(F32)
    before, after = (col > 0).astype(F32), (col < cols_of - 1).astype(F32)
    out[0] = hidden[:extent] * above
    out[1] = hidden[extent : 2 * extent] * below
    spot = lax.broadcasted_iota(jnp.int32, (length, hidden.shape[1]), 0)
    inside = jnp.where(spot == 1, above, jnp.where(spot == rows + 2, below, 1.0))
    out[2] = hidden[2 * extent : 2 * extent + length] * (inside * before)
    out[3] = hidden[2 * extent + length :] * (inside * after)


def block_kernel(x, w_qkv, w_out, w_up, w_down, out, flat, back):
    width = x.shape[-1]
    group = GRID * GRID
    flat[...] = x[...].astype(F32).reshape(flat.shape)
    groups = flat.shape[0] // group
    cells = jnp.concatenate([flat[pl.ds(g, group, stride=groups), :] for g in range(groups)], axis=0)
    normed = layer_norm(cells).astype(BF)
    qkv = jnp.dot(normed, w_qkv[...], preferred_element_type=F32).astype(BF)
    embed = w_qkv.shape[1] // 3
    keys = HEADS * group
    own = (
        lax.broadcasted_iota(jnp.int32, (keys, embed), 0) // group
        == lax.broadcasted_iota(jnp.int32, (keys, embed), 1) // HDIM
    )
    ones = (
        lax.broadcasted_iota(jnp.int32, (keys, keys), 0) // group
        == lax.broadcasted_iota(jnp.int32, (keys, keys), 1) // group
    ).astype(F32).astype(BF)
    own = own.astype(F32).astype(BF)
    raised = []
    for g in range(groups):
        part = qkv[g * group : (g + 1) * group]
        spread = jnp.concatenate([part[:, embed : 2 * embed]] * HEADS, axis=0) * own
        scores = lax.dot_general(
            part[:, :embed], spread, (((1,), (1,)), ((), ())), preferred_element_type=F32
        )
        raised.append(jnp.minimum(jnp.exp(scores * HDIM**-0.5), BF_MAX).astype(BF))
    raised = jnp.concatenate(raised, axis=0)
    total = jnp.dot(raised, ones, preferred_element_type=F32)
    attn = (raised.astype(F32) / total).astype(BF)
    heads = []
    for g in range(groups):
        part = qkv[g * group : (g + 1) * group]
        spread = jnp.concatenate([part[:, 2 * embed :]] * HEADS, axis=0) * own
        heads.append(
            jnp.dot(attn[g * group : (g + 1) * group], spread, preferred_element_type=F32).astype(BF)
        )
    heads = jnp.concatenate(heads, axis=0)
    attended = jnp.dot(heads, w_out[...], preferred_element_type=F32).astype(BF)
    mixed = cells + attended.astype(F32)
    normed_two = layer_norm(mixed).astype(BF)
    up = jnp.dot(normed_two, w_up[...], preferred_element_type=F32)
    expanded = (0.5 * up * (1.0 + jnp.tanh(0.7978845608 * (up + 0.044715 * (up * up * up))))).astype(BF)
    result = mixed + jnp.dot(expanded, w_down[...], preferred_element_type=F32)
    for g in range(groups):
        back[pl.ds(g, group, stride=groups), :] = result[g * group : (g + 1) * group]
    out[...] = back[...].reshape(x.shape).astype(BF)


def block_step(moved, devices_y, devices_x, w_qkv, w_out, w_up, w_down):
    _, piece_y, piece_cols, width = moved.shape
    lanes = devices_y // GRID
    view = moved.reshape(GRID, lanes, devices_x, piece_y, piece_cols, width)
    tokens = GRID * devices_x * piece_cols
    spec = pl.BlockSpec(
        (GRID, None, devices_x, None, piece_cols, width), lambda i, j: (0, i, 0, j, 0, 0)
    )

    def whole(array):
        return pl.BlockSpec(array.shape, lambda i, j: (0,) * array.ndim)

    total = lanes * piece_y * tokens
    out = pl.pallas_call(
        block_kernel,
        grid=(lanes, piece_y),
        in_specs=[spec, whole(w_qkv), whole(w_out), whole(w_up), whole(w_down)],
        out_specs=spec,
        out_shape=jax.ShapeDtypeStruct(view.shape, BF),
        scratch_shapes=[pltpu.VMEM((tokens, width), F32), pltpu.VMEM((tokens, width), F32)],
        compiler_params=pltpu.CompilerParams(vmem_limit_bytes=VMEM_LIMIT),
        cost_estimate=pl.CostEstimate(
            flops=total * 3_000_000, bytes_accessed=total * width * 4 + 800_000, transcendentals=total * 1100
        ),
    )(view, w_qkv, w_out, w_up, w_down)
    return out.reshape(moved.shape)


def unpack_kernel(local_m, piece_x, *refs):
    src, out = refs[0], refs[-1]
    owners_y, owners_x, piece_y, _, width = src.shape
    for owner_y in range(owners_y):
        for row in range(piece_y):
            wide = src[owner_y, :, row].astype(F32)
            out[owner_y * piece_y + row] = jnp.concatenate(
                [wide[owner, m * piece_x : (m + 1) * piece_x] for m in range(local_m) for owner in range(owners_x)],
                axis=0,
            ).astype(BF)


def unpack_step(landed, carry, chunk, rows, cols, local_m, piece_x):
    owners_y, owners_x, piece_y, _, width = landed.shape
    depth = owners_y * piece_y
    specs = [pl.BlockSpec(landed.shape, lambda i: (0,) * landed.ndim)]
    operands = [landed]
    aliases = {}
    if carry is not None:
        specs.append(pl.BlockSpec(memory_space=pl.ANY))
        operands.append(carry)
        aliases = {1: 0}
    return pl.pallas_call(
        functools.partial(unpack_kernel, local_m, piece_x),
        grid=(1,),
        in_specs=specs,
        out_specs=pl.BlockSpec((depth, cols, width), lambda i: (chunk, 0, 0)),
        out_shape=jax.ShapeDtypeStruct((rows, cols, width), BF),
        input_output_aliases=aliases,
        compiler_params=pltpu.CompilerParams(vmem_limit_bytes=VMEM_LIMIT),
        cost_estimate=pl.CostEstimate(flops=0, bytes_accessed=depth * cols * width * 4, transcendentals=0),
    )(*operands)


def body(frames, hidden_state, cell_state, w_gates, gate_bias, w_qkv, w_out, w_up, w_down):
    rows, cols, width = hidden_state.shape
    latent = frames.shape[2] // 2
    chans = latent + width
    devices_y, devices_x = lax.axis_size("gy"), lax.axis_size("gx")
    local_m = GRID // devices_x
    piece_x = cols // local_m // devices_x
    weights = w_gates.reshape(-1, w_gates.shape[3])
    bias = gate_bias.reshape(1, -1)

    def pack(row, col):
        return jnp.concatenate(
            [
                frames[row, col, :latent],
                hidden_state[row, col],
                cell_state[row, col].astype(BF),
                frames[row, col, latent:],
            ],
            axis=-1,
        )

    def shifted(value, axis, step):
        count = lax.axis_size(axis)
        pairs = [(i, i + step) for i in range(count) if 0 <= i + step < count]
        return lax.ppermute(value, axis, pairs)

    every = slice(None)
    from_left = shifted(pack(every, slice(cols - 2, cols)), "gx", 1)
    from_right = shifted(pack(every, slice(0, 2)), "gx", -1)
    line_top = pack(slice(0, 2), every)
    line_bot = pack(slice(rows - 2, rows), every)
    from_up = shifted(jnp.concatenate([line_bot, from_left[-2:], from_right[-2:]], axis=1), "gy", 1)
    from_down = shifted(jnp.concatenate([line_top, from_left[:2], from_right[:2]], axis=1), "gy", -1)

    def column(at, middle):
        return jnp.concatenate([from_up[:, at], middle, from_down[:, at]], axis=0)

    columns = [
        column(cols, from_left[:, 0]),
        column(cols + 1, from_left[:, 1]),
        column(0, pack(every, 0)),
        column(cols - 1, pack(every, cols - 1)),
        column(cols + 2, from_right[:, 0]),
        column(cols + 3, from_right[:, 1]),
    ]
    held = chans + width
    length = -(-(rows + 4) // 16) * 16
    strips = jnp.stack(columns)[:, :, :held].reshape(2, 3, rows + 4, held)
    strips = jnp.pad(strips, ((0, 0), (0, 0), (0, length - rows - 4), (0, 0)))
    low = columns[1].astype(F32)[:, None]
    high = columns[4].astype(F32)[:, None]
    lines = jnp.stack(
        [
            jnp.concatenate([from_up[:, :cols, :held], line_top[:1, :, :held]], axis=0),
            jnp.concatenate([line_bot[1:, :, :held], from_down[:, :cols, :held]], axis=0),
        ]
    )
    cell_one_shape = jax.ShapeDtypeStruct((rows, cols, width), F32)
    row_spec = pl.BlockSpec((STEP, cols, width), lambda i: (i, 0, 0))
    hidden_one, cell_one = conv_step(
        frames, 0, hidden_state, cell_state,
        (from_up[1:, :cols, :latent], from_up[1:, :cols, latent:chans]),
        (from_down[:1, :cols, :latent], from_down[:1, :cols, latent:chans]),
        low[1:-1, :, :chans], high[1:-1, :, :chans], weights, bias, (0, rows // STEP),
        (jax.ShapeDtypeStruct((rows, cols, width), BF), cell_one_shape), (row_spec, row_spec), None, None,
    )
    halo = pl.pallas_call(
        halo_kernel,
        out_shape=jax.ShapeDtypeStruct((4, length, width), F32),
        compiler_params=pltpu.CompilerParams(vmem_limit_bytes=VMEM_LIMIT),
        cost_estimate=pl.CostEstimate(flops=2 * 4 * length * weights.size, bytes_accessed=2 * weights.size, transcendentals=0),
    )(lines, strips, low[:, :, :chans], high[:, :, :chans], weights, bias)
    second_low = jnp.concatenate([low[1:-1, :, held:], halo[2, 1 : rows + 3][:, None]], axis=2)
    second_high = jnp.concatenate([high[1:-1, :, held:], halo[3, 1 : rows + 3][:, None]], axis=2)
    tops = (from_up[1:, :cols, held:], halo[0:1].astype(BF))
    bots = (from_down[:1, :cols, held:], halo[1:2].astype(BF))

    depth = 2 * devices_y if devices_y == GRID else devices_y
    chunks = rows // depth
    piece_y = depth // devices_y
    piece_cols = local_m * piece_x
    per_chunk = depth // STEP
    cell_out, moved = None, []
    for chunk in range(chunks):
        first = chunk * per_chunk
        sent, cell_out = conv_step(
            frames, 1, hidden_one, cell_one, tops, bots, second_low, second_high, weights, bias, (first, per_chunk),
            (jax.ShapeDtypeStruct((devices_y, devices_x, piece_y, piece_cols, width), BF), cell_one_shape),
            (
                pl.BlockSpec((STEP // piece_y, devices_x, piece_y, piece_cols, width), lambda i: (i, 0, 0, 0, 0)),
                pl.BlockSpec((STEP, cols, width), lambda i, first=first: (first + i, 0, 0)),
            ),
            (local_m, piece_x), cell_out,
        )
        sent = sent.reshape(devices_y * devices_x, piece_y, piece_cols, width)
        moved.append(lax.all_to_all(sent, ("gy", "gx"), split_axis=0, concat_axis=0, tiled=True))
    landed = []
    for chunk in range(chunks):
        done = block_step(moved[chunk], devices_y, devices_x, w_qkv, w_out, w_up, w_down)
        landed.append(lax.all_to_all(done, ("gy", "gx"), split_axis=0, concat_axis=0, tiled=True))
    result = None
    for chunk in range(chunks):
        view = landed[chunk].reshape(devices_y, devices_x, piece_y, piece_cols, width)
        result = unpack_step(view, result, chunk, rows, cols, local_m, piece_x)
    return result, cell_out


def solution(mesh):
    tiled = P("gy", "gx", None)
    in_specs = (tiled, tiled, tiled, P(), P(), P(), P(), P(), P())
    return jax.shard_map(body, mesh=mesh, in_specs=in_specs, out_specs=(tiled, tiled), check_vma=False)
```

```python
import functools

import jax
import jax.numpy as jnp
from jax import lax
from jax.experimental import pallas as pl
from jax.experimental.pallas import tpu as pltpu
from jax.sharding import PartitionSpec as P

HEADS = 8
HDIM = 32
GRID = 8
STEP = 8
SUB = 4
BF = jnp.bfloat16
F32 = jnp.float32
BF_MAX = 3.3895313892515355e38
VMEM_LIMIT = 60 * 1024 * 1024


def sigmoid(x):
    return 0.5 * jnp.tanh(0.5 * x) + 0.5


def lstm(gates, cell_prev):
    width = cell_prev.shape[-1]
    in_gate = sigmoid(gates[:, 0:width])
    forget_gate = sigmoid(gates[:, width : 2 * width])
    candidate = jnp.tanh(gates[:, 2 * width : 3 * width])
    out_gate = sigmoid(gates[:, 3 * width :])
    cell = forget_gate * cell_prev + in_gate * candidate
    return cell, out_gate * jnp.tanh(cell)


def layer_norm(values):
    center = values - jnp.mean(values, axis=-1, keepdims=True)
    spread = jnp.mean(center * center, axis=-1, keepdims=True)
    return center * lax.rsqrt(spread + 1e-05)


def three_columns(wide, left, right):
    count = wide.shape[0]
    place = lax.broadcasted_iota(jnp.int32, wide.shape, 0)
    before = jnp.where(place == 0, left, pltpu.roll(wide, 1, axis=0))
    after = jnp.where(place == count - 1, right, pltpu.roll(wide, count - 1, axis=0))
    return before.astype(BF), wide.astype(BF), after.astype(BF)


def conv_kernel(first, count, last, refs, packed, *args):
    ref = dict(zip(refs, args))
    frame, hid, bias = ref["frame"], ref["hid"], ref["bias"]
    hid_out, cell_out = ref["hid_out"], ref["cell_out"]
    ring = "left" in ref
    step = pl.program_id(0)
    latent, width = frame.shape[2], hid.shape[2]
    chans = latent + width
    cols = hid.shape[1]
    load = pltpu.make_async_copy(ref["weights"], ref["held"], ref["sem"])

    def build(spread):
        block = first + step
        base = block * STEP
        top, bot = block == 0, block == last
        for pos in range(STEP + 2):
            if pos == 0:
                x, h = ref["frame_prev"][0].astype(F32), ref["hid_prev"][0].astype(F32)
            elif pos == STEP + 1:
                x, h = ref["frame_next"][0].astype(F32), ref["hid_next"][0].astype(F32)
            else:
                x, h = frame[pos - 1].astype(F32), hid[pos - 1].astype(F32)
            low = high = jnp.zeros((1, chans), F32)
            if ring:
                low, high = ref["left"][base + pos], ref["right"][base + pos]
                place = lax.broadcasted_iota(jnp.int32, h.shape, 0)
                h = jnp.where(place == 0, ref["first_col"][base + pos], h)
                h = jnp.where(place == cols - 1, ref["last_col"][base + pos], h)
                for spot, edge, line in ((0, top, 0), (1, top, 1), (STEP, bot, 2), (STEP + 1, bot, 3)):
                    if pos == spot:
                        h = jnp.where(edge, ref["lines"][line], h)
                if pos == 0:
                    x = jnp.where(top, ref["frame_top"][0].astype(F32), x)
                if pos == STEP + 1:
                    x = jnp.where(bot, ref["frame_bot"][0].astype(F32), x)
            elif pos == 0:
                x, h = jnp.where(top, 0.0, x), jnp.where(top, 0.0, h)
            elif pos == STEP + 1:
                x, h = jnp.where(bot, 0.0, x), jnp.where(bot, 0.0, h)
            for part, start in ((x, 0), (h, latent)):
                size = part.shape[1]
                pieces = three_columns(part, low[:, start : start + size], high[:, start : start + size])
                for tap in range(3):
                    spread[pos, :, tap * chans + start : tap * chans + start + size] = pieces[tap]

    def multiply(spread):
        block = first + step - 1
        base = block * STEP
        for at in range(0, STEP, SUB):
            lhs = jnp.concatenate(
                [spread[at + tap : at + tap + SUB].reshape(SUB * cols, 3 * chans) for tap in range(3)], axis=1
            )
            gates = jnp.dot(lhs, ref["held"][...], preferred_element_type=F32) + bias[...]
            cell_prev = ref["cell"][at : at + SUB]
            if ring:
                place = lax.broadcasted_iota(jnp.int32, cell_prev.shape, 1)
                cell_prev = jnp.where(place == 0, ref["first_cell"][pl.ds(base + at + 1, SUB)], cell_prev)
                cell_prev = jnp.where(place == cols - 1, ref["last_cell"][pl.ds(base + at + 1, SUB)], cell_prev)
                if at == 0:
                    edge = jnp.where(block == 0, ref["cell_lines"][1:2], cell_prev[:1])
                    cell_prev = jnp.concatenate([edge, cell_prev[1:]], axis=0)
                if at == STEP - SUB:
                    edge = jnp.where(block == last, ref["cell_lines"][2:3], cell_prev[-1:])
                    cell_prev = jnp.concatenate([cell_prev[:-1], edge], axis=0)
            new_cell, new_hidden = lstm(gates, cell_prev.reshape(SUB * cols, width))
            cell_out[at : at + SUB] = new_cell.reshape(SUB, cols, width)
            new_hidden = new_hidden.reshape(SUB, cols, width)
            if not packed:
                hid_out[at : at + SUB] = new_hidden.astype(BF)
                continue
            owners_x, piece_y = hid_out.shape[1:3]
            local_m, piece_x = packed
            for owner in range(owners_x):
                picked = jnp.concatenate(
                    [
                        new_hidden[:, (m * owners_x + owner) * piece_x : (m * owners_x + owner + 1) * piece_x]
                        for m in range(local_m)
                    ],
                    axis=1,
                ).astype(BF)
                for row in range(SUB):
                    line = (step - 1) * STEP + at + row
                    hid_out[lax.div(line, piece_y), owner, lax.rem(line, piece_y)] = picked[row]

    slots = ref["even"], ref["odd"]

    @pl.when(step == 0)
    def _():
        load.start()
        build(slots[0])

    @pl.when(step == 1)
    def _():
        load.wait()

    for parity in range(2):

        @pl.when((step > 0) & (step < count) & (lax.rem(step, 2) == parity))
        def _():
            build(slots[parity])
            multiply(slots[1 - parity])

    @pl.when(step == count)
    def _():
        multiply(slots[(count - 1) % 2])


def conv_step(frames, part, hid, cell, ring, weights, bias, blocks, out_shapes, out_specs, packed, carry):
    rows, cols, width = hid.shape
    latent = weights.shape[0] // 9 - width
    first, count = blocks
    last = rows // STEP - 1

    def rowed(depth, channels, channel, index):
        def place(step):
            return index(first + jnp.minimum(step, count - 1)), 0, channel

        return pl.BlockSpec((depth, cols, channels), place)

    def whole(array):
        return pl.BlockSpec(array.shape, lambda step: (0,) * array.ndim)

    def before(block):
        return jnp.maximum(block * STEP - 1, 0)

    def after(block):
        return jnp.minimum(block * STEP + STEP, rows - 1)

    inputs = {
        "frame": (frames, rowed(STEP, latent, part, lambda block: block)),
        "frame_prev": (frames, rowed(1, latent, part, before)),
        "frame_next": (frames, rowed(1, latent, part, after)),
        "hid": (hid, rowed(STEP, width, 0, lambda block: block)),
        "hid_prev": (hid, rowed(1, width, 0, before)),
        "hid_next": (hid, rowed(1, width, 0, after)),
        "cell": (cell, pl.BlockSpec((STEP, cols, width), lambda step: (first + jnp.maximum(step - 1, 0), 0, 0))),
        "weights": (weights, pl.BlockSpec(memory_space=pl.ANY)),
        "bias": (bias, whole(bias)),
    }
    inputs |= {name: (array, whole(array)) for name, array in ring.items()}
    aliases = {}
    for place, array in enumerate(carry):
        if array is not None:
            aliases[len(inputs)] = place
            inputs[f"carry{place}"] = (array, pl.BlockSpec(memory_space=pl.ANY))
    refs = (*inputs, "hid_out", "cell_out", "even", "odd", "held", "sem")
    cells = count * STEP * cols
    slot = pltpu.VMEM((STEP + 2, cols, 3 * (latent + width)), BF)
    return pl.pallas_call(
        functools.partial(conv_kernel, first, count, last, refs, packed),
        grid=(count + 1,),
        in_specs=[spec for _, spec in inputs.values()],
        out_specs=out_specs,
        out_shape=out_shapes,
        scratch_shapes=[slot, slot, pltpu.VMEM(weights.shape, BF), pltpu.SemaphoreType.DMA(())],
        input_output_aliases=aliases,
        compiler_params=pltpu.CompilerParams(vmem_limit_bytes=VMEM_LIMIT),
        cost_estimate=pl.CostEstimate(
            flops=2 * cells * weights.size, bytes_accessed=2 * weights.size + cells * 2048, transcendentals=cells * width * 5
        ),
    )(*(array for array, _ in inputs.values()))


def ring_kernel(lines, strips, left, right, weights, bias, line_hid, line_cell, strip_hid, strip_cell):
    chans = left.shape[2]
    cols, length = lines.shape[2], strips.shape[2]
    rows = left.shape[0] - 4
    parts = []
    for side in range(2):
        pieces = [
            three_columns(lines[side, row, :, :chans].astype(F32), left[side * rows + row], right[side * rows + row])
            for row in range(4)
        ]
        for row in range(2):
            parts.append(jnp.concatenate([pieces[row + tap][col] for tap in range(3) for col in range(3)], axis=1))
    for side in range(2):
        rolled = []
        for col in range(4):
            wide = strips[side, col, :, :chans].astype(F32)
            rolled.append((pltpu.roll(wide, 1, axis=0), wide, pltpu.roll(wide, length - 1, axis=0)))
        for col in range(2):
            parts.append(
                jnp.concatenate([rolled[col + tap][row].astype(BF) for row in range(3) for tap in range(3)], axis=1)
            )
    row_at, col_at = lax.axis_index("gy"), lax.axis_index("gx")
    above = (row_at > 0).astype(F32)
    below = (row_at < lax.axis_size("gy") - 1).astype(F32)
    before = (col_at > 0).astype(F32)
    after = (col_at < lax.axis_size("gx") - 1).astype(F32)
    width = line_hid.shape[2]
    spot = lax.broadcasted_iota(jnp.int32, (length, width), 0)
    inside = jnp.where(spot == 1, above, jnp.where(spot == rows + 2, below, 1.0))
    keep = [above, 1.0, 1.0, below, inside * before, inside, inside, inside * after]
    for half, (hid, cell) in enumerate(((line_hid, line_cell), (strip_hid, strip_cell))):
        lhs = jnp.concatenate(parts[4 * half : 4 * half + 4], axis=0)
        gates = jnp.dot(lhs, weights[...], preferred_element_type=F32) + bias[...]
        if half == 0:
            held = [lines[side, row, :, chans:] for side in range(2) for row in (1, 2)]
        else:
            held = [strips[side, col, :, chans:] for side in range(2) for col in (1, 2)]
        new_cell, hidden = lstm(gates, jnp.concatenate(held, axis=0).astype(F32))
        hidden = hidden.astype(BF).astype(F32)
        size = hid.shape[1]
        for place in range(4):
            hid[place] = hidden[place * size : (place + 1) * size] * keep[4 * half + place]
            cell[place] = new_cell[place * size : (place + 1) * size]


def block_kernel(x, w_qkv, w_out, w_up, w_down, out, flat, back, own, ones):
    width = x.shape[-1]
    group = GRID * GRID
    flat[...] = x[...].astype(F32).reshape(flat.shape)
    groups = flat.shape[0] // group
    cells = jnp.concatenate([flat[pl.ds(g, group, stride=groups), :] for g in range(groups)], axis=0)
    normed = layer_norm(cells).astype(BF)
    qkv = jnp.dot(normed, w_qkv[...], preferred_element_type=F32).astype(BF)
    embed = w_qkv.shape[1] // 3

    @pl.when((pl.program_id(0) == 0) & (pl.program_id(1) == 0))
    def _():
        def fill(target, size):
            down = lax.broadcasted_iota(jnp.int32, target.shape, 0) // group
            across = lax.broadcasted_iota(jnp.int32, target.shape, 1) // size
            target[...] = (down == across).astype(F32).astype(BF)

        fill(own, HDIM)
        fill(ones, group)

    raised = []
    for g in range(groups):
        part = qkv[g * group : (g + 1) * group]
        spread = jnp.concatenate([part[:, embed : 2 * embed]] * HEADS, axis=0) * own[...]
        scores = lax.dot_general(
            part[:, :embed], spread, (((1,), (1,)), ((), ())), preferred_element_type=F32
        )
        raised.append(jnp.minimum(jnp.exp(scores * HDIM**-0.5), BF_MAX).astype(BF))
    raised = jnp.concatenate(raised, axis=0)
    total = jnp.dot(raised, ones[...], preferred_element_type=F32)
    attn = (raised.astype(F32) / total).astype(BF)
    heads = []
    for g in range(groups):
        part = qkv[g * group : (g + 1) * group]
        spread = jnp.concatenate([part[:, 2 * embed :]] * HEADS, axis=0) * own[...]
        heads.append(
            jnp.dot(attn[g * group : (g + 1) * group], spread, preferred_element_type=F32).astype(BF)
        )
    heads = jnp.concatenate(heads, axis=0)
    attended = jnp.dot(heads, w_out[...], preferred_element_type=F32).astype(BF)
    mixed = cells + attended.astype(F32)
    normed_two = layer_norm(mixed).astype(BF)
    up = jnp.dot(normed_two, w_up[...], preferred_element_type=F32)
    expanded = (0.5 * up * (1.0 + jnp.tanh(0.7978845608 * (up + 0.044715 * (up * up * up))))).astype(BF)
    result = mixed + jnp.dot(expanded, w_down[...], preferred_element_type=F32)
    for g in range(groups):
        back[pl.ds(g, group, stride=groups), :] = result[g * group : (g + 1) * group]
    out[...] = back[...].reshape(x.shape).astype(BF)


def block_step(moved, devices_y, devices_x, w_qkv, w_out, w_up, w_down):
    _, piece_y, piece_cols, width = moved.shape
    lanes = devices_y // GRID
    view = moved.reshape(GRID, lanes, devices_x, piece_y, piece_cols, width)
    tokens = GRID * devices_x * piece_cols
    spec = pl.BlockSpec(
        (GRID, None, devices_x, None, piece_cols, width), lambda i, j: (0, i, 0, j, 0, 0)
    )

    def whole(array):
        return pl.BlockSpec(array.shape, lambda i, j: (0,) * array.ndim)

    total = lanes * piece_y * tokens
    out = pl.pallas_call(
        block_kernel,
        grid=(lanes, piece_y),
        in_specs=[spec, whole(w_qkv), whole(w_out), whole(w_up), whole(w_down)],
        out_specs=spec,
        out_shape=jax.ShapeDtypeStruct(view.shape, BF),
        scratch_shapes=[
            pltpu.VMEM((tokens, width), F32),
            pltpu.VMEM((tokens, width), F32),
            pltpu.VMEM((HEADS * GRID * GRID, w_out.shape[0]), BF),
            pltpu.VMEM((HEADS * GRID * GRID, HEADS * GRID * GRID), BF),
        ],
        compiler_params=pltpu.CompilerParams(vmem_limit_bytes=VMEM_LIMIT),
        cost_estimate=pl.CostEstimate(
            flops=total * 3_000_000, bytes_accessed=total * width * 4 + 800_000, transcendentals=total * 1100
        ),
    )(view, w_qkv, w_out, w_up, w_down)
    return out.reshape(moved.shape)


def unpack_kernel(local_m, piece_x, *refs):
    src, out = refs[0], refs[-1]
    owners_y, owners_x, piece_y, _, width = src.shape
    for owner_y in range(owners_y):
        for row in range(piece_y):
            wide = src[owner_y, :, row].astype(F32)
            out[owner_y * piece_y + row] = jnp.concatenate(
                [wide[owner, m * piece_x : (m + 1) * piece_x] for m in range(local_m) for owner in range(owners_x)],
                axis=0,
            ).astype(BF)


def unpack_step(landed, carry, start, rows, cols, local_m, piece_x):
    owners_y, owners_x, piece_y, _, width = landed.shape
    depth = owners_y * piece_y
    specs = [pl.BlockSpec(landed.shape, lambda i: (0,) * landed.ndim)]
    operands = [landed]
    aliases = {}
    if carry is not None:
        specs.append(pl.BlockSpec(memory_space=pl.ANY))
        operands.append(carry)
        aliases = {1: 0}
    return pl.pallas_call(
        functools.partial(unpack_kernel, local_m, piece_x),
        grid=(1,),
        in_specs=specs,
        out_specs=pl.BlockSpec((depth, cols, width), lambda i: (start // depth, 0, 0)),
        out_shape=jax.ShapeDtypeStruct((rows, cols, width), BF),
        input_output_aliases=aliases,
        compiler_params=pltpu.CompilerParams(vmem_limit_bytes=VMEM_LIMIT),
        cost_estimate=pl.CostEstimate(flops=0, bytes_accessed=depth * cols * width * 4, transcendentals=0),
    )(*operands)


def body(frames, hidden_state, cell_state, w_gates, gate_bias, w_qkv, w_out, w_up, w_down):
    rows, cols, width = hidden_state.shape
    latent = frames.shape[2] // 2
    chans = latent + width
    held = chans + width
    devices_y, devices_x = lax.axis_size("gy"), lax.axis_size("gx")
    local_m = GRID // devices_x
    piece_x = cols // local_m // devices_x
    weights = w_gates.reshape(-1, w_gates.shape[3])
    bias = gate_bias.reshape(1, -1)

    def pack(row, col):
        return jnp.concatenate(
            [
                frames[row, col, :latent],
                hidden_state[row, col],
                cell_state[row, col].astype(BF),
                frames[row, col, latent:],
            ],
            axis=-1,
        )

    def shifted(value, axis, step):
        count = lax.axis_size(axis)
        pairs = [(i, i + step) for i in range(count) if 0 <= i + step < count]
        return lax.ppermute(value, axis, pairs)

    every = slice(None)
    side_left, side_right = pack(every, slice(0, 2)), pack(every, slice(cols - 2, cols))
    from_left = shifted(side_right, "gx", 1)
    from_right = shifted(side_left, "gx", -1)
    line_top, line_bot = pack(slice(0, 2), every), pack(slice(rows - 2, rows), every)
    from_up = shifted(jnp.concatenate([line_bot, from_left[-2:], from_right[-2:]], axis=1), "gy", 1)
    from_down = shifted(jnp.concatenate([line_top, from_left[:2], from_right[:2]], axis=1), "gy", -1)

    tile_shapes = (jax.ShapeDtypeStruct((rows, cols, width), BF), jax.ShapeDtypeStruct((rows, cols, width), F32))
    half = rows // STEP // 2
    hidden_one = cell_one = None
    for first, count in ((0, half), (half, rows // STEP - half)):
        spec = pl.BlockSpec((STEP, cols, width), lambda j, first=first: (first + jnp.maximum(j - 1, 0), 0, 0))
        hidden_one, cell_one = conv_step(
            frames, 0, hidden_state, cell_state, {}, weights, bias, (first, count), tile_shapes, (spec, spec),
            None, (hidden_one, cell_one),
        )

    def column(at, middle):
        return jnp.concatenate([from_up[:, at], middle, from_down[:, at]], axis=0)

    columns = [
        column(cols, from_left[:, 0]),
        column(cols + 1, from_left[:, 1]),
        column(0, side_left[:, 0]),
        column(1, side_left[:, 1]),
        column(cols - 2, side_right[:, 0]),
        column(cols - 1, side_right[:, 1]),
        column(cols + 2, from_right[:, 0]),
        column(cols + 3, from_right[:, 1]),
    ]
    length = -(-(rows + 4) // 16) * 16
    strips = jnp.stack(columns)[:, :, :held].reshape(2, 4, rows + 4, held)
    strips = jnp.pad(strips, ((0, 0), (0, 0), (0, length - rows - 4), (0, 0)))
    low, high = columns[1].astype(F32)[:, None], columns[6].astype(F32)[:, None]
    lines = jnp.stack(
        [
            jnp.concatenate([from_up[:, :cols, :held], line_top[:, :, :held]], axis=0),
            jnp.concatenate([line_bot[:, :, :held], from_down[:, :cols, :held]], axis=0),
        ]
    )
    ring_shapes = [jax.ShapeDtypeStruct((4, cols, width), F32)] * 2 + [jax.ShapeDtypeStruct((4, length, width), F32)] * 2
    line_hid, line_cell, strip_hid, strip_cell = pl.pallas_call(
        ring_kernel,
        out_shape=ring_shapes,
        compiler_params=pltpu.CompilerParams(vmem_limit_bytes=VMEM_LIMIT),
        cost_estimate=pl.CostEstimate(flops=16 * length * weights.size, bytes_accessed=2 * weights.size, transcendentals=0),
    )(lines, strips, low[:, :, :chans], high[:, :, :chans], weights, bias)

    def sided(strip, at):
        return strip[at, 1 : rows + 3][:, None]

    ring = {
        "left": jnp.concatenate([low[1:-1, :, held:], sided(strip_hid, 0)], axis=2),
        "right": jnp.concatenate([high[1:-1, :, held:], sided(strip_hid, 3)], axis=2),
        "first_col": sided(strip_hid, 1),
        "last_col": sided(strip_hid, 2),
        "first_cell": sided(strip_cell, 1),
        "last_cell": sided(strip_cell, 2),
        "lines": line_hid,
        "cell_lines": line_cell,
        "frame_top": from_up[1:, :cols, held:],
        "frame_bot": from_down[:1, :cols, held:],
    }

    pieces = rows // devices_y
    piece_cols = local_m * piece_x
    cell_out, moved, start = None, [], 0
    for piece_y in (pieces - pieces // 2, pieces // 2):
        first, count = start // STEP, piece_y * devices_y // STEP
        sent_shape = (devices_y, devices_x, piece_y, piece_cols, width)
        sent, cell_out = conv_step(
            frames, 1, hidden_one, cell_one, ring, weights, bias, (first, count),
            (jax.ShapeDtypeStruct(sent_shape, BF), tile_shapes[1]),
            (
                pl.BlockSpec(sent_shape, lambda j: (0,) * 5),
                pl.BlockSpec((STEP, cols, width), lambda j, first=first: (first + jnp.maximum(j - 1, 0), 0, 0)),
            ),
            (local_m, piece_x), (None, cell_out),
        )
        sent = sent.reshape(devices_y * devices_x, piece_y, piece_cols, width)
        moved.append((start, lax.all_to_all(sent, ("gy", "gx"), split_axis=0, concat_axis=0, tiled=True)))
        start += piece_y * devices_y
    landed = []
    for start, value in moved:
        done = block_step(value, devices_y, devices_x, w_qkv, w_out, w_up, w_down)
        landed.append((start, lax.all_to_all(done, ("gy", "gx"), split_axis=0, concat_axis=0, tiled=True)))
    result = None
    for start, value in landed:
        view = value.reshape(devices_y, devices_x, *value.shape[1:])
        result = unpack_step(view, result, start, rows, cols, local_m, piece_x)
    return result, cell_out


def solution(mesh):
    tiled = P("gy", "gx", None)
    in_specs = (tiled, tiled, tiled, P(), P(), P(), P(), P(), P())
    return jax.shard_map(body, mesh=mesh, in_specs=in_specs, out_specs=(tiled, tiled), check_vma=False)
```

```python
import functools

import jax
import jax.numpy as jnp
from jax import lax
from jax.experimental import pallas as pl
from jax.experimental.pallas import tpu as pltpu
from jax.sharding import PartitionSpec as P

HEADS = 8
HDIM = 32
GRID = 8
BF = jnp.bfloat16
F32 = jnp.float32
LOG2E = 1.4426950408889634
BF_MAX = 3.3895313892515355e38
VMEM_LIMIT = 60 * 1024 * 1024


def sigmoid(x):
    return 0.5 * jnp.tanh(0.5 * x) + 0.5


def lstm(gates, cell_prev):
    width = cell_prev.shape[-1]
    in_gate = sigmoid(gates[:, 0:width])
    forget_gate = sigmoid(gates[:, width : 2 * width])
    candidate = jnp.tanh(gates[:, 2 * width : 3 * width])
    out_gate = sigmoid(gates[:, 3 * width :])
    cell = forget_gate * cell_prev + in_gate * candidate
    return cell, out_gate * jnp.tanh(cell)


def layer_norm(values):
    center = values - jnp.mean(values, axis=-1, keepdims=True)
    spread = jnp.mean(center * center, axis=-1, keepdims=True)
    return center * lax.rsqrt(spread + 1e-05)


def three_columns(wide, left, right):
    count = wide.shape[0]
    place = lax.broadcasted_iota(jnp.int32, wide.shape, 0)
    before = jnp.where(place == 0, left, pltpu.roll(wide, 1, axis=0))
    after = jnp.where(place == count - 1, right, pltpu.roll(wide, count - 1, axis=0))
    return before.astype(BF), wide.astype(BF), after.astype(BF)


def conv_kernel(first, last, refs, packed, *args):
    ref = dict(zip(refs, args))
    frame, hid = ref["frame"], ref["hid"]
    hid_out, cell_out, spread = ref["hid_out"], ref["cell_out"], ref["spread"]
    ring = "strips_hid" in ref
    step = pl.program_id(0)
    depth, cols, latent = frame.shape
    width = hid.shape[2]
    chans = latent + width
    load = pltpu.make_async_copy(ref["weights"], ref["held"], ref["sem"])

    @pl.when(step == 0)
    def _():
        load.start()
        if ring:
            for side, strip, frames_beside in (("left", 0, "frame_left"), ("right", 3, "frame_right")):
                ref[side][:, :latent] = ref[frames_beside][0, 0].astype(F32)
                ref[side][:, latent:] = ref["strips_hid"][strip]

    block = first + step
    base = block * depth
    top, bot = block == 0, block == last
    for pos in range(depth + 2):
        if pos == 0:
            x, h = ref["frame_prev"][0].astype(F32), ref["hid_prev"][0].astype(F32)
        elif pos == depth + 1:
            x, h = ref["frame_next"][0].astype(F32), ref["hid_next"][0].astype(F32)
        else:
            x, h = frame[pos - 1].astype(F32), hid[pos - 1].astype(F32)
        low = high = jnp.zeros((1, chans), F32)
        if ring:
            here = pl.ds(base + pos + 1, 1)
            low, high = ref["left"][here, :], ref["right"][here, :]
            place = lax.broadcasted_iota(jnp.int32, h.shape, 0)
            h = jnp.where(place == 0, ref["strips_hid"][1, here, :], h)
            h = jnp.where(place == cols - 1, ref["strips_hid"][2, here, :], h)
            for spot, edge, line in ((0, top, 0), (1, top, 1), (depth, bot, 2), (depth + 1, bot, 3)):
                if pos == spot:
                    h = jnp.where(edge, ref["lines_hid"][line], h)
            if pos == 0:
                x = jnp.where(top, ref["frame_top"][0, :cols].astype(F32), x)
            if pos == depth + 1:
                x = jnp.where(bot, ref["frame_bot"][0, :cols].astype(F32), x)
        elif pos == 0:
            x, h = jnp.where(top, 0.0, x), jnp.where(top, 0.0, h)
        elif pos == depth + 1:
            x, h = jnp.where(bot, 0.0, x), jnp.where(bot, 0.0, h)
        for part, start in ((x, 0), (h, latent)):
            size = part.shape[1]
            pieces = three_columns(part, low[:, start : start + size], high[:, start : start + size])
            for tap in range(3):
                spread[pos, :, tap * chans + start : tap * chans + start + size] = pieces[tap]

    @pl.when(step == 0)
    def _():
        load.wait()

    lhs = jnp.concatenate(
        [spread[tap : tap + depth].reshape(depth * cols, 3 * chans) for tap in range(3)], axis=1
    )
    gates = jnp.dot(lhs, ref["held"][...], preferred_element_type=F32) + ref["bias"][...]
    for row in range(depth):
        cell_prev = ref["cell"][row]
        if ring:
            here = pl.ds(base + row + 2, 1)
            place = lax.broadcasted_iota(jnp.int32, cell_prev.shape, 0)
            cell_prev = jnp.where(place == 0, ref["strips_cell"][1, here, :], cell_prev)
            cell_prev = jnp.where(place == cols - 1, ref["strips_cell"][2, here, :], cell_prev)
            if row == 0:
                cell_prev = jnp.where(top, ref["lines_cell"][1], cell_prev)
            if row == depth - 1:
                cell_prev = jnp.where(bot, ref["lines_cell"][2], cell_prev)
        new_cell, new_hidden = lstm(gates[row * cols : (row + 1) * cols], cell_prev)
        cell_out[row] = new_cell
        if not packed:
            hid_out[row] = new_hidden.astype(BF)
            continue
        owners_x, piece_y = hid_out.shape[1:3]
        local_m, piece_x = packed
        line = step * depth + row
        for owner in range(owners_x):
            picked = [
                new_hidden[(m * owners_x + owner) * piece_x : (m * owners_x + owner + 1) * piece_x]
                for m in range(local_m)
            ]
            hid_out[lax.div(line, piece_y), owner, lax.rem(line, piece_y)] = jnp.concatenate(picked, axis=0).astype(BF)


def whole(array):
    return pl.BlockSpec(array.shape, lambda *step: (0,) * array.ndim)


def conv_step(frames, part, hid, cell, ring, weights, bias, extent, depth, out_shapes, out_specs, packed, carry):
    rows, cols, width = hid.shape
    latent = weights.shape[0] // 9 - width
    first, count = extent[0] // depth, extent[1] // depth
    last = rows // depth - 1

    def rowed(size, channels, channel, index):
        return pl.BlockSpec((size, cols, channels), lambda step: (index(first + step), 0, channel))

    def before(block):
        return jnp.maximum(block * depth - 1, 0)

    def after(block):
        return jnp.minimum(block * depth + depth, rows - 1)

    inputs = {
        "frame": (frames, rowed(depth, latent, part, lambda block: block)),
        "frame_prev": (frames, rowed(1, latent, part, before)),
        "frame_next": (frames, rowed(1, latent, part, after)),
        "hid": (hid, rowed(depth, width, 0, lambda block: block)),
        "hid_prev": (hid, rowed(1, width, 0, before)),
        "hid_next": (hid, rowed(1, width, 0, after)),
        "cell": (cell, rowed(depth, width, 0, lambda block: block)),
        "weights": (weights, pl.BlockSpec(memory_space=pl.ANY)),
        "bias": (bias, whole(bias)),
    }
    inputs |= ring
    aliases = {}
    for place, array in enumerate(carry):
        if array is not None:
            aliases[len(inputs)] = place
            inputs[f"carry{place}"] = (array, pl.BlockSpec(memory_space=pl.ANY))
    refs = [*inputs, "hid_out", "cell_out", "spread", "held", "sem"]
    scratch = [
        pltpu.VMEM((depth + 2, cols, 3 * (latent + width)), BF),
        pltpu.VMEM(weights.shape, BF),
        pltpu.SemaphoreType.DMA(()),
    ]
    if ring:
        refs += ["left", "right"]
        scratch += [pltpu.VMEM((ring["strips_hid"][0].shape[1], latent + width), F32)] * 2
    cells = extent[1] * cols
    return pl.pallas_call(
        functools.partial(conv_kernel, first, last, refs, packed),
        grid=(count,),
        in_specs=[spec for _, spec in inputs.values()],
        out_specs=out_specs,
        out_shape=out_shapes,
        scratch_shapes=scratch,
        input_output_aliases=aliases,
        compiler_params=pltpu.CompilerParams(vmem_limit_bytes=VMEM_LIMIT),
        cost_estimate=pl.CostEstimate(
            flops=2 * cells * weights.size, bytes_accessed=2 * weights.size + cells * 2048, transcendentals=cells * width * 5
        ),
    )(*(array for array, _ in inputs.values()))


def ring_kernel(
    rows, above, below, frame_top, frame_bot, hid_top, hid_bot, cell_top, cell_bot, strips, weights, bias,
    line_hid, line_cell, strip_hid, strip_cell,
):
    latent, width = frame_top.shape[2], hid_top.shape[2]
    chans = latent + width
    cols, length = frame_top.shape[1], strips.shape[2]
    low, high = strips[0, 1, :, :chans].astype(F32), strips[1, 2, :, :chans].astype(F32)

    def beside(ref, row):
        line = ref[row, :cols].astype(F32)
        return line[:, :chans], line[:, chans : chans + width]

    def within(frame, hid, cell, row):
        return jnp.concatenate([frame[row].astype(F32), hid[row].astype(F32)], axis=1), cell[row]

    tops = [beside(above, 0), beside(above, 1)] + [within(frame_top, hid_top, cell_top, row) for row in range(2)]
    bots = [within(frame_bot, hid_bot, cell_bot, row) for row in range(2)] + [beside(below, 0), beside(below, 1)]
    parts, held = [], []
    for lead, lines in ((0, tops), (rows, bots)):
        pieces = []
        for row in range(4):
            at = lead + row
            pieces.append(three_columns(lines[row][0], low[at : at + 1], high[at : at + 1]))
        for row in range(2):
            parts.append(jnp.concatenate([pieces[row + tap][col] for tap in range(3) for col in range(3)], axis=1))
            held.append(lines[row + 1][1])
    for side in range(2):
        rolled = []
        for col in range(4):
            wide = strips[side, col, :, :chans].astype(F32)
            rolled.append((pltpu.roll(wide, 1, axis=0), wide, pltpu.roll(wide, length - 1, axis=0)))
        for col in range(2):
            parts.append(
                jnp.concatenate([rolled[col + tap][row].astype(BF) for row in range(3) for tap in range(3)], axis=1)
            )
            held.append(strips[side, col + 1, :, chans : chans + width].astype(F32))
    row_at, col_at = lax.axis_index("gy"), lax.axis_index("gx")
    upper = (row_at > 0).astype(F32)
    lower = (row_at < lax.axis_size("gy") - 1).astype(F32)
    before = (col_at > 0).astype(F32)
    after = (col_at < lax.axis_size("gx") - 1).astype(F32)
    spot = lax.broadcasted_iota(jnp.int32, (length, width), 0)
    inside = jnp.where(spot == 1, upper, jnp.where(spot == rows + 2, lower, 1.0))
    keep = [upper, 1.0, 1.0, lower, inside * before, inside, inside, inside * after]
    lhs = jnp.concatenate(parts, axis=0)
    gates = jnp.dot(lhs, weights[...], preferred_element_type=F32) + bias[...]
    start = 0
    for place in range(8):
        hid, cell = (line_hid, line_cell) if place < 4 else (strip_hid, strip_cell)
        size = hid.shape[1]
        new_cell, hidden = lstm(gates[start : start + size], held[place])
        hid[place % 4] = hidden.astype(BF).astype(F32) * keep[place]
        cell[place % 4] = new_cell
        start += size


def block_kernel(x, w_qkv, w_out, w_up, w_down, out, flat, back, keys_t, own_low, own_high, own_values, ones):
    group = GRID * GRID
    embed = w_out.shape[0]
    tile = embed // 2

    @pl.when((pl.program_id(0) == 0) & (pl.program_id(1) == 0))
    def _():
        def fill(target, down, across, add):
            above = lax.broadcasted_iota(jnp.int32, target.shape, 0) // down
            along = lax.broadcasted_iota(jnp.int32, target.shape, 1) // across
            target[...] = (above == along + add).astype(F32).astype(BF)

        fill(own_low, HDIM, group, 0)
        fill(own_high, HDIM, group, HEADS // 4)
        fill(own_values, group, HDIM, 0)
        fill(ones, group, group, 0)
        keys_t[...] = w_qkv[:, embed : 2 * embed].astype(F32).T.astype(BF)

    flat[...] = x[...].astype(F32).reshape(flat.shape)
    groups = flat.shape[0] // group
    cells = jnp.concatenate([flat[pl.ds(g, group, stride=groups), :] for g in range(groups)], axis=0)
    normed = layer_norm(cells).astype(BF)
    queries = jnp.dot(normed, w_qkv[:, :embed], preferred_element_type=F32).astype(BF)
    values = jnp.dot(normed, w_qkv[:, 2 * embed :], preferred_element_type=F32).astype(BF)
    keys = lax.dot_general(keys_t[...], normed, (((1,), (1,)), ((), ())), preferred_element_type=F32)
    side = lax.broadcasted_iota(jnp.int32, (embed, 2 * group), 1) < group
    raised = [[], []]
    for pair in range(groups // 2):
        both = keys[:, pair * 2 * group : (pair + 1) * 2 * group]
        turned = pltpu.roll(both, group, axis=1)
        for place, twice in enumerate((jnp.where(side, both, turned), jnp.where(side, turned, both))):
            twice = twice.astype(BF)
            start = (2 * pair + place) * group
            for half in range(2):
                part = twice[half * tile : (half + 1) * tile]
                spread = jnp.concatenate([part * own_low[...], part * own_high[...]], axis=1)
                scores = jnp.dot(
                    queries[start : start + group, half * tile : (half + 1) * tile], spread, preferred_element_type=F32
                )
                raised[half].append(jnp.minimum(jnp.exp2(scores * (LOG2E * HDIM**-0.5)), BF_MAX).astype(BF))
    heads = []
    for half in range(2):
        part = jnp.concatenate(raised[half], axis=0)
        total = jnp.dot(part, ones[...], preferred_element_type=F32)
        attn = (part.astype(F32) * pl.reciprocal(total)).astype(BF)
        column = []
        for g in range(groups):
            held = values[g * group : (g + 1) * group, half * tile : (half + 1) * tile]
            spread = jnp.concatenate([held] * (HEADS // 2), axis=0) * own_values[...]
            column.append(
                jnp.dot(attn[g * group : (g + 1) * group], spread, preferred_element_type=F32).astype(BF)
            )
        heads.append(jnp.concatenate(column, axis=0))
    heads = jnp.concatenate(heads, axis=1)
    attended = jnp.dot(heads, w_out[...], preferred_element_type=F32).astype(BF)
    mixed = cells + attended.astype(F32)
    normed_two = layer_norm(mixed).astype(BF)
    up = jnp.dot(normed_two, w_up[...], preferred_element_type=F32)
    bent = jnp.tanh(up * (0.7978845608 + (0.7978845608 * 0.044715) * (up * up)))
    half_up = 0.5 * up
    expanded = (half_up + half_up * bent).astype(BF)
    result = mixed + jnp.dot(expanded, w_down[...], preferred_element_type=F32)
    for g in range(groups):
        back[pl.ds(g, group, stride=groups), :] = result[g * group : (g + 1) * group]
    out[...] = back[...].reshape(x.shape).astype(BF)


def block_step(moved, devices_y, devices_x, w_qkv, w_out, w_up, w_down):
    _, piece_y, piece_cols, width = moved.shape
    lanes = devices_y // GRID
    view = moved.reshape(GRID, lanes, devices_x, piece_y, piece_cols, width)
    tokens = GRID * devices_x * piece_cols
    spec = pl.BlockSpec(
        (GRID, None, devices_x, None, piece_cols, width), lambda i, j: (0, i, 0, j, 0, 0)
    )

    total = lanes * piece_y * tokens
    out = pl.pallas_call(
        block_kernel,
        grid=(lanes, piece_y),
        in_specs=[spec, whole(w_qkv), whole(w_out), whole(w_up), whole(w_down)],
        out_specs=spec,
        out_shape=jax.ShapeDtypeStruct(view.shape, BF),
        scratch_shapes=[
            pltpu.VMEM((tokens, width), F32),
            pltpu.VMEM((tokens, width), F32),
            pltpu.VMEM((w_out.shape[0], width), BF),
            pltpu.VMEM((HEADS // 2 * HDIM, 2 * GRID * GRID), BF),
            pltpu.VMEM((HEADS // 2 * HDIM, 2 * GRID * GRID), BF),
            pltpu.VMEM((HEADS // 2 * GRID * GRID, HEADS // 2 * HDIM), BF),
            pltpu.VMEM((HEADS // 2 * GRID * GRID, HEADS // 2 * GRID * GRID), BF),
        ],
        compiler_params=pltpu.CompilerParams(vmem_limit_bytes=VMEM_LIMIT),
        cost_estimate=pl.CostEstimate(
            flops=total * 3_000_000, bytes_accessed=total * width * 4 + 800_000, transcendentals=total * 1100
        ),
    )(view, w_qkv, w_out, w_up, w_down)
    return out.reshape(moved.shape)


def unpack_kernel(local_m, piece_x, *refs):
    src, out = refs[0], refs[-1]
    owners_y, owners_x, piece_y, _, width = src.shape
    for owner_y in range(owners_y):
        for row in range(piece_y):
            wide = src[owner_y, :, row].astype(F32)
            out[owner_y * piece_y + row] = jnp.concatenate(
                [wide[owner, m * piece_x : (m + 1) * piece_x] for m in range(local_m) for owner in range(owners_x)],
                axis=0,
            ).astype(BF)


def unpack_step(landed, carry, start, rows, cols, local_m, piece_x):
    owners_y, owners_x, piece_y, _, width = landed.shape
    depth = owners_y * piece_y
    specs = [pl.BlockSpec(landed.shape, lambda i: (0,) * landed.ndim)]
    operands = [landed]
    aliases = {}
    if carry is not None:
        specs.append(pl.BlockSpec(memory_space=pl.ANY))
        operands.append(carry)
        aliases = {1: 0}
    return pl.pallas_call(
        functools.partial(unpack_kernel, local_m, piece_x),
        grid=(1,),
        in_specs=specs,
        out_specs=pl.BlockSpec((depth, cols, width), lambda i: (start // depth, 0, 0)),
        out_shape=jax.ShapeDtypeStruct((rows, cols, width), BF),
        input_output_aliases=aliases,
        compiler_params=pltpu.CompilerParams(vmem_limit_bytes=VMEM_LIMIT),
        cost_estimate=pl.CostEstimate(flops=0, bytes_accessed=depth * cols * width * 4, transcendentals=0),
    )(*operands)


def step_rows(start, extent):
    return max(size for size in range(1, 17) if extent % size == 0 and start % size == 0)


def body(frames, hidden_state, cell_state, w_gates, gate_bias, w_qkv, w_out, w_up, w_down):
    rows, cols, width = hidden_state.shape
    latent = frames.shape[2] // 2
    chans = latent + width
    held = chans + width
    devices_y, devices_x = lax.axis_size("gy"), lax.axis_size("gx")
    local_m = GRID // devices_x
    piece_x = cols // local_m // devices_x
    weights = w_gates.reshape(-1, w_gates.shape[3])
    bias = gate_bias.reshape(1, -1)

    every, left_two, right_two = slice(None), slice(0, 2), slice(cols - 2, cols)
    top_two, bot_two = slice(0, 2), slice(rows - 2, rows)
    edges = ((every, left_two), (every, right_two), (top_two, every), (bot_two, every))
    edge_cells = lax.optimization_barrier(tuple(cell_state[edge] for edge in edges))

    def pack(edge, cells):
        return jnp.concatenate(
            [frames[edge][:, :, :latent], hidden_state[edge], cells.astype(BF), frames[edge][:, :, latent:]], axis=-1
        )

    def shifted(value, axis, step):
        count = lax.axis_size(axis)
        pairs = [(i, i + step) for i in range(count) if 0 <= i + step < count]
        return lax.ppermute(value, axis, pairs)

    side_left, side_right, line_top, line_bot = (pack(edge, cells) for edge, cells in zip(edges, edge_cells))
    from_left = shifted(side_right, "gx", 1)
    from_right = shifted(side_left, "gx", -1)
    from_up = shifted(jnp.concatenate([line_bot, from_left[-2:], from_right[-2:]], axis=1), "gy", 1)
    from_down = shifted(jnp.concatenate([line_top, from_left[:2], from_right[:2]], axis=1), "gy", -1)

    tile_shapes = (jax.ShapeDtypeStruct((rows, cols, width), BF), jax.ShapeDtypeStruct((rows, cols, width), F32))
    depth = step_rows(0, rows)
    spec = pl.BlockSpec((depth, cols, width), lambda step: (step, 0, 0))
    hidden_one, cell_one = conv_step(
        frames, 0, hidden_state, cell_state, {}, weights, bias, (0, rows), depth, tile_shapes, (spec, spec), None, ()
    )

    def column(at, middle):
        return jnp.concatenate([from_up[:, at], middle, from_down[:, at]], axis=0)

    columns = [
        column(cols, from_left[:, 0]),
        column(cols + 1, from_left[:, 1]),
        column(0, side_left[:, 0]),
        column(1, side_left[:, 1]),
        column(cols - 2, side_right[:, 0]),
        column(cols - 1, side_right[:, 1]),
        column(cols + 2, from_right[:, 0]),
        column(cols + 3, from_right[:, 1]),
    ]
    length = -(-(rows + 4) // 16) * 16
    strips = jnp.stack(columns).reshape(2, 4, rows + 4, held + latent)
    strips = jnp.pad(strips, ((0, 0), (0, 0), (0, length - rows - 4), (0, 0)))

    def two_rows(channels, at):
        return pl.BlockSpec((2, cols, channels), lambda step: (at, 0, 0))

    last_two = rows // 2 - 1
    line_shape = jax.ShapeDtypeStruct((4, cols, width), F32)
    strip_shape = jax.ShapeDtypeStruct((4, length, width), F32)
    line_hid, line_cell, strip_hid, strip_cell = pl.pallas_call(
        functools.partial(ring_kernel, rows),
        grid=(1,),
        in_specs=[
            whole(from_up), whole(from_down), two_rows(latent, 0), two_rows(latent, last_two), two_rows(width, 0),
            two_rows(width, last_two), two_rows(width, 0), two_rows(width, last_two), whole(strips), whole(weights),
            whole(bias),
        ],
        out_specs=[whole(line_shape), whole(line_shape), whole(strip_shape), whole(strip_shape)],
        out_shape=[line_shape, line_shape, strip_shape, strip_shape],
        compiler_params=pltpu.CompilerParams(vmem_limit_bytes=VMEM_LIMIT),
        cost_estimate=pl.CostEstimate(flops=16 * length * weights.size, bytes_accessed=2 * weights.size, transcendentals=0),
    )(
        from_up, from_down, frames, frames, hidden_state, hidden_state, cell_state, cell_state, strips, weights, bias
    )

    second = held // latent
    beside = (1, 1, length, latent)
    line = (1, from_up.shape[1], latent)
    ring = {name: (array, whole(array)) for name, array in (
        ("strips_hid", strip_hid), ("strips_cell", strip_cell), ("lines_hid", line_hid), ("lines_cell", line_cell)
    )}
    ring["frame_left"] = strips, pl.BlockSpec(beside, lambda step: (0, 1, 0, second))
    ring["frame_right"] = strips, pl.BlockSpec(beside, lambda step: (1, 2, 0, second))
    ring["frame_top"] = from_up, pl.BlockSpec(line, lambda step: (1, 0, second))
    ring["frame_bot"] = from_down, pl.BlockSpec(line, lambda step: (0, 0, second))

    pieces = rows // devices_y
    piece_cols = local_m * piece_x
    cell_out, moved, start = None, [], 0
    for piece_y in (pieces - pieces // 2, pieces // 2):
        extent = piece_y * devices_y
        depth = step_rows(start, extent)
        sent_shape = jax.ShapeDtypeStruct((devices_y, devices_x, piece_y, piece_cols, width), BF)
        sent, cell_out = conv_step(
            frames, 1, hidden_one, cell_one, ring, weights, bias, (start, extent), depth, (sent_shape, tile_shapes[1]),
            (
                whole(sent_shape),
                pl.BlockSpec((depth, cols, width), lambda step, first=start // depth: (first + step, 0, 0)),
            ),
            (local_m, piece_x), (None, cell_out),
        )
        sent = sent.reshape(devices_y * devices_x, piece_y, piece_cols, width)
        moved.append((start, lax.all_to_all(sent, ("gy", "gx"), split_axis=0, concat_axis=0, tiled=True)))
        start += extent
    landed = []
    for start, value in moved:
        done = block_step(value, devices_y, devices_x, w_qkv, w_out, w_up, w_down)
        landed.append((start, lax.all_to_all(done, ("gy", "gx"), split_axis=0, concat_axis=0, tiled=True)))
    result = None
    for start, value in landed:
        view = value.reshape(devices_y, devices_x, *value.shape[1:])
        result = unpack_step(view, result, start, rows, cols, local_m, piece_x)
    return result, cell_out


def solution(mesh):
    tiled = P("gy", "gx", None)
    in_specs = (tiled, tiled, tiled, P(), P(), P(), P(), P(), P())
    return jax.shard_map(body, mesh=mesh, in_specs=in_specs, out_specs=(tiled, tiled), check_vma=False)
```

```python
import functools

import jax
import jax.numpy as jnp
from jax import lax
from jax.experimental import pallas as pl
from jax.experimental.pallas import tpu as pltpu
from jax.sharding import PartitionSpec as P

HEADS = 8
HDIM = 32
GRID = 8
BF = jnp.bfloat16
F32 = jnp.float32
LOG2E = 1.4426950408889634
BF_MAX = 3.3895313892515355e38
VMEM_LIMIT = 32 * 1024 * 1024
VMEM_ALL = 60 * 1024 * 1024
LOADS = 9


def sigmoid(x):
    return 0.5 * jnp.tanh(0.5 * x) + 0.5


def lstm(gates, cell_prev):
    width = cell_prev.shape[-1]
    in_gate = sigmoid(gates[:, 0:width])
    forget_gate = sigmoid(gates[:, width : 2 * width])
    candidate = jnp.tanh(gates[:, 2 * width : 3 * width])
    out_gate = sigmoid(gates[:, 3 * width :])
    cell = forget_gate * cell_prev + in_gate * candidate
    return cell, out_gate * jnp.tanh(cell)


def layer_norm(values):
    center = values - jnp.mean(values, axis=-1, keepdims=True)
    spread = jnp.mean(center * center, axis=-1, keepdims=True)
    return center * lax.rsqrt(spread + 1e-05)


def three_columns(wide, left, right):
    count = wide.shape[0]
    place = lax.broadcasted_iota(jnp.int32, wide.shape, 0)
    before = jnp.where(place == 0, left, pltpu.roll(wide, 1, axis=0))
    after = jnp.where(place == count - 1, right, pltpu.roll(wide, count - 1, axis=0))
    return before.astype(BF), wide.astype(BF), after.astype(BF)


def conv_kernel(first, last, refs, packed, *args):
    ref = dict(zip(refs, args))
    frame, hid = ref["frame"], ref["hid"]
    cell_out, spread = ref["cell_out"], ref["spread"]
    ring = "strips_hid" in ref
    step = pl.program_id(0)
    depth, cols, latent = frame.shape
    width = hid.shape[2]
    chans = latent + width
    loads = []
    if "weights" in ref:
        size = ref["weights"].shape[0] // LOADS
        for place in range(LOADS):
            part = pl.ds(place * size, size)
            loads.append(
                pltpu.make_async_copy(ref["weights"].at[part], ref["held"].at[part], ref["sem"].at[place])
            )

    if loads:

        @pl.when(step == 0)
        def _():
            for load in loads:
                load.start()

    if ring:

        @pl.when(step == 0)
        def _():
            for side, strip, frames_beside in (("left", 0, "frame_left"), ("right", 3, "frame_right")):
                ref[side][:, :latent] = ref[frames_beside][0, 0].astype(F32)
                ref[side][:, latent:] = ref["strips_hid"][strip]

    block = first + step
    base = block * depth
    top, bot = block == 0, block == last
    for pos in range(depth + 2):
        if pos == 0:
            x, h = ref["frame_prev"][0].astype(F32), ref["hid_prev"][0].astype(F32)
        elif pos == depth + 1:
            x, h = ref["frame_next"][0].astype(F32), ref["hid_next"][0].astype(F32)
        else:
            x, h = frame[pos - 1].astype(F32), hid[pos - 1].astype(F32)
        low = high = jnp.zeros((1, chans), F32)
        if ring:
            here = pl.ds(base + pos + 1, 1)
            low, high = ref["left"][here, :], ref["right"][here, :]
            place = lax.broadcasted_iota(jnp.int32, h.shape, 0)
            h = jnp.where(place == 0, ref["strips_hid"][1, here, :], h)
            h = jnp.where(place == cols - 1, ref["strips_hid"][2, here, :], h)
            for spot, edge, line in ((0, top, 0), (1, top, 1), (depth, bot, 2), (depth + 1, bot, 3)):
                if pos == spot:
                    h = jnp.where(edge, ref["lines_hid"][line], h)
            if pos == 0:
                x = jnp.where(top, ref["frame_top"][0, :cols].astype(F32), x)
            if pos == depth + 1:
                x = jnp.where(bot, ref["frame_bot"][0, :cols].astype(F32), x)
        elif pos == 0:
            x, h = jnp.where(top, 0.0, x), jnp.where(top, 0.0, h)
        elif pos == depth + 1:
            x, h = jnp.where(bot, 0.0, x), jnp.where(bot, 0.0, h)
        for part, start in ((x, 0), (h, latent)):
            size = part.shape[1]
            pieces = three_columns(part, low[:, start : start + size], high[:, start : start + size])
            for tap in range(3):
                spread[pos, :, tap * chans + start : tap * chans + start + size] = pieces[tap]

    if loads:

        @pl.when(step == 0)
        def _():
            for load in loads:
                load.wait()

    lhs = jnp.concatenate(
        [spread[tap : tap + depth].reshape(depth * cols, 3 * chans) for tap in range(3)], axis=1
    )
    gates = jnp.dot(lhs, ref["held"][...], preferred_element_type=F32) + ref["bias"][...]
    for row in range(depth):
        cell_prev = ref["cell"][row]
        if ring:
            here = pl.ds(base + row + 2, 1)
            place = lax.broadcasted_iota(jnp.int32, cell_prev.shape, 0)
            cell_prev = jnp.where(place == 0, ref["strips_cell"][1, here, :], cell_prev)
            cell_prev = jnp.where(place == cols - 1, ref["strips_cell"][2, here, :], cell_prev)
            if row == 0:
                cell_prev = jnp.where(top, ref["lines_cell"][1], cell_prev)
            if row == depth - 1:
                cell_prev = jnp.where(bot, ref["lines_cell"][2], cell_prev)
        new_cell, new_hidden = lstm(gates[row * cols : (row + 1) * cols], cell_prev)
        cell_out[row] = new_cell
        hid_out = ref["hid_out"]
        if not packed:
            hid_out[row] = new_hidden.astype(BF)
            continue
        owners_x, piece_y = hid_out.shape[1:3]
        local_m, piece_x = packed
        line = step * depth + row
        for owner in range(owners_x):
            picked = [
                new_hidden[(m * owners_x + owner) * piece_x : (m * owners_x + owner + 1) * piece_x]
                for m in range(local_m)
            ]
            hid_out[lax.div(line, piece_y), owner, lax.rem(line, piece_y)] = jnp.concatenate(picked, axis=0).astype(BF)


def whole(array):
    return pl.BlockSpec(array.shape, lambda *step: (0,) * array.ndim)


def conv_step(frames, part, hid, cell, ring, weights, bias, extent, depth, names, out_shapes, out_specs, packed, carry, load):
    rows, cols, width = hid.shape
    latent = weights.shape[0] // 9 - width
    first, count = extent[0] // depth, extent[1] // depth
    last = rows // depth - 1

    def rowed(size, channels, channel, index):
        return pl.BlockSpec((size, cols, channels), lambda step: (index(first + step), 0, channel))

    def before(block):
        return jnp.maximum(block * depth - 1, 0)

    def after(block):
        return jnp.minimum(block * depth + depth, rows - 1)

    inputs = {
        "frame": (frames, rowed(depth, latent, part, lambda block: block)),
        "frame_prev": (frames, rowed(1, latent, part, before)),
        "frame_next": (frames, rowed(1, latent, part, after)),
        "hid": (hid, rowed(depth, width, 0, lambda block: block)),
        "hid_prev": (hid, rowed(1, width, 0, before)),
        "hid_next": (hid, rowed(1, width, 0, after)),
        "cell": (cell, rowed(depth, width, 0, lambda block: block)),
        "bias": (bias, whole(bias)),
    }
    if load:
        inputs["weights"] = weights, pl.BlockSpec(memory_space=pl.ANY)
    else:
        inputs["held"] = weights, pl.BlockSpec(memory_space=pltpu.VMEM)
    inputs |= ring
    aliases = {}
    for place, array in enumerate(carry):
        if array is not None:
            aliases[len(inputs)] = place
            inputs[f"carry{place}"] = (array, pl.BlockSpec(memory_space=pl.ANY))
    refs = [*inputs, *names, "spread"]
    scratch = [pltpu.VMEM((depth + 2, cols, 3 * (latent + width)), BF)]
    if ring:
        refs += ["left", "right"]
        scratch += [pltpu.VMEM((ring["strips_hid"][0].shape[1], latent + width), F32)] * 2
    if load:
        refs += ["held", "sem"]
        scratch += [pltpu.VMEM(weights.shape, BF), pltpu.SemaphoreType.DMA((LOADS,))]
    cells = extent[1] * cols
    return pl.pallas_call(
        functools.partial(conv_kernel, first, last, refs, packed),
        grid=(count,),
        in_specs=[spec for _, spec in inputs.values()],
        out_specs=out_specs,
        out_shape=out_shapes,
        scratch_shapes=scratch,
        input_output_aliases=aliases,
        compiler_params=pltpu.CompilerParams(vmem_limit_bytes=VMEM_ALL if load else VMEM_LIMIT),
        cost_estimate=pl.CostEstimate(
            flops=2 * cells * weights.size, bytes_accessed=2 * weights.size + cells * 2048, transcendentals=cells * width * 5
        ),
    )(*(array for array, _ in inputs.values()))


def ring_kernel(
    rows, above, below, frame_top, frame_bot, hid_top, hid_bot, cell_top, cell_bot, strips, weights, bias,
    line_hid, line_cell, strip_hid, strip_cell,
):
    latent, width = frame_top.shape[2], hid_top.shape[2]
    chans = latent + width
    cols, length = frame_top.shape[1], strips.shape[2]
    low, high = strips[0, 1, :, :chans].astype(F32), strips[1, 2, :, :chans].astype(F32)

    def beside(ref, row):
        line = ref[row, :cols].astype(F32)
        return line[:, :chans], line[:, chans : chans + width]

    def within(frame, hid, cell, row):
        return jnp.concatenate([frame[row].astype(F32), hid[row].astype(F32)], axis=1), cell[row]

    tops = [beside(above, 0), beside(above, 1)] + [within(frame_top, hid_top, cell_top, row) for row in range(2)]
    bots = [within(frame_bot, hid_bot, cell_bot, row) for row in range(2)] + [beside(below, 0), beside(below, 1)]
    parts, held = [], []
    for lead, lines in ((0, tops), (rows, bots)):
        pieces = []
        for row in range(4):
            at = lead + row
            pieces.append(three_columns(lines[row][0], low[at : at + 1], high[at : at + 1]))
        for row in range(2):
            parts.append(jnp.concatenate([pieces[row + tap][col] for tap in range(3) for col in range(3)], axis=1))
            held.append(lines[row + 1][1])
    for side in range(2):
        rolled = []
        for col in range(4):
            wide = strips[side, col, :, :chans].astype(F32)
            rolled.append((pltpu.roll(wide, 1, axis=0), wide, pltpu.roll(wide, length - 1, axis=0)))
        for col in range(2):
            parts.append(
                jnp.concatenate([rolled[col + tap][row].astype(BF) for row in range(3) for tap in range(3)], axis=1)
            )
            held.append(strips[side, col + 1, :, chans : chans + width].astype(F32))
    row_at, col_at = lax.axis_index("gy"), lax.axis_index("gx")
    upper = (row_at > 0).astype(F32)
    lower = (row_at < lax.axis_size("gy") - 1).astype(F32)
    before = (col_at > 0).astype(F32)
    after = (col_at < lax.axis_size("gx") - 1).astype(F32)
    spot = lax.broadcasted_iota(jnp.int32, (length, width), 0)
    inside = jnp.where(spot == 1, upper, jnp.where(spot == rows + 2, lower, 1.0))
    keep = [upper, 1.0, 1.0, lower, inside * before, inside, inside, inside * after]
    lhs = jnp.concatenate(parts, axis=0)
    gates = jnp.dot(lhs, weights[...], preferred_element_type=F32) + bias[...]
    start = 0
    for place in range(8):
        hid, cell = (line_hid, line_cell) if place < 4 else (strip_hid, strip_cell)
        size = hid.shape[1]
        new_cell, hidden = lstm(gates[start : start + size], held[place])
        hid[place % 4] = hidden.astype(BF).astype(F32) * keep[place]
        cell[place % 4] = new_cell
        start += size


def block_kernel(x, w_qkv, w_out, w_up, w_down, out, flat, back, keys_t, own_low, own_high, own_values, ones):
    group = GRID * GRID
    embed = w_out.shape[0]
    tile = embed // 2

    @pl.when((pl.program_id(0) == 0) & (pl.program_id(1) == 0))
    def _():
        def fill(target, down, across, add):
            above = lax.broadcasted_iota(jnp.int32, target.shape, 0) // down
            along = lax.broadcasted_iota(jnp.int32, target.shape, 1) // across
            target[...] = (above == along + add).astype(F32).astype(BF)

        fill(own_low, HDIM, group, 0)
        fill(own_high, HDIM, group, HEADS // 4)
        fill(own_values, group, HDIM, 0)
        fill(ones, group, group, 0)
        keys_t[...] = w_qkv[:, embed : 2 * embed].astype(F32).T.astype(BF)

    flat[...] = x[...].astype(F32).reshape(flat.shape)
    groups = flat.shape[0] // group
    cells = jnp.concatenate([flat[pl.ds(g, group, stride=groups), :] for g in range(groups)], axis=0)
    normed = layer_norm(cells).astype(BF)
    queries = jnp.dot(normed, w_qkv[:, :embed], preferred_element_type=F32).astype(BF)
    values = jnp.dot(normed, w_qkv[:, 2 * embed :], preferred_element_type=F32).astype(BF)
    keys = lax.dot_general(keys_t[...], normed, (((1,), (1,)), ((), ())), preferred_element_type=F32)
    side = lax.broadcasted_iota(jnp.int32, (embed, 2 * group), 1) < group
    raised = [[], []]
    for pair in range(groups // 2):
        both = keys[:, pair * 2 * group : (pair + 1) * 2 * group]
        turned = pltpu.roll(both, group, axis=1)
        for place, twice in enumerate((jnp.where(side, both, turned), jnp.where(side, turned, both))):
            twice = twice.astype(BF)
            start = (2 * pair + place) * group
            for half in range(2):
                part = twice[half * tile : (half + 1) * tile]
                spread = jnp.concatenate([part * own_low[...], part * own_high[...]], axis=1)
                scores = jnp.dot(
                    queries[start : start + group, half * tile : (half + 1) * tile], spread, preferred_element_type=F32
                )
                raised[half].append(jnp.minimum(jnp.exp2(scores * (LOG2E * HDIM**-0.5)), BF_MAX).astype(BF))
    heads = []
    for half in range(2):
        part = jnp.concatenate(raised[half], axis=0)
        total = jnp.dot(part, ones[...], preferred_element_type=F32)
        attn = (part.astype(F32) * pl.reciprocal(total)).astype(BF)
        column = []
        for g in range(groups):
            held = values[g * group : (g + 1) * group, half * tile : (half + 1) * tile]
            spread = jnp.concatenate([held] * (HEADS // 2), axis=0) * own_values[...]
            column.append(
                jnp.dot(attn[g * group : (g + 1) * group], spread, preferred_element_type=F32).astype(BF)
            )
        heads.append(jnp.concatenate(column, axis=0))
    heads = jnp.concatenate(heads, axis=1)
    attended = jnp.dot(heads, w_out[...], preferred_element_type=F32).astype(BF)
    mixed = cells + attended.astype(F32)
    normed_two = layer_norm(mixed).astype(BF)
    up = jnp.dot(normed_two, w_up[...], preferred_element_type=F32)
    bent = jnp.tanh(up * (0.7978845608 + (0.7978845608 * 0.044715) * (up * up)))
    half_up = 0.5 * up
    expanded = (half_up + half_up * bent).astype(BF)
    result = mixed + jnp.dot(expanded, w_down[...], preferred_element_type=F32)
    for g in range(groups):
        back[pl.ds(g, group, stride=groups), :] = result[g * group : (g + 1) * group]
    out[...] = back[...].reshape(x.shape).astype(BF)


def block_step(moved, devices_y, devices_x, w_qkv, w_out, w_up, w_down):
    _, piece_y, piece_cols, width = moved.shape
    lanes = devices_y // GRID
    view = moved.reshape(GRID, lanes, devices_x, piece_y, piece_cols, width)
    tokens = GRID * devices_x * piece_cols
    spec = pl.BlockSpec(
        (GRID, None, devices_x, None, piece_cols, width), lambda i, j: (0, i, 0, j, 0, 0)
    )

    total = lanes * piece_y * tokens
    out = pl.pallas_call(
        block_kernel,
        grid=(lanes, piece_y),
        in_specs=[spec, whole(w_qkv), whole(w_out), whole(w_up), whole(w_down)],
        out_specs=spec,
        out_shape=jax.ShapeDtypeStruct(view.shape, BF),
        scratch_shapes=[
            pltpu.VMEM((tokens, width), F32),
            pltpu.VMEM((tokens, width), F32),
            pltpu.VMEM((w_out.shape[0], width), BF),
            pltpu.VMEM((HEADS // 2 * HDIM, 2 * GRID * GRID), BF),
            pltpu.VMEM((HEADS // 2 * HDIM, 2 * GRID * GRID), BF),
            pltpu.VMEM((HEADS // 2 * GRID * GRID, HEADS // 2 * HDIM), BF),
            pltpu.VMEM((HEADS // 2 * GRID * GRID, HEADS // 2 * GRID * GRID), BF),
        ],
        compiler_params=pltpu.CompilerParams(vmem_limit_bytes=VMEM_LIMIT),
        cost_estimate=pl.CostEstimate(
            flops=total * 3_000_000, bytes_accessed=total * width * 4 + 800_000, transcendentals=total * 1100
        ),
    )(view, w_qkv, w_out, w_up, w_down)
    return out.reshape(moved.shape)


def unpack_kernel(local_m, piece_x, *refs):
    src, out = refs[0], refs[-1]
    owners_y, owners_x, piece_y, _, width = src.shape
    for owner_y in range(owners_y):
        for row in range(piece_y):
            wide = src[owner_y, :, row].astype(F32)
            out[owner_y * piece_y + row] = jnp.concatenate(
                [wide[owner, m * piece_x : (m + 1) * piece_x] for m in range(local_m) for owner in range(owners_x)],
                axis=0,
            ).astype(BF)


def unpack_step(landed, carry, start, rows, cols, local_m, piece_x):
    owners_y, owners_x, piece_y, _, width = landed.shape
    depth = owners_y * piece_y
    specs = [pl.BlockSpec(landed.shape, lambda i: (0,) * landed.ndim)]
    operands = [landed]
    aliases = {}
    if carry is not None:
        specs.append(pl.BlockSpec(memory_space=pl.ANY))
        operands.append(carry)
        aliases = {1: 0}
    return pl.pallas_call(
        functools.partial(unpack_kernel, local_m, piece_x),
        grid=(1,),
        in_specs=specs,
        out_specs=pl.BlockSpec((depth, cols, width), lambda i: (start // depth, 0, 0)),
        out_shape=jax.ShapeDtypeStruct((rows, cols, width), BF),
        input_output_aliases=aliases,
        compiler_params=pltpu.CompilerParams(vmem_limit_bytes=VMEM_LIMIT),
        cost_estimate=pl.CostEstimate(flops=0, bytes_accessed=depth * cols * width * 4, transcendentals=0),
    )(*operands)


def step_rows(start, extent):
    return max(size for size in range(1, 17) if extent % size == 0 and start % size == 0)


def body(frames, hidden_state, cell_state, w_gates, gate_bias, w_qkv, w_out, w_up, w_down):
    rows, cols, width = hidden_state.shape
    latent = frames.shape[2] // 2
    chans = latent + width
    held = chans + width
    devices_y, devices_x = lax.axis_size("gy"), lax.axis_size("gx")
    local_m = GRID // devices_x
    piece_x = cols // local_m // devices_x
    weights = w_gates.reshape(-1, w_gates.shape[3])
    bias = gate_bias.reshape(1, -1)

    every, left_two, right_two = slice(None), slice(0, 2), slice(cols - 2, cols)
    top_two, bot_two = slice(0, 2), slice(rows - 2, rows)
    edges = ((every, left_two), (every, right_two), (top_two, every), (bot_two, every))
    edge_cells = lax.optimization_barrier(tuple(cell_state[edge] for edge in edges))

    def pack(edge, cells):
        return jnp.concatenate(
            [frames[edge][:, :, :latent], hidden_state[edge], cells.astype(BF), frames[edge][:, :, latent:]], axis=-1
        )

    def shifted(value, axis, step):
        count = lax.axis_size(axis)
        pairs = [(i, i + step) for i in range(count) if 0 <= i + step < count]
        return lax.ppermute(value, axis, pairs)

    side_left, side_right, line_top, line_bot = (pack(edge, cells) for edge, cells in zip(edges, edge_cells))
    from_left = shifted(side_right, "gx", 1)
    from_right = shifted(side_left, "gx", -1)
    to_down = jnp.concatenate([line_bot, from_left[-2:], from_right[-2:]], axis=1)
    to_up = jnp.concatenate([line_top, from_left[:2], from_right[:2]], axis=1)

    tile_shapes = (jax.ShapeDtypeStruct((rows, cols, width), BF), jax.ShapeDtypeStruct((rows, cols, width), F32))
    carry = ()
    for start, extent in ((0, rows // 2), (rows // 2, rows - rows // 2)):
        depth = step_rows(start, extent)
        spec = pl.BlockSpec((depth, cols, width), lambda step, first=start // depth: (first + step, 0, 0))
        if carry:
            *carry, to_down, to_up = lax.optimization_barrier((*carry, to_down, to_up))
            from_up, from_down = shifted(to_down, "gy", 1), shifted(to_up, "gy", -1)
        carry = conv_step(
            frames, 0, hidden_state, cell_state, {}, weights, bias, (start, extent), depth, ("hid_out", "cell_out"),
            tile_shapes, (spec, spec), None, carry, False,
        )
    hidden_one, cell_one = carry

    def column(at, middle):
        return jnp.concatenate([from_up[:, at], middle, from_down[:, at]], axis=0)

    columns = [
        column(cols, from_left[:, 0]),
        column(cols + 1, from_left[:, 1]),
        column(0, side_left[:, 0]),
        column(1, side_left[:, 1]),
        column(cols - 2, side_right[:, 0]),
        column(cols - 1, side_right[:, 1]),
        column(cols + 2, from_right[:, 0]),
        column(cols + 3, from_right[:, 1]),
    ]
    length = -(-(rows + 4) // 16) * 16
    strips = jnp.stack(columns).reshape(2, 4, rows + 4, held + latent)
    strips = jnp.pad(strips, ((0, 0), (0, 0), (0, length - rows - 4), (0, 0)))

    def two_rows(channels, at):
        return pl.BlockSpec((2, cols, channels), lambda step: (at, 0, 0))

    last_two = rows // 2 - 1
    line_shape = jax.ShapeDtypeStruct((4, cols, width), F32)
    strip_shape = jax.ShapeDtypeStruct((4, length, width), F32)
    line_hid, line_cell, strip_hid, strip_cell = pl.pallas_call(
        functools.partial(ring_kernel, rows),
        grid=(1,),
        in_specs=[
            whole(from_up), whole(from_down), two_rows(latent, 0), two_rows(latent, last_two), two_rows(width, 0),
            two_rows(width, last_two), two_rows(width, 0), two_rows(width, last_two), whole(strips),
            pl.BlockSpec(memory_space=pltpu.VMEM),            whole(bias),
        ],
        out_specs=[whole(line_shape), whole(line_shape), whole(strip_shape), whole(strip_shape)],
        out_shape=[line_shape, line_shape, strip_shape, strip_shape],
        compiler_params=pltpu.CompilerParams(vmem_limit_bytes=VMEM_LIMIT),
        cost_estimate=pl.CostEstimate(flops=16 * length * weights.size, bytes_accessed=2 * weights.size, transcendentals=0),
    )(
        from_up, from_down, frames, frames, hidden_state, hidden_state, cell_state, cell_state, strips, weights, bias
    )

    second = held // latent
    beside = (1, 1, length, latent)
    line = (1, from_up.shape[1], latent)
    ring = {name: (array, whole(array)) for name, array in (
        ("strips_hid", strip_hid), ("strips_cell", strip_cell), ("lines_hid", line_hid), ("lines_cell", line_cell)
    )}
    ring["frame_left"] = strips, pl.BlockSpec(beside, lambda step: (0, 1, 0, second))
    ring["frame_right"] = strips, pl.BlockSpec(beside, lambda step: (1, 2, 0, second))
    ring["frame_top"] = from_up, pl.BlockSpec(line, lambda step: (1, 0, second))
    ring["frame_bot"] = from_down, pl.BlockSpec(line, lambda step: (0, 0, second))

    pieces = rows // devices_y
    piece_cols = local_m * piece_x
    moved, start, carry = [], 0, ()
    for piece_y in (pieces - pieces // 2, pieces // 2):
        extent = piece_y * devices_y
        depth = step_rows(start, extent)
        sent_shape = jax.ShapeDtypeStruct((devices_y, devices_x, piece_y, piece_cols, width), BF)
        spec = pl.BlockSpec((depth, cols, width), lambda step, first=start // depth: (first + step, 0, 0))
        sent, cell_out = conv_step(
            frames, 1, hidden_one, cell_one, ring, weights, bias, (start, extent), depth, ("hid_out", "cell_out"),
            (sent_shape, tile_shapes[1]), (whole(sent_shape), spec), (local_m, piece_x), carry, bool(carry),
        )
        carry = (None, cell_out)
        sent = sent.reshape(devices_y * devices_x, piece_y, piece_cols, width)
        moved.append((start, lax.all_to_all(sent, ("gy", "gx"), split_axis=0, concat_axis=0, tiled=True)))
        start += extent
    landed = []
    for start, value in moved:
        done = block_step(value, devices_y, devices_x, w_qkv, w_out, w_up, w_down)
        landed.append((start, lax.all_to_all(done, ("gy", "gx"), split_axis=0, concat_axis=0, tiled=True)))
    result = None
    for start, value in landed:
        view = value.reshape(devices_y, devices_x, *value.shape[1:])
        result = unpack_step(view, result, start, rows, cols, local_m, piece_x)
    return result, cell_out


def solution(mesh):
    tiled = P("gy", "gx", None)
    in_specs = (tiled, tiled, tiled, P(), P(), P(), P(), P(), P())
    return jax.shard_map(body, mesh=mesh, in_specs=in_specs, out_specs=(tiled, tiled), check_vma=False)
```

```python
import functools

import jax
import jax.numpy as jnp
from jax import lax
from jax.experimental import pallas as pl
from jax.experimental.pallas import tpu as pltpu
from jax.sharding import PartitionSpec as P

HEADS = 8
HDIM = 32
GRID = 8
BF = jnp.bfloat16
F32 = jnp.float32
LOG2E = 1.4426950408889634
BF_MAX = 3.3895313892515355e38
VMEM_LIMIT = 32 * 1024 * 1024
VMEM_ALL = 60 * 1024 * 1024
LOADS = 9
LANES = 128


def sigmoid(x):
    return 0.5 * jnp.tanh(0.5 * x) + 0.5


def lstm(gates, cell_prev):
    width = cell_prev.shape[-1]
    in_gate = sigmoid(gates[:, 0:width])
    forget_gate = sigmoid(gates[:, width : 2 * width])
    candidate = jnp.tanh(gates[:, 2 * width : 3 * width])
    out_gate = sigmoid(gates[:, 3 * width :])
    cell = forget_gate * cell_prev + in_gate * candidate
    return cell, out_gate * jnp.tanh(cell)


def layer_norm(values):
    center = values - jnp.mean(values, axis=-1, keepdims=True)
    spread = jnp.mean(center * center, axis=-1, keepdims=True)
    return center * lax.rsqrt(spread + 1e-05)


def three_columns(wide, left, right):
    count = wide.shape[0]
    place = lax.broadcasted_iota(jnp.int32, wide.shape, 0)
    before = jnp.where(place == 0, left, pltpu.roll(wide, 1, axis=0))
    after = jnp.where(place == count - 1, right, pltpu.roll(wide, count - 1, axis=0))
    return before.astype(BF), wide.astype(BF), after.astype(BF)


def conv_kernel(first, last, refs, packed, *args):
    ref = dict(zip(refs, args))
    frame, hid = ref["frame"], ref["hid"]
    cell_out, spread = ref["cell_out"], ref["spread"]
    ring = "strips_hid" in ref
    step = pl.program_id(0)
    depth, cols, latent = frame.shape
    width = hid.shape[2]
    chans = latent + width
    loads = []
    if "weights" in ref:
        size = ref["weights"].shape[0] // LOADS
        for place in range(LOADS):
            part = pl.ds(place * size, size)
            loads.append(
                pltpu.make_async_copy(ref["weights"].at[part], ref["held"].at[part], ref["sem"].at[place])
            )

    if loads:

        @pl.when(step == 0)
        def _():
            for load in loads:
                load.start()

    if ring:

        @pl.when(step == 0)
        def _():
            for place, side in enumerate(("left", "right")):
                ref[side][:, :latent] = ref["beside"][place]
                ref[side][:, latent:] = ref["strips_hid"][3 * place]

    block = first + step
    base = block * depth
    top, bot = block == 0, block == last
    for pos in range(depth + 2):
        if pos == 0:
            x, h = ref["frame_prev"][0].astype(F32), ref["hid_prev"][0].astype(F32)
        elif pos == depth + 1:
            x, h = ref["frame_next"][0].astype(F32), ref["hid_next"][0].astype(F32)
        else:
            x, h = frame[pos - 1].astype(F32), hid[pos - 1].astype(F32)
        low = high = jnp.zeros((1, chans), F32)
        if ring:
            here = pl.ds(base + pos + 1, 1)
            low, high = ref["left"][here, :], ref["right"][here, :]
            place = lax.broadcasted_iota(jnp.int32, h.shape, 0)
            h = jnp.where(place == 0, ref["strips_hid"][1, here, :], h)
            h = jnp.where(place == cols - 1, ref["strips_hid"][2, here, :], h)
            for spot, edge, line in ((0, top, 0), (1, top, 1), (depth, bot, 2), (depth + 1, bot, 3)):
                if pos == spot:
                    h = jnp.where(edge, ref["lines_hid"][line], h)
            if pos == 0:
                x = jnp.where(top, ref["frame_top"][0, :cols].astype(F32), x)
            if pos == depth + 1:
                x = jnp.where(bot, ref["frame_bot"][0, :cols].astype(F32), x)
        elif pos == 0:
            x, h = jnp.where(top, 0.0, x), jnp.where(top, 0.0, h)
        elif pos == depth + 1:
            x, h = jnp.where(bot, 0.0, x), jnp.where(bot, 0.0, h)
        for part, start in ((x, 0), (h, latent)):
            size = part.shape[1]
            pieces = three_columns(part, low[:, start : start + size], high[:, start : start + size])
            for tap in range(3):
                spread[pos, :, tap * chans + start : tap * chans + start + size] = pieces[tap]

    if loads:

        @pl.when(step == 0)
        def _():
            for load in loads:
                load.wait()

    lhs = jnp.concatenate(
        [spread[tap : tap + depth].reshape(depth * cols, 3 * chans) for tap in range(3)], axis=1
    )
    gates = jnp.dot(lhs, ref["held"][...], preferred_element_type=F32) + ref["bias"][...]
    for row in range(depth):
        cell_prev = ref["cell"][row]
        if ring:
            here = pl.ds(base + row + 2, 1)
            place = lax.broadcasted_iota(jnp.int32, cell_prev.shape, 0)
            cell_prev = jnp.where(place == 0, ref["strips_cell"][1, here, :], cell_prev)
            cell_prev = jnp.where(place == cols - 1, ref["strips_cell"][2, here, :], cell_prev)
            if row == 0:
                cell_prev = jnp.where(top, ref["lines_cell"][1], cell_prev)
            if row == depth - 1:
                cell_prev = jnp.where(bot, ref["lines_cell"][2], cell_prev)
        new_cell, new_hidden = lstm(gates[row * cols : (row + 1) * cols], cell_prev)
        cell_out[row] = new_cell
        hid_out = ref["hid_out"]
        if not packed:
            hid_out[row] = new_hidden.astype(BF)
            continue
        owners_x, piece_y = hid_out.shape[1:3]
        local_m, piece_x = packed
        line = step * depth + row
        for owner in range(owners_x):
            picked = [
                new_hidden[(m * owners_x + owner) * piece_x : (m * owners_x + owner + 1) * piece_x]
                for m in range(local_m)
            ]
            hid_out[lax.div(line, piece_y), owner, lax.rem(line, piece_y)] = jnp.concatenate(picked, axis=0).astype(BF)


def whole(array):
    return pl.BlockSpec(array.shape, lambda *step: (0,) * array.ndim)


def conv_step(frames, part, hid, cell, ring, weights, bias, extent, depth, names, out_shapes, out_specs, packed, carry, load):
    rows, cols, width = hid.shape
    latent = weights.shape[0] // 9 - width
    first, count = extent[0] // depth, extent[1] // depth
    last = rows // depth - 1

    def rowed(size, channels, channel, index):
        return pl.BlockSpec((size, cols, channels), lambda step: (index(first + step), 0, channel))

    def before(block):
        return jnp.maximum(block * depth - 1, 0)

    def after(block):
        return jnp.minimum(block * depth + depth, rows - 1)

    inputs = {
        "frame": (frames, rowed(depth, latent, part, lambda block: block)),
        "frame_prev": (frames, rowed(1, latent, part, before)),
        "frame_next": (frames, rowed(1, latent, part, after)),
        "hid": (hid, rowed(depth, width, 0, lambda block: block)),
        "hid_prev": (hid, rowed(1, width, 0, before)),
        "hid_next": (hid, rowed(1, width, 0, after)),
        "cell": (cell, rowed(depth, width, 0, lambda block: block)),
        "bias": (bias, whole(bias)),
    }
    if load:
        inputs["weights"] = weights, pl.BlockSpec(memory_space=pl.ANY)
    else:
        inputs["held"] = weights, pl.BlockSpec(memory_space=pltpu.VMEM)
    inputs |= ring
    aliases = {}
    for place, array in enumerate(carry):
        if array is not None:
            aliases[len(inputs)] = place
            inputs[f"carry{place}"] = (array, pl.BlockSpec(memory_space=pl.ANY))
    refs = [*inputs, *names, "spread"]
    scratch = [pltpu.VMEM((depth + 2, cols, 3 * (latent + width)), BF)]
    if ring:
        refs += ["left", "right"]
        scratch += [pltpu.VMEM((ring["strips_hid"][0].shape[1], latent + width), F32)] * 2
    if load:
        refs += ["held", "sem"]
        scratch += [pltpu.VMEM(weights.shape, BF), pltpu.SemaphoreType.DMA((LOADS,))]
    cells = extent[1] * cols
    return pl.pallas_call(
        functools.partial(conv_kernel, first, last, refs, packed),
        grid=(count,),
        in_specs=[spec for _, spec in inputs.values()],
        out_specs=out_specs,
        out_shape=out_shapes,
        scratch_shapes=scratch,
        input_output_aliases=aliases,
        compiler_params=pltpu.CompilerParams(vmem_limit_bytes=VMEM_ALL if load else VMEM_LIMIT),
        cost_estimate=pl.CostEstimate(
            flops=2 * cells * weights.size, bytes_accessed=2 * weights.size + cells * 2048, transcendentals=cells * width * 5
        ),
    )(*(array for array, _ in inputs.values()))


def pack_kernel(
    frame_low, frame_high, frame_top, frame_bot, hid_low, hid_high, hid_top, hid_bot,
    cell_low, cell_high, cell_top, cell_bot, side_low, side_high, line_top, line_bot, flat,
):
    latent, width = frame_low.shape[2] // 2, hid_low.shape[2]
    chans = latent + width
    places = ((0, 0, latent), (chans + width, latent, latent))
    for out, frame, hid, cell in (
        (line_top, frame_top, hid_top, cell_top),
        (line_bot, frame_bot, hid_bot, cell_bot),
    ):
        for to, start, size in places:
            out[:, :, to : to + size] = frame[:, :, start : start + size]
        out[:, :, latent:chans] = hid[...]
        out[:, :, chans : chans + width] = cell[...].astype(BF)
    for out, frame, hid, cell, first, start in (
        (side_low, frame_low, hid_low, cell_low, 0, 0),
        (side_high, frame_high, hid_high, cell_high, frame_high.shape[1] - 8, 6),
    ):
        tall = frame.shape[0]
        near = slice(first, first + 8)
        for slab in range(out.shape[2] // LANES):
            to = slab * LANES
            if to < latent or to >= chans + width:
                begin = to if to < latent else to - 2 * width
                part = frame[:, near, begin : begin + LANES].astype(F32)
            elif to < chans:
                part = hid[:, near, to - latent : to - latent + LANES].astype(F32)
            else:
                part = cell[:, :, to - chans : to - chans + LANES]
            flat[...] = part.reshape(tall * 8, LANES)
            for place in range(2):
                out[place, :, to : to + LANES] = flat[pl.ds(start + place, tall, stride=8), :].astype(BF)


def pack_step(frames, hid, cell):
    rows, cols, width = hid.shape
    span = frames.shape[2]
    near = 16

    def edge(array, size):
        deep = array.shape[2]
        return [
            pl.BlockSpec((rows, size, deep), lambda step: (0, 0, 0)),
            pl.BlockSpec((rows, size, deep), lambda step: (0, cols // size - 1, 0)),
            pl.BlockSpec((2, cols, deep), lambda step: (0, 0, 0)),
            pl.BlockSpec((2, cols, deep), lambda step: (rows // 2 - 1, 0, 0)),
        ]

    deep = span + 2 * width
    shapes = [jax.ShapeDtypeStruct((2, rows, deep), BF)] * 2 + [jax.ShapeDtypeStruct((2, cols, deep), BF)] * 2
    return pl.pallas_call(
        pack_kernel,
        grid=(1,),
        in_specs=[*edge(frames, near), *edge(hid, near), *edge(cell, 8)],
        out_specs=[whole(shape) for shape in shapes],
        out_shape=shapes,
        scratch_shapes=[pltpu.VMEM((rows * 8, LANES), F32)],
        compiler_params=pltpu.CompilerParams(vmem_limit_bytes=VMEM_ALL),
        cost_estimate=pl.CostEstimate(flops=0, bytes_accessed=4_000_000, transcendentals=0),
    )(*[frames] * 4, *[hid] * 4, *[cell] * 4)


def ring_kernel(
    above, below, line_top, line_bot, from_left, from_right, side_left, side_right, weights, bias,
    line_hid, line_cell, strip_hid, strip_cell, beside, strips,
):
    width = line_hid.shape[2]
    chans = weights.shape[0] // 9
    cols, length = line_top.shape[1], strip_hid.shape[1]
    rows = from_left.shape[1]
    columns = (
        (from_left, 0, cols), (from_left, 1, cols + 1), (side_left, 0, 0), (side_left, 1, 1),
        (side_right, 0, cols - 2), (side_right, 1, cols - 1), (from_right, 0, cols + 2), (from_right, 1, cols + 3),
    )
    ends = [(ref[row].astype(F32), at + row) for ref, at in ((above, 0), (below, rows + 2)) for row in range(2)]
    strips[:, rows + 4 :, :] = jnp.zeros((8, length - rows - 4, strips.shape[2]), F32)
    for place, (source, at, end) in enumerate(columns):
        strips[place, 2 : rows + 2, :] = source[at].astype(F32)
        for value, spot in ends:
            strips[place, spot : spot + 1, :] = value[end : end + 1]
    beside[0] = strips[1, :, chans + width :]
    beside[1] = strips[6, :, chans + width :]
    low, high = strips[1, :, :chans], strips[6, :, :chans]

    def line(ref, row):
        held = ref[row, :cols].astype(F32)
        return held[:, :chans], held[:, chans : chans + width]

    tops = [line(above, 0), line(above, 1), line(line_top, 0), line(line_top, 1)]
    bots = [line(line_bot, 0), line(line_bot, 1), line(below, 0), line(below, 1)]
    parts, held = [], []
    for lead, lines in ((0, tops), (rows, bots)):
        pieces = []
        for row in range(4):
            at = lead + row
            pieces.append(three_columns(lines[row][0], low[at : at + 1], high[at : at + 1]))
        for row in range(2):
            parts.append(jnp.concatenate([pieces[row + tap][col] for tap in range(3) for col in range(3)], axis=1))
            held.append(lines[row + 1][1])
    for side in range(2):
        rolled = []
        for col in range(4):
            wide = strips[4 * side + col, :, :chans]
            rolled.append((pltpu.roll(wide, 1, axis=0), wide, pltpu.roll(wide, length - 1, axis=0)))
        for col in range(2):
            parts.append(
                jnp.concatenate([rolled[col + tap][row].astype(BF) for row in range(3) for tap in range(3)], axis=1)
            )
            held.append(strips[4 * side + col + 1, :, chans : chans + width])
    row_at, col_at = lax.axis_index("gy"), lax.axis_index("gx")
    upper = (row_at > 0).astype(F32)
    lower = (row_at < lax.axis_size("gy") - 1).astype(F32)
    before = (col_at > 0).astype(F32)
    after = (col_at < lax.axis_size("gx") - 1).astype(F32)
    spot = lax.broadcasted_iota(jnp.int32, (length, width), 0)
    inside = jnp.where(spot == 1, upper, jnp.where(spot == rows + 2, lower, 1.0))
    keep = [upper, 1.0, 1.0, lower, inside * before, inside, inside, inside * after]
    lhs = jnp.concatenate(parts, axis=0)
    gates = jnp.dot(lhs, weights[...], preferred_element_type=F32) + bias[...]
    start = 0
    for place in range(8):
        hid, cell = (line_hid, line_cell) if place < 4 else (strip_hid, strip_cell)
        size = hid.shape[1]
        new_cell, hidden = lstm(gates[start : start + size], held[place])
        hid[place % 4] = hidden.astype(BF).astype(F32) * keep[place]
        cell[place % 4] = new_cell
        start += size


def block_kernel(x, w_qkv, w_out, w_up, w_down, *rest):
    out, flat, back, keys_t, own_low, own_high, own_values, ones = rest[-8:]
    group = GRID * GRID
    embed = w_out.shape[0]
    tile = embed // 2

    @pl.when((pl.program_id(0) == 0) & (pl.program_id(1) == 0))
    def _():
        def fill(target, down, across, add):
            above = lax.broadcasted_iota(jnp.int32, target.shape, 0) // down
            along = lax.broadcasted_iota(jnp.int32, target.shape, 1) // across
            target[...] = (above == along + add).astype(F32).astype(BF)

        fill(own_low, HDIM, group, 0)
        fill(own_high, HDIM, group, HEADS // 4)
        fill(own_values, group, HDIM, 0)
        fill(ones, group, group, 0)
        keys_t[...] = w_qkv[:, embed : 2 * embed].astype(F32).T.astype(BF)

    flat[...] = x[...].astype(F32).reshape(flat.shape)
    groups = flat.shape[0] // group
    cells = jnp.concatenate([flat[pl.ds(g, group, stride=groups), :] for g in range(groups)], axis=0)
    normed = layer_norm(cells).astype(BF)
    queries = jnp.dot(normed, w_qkv[:, :embed], preferred_element_type=F32).astype(BF)
    values = jnp.dot(normed, w_qkv[:, 2 * embed :], preferred_element_type=F32).astype(BF)
    keys = lax.dot_general(keys_t[...], normed, (((1,), (1,)), ((), ())), preferred_element_type=F32)
    side = lax.broadcasted_iota(jnp.int32, (embed, 2 * group), 1) < group
    raised = [[], []]
    for pair in range(groups // 2):
        both = keys[:, pair * 2 * group : (pair + 1) * 2 * group]
        turned = pltpu.roll(both, group, axis=1)
        for place, twice in enumerate((jnp.where(side, both, turned), jnp.where(side, turned, both))):
            twice = twice.astype(BF)
            start = (2 * pair + place) * group
            for half in range(2):
                part = twice[half * tile : (half + 1) * tile]
                spread = jnp.concatenate([part * own_low[...], part * own_high[...]], axis=1)
                scores = jnp.dot(
                    queries[start : start + group, half * tile : (half + 1) * tile], spread, preferred_element_type=F32
                )
                raised[half].append(jnp.minimum(jnp.exp2(scores * (LOG2E * HDIM**-0.5)), BF_MAX).astype(BF))
    heads = []
    for half in range(2):
        part = jnp.concatenate(raised[half], axis=0)
        total = jnp.dot(part, ones[...], preferred_element_type=F32)
        attn = (part.astype(F32) * pl.reciprocal(total)).astype(BF)
        column = []
        for g in range(groups):
            held = values[g * group : (g + 1) * group, half * tile : (half + 1) * tile]
            spread = jnp.concatenate([held] * (HEADS // 2), axis=0) * own_values[...]
            column.append(
                jnp.dot(attn[g * group : (g + 1) * group], spread, preferred_element_type=F32).astype(BF)
            )
        heads.append(jnp.concatenate(column, axis=0))
    heads = jnp.concatenate(heads, axis=1)
    attended = jnp.dot(heads, w_out[...], preferred_element_type=F32).astype(BF)
    mixed = cells + attended.astype(F32)
    normed_two = layer_norm(mixed).astype(BF)
    up = jnp.dot(normed_two, w_up[...], preferred_element_type=F32)
    bent = jnp.tanh(up * (0.7978845608 + (0.7978845608 * 0.044715) * (up * up)))
    half_up = 0.5 * up
    expanded = (half_up + half_up * bent).astype(BF)
    result = mixed + jnp.dot(expanded, w_down[...], preferred_element_type=F32)
    for g in range(groups):
        back[pl.ds(g, group, stride=groups), :] = result[g * group : (g + 1) * group]
    out[...] = back[...].reshape(x.shape).astype(BF)


def block_step(moved, carry, first, pieces, devices_y, devices_x, w_qkv, w_out, w_up, w_down):
    _, piece_y, piece_cols, width = moved.shape
    lanes = devices_y // GRID
    view = moved.reshape(GRID, lanes, devices_x, piece_y, piece_cols, width)
    tokens = GRID * devices_x * piece_cols
    block = (GRID, None, devices_x, None, piece_cols, width)
    operands = [view, w_qkv, w_out, w_up, w_down]
    in_specs = [pl.BlockSpec(block, lambda i, j: (0, i, 0, j, 0, 0)), *(whole(array) for array in operands[1:])]
    aliases = {}
    if carry is not None:
        aliases = {len(operands): 0}
        operands.append(carry)
        in_specs.append(pl.BlockSpec(memory_space=pl.ANY))
    total = lanes * piece_y * tokens
    return pl.pallas_call(
        block_kernel,
        grid=(lanes, piece_y),
        in_specs=in_specs,
        out_specs=pl.BlockSpec(block, lambda i, j: (0, i, 0, first + j, 0, 0)),
        out_shape=jax.ShapeDtypeStruct((GRID, lanes, devices_x, pieces, piece_cols, width), BF),
        scratch_shapes=[
            pltpu.VMEM((tokens, width), F32),
            pltpu.VMEM((tokens, width), F32),
            pltpu.VMEM((w_out.shape[0], width), BF),
            pltpu.VMEM((HEADS // 2 * HDIM, 2 * GRID * GRID), BF),
            pltpu.VMEM((HEADS // 2 * HDIM, 2 * GRID * GRID), BF),
            pltpu.VMEM((HEADS // 2 * GRID * GRID, HEADS // 2 * HDIM), BF),
            pltpu.VMEM((HEADS // 2 * GRID * GRID, HEADS // 2 * GRID * GRID), BF),
        ],
        input_output_aliases=aliases,
        compiler_params=pltpu.CompilerParams(vmem_limit_bytes=VMEM_LIMIT),
        cost_estimate=pl.CostEstimate(
            flops=total * 3_000_000, bytes_accessed=total * width * 4 + 800_000, transcendentals=total * 1100
        ),
    )(*operands)


def unpack_kernel(shares, local_m, piece_x, src, out):
    owners_y, owners_x = src.shape[:2]
    unit = out.shape[0]
    lines, first = [], 0
    for share in shares:
        lines += [(owner_y, first + piece) for owner_y in range(owners_y) for piece in range(share)]
        first += share
    for step in range(len(lines) // unit):

        @pl.when(pl.program_id(0) == step)
        def _():
            for row, (owner_y, piece) in enumerate(lines[step * unit : (step + 1) * unit]):
                wide = src[owner_y, :, piece].astype(F32)
                parts = [
                    wide[owner, m * piece_x : (m + 1) * piece_x] for m in range(local_m) for owner in range(owners_x)
                ]
                out[row] = jnp.concatenate(parts, axis=0).astype(BF)


def unpack_step(landed, shares, cols, local_m, piece_x):
    owners_y, _, pieces, _, width = landed.shape
    rows = owners_y * pieces
    unit = 16 if rows % 16 == 0 else rows
    return pl.pallas_call(
        functools.partial(unpack_kernel, shares, local_m, piece_x),
        grid=(rows // unit,),
        in_specs=[pl.BlockSpec(memory_space=pltpu.VMEM)],
        out_specs=pl.BlockSpec((unit, cols, width), lambda step: (step, 0, 0)),
        out_shape=jax.ShapeDtypeStruct((rows, cols, width), BF),
        compiler_params=pltpu.CompilerParams(vmem_limit_bytes=VMEM_LIMIT),
        cost_estimate=pl.CostEstimate(flops=0, bytes_accessed=rows * cols * width * 4, transcendentals=0),
    )(landed)


def step_rows(start, extent, most=16):
    return max(size for size in range(1, most + 1) if extent % size == 0 and start % size == 0)


def body(frames, hidden_state, cell_state, w_gates, gate_bias, w_qkv, w_out, w_up, w_down):
    rows, cols, width = hidden_state.shape
    latent = frames.shape[2] // 2
    chans = latent + width
    held = chans + width
    devices_y, devices_x = lax.axis_size("gy"), lax.axis_size("gx")
    local_m = GRID // devices_x
    piece_x = cols // local_m // devices_x
    weights = w_gates.reshape(-1, w_gates.shape[3])
    bias = gate_bias.reshape(1, -1)

    def shifted(value, axis, step):
        count = lax.axis_size(axis)
        pairs = [(i, i + step) for i in range(count) if 0 <= i + step < count]
        return lax.ppermute(value, axis, pairs)

    side_left, side_right, line_top, line_bot = pack_step(frames, hidden_state, cell_state)
    from_left = shifted(side_right, "gx", 1)
    from_right = shifted(side_left, "gx", -1)
    from_left, from_right = lax.optimization_barrier((from_left, from_right))
    beside = jnp.concatenate([from_left, from_right], axis=0)
    to_down = jnp.concatenate([line_bot, beside[:, -2:].transpose(1, 0, 2)], axis=1)
    to_up = jnp.concatenate([line_top, beside[:, :2].transpose(1, 0, 2)], axis=1)

    tile_shapes = (jax.ShapeDtypeStruct((rows, cols, width), BF), jax.ShapeDtypeStruct((rows, cols, width), F32))
    carry = ()
    for start, extent in ((0, rows // 2), (rows // 2, rows - rows // 2)):
        depth = step_rows(start, extent)
        spec = pl.BlockSpec((depth, cols, width), lambda step, first=start // depth: (first + step, 0, 0))
        if carry:
            *carry, to_down, to_up = lax.optimization_barrier((*carry, to_down, to_up))
            from_up, from_down = shifted(to_down, "gy", 1), shifted(to_up, "gy", -1)
        carry = conv_step(
            frames, 0, hidden_state, cell_state, {}, weights, bias, (start, extent), depth, ("hid_out", "cell_out"),
            tile_shapes, (spec, spec), None, carry, False,
        )
    hidden_one, cell_one = carry

    length = -(-(rows + 4) // 16) * 16
    line_shape = jax.ShapeDtypeStruct((4, cols, width), F32)
    strip_shape = jax.ShapeDtypeStruct((4, length, width), F32)
    beside_shape = jax.ShapeDtypeStruct((2, length, latent), F32)
    shapes = (line_shape, line_shape, strip_shape, strip_shape, beside_shape)
    around = (from_up, from_down, line_top, line_bot, from_left, from_right, side_left, side_right)
    line_hid, line_cell, strip_hid, strip_cell, beside = pl.pallas_call(
        ring_kernel,
        grid=(1,),
        in_specs=[*(whole(array) for array in around), pl.BlockSpec(memory_space=pltpu.VMEM), whole(bias)],
        out_specs=[whole(shape) for shape in shapes],
        out_shape=shapes,
        scratch_shapes=[pltpu.VMEM((8, length, held + latent), F32)],
        compiler_params=pltpu.CompilerParams(vmem_limit_bytes=VMEM_LIMIT),
        cost_estimate=pl.CostEstimate(flops=16 * length * weights.size, bytes_accessed=2 * weights.size, transcendentals=0),
    )(*around, weights, bias)

    second = held // latent
    line = (1, from_up.shape[1], latent)
    ring = {name: (array, whole(array)) for name, array in (
        ("strips_hid", strip_hid), ("strips_cell", strip_cell), ("lines_hid", line_hid), ("lines_cell", line_cell),
        ("beside", beside),
    )}
    ring["frame_top"] = from_up, pl.BlockSpec(line, lambda step: (1, 0, second))
    ring["frame_bot"] = from_down, pl.BlockSpec(line, lambda step: (0, 0, second))

    pieces = rows // devices_y
    piece_cols = local_m * piece_x
    shares = (pieces - pieces // 3, pieces // 3)
    moved, start, carry = [], 0, ()
    for piece_y in shares:
        extent = piece_y * devices_y
        depth = step_rows(start, extent, 8 if carry else 16)
        sent_shape = jax.ShapeDtypeStruct((devices_y, devices_x, piece_y, piece_cols, width), BF)
        spec = pl.BlockSpec((depth, cols, width), lambda step, first=start // depth: (first + step, 0, 0))
        sent, cell_out = conv_step(
            frames, 1, hidden_one, cell_one, ring, weights, bias, (start, extent), depth,
            ("hid_out", "cell_out"), (sent_shape, tile_shapes[1]), (whole(sent_shape), spec), (local_m, piece_x), carry,
            bool(carry),
        )
        carry = (None, cell_out)
        sent = sent.reshape(devices_y * devices_x, piece_y, piece_cols, width)
        moved.append(lax.all_to_all(sent, ("gy", "gx"), split_axis=0, concat_axis=0, tiled=True))
        start += extent
    done, first = None, 0
    for piece_y, value in zip(shares, moved):
        done = block_step(value, done, first, pieces, devices_y, devices_x, w_qkv, w_out, w_up, w_down)
        first += piece_y
    done = done.reshape(devices_y * devices_x, pieces, piece_cols, width)
    landed = lax.all_to_all(done, ("gy", "gx"), split_axis=0, concat_axis=0, tiled=True)
    result = unpack_step(landed.reshape(devices_y, devices_x, *landed.shape[1:]), shares, cols, local_m, piece_x)
    return result, cell_out


def solution(mesh):
    tiled = P("gy", "gx", None)
    in_specs = (tiled, tiled, tiled, P(), P(), P(), P(), P(), P())
    return jax.shard_map(body, mesh=mesh, in_specs=in_specs, out_specs=(tiled, tiled), check_vma=False)
```

```python
import functools

import jax
import jax.numpy as jnp
from jax import lax
from jax.experimental import pallas as pl
from jax.experimental.pallas import tpu as pltpu
from jax.sharding import PartitionSpec as P

HEADS = 8
HDIM = 32
GRID = 8
BF = jnp.bfloat16
F32 = jnp.float32
LOG2E = 1.4426950408889634
BF_MAX = 3.3895313892515355e38
VMEM_LIMIT = 32 * 1024 * 1024
VMEM_ALL = 60 * 1024 * 1024
LOADS = 9
LANES = 128


def sigmoid(x):
    return 0.5 * jnp.tanh(0.5 * x) + 0.5


def lstm(gates, cell_prev):
    width = cell_prev.shape[-1]
    in_gate = sigmoid(gates[:, 0:width])
    forget_gate = sigmoid(gates[:, width : 2 * width])
    candidate = jnp.tanh(gates[:, 2 * width : 3 * width])
    out_gate = sigmoid(gates[:, 3 * width :])
    cell = forget_gate * cell_prev + in_gate * candidate
    return cell, out_gate * jnp.tanh(cell)


def layer_norm(values):
    center = values - jnp.mean(values, axis=-1, keepdims=True)
    spread = jnp.mean(center * center, axis=-1, keepdims=True)
    return center * lax.rsqrt(spread + 1e-05)


def three_columns(wide, left, right):
    count = wide.shape[0]
    place = lax.broadcasted_iota(jnp.int32, wide.shape, 0)
    before = jnp.where(place == 0, left, pltpu.roll(wide, 1, axis=0))
    after = jnp.where(place == count - 1, right, pltpu.roll(wide, count - 1, axis=0))
    return before.astype(BF), wide.astype(BF), after.astype(BF)


def conv_kernel(first, last, refs, packed, *args):
    ref = dict(zip(refs, args))
    frame, hid = ref["frame"], ref["hid"]
    cell_out, spread = ref["cell_out"], ref["spread"]
    ring = "strips_hid" in ref
    step = pl.program_id(0)
    depth, cols, latent = frame.shape
    width = hid.shape[2]
    chans = latent + width
    loads = []
    if "weights" in ref:
        size = ref["weights"].shape[0] // LOADS
        for place in range(LOADS):
            part = pl.ds(place * size, size)
            loads.append(
                pltpu.make_async_copy(ref["weights"].at[part], ref["held"].at[part], ref["sem"].at[place])
            )

    if loads:

        @pl.when(step == 0)
        def _():
            for load in loads:
                load.start()

    if ring:

        @pl.when(step == 0)
        def _():
            for place, side in enumerate(("left", "right")):
                ref[side][:, :latent] = ref["beside"][place]
                ref[side][:, latent:] = ref["strips_hid"][3 * place]

    block = first + step
    base = block * depth
    top, bot = block == 0, block == last
    for pos in range(depth + 2):
        if pos == 0:
            x, h = ref["frame_prev"][0].astype(F32), ref["hid_prev"][0].astype(F32)
        elif pos == depth + 1:
            x, h = ref["frame_next"][0].astype(F32), ref["hid_next"][0].astype(F32)
        else:
            x, h = frame[pos - 1].astype(F32), hid[pos - 1].astype(F32)
        low = high = jnp.zeros((1, chans), F32)
        if ring:
            here = pl.ds(base + pos + 1, 1)
            low, high = ref["left"][here, :], ref["right"][here, :]
            place = lax.broadcasted_iota(jnp.int32, h.shape, 0)
            h = jnp.where(place == 0, ref["strips_hid"][1, here, :], h)
            h = jnp.where(place == cols - 1, ref["strips_hid"][2, here, :], h)
            for spot, edge, line in ((0, top, 0), (1, top, 1), (depth, bot, 2), (depth + 1, bot, 3)):
                if pos == spot:
                    h = jnp.where(edge, ref["lines_hid"][line], h)
            if pos == 0:
                x = jnp.where(top, ref["frame_top"][0, :cols].astype(F32), x)
            if pos == depth + 1:
                x = jnp.where(bot, ref["frame_bot"][0, :cols].astype(F32), x)
        elif pos == 0:
            x, h = jnp.where(top, 0.0, x), jnp.where(top, 0.0, h)
        elif pos == depth + 1:
            x, h = jnp.where(bot, 0.0, x), jnp.where(bot, 0.0, h)
        for part, start in ((x, 0), (h, latent)):
            size = part.shape[1]
            pieces = three_columns(part, low[:, start : start + size], high[:, start : start + size])
            if 0 < pos <= depth and (start == 0 or not ring):
                pieces = pieces[0], (frame, hid)[start > 0][pos - 1], pieces[2]
            for tap in range(3):
                spread[pos, :, tap * chans + start : tap * chans + start + size] = pieces[tap]

    if loads:

        @pl.when(step == 0)
        def _():
            for load in loads:
                load.wait()

    gates = ref["bias"][...]
    for tap in range(3):
        lhs = spread[tap : tap + depth].reshape(depth * cols, 3 * chans)
        taps = ref["held"][tap * 3 * chans : (tap + 1) * 3 * chans, :]
        gates = gates + jnp.dot(lhs, taps, preferred_element_type=F32)
    for row in range(depth):
        cell_prev = ref["cell"][row]
        if ring:
            here = pl.ds(base + row + 2, 1)
            place = lax.broadcasted_iota(jnp.int32, cell_prev.shape, 0)
            cell_prev = jnp.where(place == 0, ref["strips_cell"][1, here, :], cell_prev)
            cell_prev = jnp.where(place == cols - 1, ref["strips_cell"][2, here, :], cell_prev)
            if row == 0:
                cell_prev = jnp.where(top, ref["lines_cell"][1], cell_prev)
            if row == depth - 1:
                cell_prev = jnp.where(bot, ref["lines_cell"][2], cell_prev)
        new_cell, new_hidden = lstm(gates[row * cols : (row + 1) * cols], cell_prev)
        cell_out[row] = new_cell
        hid_out = ref["hid_out"]
        if not packed:
            hid_out[row] = new_hidden.astype(BF)
            continue
        owners_x, piece_y = hid_out.shape[1:3]
        local_m, piece_x = packed
        line = step * depth + row
        for owner in range(owners_x):
            picked = [
                new_hidden[(m * owners_x + owner) * piece_x : (m * owners_x + owner + 1) * piece_x]
                for m in range(local_m)
            ]
            hid_out[lax.div(line, piece_y), owner, lax.rem(line, piece_y)] = jnp.concatenate(picked, axis=0).astype(BF)


def whole(array):
    return pl.BlockSpec(array.shape, lambda *step: (0,) * array.ndim)


def conv_step(frames, part, hid, cell, ring, weights, bias, extent, depth, names, out_shapes, out_specs, packed, carry, load):
    rows, cols, width = hid.shape
    latent = weights.shape[0] // 9 - width
    first, count = extent[0] // depth, extent[1] // depth
    last = rows // depth - 1

    def rowed(size, channels, channel, index):
        return pl.BlockSpec((size, cols, channels), lambda step: (index(first + step), 0, channel))

    def before(block):
        return jnp.maximum(block * depth - 1, 0)

    def after(block):
        return jnp.minimum(block * depth + depth, rows - 1)

    inputs = {
        "frame": (frames, rowed(depth, latent, part, lambda block: block)),
        "frame_prev": (frames, rowed(1, latent, part, before)),
        "frame_next": (frames, rowed(1, latent, part, after)),
        "hid": (hid, rowed(depth, width, 0, lambda block: block)),
        "hid_prev": (hid, rowed(1, width, 0, before)),
        "hid_next": (hid, rowed(1, width, 0, after)),
        "cell": (cell, rowed(depth, width, 0, lambda block: block)),
        "bias": (bias, whole(bias)),
    }
    if load:
        inputs["weights"] = weights, pl.BlockSpec(memory_space=pl.ANY)
    else:
        inputs["held"] = weights, pl.BlockSpec(memory_space=pltpu.VMEM)
    inputs |= ring
    aliases = {}
    for place, array in enumerate(carry):
        if array is not None:
            aliases[len(inputs)] = place
            inputs[f"carry{place}"] = (array, pl.BlockSpec(memory_space=pl.ANY))
    refs = [*inputs, *names, "spread"]
    scratch = [pltpu.VMEM((depth + 2, cols, 3 * (latent + width)), BF)]
    if ring:
        refs += ["left", "right"]
        scratch += [pltpu.VMEM((ring["strips_hid"][0].shape[1], latent + width), F32)] * 2
    if load:
        refs += ["held", "sem"]
        scratch += [pltpu.VMEM(weights.shape, BF), pltpu.SemaphoreType.DMA((LOADS,))]
    cells = extent[1] * cols
    return pl.pallas_call(
        functools.partial(conv_kernel, first, last, refs, packed),
        grid=(count,),
        in_specs=[spec for _, spec in inputs.values()],
        out_specs=out_specs,
        out_shape=out_shapes,
        scratch_shapes=scratch,
        input_output_aliases=aliases,
        compiler_params=pltpu.CompilerParams(vmem_limit_bytes=VMEM_ALL if load else VMEM_LIMIT),
        cost_estimate=pl.CostEstimate(
            flops=2 * cells * weights.size, bytes_accessed=2 * weights.size + cells * 2048, transcendentals=cells * width * 5
        ),
    )(*(array for array, _ in inputs.values()))


def pack_kernel(
    frame_low, frame_high, frame_top, frame_bot, hid_low, hid_high, hid_top, hid_bot,
    cell_low, cell_high, cell_top, cell_bot, send_low, send_high, side_low, side_high, line_top, line_bot, flat,
):
    latent, width = frame_low.shape[2] // 2, hid_low.shape[2]
    chans = latent + width
    places = ((0, 0, latent), (chans + width, latent, latent))
    for out, frame, hid, cell in (
        (line_top, frame_top, hid_top, cell_top),
        (line_bot, frame_bot, hid_bot, cell_bot),
    ):
        for to, start, size in places:
            out[:, :, to : to + size] = frame[:, :, start : start + size]
        out[:, :, latent:chans] = hid[...]
        out[:, :, chans : chans + width] = cell[...].astype(BF)
    for out, send, frame, hid, cell, first, start in (
        (side_low, send_low, frame_low, hid_low, cell_low, 0, 0),
        (side_high, send_high, frame_high, hid_high, cell_high, frame_high.shape[1] - 8, 6),
    ):
        tall = frame.shape[0]
        near = slice(first, first + 8)
        for slab in range(out.shape[2] // LANES):
            to = slab * LANES
            if to < latent or to >= chans + width:
                begin = to if to < latent else to - 2 * width
                part = frame[:, near, begin : begin + LANES].astype(F32)
            elif to < chans:
                part = hid[:, near, to - latent : to - latent + LANES].astype(F32)
            else:
                part = cell[:, :, to - chans : to - chans + LANES]
            send[:, :, to : to + LANES] = part[:, start : start + 2].astype(BF)
            flat[...] = part.reshape(tall * 8, LANES)
            for place in range(2):
                out[place, :, to : to + LANES] = flat[pl.ds(start + place, tall, stride=8), :].astype(BF)


def pack_step(frames, hid, cell):
    rows, cols, width = hid.shape
    span = frames.shape[2]
    near = 16

    def edge(array, size):
        deep = array.shape[2]
        return [
            pl.BlockSpec((rows, size, deep), lambda step: (0, 0, 0)),
            pl.BlockSpec((rows, size, deep), lambda step: (0, cols // size - 1, 0)),
            pl.BlockSpec((2, cols, deep), lambda step: (0, 0, 0)),
            pl.BlockSpec((2, cols, deep), lambda step: (rows // 2 - 1, 0, 0)),
        ]

    deep = span + 2 * width
    shapes = [jax.ShapeDtypeStruct((rows, 2, deep), BF)] * 2 + [jax.ShapeDtypeStruct((2, rows, deep), BF)] * 2
    shapes += [jax.ShapeDtypeStruct((2, cols, deep), BF)] * 2
    return pl.pallas_call(
        pack_kernel,
        grid=(1,),
        in_specs=[*edge(frames, near), *edge(hid, near), *edge(cell, 8)],
        out_specs=[whole(shape) for shape in shapes],
        out_shape=shapes,
        scratch_shapes=[pltpu.VMEM((rows * 8, LANES), F32)],
        compiler_params=pltpu.CompilerParams(vmem_limit_bytes=VMEM_ALL),
        cost_estimate=pl.CostEstimate(flops=0, bytes_accessed=4_000_000, transcendentals=0),
    )(*[frames] * 4, *[hid] * 4, *[cell] * 4)


def ring_kernel(
    above, below, line_top, line_bot, from_left, from_right, side_left, side_right, weights, bias,
    line_hid, line_cell, strip_hid, strip_cell, beside, strips,
):
    width = line_hid.shape[2]
    chans = weights.shape[0] // 9
    cols, length = line_top.shape[1], strip_hid.shape[1]
    rows = from_left.shape[1]
    columns = (
        (from_left, 0, cols), (from_left, 1, cols + 1), (side_left, 0, 0), (side_left, 1, 1),
        (side_right, 0, cols - 2), (side_right, 1, cols - 1), (from_right, 0, cols + 2), (from_right, 1, cols + 3),
    )
    ends = [(ref[row].astype(F32), at + row) for ref, at in ((above, 0), (below, rows + 2)) for row in range(2)]
    strips[:, rows + 4 :, :] = jnp.zeros((8, length - rows - 4, strips.shape[2]), F32)
    for place, (source, at, end) in enumerate(columns):
        strips[place, 2 : rows + 2, :] = source[at].astype(F32)
        for value, spot in ends:
            strips[place, spot : spot + 1, :] = value[end : end + 1]
    beside[0] = strips[1, :, chans + width :]
    beside[1] = strips[6, :, chans + width :]
    low, high = strips[1, :, :chans], strips[6, :, :chans]

    def line(ref, row):
        held = ref[row, :cols].astype(F32)
        return held[:, :chans], held[:, chans : chans + width]

    tops = [line(above, 0), line(above, 1), line(line_top, 0), line(line_top, 1)]
    bots = [line(line_bot, 0), line(line_bot, 1), line(below, 0), line(below, 1)]
    parts, held = [], []
    for lead, lines in ((0, tops), (rows, bots)):
        pieces = []
        for row in range(4):
            at = lead + row
            pieces.append(three_columns(lines[row][0], low[at : at + 1], high[at : at + 1]))
        for row in range(2):
            parts.append(jnp.concatenate([pieces[row + tap][col] for tap in range(3) for col in range(3)], axis=1))
            held.append(lines[row + 1][1])
    for side in range(2):
        rolled = []
        for col in range(4):
            wide = strips[4 * side + col, :, :chans]
            rolled.append((pltpu.roll(wide, 1, axis=0), wide, pltpu.roll(wide, length - 1, axis=0)))
        for col in range(2):
            parts.append(
                jnp.concatenate([rolled[col + tap][row].astype(BF) for row in range(3) for tap in range(3)], axis=1)
            )
            held.append(strips[4 * side + col + 1, :, chans : chans + width])
    row_at, col_at = lax.axis_index("gy"), lax.axis_index("gx")
    upper = (row_at > 0).astype(F32)
    lower = (row_at < lax.axis_size("gy") - 1).astype(F32)
    before = (col_at > 0).astype(F32)
    after = (col_at < lax.axis_size("gx") - 1).astype(F32)
    spot = lax.broadcasted_iota(jnp.int32, (length, width), 0)
    inside = jnp.where(spot == 1, upper, jnp.where(spot == rows + 2, lower, 1.0))
    keep = [upper, 1.0, 1.0, lower, inside * before, inside, inside, inside * after]
    lhs = jnp.concatenate(parts, axis=0)
    gates = jnp.dot(lhs, weights[...], preferred_element_type=F32) + bias[...]
    start = 0
    for place in range(8):
        hid, cell = (line_hid, line_cell) if place < 4 else (strip_hid, strip_cell)
        size = hid.shape[1]
        new_cell, hidden = lstm(gates[start : start + size], held[place])
        hid[place % 4] = hidden.astype(BF).astype(F32) * keep[place]
        cell[place % 4] = new_cell
        start += size


def block_kernel(x, w_qkv, w_out, w_up, w_down, *rest):
    out, flat, back, keys_t, own_low, own_high, own_values, ones = rest[-8:]
    group = GRID * GRID
    embed = w_out.shape[0]
    tile = embed // 2

    @pl.when((pl.program_id(0) == 0) & (pl.program_id(1) == 0))
    def _():
        def fill(target, down, across, add):
            above = lax.broadcasted_iota(jnp.int32, target.shape, 0) // down
            along = lax.broadcasted_iota(jnp.int32, target.shape, 1) // across
            target[...] = (above == along + add).astype(F32).astype(BF)

        fill(own_low, HDIM, group, 0)
        fill(own_high, HDIM, group, HEADS // 4)
        fill(own_values, group, HDIM, 0)
        fill(ones, group, group, 0)
        keys_t[...] = w_qkv[:, embed : 2 * embed].astype(F32).T.astype(BF)

    flat[...] = x[...].astype(F32).reshape(flat.shape)
    groups = flat.shape[0] // group
    cells = jnp.concatenate([flat[pl.ds(g, group, stride=groups), :] for g in range(groups)], axis=0)
    normed = layer_norm(cells).astype(BF)
    queries = jnp.dot(normed, w_qkv[:, :embed], preferred_element_type=F32).astype(BF)
    values = jnp.dot(normed, w_qkv[:, 2 * embed :], preferred_element_type=F32).astype(BF)
    keys = lax.dot_general(keys_t[...], normed, (((1,), (1,)), ((), ())), preferred_element_type=F32)
    side = lax.broadcasted_iota(jnp.int32, (embed, 2 * group), 1) < group
    raised = [[], []]
    for pair in range(groups // 2):
        both = keys[:, pair * 2 * group : (pair + 1) * 2 * group]
        turned = pltpu.roll(both, group, axis=1)
        for place, twice in enumerate((jnp.where(side, both, turned), jnp.where(side, turned, both))):
            twice = twice.astype(BF)
            start = (2 * pair + place) * group
            for half in range(2):
                part = twice[half * tile : (half + 1) * tile]
                spread = jnp.concatenate([part * own_low[...], part * own_high[...]], axis=1)
                scores = jnp.dot(
                    queries[start : start + group, half * tile : (half + 1) * tile], spread, preferred_element_type=F32
                )
                raised[half].append(jnp.minimum(jnp.exp2(scores * (LOG2E * HDIM**-0.5)), BF_MAX).astype(BF))
    heads = []
    for half in range(2):
        part = jnp.concatenate(raised[half], axis=0)
        total = jnp.dot(part, ones[...], preferred_element_type=F32)
        guess = pl.reciprocal(total, approx=True)
        attn = (part.astype(F32) * (guess * (2.0 - total * guess))).astype(BF)
        column = []
        for g in range(groups):
            held = values[g * group : (g + 1) * group, half * tile : (half + 1) * tile]
            spread = jnp.concatenate([held] * (HEADS // 2), axis=0) * own_values[...]
            column.append(
                jnp.dot(attn[g * group : (g + 1) * group], spread, preferred_element_type=F32).astype(BF)
            )
        heads.append(jnp.concatenate(column, axis=0))
    heads = jnp.concatenate(heads, axis=1)
    attended = jnp.dot(heads, w_out[...], preferred_element_type=F32).astype(BF)
    mixed = cells + attended.astype(F32)
    normed_two = layer_norm(mixed).astype(BF)
    up = jnp.dot(normed_two, w_up[...], preferred_element_type=F32)
    bent = jnp.tanh(up * (0.7978845608 + (0.7978845608 * 0.044715) * (up * up)))
    half_up = 0.5 * up
    expanded = (half_up + half_up * bent).astype(BF)
    result = mixed + jnp.dot(expanded, w_down[...], preferred_element_type=F32)
    for g in range(groups):
        back[pl.ds(g, group, stride=groups), :] = result[g * group : (g + 1) * group]
    out[...] = back[...].reshape(x.shape).astype(BF)


def block_step(moved, carry, first, pieces, devices_y, devices_x, w_qkv, w_out, w_up, w_down):
    _, piece_y, piece_cols, width = moved.shape
    lanes = devices_y // GRID
    view = moved.reshape(GRID, lanes, devices_x, piece_y, piece_cols, width)
    tokens = GRID * devices_x * piece_cols
    block = (GRID, None, devices_x, None, piece_cols, width)
    operands = [view, w_qkv, w_out, w_up, w_down]
    in_specs = [pl.BlockSpec(block, lambda i, j: (0, i, 0, j, 0, 0)), *(whole(array) for array in operands[1:])]
    aliases = {}
    if carry is not None:
        aliases = {len(operands): 0}
        operands.append(carry)
        in_specs.append(pl.BlockSpec(memory_space=pl.ANY))
    total = lanes * piece_y * tokens
    return pl.pallas_call(
        block_kernel,
        grid=(lanes, piece_y),
        in_specs=in_specs,
        out_specs=pl.BlockSpec(block, lambda i, j: (0, i, 0, first + j, 0, 0)),
        out_shape=jax.ShapeDtypeStruct((GRID, lanes, devices_x, pieces, piece_cols, width), BF),
        scratch_shapes=[
            pltpu.VMEM((tokens, width), F32),
            pltpu.VMEM((tokens, width), F32),
            pltpu.VMEM((w_out.shape[0], width), BF),
            pltpu.VMEM((HEADS // 2 * HDIM, 2 * GRID * GRID), BF),
            pltpu.VMEM((HEADS // 2 * HDIM, 2 * GRID * GRID), BF),
            pltpu.VMEM((HEADS // 2 * GRID * GRID, HEADS // 2 * HDIM), BF),
            pltpu.VMEM((HEADS // 2 * GRID * GRID, HEADS // 2 * GRID * GRID), BF),
        ],
        input_output_aliases=aliases,
        compiler_params=pltpu.CompilerParams(vmem_limit_bytes=VMEM_LIMIT),
        cost_estimate=pl.CostEstimate(
            flops=total * 3_000_000, bytes_accessed=total * width * 4 + 800_000, transcendentals=total * 1100
        ),
    )(*operands)


def unpack_kernel(shares, local_m, piece_x, src, out):
    owners_y, owners_x = src.shape[:2]
    unit = out.shape[0]
    lines, first = [], 0
    for share in shares:
        lines += [(owner_y, first + piece) for owner_y in range(owners_y) for piece in range(share)]
        first += share
    for step in range(len(lines) // unit):

        @pl.when(pl.program_id(0) == step)
        def _():
            for row, (owner_y, piece) in enumerate(lines[step * unit : (step + 1) * unit]):
                wide = src[owner_y, :, piece].astype(F32)
                parts = [
                    wide[owner, m * piece_x : (m + 1) * piece_x] for m in range(local_m) for owner in range(owners_x)
                ]
                out[row] = jnp.concatenate(parts, axis=0).astype(BF)


def unpack_step(landed, shares, cols, local_m, piece_x):
    owners_y, _, pieces, _, width = landed.shape
    rows = owners_y * pieces
    unit = 16 if rows % 16 == 0 else rows
    return pl.pallas_call(
        functools.partial(unpack_kernel, shares, local_m, piece_x),
        grid=(rows // unit,),
        in_specs=[pl.BlockSpec(memory_space=pltpu.VMEM)],
        out_specs=pl.BlockSpec((unit, cols, width), lambda step: (step, 0, 0)),
        out_shape=jax.ShapeDtypeStruct((rows, cols, width), BF),
        compiler_params=pltpu.CompilerParams(vmem_limit_bytes=VMEM_LIMIT),
        cost_estimate=pl.CostEstimate(flops=0, bytes_accessed=rows * cols * width * 4, transcendentals=0),
    )(landed)


def step_rows(start, extent, most=16):
    return max(size for size in range(1, most + 1) if extent % size == 0 and start % size == 0)


def body(frames, hidden_state, cell_state, w_gates, gate_bias, w_qkv, w_out, w_up, w_down):
    rows, cols, width = hidden_state.shape
    latent = frames.shape[2] // 2
    chans = latent + width
    held = chans + width
    devices_y, devices_x = lax.axis_size("gy"), lax.axis_size("gx")
    local_m = GRID // devices_x
    piece_x = cols // local_m // devices_x
    weights = w_gates.reshape(-1, w_gates.shape[3])
    bias = gate_bias.reshape(1, -1)

    def shifted(value, axis, step):
        count = lax.axis_size(axis)
        pairs = [(i, i + step) for i in range(count) if 0 <= i + step < count]
        return lax.ppermute(value, axis, pairs)

    send_left, send_right, side_left, side_right, line_top, line_bot = pack_step(frames, hidden_state, cell_state)
    from_left = shifted(send_right, "gx", 1)
    from_right = shifted(send_left, "gx", -1)
    to_down = jnp.concatenate([line_bot, from_left[-2:], from_right[-2:]], axis=1)
    to_up = jnp.concatenate([line_top, from_left[:2], from_right[:2]], axis=1)

    tile_shapes = (jax.ShapeDtypeStruct((rows, cols, width), BF), jax.ShapeDtypeStruct((rows, cols, width), F32))
    carry = ()
    for start, extent in ((0, rows // 2), (rows // 2, rows - rows // 2)):
        depth = step_rows(start, extent)
        spec = pl.BlockSpec((depth, cols, width), lambda step, first=start // depth: (first + step, 0, 0))
        if carry:
            *carry, to_down, to_up = lax.optimization_barrier((*carry, to_down, to_up))
            from_up, from_down = shifted(to_down, "gy", 1), shifted(to_up, "gy", -1)
        carry = conv_step(
            frames, 0, hidden_state, cell_state, {}, weights, bias, (start, extent), depth, ("hid_out", "cell_out"),
            tile_shapes, (spec, spec), None, carry, False,
        )
    hidden_one, cell_one = carry

    length = -(-(rows + 4) // 16) * 16
    line_shape = jax.ShapeDtypeStruct((4, cols, width), F32)
    strip_shape = jax.ShapeDtypeStruct((4, length, width), F32)
    beside_shape = jax.ShapeDtypeStruct((2, length, latent), F32)
    shapes = (line_shape, line_shape, strip_shape, strip_shape, beside_shape)
    turned = from_left.transpose(1, 0, 2), from_right.transpose(1, 0, 2)
    around = (from_up, from_down, line_top, line_bot, *turned, side_left, side_right)
    line_hid, line_cell, strip_hid, strip_cell, beside = pl.pallas_call(
        ring_kernel,
        grid=(1,),
        in_specs=[*(whole(array) for array in around), pl.BlockSpec(memory_space=pltpu.VMEM), whole(bias)],
        out_specs=[whole(shape) for shape in shapes],
        out_shape=shapes,
        scratch_shapes=[pltpu.VMEM((8, length, held + latent), F32)],
        compiler_params=pltpu.CompilerParams(vmem_limit_bytes=VMEM_LIMIT),
        cost_estimate=pl.CostEstimate(flops=16 * length * weights.size, bytes_accessed=2 * weights.size, transcendentals=0),
    )(*around, weights, bias)

    second = held // latent
    line = (1, from_up.shape[1], latent)
    ring = {name: (array, whole(array)) for name, array in (
        ("strips_hid", strip_hid), ("strips_cell", strip_cell), ("lines_hid", line_hid), ("lines_cell", line_cell),
        ("beside", beside),
    )}
    ring["frame_top"] = from_up, pl.BlockSpec(line, lambda step: (1, 0, second))
    ring["frame_bot"] = from_down, pl.BlockSpec(line, lambda step: (0, 0, second))

    pieces = rows // devices_y
    piece_cols = local_m * piece_x
    shares = (pieces - pieces // 3, pieces // 3)
    moved, start, carry = [], 0, ()
    for piece_y in shares:
        extent = piece_y * devices_y
        depth = step_rows(start, extent, 8 if carry else 16)
        sent_shape = jax.ShapeDtypeStruct((devices_y, devices_x, piece_y, piece_cols, width), BF)
        spec = pl.BlockSpec((depth, cols, width), lambda step, first=start // depth: (first + step, 0, 0))
        sent, cell_out = conv_step(
            frames, 1, hidden_one, cell_one, ring, weights, bias, (start, extent), depth,
            ("hid_out", "cell_out"), (sent_shape, tile_shapes[1]), (whole(sent_shape), spec), (local_m, piece_x), carry,
            bool(carry),
        )
        carry = (None, cell_out)
        sent = sent.reshape(devices_y * devices_x, piece_y, piece_cols, width)
        moved.append(lax.all_to_all(sent, ("gy", "gx"), split_axis=0, concat_axis=0, tiled=True))
        start += extent
    done, first = None, 0
    for piece_y, value in zip(shares, moved):
        done = block_step(value, done, first, pieces, devices_y, devices_x, w_qkv, w_out, w_up, w_down)
        first += piece_y
    done = done.reshape(devices_y * devices_x, pieces, piece_cols, width)
    landed = lax.all_to_all(done, ("gy", "gx"), split_axis=0, concat_axis=0, tiled=True)
    result = unpack_step(landed.reshape(devices_y, devices_x, *landed.shape[1:]), shares, cols, local_m, piece_x)
    return result, cell_out


def solution(mesh):
    tiled = P("gy", "gx", None)
    in_specs = (tiled, tiled, tiled, P(), P(), P(), P(), P(), P())
    return jax.shard_map(body, mesh=mesh, in_specs=in_specs, out_specs=(tiled, tiled), check_vma=False)
```

```python
import functools

import jax
import jax.numpy as jnp
from jax import lax
from jax.experimental import pallas as pl
from jax.experimental.pallas import tpu as pltpu
from jax.sharding import PartitionSpec as P

HEADS = 8
HDIM = 32
GRID = 8
BF = jnp.bfloat16
F32 = jnp.float32
LOG2E = 1.4426950408889634
BF_MAX = 3.3895313892515355e38
VMEM_LIMIT = 32 * 1024 * 1024
VMEM_ALL = 60 * 1024 * 1024
LOADS = 9
LANES = 128


def sigmoid(x):
    return 0.5 * jnp.tanh(0.5 * x) + 0.5


def lstm(gates, cell_prev):
    width = cell_prev.shape[-1]
    in_gate = sigmoid(gates[:, 0:width])
    forget_gate = sigmoid(gates[:, width : 2 * width])
    candidate = jnp.tanh(gates[:, 2 * width : 3 * width])
    out_gate = sigmoid(gates[:, 3 * width :])
    cell = forget_gate * cell_prev + in_gate * candidate
    return cell, out_gate * jnp.tanh(cell)


def layer_norm(values):
    center = values - jnp.mean(values, axis=-1, keepdims=True)
    spread = jnp.mean(center * center, axis=-1, keepdims=True)
    return center * lax.rsqrt(spread + 1e-05)


def three_columns(wide, left, right):
    count = wide.shape[0]
    place = lax.broadcasted_iota(jnp.int32, wide.shape, 0)
    before = jnp.where(place == 0, left, pltpu.roll(wide, 1, axis=0))
    after = jnp.where(place == count - 1, right, pltpu.roll(wide, count - 1, axis=0))
    return before.astype(BF), wide.astype(BF), after.astype(BF)


def conv_kernel(start, rows, refs, packed, *args):
    ref = dict(zip(refs, args))
    frame, hid, spread = ref["frame"], ref["hid"], ref["spread"]
    hid_out, cell_out = ref["hid_out"], ref["cell_out"]
    ring = "strips_hid" in ref
    extent, cols, latent = frame.shape
    width = hid.shape[2]
    chans = latent + width
    top, bot = start == 0, start + extent == rows
    loads = []
    if "weights" in ref:
        size = ref["weights"].shape[0] // LOADS
        for place in range(LOADS):
            part = pl.ds(place * size, size)
            loads.append(
                pltpu.make_async_copy(ref["weights"].at[part], ref["held"].at[part], ref["sem"].at[place])
            )
    for load in loads:
        load.start()

    def beside(row):
        if not ring:
            return jnp.zeros((1, chans), F32), jnp.zeros((1, chans), F32)
        at = row + 2
        return tuple(
            jnp.concatenate(
                [ref["beside"][place, at : at + 1, :], ref["strips_hid"][3 * place, at : at + 1, :]], axis=1
            )
            for place in range(2)
        )

    def build(pos):
        row = start + pos - 1
        raw = None
        if pos == 0 or pos == extent + 1:
            name, outside = ("prev", top) if pos == 0 else ("next", bot)
            if outside and not ring:
                spread[pos] = jnp.zeros(spread.shape[1:], BF)
                return
            x, h = ref["frame_" + name][0].astype(F32), ref["hid_" + name][0].astype(F32)
            if outside:
                x = ref["frame_top" if pos == 0 else "frame_bot"][0, :cols].astype(F32)
        else:
            raw = frame[pos - 1], hid[pos - 1]
            x, h = raw[0].astype(F32), raw[1].astype(F32)
        low, high = beside(row)
        if ring:
            at = row + 2
            place = lax.broadcasted_iota(jnp.int32, h.shape, 0)
            h = jnp.where(place == 0, ref["strips_hid"][1, at : at + 1, :], h)
            h = jnp.where(place == cols - 1, ref["strips_hid"][2, at : at + 1, :], h)
            for spot, line in ((-1, 0), (0, 1), (rows - 1, 2), (rows, 3)):
                if row == spot:
                    h = ref["lines_hid"][line]
        for part, (value, first) in enumerate(((x, 0), (h, latent))):
            size = value.shape[1]
            pieces = three_columns(value, low[:, first : first + size], high[:, first : first + size])
            if raw is not None and (part == 0 or not ring):
                pieces = pieces[0], raw[part], pieces[2]
            for tap in range(3):
                spread[pos, :, tap * chans + first : tap * chans + first + size] = pieces[tap]

    def multiply(first, depth):
        lhs = jnp.concatenate(
            [spread[first + tap : first + tap + depth].reshape(depth * cols, 3 * chans) for tap in range(3)], axis=1
        )
        return jnp.dot(lhs, ref["held"][...], preferred_element_type=F32)

    def activate(first, depth, gates):
        for line in range(first, first + depth):
            row = start + line
            cell_prev = ref["cell"][line]
            if ring:
                at = row + 2
                place = lax.broadcasted_iota(jnp.int32, cell_prev.shape, 0)
                cell_prev = jnp.where(place == 0, ref["strips_cell"][1, at : at + 1, :], cell_prev)
                cell_prev = jnp.where(place == cols - 1, ref["strips_cell"][2, at : at + 1, :], cell_prev)
                if row == 0:
                    cell_prev = ref["lines_cell"][1]
                if row == rows - 1:
                    cell_prev = ref["lines_cell"][2]
            own = gates[(line - first) * cols : (line - first + 1) * cols] + ref["bias"][...]
            new_cell, new_hidden = lstm(own, cell_prev)
            cell_out[line] = new_cell
            if not packed:
                hid_out[line] = new_hidden.astype(BF)
                continue
            owners_x, piece_y = hid_out.shape[1:3]
            local_m, piece_x = packed
            for owner in range(owners_x):
                picked = [
                    new_hidden[(m * owners_x + owner) * piece_x : (m * owners_x + owner + 1) * piece_x]
                    for m in range(local_m)
                ]
                hid_out[line // piece_y, owner, line % piece_y] = jnp.concatenate(picked, axis=0).astype(BF)

    depth = step_rows(0, extent, 12)
    for pos in range(depth + 2):
        build(pos)
    for load in loads:
        load.wait()
    waiting = None
    for first in range(0, extent, depth):
        for pos in range(first + depth + 2, min(first + 2 * depth, extent) + 2):
            build(pos)
        gates = multiply(first, depth)
        if waiting:
            activate(*waiting)
        waiting = first, depth, gates
    activate(*waiting)


def whole(array):
    return pl.BlockSpec(array.shape, lambda *step: (0,) * array.ndim)


def conv_step(frames, part, hid, cell, ring, weights, bias, rows_of, names, out_shapes, out_specs, packed, carry, load):
    rows, cols, width = hid.shape
    latent = weights.shape[0] // 9 - width
    start, extent = rows_of

    def rowed(size, channels, channel, row):
        return pl.BlockSpec((size, cols, channels), lambda step: (row // size, 0, channel))

    before, after = max(start - 1, 0), min(start + extent, rows - 1)
    inputs = {
        "frame": (frames, rowed(extent, latent, part, start)),
        "frame_prev": (frames, rowed(1, latent, part, before)),
        "frame_next": (frames, rowed(1, latent, part, after)),
        "hid": (hid, rowed(extent, width, 0, start)),
        "hid_prev": (hid, rowed(1, width, 0, before)),
        "hid_next": (hid, rowed(1, width, 0, after)),
        "cell": (cell, rowed(extent, width, 0, start)),
        "bias": (bias, whole(bias)),
    }
    if load:
        inputs["weights"] = weights, pl.BlockSpec(memory_space=pl.ANY)
    else:
        inputs["held"] = weights, pl.BlockSpec(memory_space=pltpu.VMEM)
    inputs |= ring
    aliases = {}
    for place, array in enumerate(carry):
        if array is not None:
            aliases[len(inputs)] = place
            inputs[f"carry{place}"] = (array, pl.BlockSpec(memory_space=pl.ANY))
    refs = [*inputs, *names, "spread"]
    scratch = [pltpu.VMEM((extent + 2, cols, 3 * (latent + width)), BF)]
    if load:
        refs += ["held", "sem"]
        scratch += [pltpu.VMEM(weights.shape, BF), pltpu.SemaphoreType.DMA((LOADS,))]
    cells = extent * cols
    return pl.pallas_call(
        functools.partial(conv_kernel, start, rows, refs, packed),
        grid=(1,),
        in_specs=[spec for _, spec in inputs.values()],
        out_specs=out_specs,
        out_shape=out_shapes,
        scratch_shapes=scratch,
        input_output_aliases=aliases,
        compiler_params=pltpu.CompilerParams(vmem_limit_bytes=VMEM_ALL if load else VMEM_LIMIT),
        cost_estimate=pl.CostEstimate(
            flops=2 * cells * weights.size, bytes_accessed=2 * weights.size + cells * 2048, transcendentals=cells * width * 5
        ),
    )(*(array for array, _ in inputs.values()))


def pack_kernel(
    frame_low, frame_high, frame_top, frame_bot, hid_low, hid_high, hid_top, hid_bot,
    cell_low, cell_high, cell_top, cell_bot, send_low, send_high, side_low, side_high, line_top, line_bot, flat,
):
    latent, width = frame_low.shape[2] // 2, hid_low.shape[2]
    chans = latent + width
    places = ((0, 0, latent), (chans + width, latent, latent))
    for out, frame, hid, cell in (
        (line_top, frame_top, hid_top, cell_top),
        (line_bot, frame_bot, hid_bot, cell_bot),
    ):
        for to, start, size in places:
            out[:, :, to : to + size] = frame[:, :, start : start + size]
        out[:, :, latent:chans] = hid[...]
        out[:, :, chans : chans + width] = cell[...].astype(BF)
    for out, send, frame, hid, cell, first, start in (
        (side_low, send_low, frame_low, hid_low, cell_low, 0, 0),
        (side_high, send_high, frame_high, hid_high, cell_high, frame_high.shape[1] - 8, 6),
    ):
        tall = frame.shape[0]
        near = slice(first, first + 8)
        for slab in range(out.shape[2] // LANES):
            to = slab * LANES
            if to < latent or to >= chans + width:
                begin = to if to < latent else to - 2 * width
                part = frame[:, near, begin : begin + LANES].astype(F32)
            elif to < chans:
                part = hid[:, near, to - latent : to - latent + LANES].astype(F32)
            else:
                part = cell[:, :, to - chans : to - chans + LANES]
            send[:, :, to : to + LANES] = part[:, start : start + 2].astype(BF)
            flat[...] = part.reshape(tall * 8, LANES)
            for place in range(2):
                out[place, :, to : to + LANES] = flat[pl.ds(start + place, tall, stride=8), :].astype(BF)


def pack_step(frames, hid, cell):
    rows, cols, width = hid.shape
    span = frames.shape[2]
    near = 16

    def edge(array, size):
        deep = array.shape[2]
        return [
            pl.BlockSpec((rows, size, deep), lambda step: (0, 0, 0)),
            pl.BlockSpec((rows, size, deep), lambda step: (0, cols // size - 1, 0)),
            pl.BlockSpec((2, cols, deep), lambda step: (0, 0, 0)),
            pl.BlockSpec((2, cols, deep), lambda step: (rows // 2 - 1, 0, 0)),
        ]

    deep = span + 2 * width
    shapes = [jax.ShapeDtypeStruct((rows, 2, deep), BF)] * 2 + [jax.ShapeDtypeStruct((2, rows, deep), BF)] * 2
    shapes += [jax.ShapeDtypeStruct((2, cols, deep), BF)] * 2
    return pl.pallas_call(
        pack_kernel,
        grid=(1,),
        in_specs=[*edge(frames, near), *edge(hid, near), *edge(cell, 8)],
        out_specs=[whole(shape) for shape in shapes],
        out_shape=shapes,
        scratch_shapes=[pltpu.VMEM((rows * 8, LANES), F32)],
        compiler_params=pltpu.CompilerParams(vmem_limit_bytes=VMEM_ALL),
        cost_estimate=pl.CostEstimate(flops=0, bytes_accessed=4_000_000, transcendentals=0),
    )(*[frames] * 4, *[hid] * 4, *[cell] * 4)


def ring_kernel(
    above, below, line_top, line_bot, from_left, from_right, side_left, side_right, weights, bias,
    line_hid, line_cell, strip_hid, strip_cell, beside, strips,
):
    width = line_hid.shape[2]
    chans = weights.shape[0] // 9
    cols, length = line_top.shape[1], strip_hid.shape[1]
    rows = from_left.shape[1]
    columns = (
        (from_left, 0, cols), (from_left, 1, cols + 1), (side_left, 0, 0), (side_left, 1, 1),
        (side_right, 0, cols - 2), (side_right, 1, cols - 1), (from_right, 0, cols + 2), (from_right, 1, cols + 3),
    )
    ends = [(ref[row].astype(F32), at + row) for ref, at in ((above, 0), (below, rows + 2)) for row in range(2)]
    strips[:, rows + 4 :, :] = jnp.zeros((8, length - rows - 4, strips.shape[2]), F32)
    for place, (source, at, end) in enumerate(columns):
        strips[place, 2 : rows + 2, :] = source[at].astype(F32)
        for value, spot in ends:
            strips[place, spot : spot + 1, :] = value[end : end + 1]
    beside[0] = strips[1, :, chans + width :]
    beside[1] = strips[6, :, chans + width :]
    low, high = strips[1, :, :chans], strips[6, :, :chans]

    def line(ref, row):
        held = ref[row, :cols].astype(F32)
        return held[:, :chans], held[:, chans : chans + width]

    tops = [line(above, 0), line(above, 1), line(line_top, 0), line(line_top, 1)]
    bots = [line(line_bot, 0), line(line_bot, 1), line(below, 0), line(below, 1)]
    parts, held = [], []
    for lead, lines in ((0, tops), (rows, bots)):
        pieces = []
        for row in range(4):
            at = lead + row
            pieces.append(three_columns(lines[row][0], low[at : at + 1], high[at : at + 1]))
        for row in range(2):
            parts.append(jnp.concatenate([pieces[row + tap][col] for tap in range(3) for col in range(3)], axis=1))
            held.append(lines[row + 1][1])
    for side in range(2):
        rolled = []
        for col in range(4):
            wide = strips[4 * side + col, :, :chans]
            rolled.append((pltpu.roll(wide, 1, axis=0), wide, pltpu.roll(wide, length - 1, axis=0)))
        for col in range(2):
            parts.append(
                jnp.concatenate([rolled[col + tap][row].astype(BF) for row in range(3) for tap in range(3)], axis=1)
            )
            held.append(strips[4 * side + col + 1, :, chans : chans + width])
    row_at, col_at = lax.axis_index("gy"), lax.axis_index("gx")
    upper = (row_at > 0).astype(F32)
    lower = (row_at < lax.axis_size("gy") - 1).astype(F32)
    before = (col_at > 0).astype(F32)
    after = (col_at < lax.axis_size("gx") - 1).astype(F32)
    spot = lax.broadcasted_iota(jnp.int32, (length, width), 0)
    inside = jnp.where(spot == 1, upper, jnp.where(spot == rows + 2, lower, 1.0))
    keep = [upper, 1.0, 1.0, lower, inside * before, inside, inside, inside * after]
    lhs = jnp.concatenate(parts, axis=0)
    gates = jnp.dot(lhs, weights[...], preferred_element_type=F32) + bias[...]
    start = 0
    for place in range(8):
        hid, cell = (line_hid, line_cell) if place < 4 else (strip_hid, strip_cell)
        size = hid.shape[1]
        new_cell, hidden = lstm(gates[start : start + size], held[place])
        hid[place % 4] = hidden.astype(BF).astype(F32) * keep[place]
        cell[place % 4] = new_cell
        start += size


def block_kernel(x, w_qkv, w_out, w_up, w_down, *rest):
    out, flat, back, keys_t, own_low, own_high, own_values, ones = rest[-8:]
    group = GRID * GRID
    embed = w_out.shape[0]
    tile = embed // 2

    @pl.when((pl.program_id(0) == 0) & (pl.program_id(1) == 0))
    def _():
        def fill(target, down, across, add):
            above = lax.broadcasted_iota(jnp.int32, target.shape, 0) // down
            along = lax.broadcasted_iota(jnp.int32, target.shape, 1) // across
            target[...] = (above == along + add).astype(F32).astype(BF)

        fill(own_low, HDIM, group, 0)
        fill(own_high, HDIM, group, HEADS // 4)
        fill(own_values, group, HDIM, 0)
        fill(ones, group, group, 0)
        keys_t[...] = w_qkv[:, embed : 2 * embed].astype(F32).T.astype(BF)

    flat[...] = x[...].astype(F32).reshape(flat.shape)
    groups = flat.shape[0] // group
    cells = jnp.concatenate([flat[pl.ds(g, group, stride=groups), :] for g in range(groups)], axis=0)
    normed = layer_norm(cells).astype(BF)
    queries = jnp.dot(normed, w_qkv[:, :embed], preferred_element_type=F32).astype(BF)
    values = jnp.dot(normed, w_qkv[:, 2 * embed :], preferred_element_type=F32).astype(BF)
    keys = lax.dot_general(keys_t[...], normed, (((1,), (1,)), ((), ())), preferred_element_type=F32)
    side = lax.broadcasted_iota(jnp.int32, (embed, 2 * group), 1) < group
    raised = [[], []]
    for pair in range(groups // 2):
        both = keys[:, pair * 2 * group : (pair + 1) * 2 * group]
        turned = pltpu.roll(both, group, axis=1)
        for place, twice in enumerate((jnp.where(side, both, turned), jnp.where(side, turned, both))):
            twice = twice.astype(BF)
            start = (2 * pair + place) * group
            for half in range(2):
                part = twice[half * tile : (half + 1) * tile]
                spread = jnp.concatenate([part * own_low[...], part * own_high[...]], axis=1)
                scores = jnp.dot(
                    queries[start : start + group, half * tile : (half + 1) * tile], spread, preferred_element_type=F32
                )
                raised[half].append(jnp.minimum(jnp.exp2(scores * (LOG2E * HDIM**-0.5)), BF_MAX).astype(BF))
    heads = []
    for half in range(2):
        part = jnp.concatenate(raised[half], axis=0)
        total = jnp.dot(part, ones[...], preferred_element_type=F32)
        guess = pl.reciprocal(total, approx=True)
        attn = (part.astype(F32) * (guess * (2.0 - total * guess))).astype(BF)
        column = []
        for g in range(groups):
            held = values[g * group : (g + 1) * group, half * tile : (half + 1) * tile]
            spread = jnp.concatenate([held] * (HEADS // 2), axis=0) * own_values[...]
            column.append(
                jnp.dot(attn[g * group : (g + 1) * group], spread, preferred_element_type=F32).astype(BF)
            )
        heads.append(jnp.concatenate(column, axis=0))
    heads = jnp.concatenate(heads, axis=1)
    attended = jnp.dot(heads, w_out[...], preferred_element_type=F32).astype(BF)
    mixed = cells + attended.astype(F32)
    normed_two = layer_norm(mixed).astype(BF)
    up = jnp.dot(normed_two, w_up[...], preferred_element_type=F32)
    bent = jnp.tanh(up * (0.7978845608 + (0.7978845608 * 0.044715) * (up * up)))
    half_up = 0.5 * up
    expanded = (half_up + half_up * bent).astype(BF)
    result = mixed + jnp.dot(expanded, w_down[...], preferred_element_type=F32)
    for g in range(groups):
        back[pl.ds(g, group, stride=groups), :] = result[g * group : (g + 1) * group]
    out[...] = back[...].reshape(x.shape).astype(BF)


def block_step(moved, carry, first, pieces, devices_y, devices_x, w_qkv, w_out, w_up, w_down):
    _, piece_y, piece_cols, width = moved.shape
    lanes = devices_y // GRID
    view = moved.reshape(GRID, lanes, devices_x, piece_y, piece_cols, width)
    tokens = GRID * devices_x * piece_cols
    block = (GRID, None, devices_x, None, piece_cols, width)
    operands = [view, w_qkv, w_out, w_up, w_down]
    in_specs = [pl.BlockSpec(block, lambda i, j: (0, i, 0, j, 0, 0)), *(whole(array) for array in operands[1:])]
    aliases = {}
    if carry is not None:
        aliases = {len(operands): 0}
        operands.append(carry)
        in_specs.append(pl.BlockSpec(memory_space=pl.ANY))
    total = lanes * piece_y * tokens
    return pl.pallas_call(
        block_kernel,
        grid=(lanes, piece_y),
        in_specs=in_specs,
        out_specs=pl.BlockSpec(block, lambda i, j: (0, i, 0, first + j, 0, 0)),
        out_shape=jax.ShapeDtypeStruct((GRID, lanes, devices_x, pieces, piece_cols, width), BF),
        scratch_shapes=[
            pltpu.VMEM((tokens, width), F32),
            pltpu.VMEM((tokens, width), F32),
            pltpu.VMEM((w_out.shape[0], width), BF),
            pltpu.VMEM((HEADS // 2 * HDIM, 2 * GRID * GRID), BF),
            pltpu.VMEM((HEADS // 2 * HDIM, 2 * GRID * GRID), BF),
            pltpu.VMEM((HEADS // 2 * GRID * GRID, HEADS // 2 * HDIM), BF),
            pltpu.VMEM((HEADS // 2 * GRID * GRID, HEADS // 2 * GRID * GRID), BF),
        ],
        input_output_aliases=aliases,
        compiler_params=pltpu.CompilerParams(vmem_limit_bytes=VMEM_LIMIT),
        cost_estimate=pl.CostEstimate(
            flops=total * 3_000_000, bytes_accessed=total * width * 4 + 800_000, transcendentals=total * 1100
        ),
    )(*operands)


def unpack_kernel(shares, local_m, piece_x, src, out):
    owners_y, owners_x = src.shape[:2]
    unit = out.shape[0]
    lines, first = [], 0
    for share in shares:
        lines += [(owner_y, first + piece) for owner_y in range(owners_y) for piece in range(share)]
        first += share
    for step in range(len(lines) // unit):

        @pl.when(pl.program_id(0) == step)
        def _():
            for row, (owner_y, piece) in enumerate(lines[step * unit : (step + 1) * unit]):
                wide = src[owner_y, :, piece].astype(F32)
                parts = [
                    wide[owner, m * piece_x : (m + 1) * piece_x] for m in range(local_m) for owner in range(owners_x)
                ]
                out[row] = jnp.concatenate(parts, axis=0).astype(BF)


def unpack_step(landed, shares, cols, local_m, piece_x):
    owners_y, _, pieces, _, width = landed.shape
    rows = owners_y * pieces
    unit = 16 if rows % 16 == 0 else rows
    return pl.pallas_call(
        functools.partial(unpack_kernel, shares, local_m, piece_x),
        grid=(rows // unit,),
        in_specs=[pl.BlockSpec(memory_space=pltpu.VMEM)],
        out_specs=pl.BlockSpec((unit, cols, width), lambda step: (step, 0, 0)),
        out_shape=jax.ShapeDtypeStruct((rows, cols, width), BF),
        compiler_params=pltpu.CompilerParams(vmem_limit_bytes=VMEM_LIMIT),
        cost_estimate=pl.CostEstimate(flops=0, bytes_accessed=rows * cols * width * 4, transcendentals=0),
    )(landed)


def step_rows(start, extent, most=16):
    return max(size for size in range(1, most + 1) if extent % size == 0 and start % size == 0)


def body(frames, hidden_state, cell_state, w_gates, gate_bias, w_qkv, w_out, w_up, w_down):
    rows, cols, width = hidden_state.shape
    latent = frames.shape[2] // 2
    chans = latent + width
    held = chans + width
    devices_y, devices_x = lax.axis_size("gy"), lax.axis_size("gx")
    local_m = GRID // devices_x
    piece_x = cols // local_m // devices_x
    weights = w_gates.reshape(-1, w_gates.shape[3])
    bias = gate_bias.reshape(1, -1)

    def shifted(value, axis, step):
        count = lax.axis_size(axis)
        pairs = [(i, i + step) for i in range(count) if 0 <= i + step < count]
        return lax.ppermute(value, axis, pairs)

    send_left, send_right, side_left, side_right, line_top, line_bot = pack_step(frames, hidden_state, cell_state)
    from_left = shifted(send_right, "gx", 1)
    from_right = shifted(send_left, "gx", -1)
    to_down = jnp.concatenate([line_bot, from_left[-2:], from_right[-2:]], axis=1)
    to_up = jnp.concatenate([line_top, from_left[:2], from_right[:2]], axis=1)

    tile_shapes = (jax.ShapeDtypeStruct((rows, cols, width), BF), jax.ShapeDtypeStruct((rows, cols, width), F32))
    carry = ()
    for start, extent in ((0, rows // 2), (rows // 2, rows - rows // 2)):
        spec = pl.BlockSpec((extent, cols, width), lambda step, place=start // extent: (place, 0, 0))
        if carry:
            *carry, to_down, to_up = lax.optimization_barrier((*carry, to_down, to_up))
            from_up, from_down = shifted(to_down, "gy", 1), shifted(to_up, "gy", -1)
        carry = conv_step(
            frames, 0, hidden_state, cell_state, {}, weights, bias, (start, extent), ("hid_out", "cell_out"),
            tile_shapes, (spec, spec), None, carry, False,
        )
    hidden_one, cell_one = carry

    length = -(-(rows + 4) // 16) * 16
    line_shape = jax.ShapeDtypeStruct((4, cols, width), F32)
    strip_shape = jax.ShapeDtypeStruct((4, length, width), F32)
    beside_shape = jax.ShapeDtypeStruct((2, length, latent), F32)
    shapes = (line_shape, line_shape, strip_shape, strip_shape, beside_shape)
    turned = from_left.transpose(1, 0, 2), from_right.transpose(1, 0, 2)
    around = (from_up, from_down, line_top, line_bot, *turned, side_left, side_right)
    line_hid, line_cell, strip_hid, strip_cell, beside = pl.pallas_call(
        ring_kernel,
        grid=(1,),
        in_specs=[*(whole(array) for array in around), pl.BlockSpec(memory_space=pltpu.VMEM), whole(bias)],
        out_specs=[whole(shape) for shape in shapes],
        out_shape=shapes,
        scratch_shapes=[pltpu.VMEM((8, length, held + latent), F32)],
        compiler_params=pltpu.CompilerParams(vmem_limit_bytes=VMEM_LIMIT),
        cost_estimate=pl.CostEstimate(flops=16 * length * weights.size, bytes_accessed=2 * weights.size, transcendentals=0),
    )(*around, weights, bias)

    second = held // latent
    line = (1, from_up.shape[1], latent)
    ring = {name: (array, whole(array)) for name, array in (
        ("strips_hid", strip_hid), ("strips_cell", strip_cell), ("lines_hid", line_hid), ("lines_cell", line_cell),
        ("beside", beside),
    )}
    ring["frame_top"] = from_up, pl.BlockSpec(line, lambda step: (1, 0, second))
    ring["frame_bot"] = from_down, pl.BlockSpec(line, lambda step: (0, 0, second))

    pieces = rows // devices_y
    piece_cols = local_m * piece_x
    shares = (pieces - pieces // 3, pieces // 3)
    moved, start, carry = [], 0, ()
    for piece_y in shares:
        extent = piece_y * devices_y
        sent_shape = jax.ShapeDtypeStruct((devices_y, devices_x, piece_y, piece_cols, width), BF)
        spec = pl.BlockSpec((extent, cols, width), lambda step, place=start // extent: (place, 0, 0))
        sent, cell_out = conv_step(
            frames, 1, hidden_one, cell_one, ring, weights, bias, (start, extent),
            ("hid_out", "cell_out"), (sent_shape, tile_shapes[1]), (whole(sent_shape), spec), (local_m, piece_x), carry,
            bool(carry),
        )
        carry = (None, cell_out)
        sent = sent.reshape(devices_y * devices_x, piece_y, piece_cols, width)
        moved.append(lax.all_to_all(sent, ("gy", "gx"), split_axis=0, concat_axis=0, tiled=True))
        start += extent
    done, first = None, 0
    for piece_y, value in zip(shares, moved):
        done = block_step(value, done, first, pieces, devices_y, devices_x, w_qkv, w_out, w_up, w_down)
        first += piece_y
    done = done.reshape(devices_y * devices_x, pieces, piece_cols, width)
    landed = lax.all_to_all(done, ("gy", "gx"), split_axis=0, concat_axis=0, tiled=True)
    result = unpack_step(landed.reshape(devices_y, devices_x, *landed.shape[1:]), shares, cols, local_m, piece_x)
    return result, cell_out


def solution(mesh):
    tiled = P("gy", "gx", None)
    in_specs = (tiled, tiled, tiled, P(), P(), P(), P(), P(), P())
    return jax.shard_map(body, mesh=mesh, in_specs=in_specs, out_specs=(tiled, tiled), check_vma=False)
```

```python
import functools

import jax
import jax.numpy as jnp
from jax import lax
from jax.experimental import pallas as pl
from jax.experimental.pallas import tpu as pltpu
from jax.sharding import PartitionSpec as P

HEADS = 8
HDIM = 32
GRID = 8
BF = jnp.bfloat16
F32 = jnp.float32
LOG2E = 1.4426950408889634
BF_MAX = 3.3895313892515355e38
VMEM_LIMIT = 32 * 1024 * 1024
VMEM_ALL = 60 * 1024 * 1024
LOADS = 9
LANES = 128


def sigmoid(x):
    return 0.5 * jnp.tanh(0.5 * x) + 0.5


def lstm(gates, cell_prev):
    width = cell_prev.shape[-1]
    in_gate = sigmoid(gates[:, 0:width])
    forget_gate = sigmoid(gates[:, width : 2 * width])
    candidate = jnp.tanh(gates[:, 2 * width : 3 * width])
    out_gate = sigmoid(gates[:, 3 * width :])
    cell = forget_gate * cell_prev + in_gate * candidate
    return cell, out_gate * jnp.tanh(cell)


def layer_norm(values):
    center = values - jnp.mean(values, axis=-1, keepdims=True)
    spread = jnp.mean(center * center, axis=-1, keepdims=True)
    return center * lax.rsqrt(spread + 1e-05)


def three_columns(wide, left, right):
    count = wide.shape[0]
    place = lax.broadcasted_iota(jnp.int32, wide.shape, 0)
    before = jnp.where(place == 0, left, pltpu.roll(wide, 1, axis=0))
    after = jnp.where(place == count - 1, right, pltpu.roll(wide, count - 1, axis=0))
    return before.astype(BF), wide.astype(BF), after.astype(BF)


def conv_kernel(start, rows, part, refs, packed, *args):
    ref = dict(zip(refs, args))
    spread, hid_out, cell_out = ref["spread"], ref["hid_out"], ref["cell_out"]
    ring = "strips_hid" in ref
    extent = spread.shape[0] - 2
    cols, width = ref["hid"].shape[1:]
    chans = spread.shape[2] // 3
    latent = chans - width
    top, bot = start == 0, start + extent == rows

    def row_of(name, row):
        channels = slice(part * latent, (part + 1) * latent) if name == "frame" else slice(None)
        if ref[name].shape[0] == rows:
            return ref[name][row, :, channels]
        if row == start - 1:
            return ref[name + "_prev"][0]
        if row == start + extent:
            return ref[name + "_next"][0]
        return ref[name][row - start]

    loads = []
    if "weights" in ref:
        size = ref["weights"].shape[0] // LOADS
        for place in range(LOADS):
            run = pl.ds(place * size, size)
            loads.append(pltpu.make_async_copy(ref["weights"].at[run], ref["held"].at[run], ref["sem"].at[place]))
    for load in loads:
        load.start()

    def beside(row):
        if not ring:
            return jnp.zeros((1, chans), F32), jnp.zeros((1, chans), F32)
        at = row + 2
        return tuple(
            jnp.concatenate(
                [ref["beside"][place, at : at + 1, :], ref["strips_hid"][3 * place, at : at + 1, :]], axis=1
            )
            for place in range(2)
        )

    def build(pos):
        row = start + pos - 1
        raw = None
        if 0 <= row < rows:
            raw = row_of("frame", row), row_of("hid", row)
            x, h = raw[0].astype(F32), raw[1].astype(F32)
        elif ring:
            x, h = ref["frame_top" if row < 0 else "frame_bot"][0, :cols].astype(F32), ref["lines_hid"][3 * (row > 0)]
        else:
            spread[pos] = jnp.zeros(spread.shape[1:], BF)
            return
        low, high = beside(row)
        if ring:
            at = row + 2
            place = lax.broadcasted_iota(jnp.int32, h.shape, 0)
            h = jnp.where(place == 0, ref["strips_hid"][1, at : at + 1, :], h)
            h = jnp.where(place == cols - 1, ref["strips_hid"][2, at : at + 1, :], h)
            for spot, line in ((-1, 0), (0, 1), (rows - 1, 2), (rows, 3)):
                if row == spot:
                    h = ref["lines_hid"][line]
        for side, (value, first) in enumerate(((x, 0), (h, latent))):
            size = value.shape[1]
            pieces = three_columns(value, low[:, first : first + size], high[:, first : first + size])
            if raw is not None and (side == 0 or not ring):
                pieces = pieces[0], raw[side], pieces[2]
            for tap in range(3):
                spread[pos, :, tap * chans + first : tap * chans + first + size] = pieces[tap]

    def multiply(first, depth):
        lhs = jnp.concatenate(
            [spread[first + tap : first + tap + depth].reshape(depth * cols, 3 * chans) for tap in range(3)], axis=1
        )
        return jnp.dot(lhs, ref["held"][...], preferred_element_type=F32)

    def activate(first, depth, gates):
        for line in range(first, first + depth):
            row = start + line
            cell_prev = row_of("cell", row)
            if ring:
                at = row + 2
                place = lax.broadcasted_iota(jnp.int32, cell_prev.shape, 0)
                cell_prev = jnp.where(place == 0, ref["strips_cell"][1, at : at + 1, :], cell_prev)
                cell_prev = jnp.where(place == cols - 1, ref["strips_cell"][2, at : at + 1, :], cell_prev)
                if row == 0:
                    cell_prev = ref["lines_cell"][1]
                if row == rows - 1:
                    cell_prev = ref["lines_cell"][2]
            own = gates[(line - first) * cols : (line - first + 1) * cols] + ref["bias"][...]
            new_cell, new_hidden = lstm(own, cell_prev)
            if not packed:
                cell_out[row] = new_cell
                hid_out[row] = new_hidden.astype(BF)
                continue
            ref["cell_rows"][line] = new_cell
            owners_x, piece_y = hid_out.shape[1:3]
            local_m, piece_x = packed
            for owner in range(owners_x):
                picked = [
                    new_hidden[(m * owners_x + owner) * piece_x : (m * owners_x + owner + 1) * piece_x]
                    for m in range(local_m)
                ]
                hid_out[line // piece_y, owner, line % piece_y] = jnp.concatenate(picked, axis=0).astype(BF)

        if packed:
            done = pl.ds(first, depth)
            leave = pltpu.make_async_copy(
                ref["cell_rows"].at[done], cell_out.at[pl.ds(start + first, depth)], ref["left"].at[first // depth]
            )
            leave.start()
            leaving.append(leave)

    leaving = []
    depth = step_rows(0, extent, 12)
    for pos in range(depth + 2):
        build(pos)
    for load in loads:
        load.wait()
    waiting = None
    for first in range(0, extent, depth):
        for pos in range(first + depth + 2, min(first + 2 * depth, extent) + 2):
            build(pos)
        gates = multiply(first, depth)
        if waiting:
            activate(*waiting)
        waiting = first, depth, gates
    activate(*waiting)
    for leave in leaving:
        leave.wait()


def whole(array):
    return pl.BlockSpec(array.shape, lambda *step: (0,) * array.ndim)


def conv_step(frames, part, hid, cell, ring, weights, bias, rows_of, names, out_shapes, out_specs, packed, carry, load):
    rows, cols, width = hid.shape
    latent = weights.shape[0] // 9 - width
    start, extent = rows_of

    def rowed(size, channels, channel, row):
        return pl.BlockSpec((size, cols, channels), lambda step: (row // size, 0, channel))

    before, after = max(start - 1, 0), min(start + extent, rows - 1)
    near = pl.BlockSpec(memory_space=pltpu.VMEM)
    if load:
        inputs = {
            "frame": (frames, rowed(extent, latent, part, start)),
            "frame_prev": (frames, rowed(1, latent, part, before)),
            "frame_next": (frames, rowed(1, latent, part, after)),
            "hid": (hid, rowed(extent, width, 0, start)),
            "hid_prev": (hid, rowed(1, width, 0, before)),
            "hid_next": (hid, rowed(1, width, 0, after)),
            "cell": (cell, rowed(extent, width, 0, start)),
        }
    else:
        inputs = {"frame": (frames, near), "hid": (hid, near), "cell": (cell, near)}
    inputs["bias"] = bias, whole(bias)
    if load:
        inputs["weights"] = weights, pl.BlockSpec(memory_space=pl.ANY)
    else:
        inputs["held"] = weights, near
    inputs |= ring
    aliases = {}
    for place, array in enumerate(carry):
        if array is not None:
            aliases[len(inputs)] = place
            inputs[f"carry{place}"] = (array, pl.BlockSpec(memory_space=pl.ANY) if packed else near)
    refs = [*inputs, *names, "spread"]
    scratch = [pltpu.VMEM((extent + 2, cols, 3 * (latent + width)), BF)]
    if load:
        refs += ["held", "sem"]
        scratch += [pltpu.VMEM(weights.shape, BF), pltpu.SemaphoreType.DMA((LOADS,))]
    if packed:
        refs += ["cell_rows", "left"]
        scratch += [pltpu.VMEM((extent, cols, width), F32), pltpu.SemaphoreType.DMA((extent,))]
    cells = extent * cols
    return pl.pallas_call(
        functools.partial(conv_kernel, start, rows, part, refs, packed),
        grid=(1,),
        in_specs=[spec for _, spec in inputs.values()],
        out_specs=out_specs,
        out_shape=out_shapes,
        scratch_shapes=scratch,
        input_output_aliases=aliases,
        compiler_params=pltpu.CompilerParams(vmem_limit_bytes=VMEM_ALL if load else VMEM_LIMIT),
        cost_estimate=pl.CostEstimate(
            flops=2 * cells * weights.size, bytes_accessed=2 * weights.size + cells * 2048, transcendentals=cells * width * 5
        ),
    )(*(array for array, _ in inputs.values()))


def pack_kernel(frames, hids, cells, send_low, send_high, side_low, side_high, line_top, line_bot, flat):
    rows, cols, width = hids.shape
    latent = frames.shape[2] // 2
    chans = latent + width
    places = ((0, 0, latent), (chans + width, latent, latent))
    for out, near in ((line_top, slice(0, 2)), (line_bot, slice(rows - 2, rows))):
        for to, start, size in places:
            out[:, :, to : to + size] = frames[near, :, start : start + size]
        out[:, :, latent:chans] = hids[near]
        out[:, :, chans : chans + width] = cells[near].astype(BF)
    for out, send, near, start in (
        (side_low, send_low, slice(0, 8), 0),
        (side_high, send_high, slice(cols - 8, cols), 6),
    ):
        for slab in range(out.shape[2] // LANES):
            to = slab * LANES
            if to < latent or to >= chans + width:
                begin = to if to < latent else to - 2 * width
                part = frames[:, near, begin : begin + LANES].astype(F32)
            elif to < chans:
                part = hids[:, near, to - latent : to - latent + LANES].astype(F32)
            else:
                part = cells[:, near, to - chans : to - chans + LANES]
            send[:, :, to : to + LANES] = part[:, start : start + 2].astype(BF)
            flat[...] = part.reshape(rows * 8, LANES)
            for place in range(2):
                out[place, :, to : to + LANES] = flat[pl.ds(start + place, rows, stride=8), :].astype(BF)


def pack_step(frames, hid, cell):
    rows, cols, width = hid.shape
    span = frames.shape[2]
    deep = span + 2 * width
    shapes = [jax.ShapeDtypeStruct((rows, 2, deep), BF)] * 2 + [jax.ShapeDtypeStruct((2, rows, deep), BF)] * 2
    shapes += [jax.ShapeDtypeStruct((2, cols, deep), BF)] * 2
    return pl.pallas_call(
        pack_kernel,
        grid=(1,),
        in_specs=[pl.BlockSpec(memory_space=pltpu.VMEM)] * 3,
        out_specs=[whole(shape) for shape in shapes],
        out_shape=shapes,
        scratch_shapes=[pltpu.VMEM((rows * 8, LANES), F32)],
        compiler_params=pltpu.CompilerParams(vmem_limit_bytes=VMEM_LIMIT),
        cost_estimate=pl.CostEstimate(flops=0, bytes_accessed=4_000_000, transcendentals=0),
    )(frames, hid, cell)


def ring_kernel(
    above, below, line_top, line_bot, from_left, from_right, side_left, side_right, weights, bias,
    line_hid, line_cell, strip_hid, strip_cell, beside, strips,
):
    width = line_hid.shape[2]
    chans = weights.shape[0] // 9
    cols, length = line_top.shape[1], strip_hid.shape[1]
    rows = from_left.shape[1]
    columns = (
        (from_left, 0, cols), (from_left, 1, cols + 1), (side_left, 0, 0), (side_left, 1, 1),
        (side_right, 0, cols - 2), (side_right, 1, cols - 1), (from_right, 0, cols + 2), (from_right, 1, cols + 3),
    )
    ends = [(ref[row].astype(F32), at + row) for ref, at in ((above, 0), (below, rows + 2)) for row in range(2)]
    strips[:, rows + 4 :, :] = jnp.zeros((8, length - rows - 4, strips.shape[2]), F32)
    for place, (source, at, end) in enumerate(columns):
        strips[place, 2 : rows + 2, :] = source[at].astype(F32)
        for value, spot in ends:
            strips[place, spot : spot + 1, :] = value[end : end + 1]
    beside[0] = strips[1, :, chans + width :]
    beside[1] = strips[6, :, chans + width :]
    low, high = strips[1, :, :chans], strips[6, :, :chans]

    def line(ref, row):
        held = ref[row, :cols].astype(F32)
        return held[:, :chans], held[:, chans : chans + width]

    tops = [line(above, 0), line(above, 1), line(line_top, 0), line(line_top, 1)]
    bots = [line(line_bot, 0), line(line_bot, 1), line(below, 0), line(below, 1)]
    parts, held = [], []
    for lead, lines in ((0, tops), (rows, bots)):
        pieces = []
        for row in range(4):
            at = lead + row
            pieces.append(three_columns(lines[row][0], low[at : at + 1], high[at : at + 1]))
        for row in range(2):
            parts.append(jnp.concatenate([pieces[row + tap][col] for tap in range(3) for col in range(3)], axis=1))
            held.append(lines[row + 1][1])
    for side in range(2):
        rolled = []
        for col in range(4):
            wide = strips[4 * side + col, :, :chans]
            rolled.append((pltpu.roll(wide, 1, axis=0), wide, pltpu.roll(wide, length - 1, axis=0)))
        for col in range(2):
            parts.append(
                jnp.concatenate([rolled[col + tap][row].astype(BF) for row in range(3) for tap in range(3)], axis=1)
            )
            held.append(strips[4 * side + col + 1, :, chans : chans + width])
    row_at, col_at = lax.axis_index("gy"), lax.axis_index("gx")
    upper = (row_at > 0).astype(F32)
    lower = (row_at < lax.axis_size("gy") - 1).astype(F32)
    before = (col_at > 0).astype(F32)
    after = (col_at < lax.axis_size("gx") - 1).astype(F32)
    spot = lax.broadcasted_iota(jnp.int32, (length, width), 0)
    inside = jnp.where(spot == 1, upper, jnp.where(spot == rows + 2, lower, 1.0))
    keep = [upper, 1.0, 1.0, lower, inside * before, inside, inside, inside * after]
    lhs = jnp.concatenate(parts, axis=0)
    gates = jnp.dot(lhs, weights[...], preferred_element_type=F32) + bias[...]
    start = 0
    for place in range(8):
        hid, cell = (line_hid, line_cell) if place < 4 else (strip_hid, strip_cell)
        size = hid.shape[1]
        new_cell, hidden = lstm(gates[start : start + size], held[place])
        hid[place % 4] = hidden.astype(BF).astype(F32) * keep[place]
        cell[place % 4] = new_cell
        start += size


def block_kernel(x, w_qkv, w_out, w_up, w_down, *rest):
    out, flat, back, keys_t, own_low, own_high, own_values, ones = rest[-8:]
    group = GRID * GRID
    embed = w_out.shape[0]
    tile = embed // 2

    @pl.when((pl.program_id(0) == 0) & (pl.program_id(1) == 0))
    def _():
        def fill(target, down, across, add):
            above = lax.broadcasted_iota(jnp.int32, target.shape, 0) // down
            along = lax.broadcasted_iota(jnp.int32, target.shape, 1) // across
            target[...] = (above == along + add).astype(F32).astype(BF)

        fill(own_low, HDIM, group, 0)
        fill(own_high, HDIM, group, HEADS // 4)
        fill(own_values, group, HDIM, 0)
        fill(ones, group, group, 0)
        keys_t[...] = w_qkv[:, embed : 2 * embed].astype(F32).T.astype(BF)

    flat[...] = x[...].astype(F32).reshape(flat.shape)
    groups = flat.shape[0] // group
    cells = jnp.concatenate([flat[pl.ds(g, group, stride=groups), :] for g in range(groups)], axis=0)
    normed = layer_norm(cells).astype(BF)
    queries = jnp.dot(normed, w_qkv[:, :embed], preferred_element_type=F32).astype(BF)
    values = jnp.dot(normed, w_qkv[:, 2 * embed :], preferred_element_type=F32).astype(BF)
    keys = lax.dot_general(keys_t[...], normed, (((1,), (1,)), ((), ())), preferred_element_type=F32)
    side = lax.broadcasted_iota(jnp.int32, (embed, 2 * group), 1) < group
    raised = [[], []]
    for pair in range(groups // 2):
        both = keys[:, pair * 2 * group : (pair + 1) * 2 * group]
        turned = pltpu.roll(both, group, axis=1)
        for place, twice in enumerate((jnp.where(side, both, turned), jnp.where(side, turned, both))):
            twice = twice.astype(BF)
            start = (2 * pair + place) * group
            for half in range(2):
                part = twice[half * tile : (half + 1) * tile]
                spread = jnp.concatenate([part * own_low[...], part * own_high[...]], axis=1)
                scores = jnp.dot(
                    queries[start : start + group, half * tile : (half + 1) * tile], spread, preferred_element_type=F32
                )
                raised[half].append(jnp.minimum(jnp.exp2(scores * (LOG2E * HDIM**-0.5)), BF_MAX).astype(BF))
    heads = []
    for half in range(2):
        part = jnp.concatenate(raised[half], axis=0)
        total = jnp.dot(part, ones[...], preferred_element_type=F32)
        guess = pl.reciprocal(total, approx=True)
        attn = (part.astype(F32) * (guess * (2.0 - total * guess))).astype(BF)
        column = []
        for g in range(groups):
            held = values[g * group : (g + 1) * group, half * tile : (half + 1) * tile]
            spread = jnp.concatenate([held] * (HEADS // 2), axis=0) * own_values[...]
            column.append(
                jnp.dot(attn[g * group : (g + 1) * group], spread, preferred_element_type=F32).astype(BF)
            )
        heads.append(jnp.concatenate(column, axis=0))
    heads = jnp.concatenate(heads, axis=1)
    attended = jnp.dot(heads, w_out[...], preferred_element_type=F32).astype(BF)
    mixed = cells + attended.astype(F32)
    normed_two = layer_norm(mixed).astype(BF)
    up = jnp.dot(normed_two, w_up[...], preferred_element_type=F32)
    bent = jnp.tanh(up * (0.7978845608 + (0.7978845608 * 0.044715) * (up * up)))
    half_up = 0.5 * up
    expanded = (half_up + half_up * bent).astype(BF)
    result = mixed + jnp.dot(expanded, w_down[...], preferred_element_type=F32)
    for g in range(groups):
        back[pl.ds(g, group, stride=groups), :] = result[g * group : (g + 1) * group]
    out[...] = back[...].reshape(x.shape).astype(BF)


def block_step(moved, carry, first, pieces, devices_y, devices_x, w_qkv, w_out, w_up, w_down):
    _, piece_y, piece_cols, width = moved.shape
    lanes = devices_y // GRID
    view = moved.reshape(GRID, lanes, devices_x, piece_y, piece_cols, width)
    tokens = GRID * devices_x * piece_cols
    block = (GRID, None, devices_x, None, piece_cols, width)
    operands = [view, w_qkv, w_out, w_up, w_down]
    in_specs = [pl.BlockSpec(block, lambda i, j: (0, i, 0, j, 0, 0)), *(whole(array) for array in operands[1:])]
    aliases = {}
    if carry is not None:
        aliases = {len(operands): 0}
        operands.append(carry)
        in_specs.append(pl.BlockSpec(memory_space=pl.ANY))
    total = lanes * piece_y * tokens
    return pl.pallas_call(
        block_kernel,
        grid=(lanes, piece_y),
        in_specs=in_specs,
        out_specs=pl.BlockSpec(block, lambda i, j: (0, i, 0, first + j, 0, 0)),
        out_shape=jax.ShapeDtypeStruct((GRID, lanes, devices_x, pieces, piece_cols, width), BF),
        scratch_shapes=[
            pltpu.VMEM((tokens, width), F32),
            pltpu.VMEM((tokens, width), F32),
            pltpu.VMEM((w_out.shape[0], width), BF),
            pltpu.VMEM((HEADS // 2 * HDIM, 2 * GRID * GRID), BF),
            pltpu.VMEM((HEADS // 2 * HDIM, 2 * GRID * GRID), BF),
            pltpu.VMEM((HEADS // 2 * GRID * GRID, HEADS // 2 * HDIM), BF),
            pltpu.VMEM((HEADS // 2 * GRID * GRID, HEADS // 2 * GRID * GRID), BF),
        ],
        input_output_aliases=aliases,
        compiler_params=pltpu.CompilerParams(vmem_limit_bytes=VMEM_LIMIT),
        cost_estimate=pl.CostEstimate(
            flops=total * 3_000_000, bytes_accessed=total * width * 4 + 800_000, transcendentals=total * 1100
        ),
    )(*operands)


def unpack_kernel(shares, local_m, piece_x, src, out):
    owners_y, owners_x = src.shape[:2]
    unit = out.shape[0]
    lines, first = [], 0
    for share in shares:
        lines += [(owner_y, first + piece) for owner_y in range(owners_y) for piece in range(share)]
        first += share
    for step in range(len(lines) // unit):

        @pl.when(pl.program_id(0) == step)
        def _():
            for row, (owner_y, piece) in enumerate(lines[step * unit : (step + 1) * unit]):
                wide = src[owner_y, :, piece].astype(F32)
                parts = [
                    wide[owner, m * piece_x : (m + 1) * piece_x] for m in range(local_m) for owner in range(owners_x)
                ]
                out[row] = jnp.concatenate(parts, axis=0).astype(BF)


def unpack_step(landed, shares, cols, local_m, piece_x):
    owners_y, _, pieces, _, width = landed.shape
    rows = owners_y * pieces
    unit = 16 if rows % 16 == 0 else rows
    return pl.pallas_call(
        functools.partial(unpack_kernel, shares, local_m, piece_x),
        grid=(rows // unit,),
        in_specs=[pl.BlockSpec(memory_space=pltpu.VMEM)],
        out_specs=pl.BlockSpec((unit, cols, width), lambda step: (step, 0, 0)),
        out_shape=jax.ShapeDtypeStruct((rows, cols, width), BF),
        compiler_params=pltpu.CompilerParams(vmem_limit_bytes=VMEM_LIMIT),
        cost_estimate=pl.CostEstimate(flops=0, bytes_accessed=rows * cols * width * 4, transcendentals=0),
    )(landed)


def step_rows(start, extent, most=16):
    return max(size for size in range(1, most + 1) if extent % size == 0 and start % size == 0)


def body(frames, hidden_state, cell_state, w_gates, gate_bias, w_qkv, w_out, w_up, w_down):
    rows, cols, width = hidden_state.shape
    latent = frames.shape[2] // 2
    chans = latent + width
    held = chans + width
    devices_y, devices_x = lax.axis_size("gy"), lax.axis_size("gx")
    local_m = GRID // devices_x
    piece_x = cols // local_m // devices_x
    weights = w_gates.reshape(-1, w_gates.shape[3])
    bias = gate_bias.reshape(1, -1)

    def shifted(value, axis, step):
        count = lax.axis_size(axis)
        pairs = [(i, i + step) for i in range(count) if 0 <= i + step < count]
        return lax.ppermute(value, axis, pairs)

    send_left, send_right, side_left, side_right, line_top, line_bot = pack_step(frames, hidden_state, cell_state)
    from_left = shifted(send_right, "gx", 1)
    from_right = shifted(send_left, "gx", -1)
    to_down = jnp.concatenate([line_bot, from_left[-2:], from_right[-2:]], axis=1)
    to_up = jnp.concatenate([line_top, from_left[:2], from_right[:2]], axis=1)

    tile_shapes = (jax.ShapeDtypeStruct((rows, cols, width), BF), jax.ShapeDtypeStruct((rows, cols, width), F32))
    carry = ()
    for start, extent in ((0, rows // 2), (rows // 2, rows - rows // 2)):
        spec = pl.BlockSpec(memory_space=pltpu.VMEM)
        if carry:
            *carry, to_down, to_up = lax.optimization_barrier((*carry, to_down, to_up))
            from_up, from_down = shifted(to_down, "gy", 1), shifted(to_up, "gy", -1)
        carry = conv_step(
            frames, 0, hidden_state, cell_state, {}, weights, bias, (start, extent), ("hid_out", "cell_out"),
            tile_shapes, (spec, spec), None, carry, False,
        )
    hidden_one, cell_one = carry

    length = -(-(rows + 4) // 16) * 16
    line_shape = jax.ShapeDtypeStruct((4, cols, width), F32)
    strip_shape = jax.ShapeDtypeStruct((4, length, width), F32)
    beside_shape = jax.ShapeDtypeStruct((2, length, latent), F32)
    shapes = (line_shape, line_shape, strip_shape, strip_shape, beside_shape)
    turned = from_left.transpose(1, 0, 2), from_right.transpose(1, 0, 2)
    around = (from_up, from_down, line_top, line_bot, *turned, side_left, side_right)
    line_hid, line_cell, strip_hid, strip_cell, beside = pl.pallas_call(
        ring_kernel,
        grid=(1,),
        in_specs=[*(whole(array) for array in around), pl.BlockSpec(memory_space=pltpu.VMEM), whole(bias)],
        out_specs=[whole(shape) for shape in shapes],
        out_shape=shapes,
        scratch_shapes=[pltpu.VMEM((8, length, held + latent), F32)],
        compiler_params=pltpu.CompilerParams(vmem_limit_bytes=VMEM_LIMIT),
        cost_estimate=pl.CostEstimate(flops=16 * length * weights.size, bytes_accessed=2 * weights.size, transcendentals=0),
    )(*around, weights, bias)

    second = held // latent
    line = (1, from_up.shape[1], latent)
    ring = {name: (array, whole(array)) for name, array in (
        ("strips_hid", strip_hid), ("strips_cell", strip_cell), ("lines_hid", line_hid), ("lines_cell", line_cell),
        ("beside", beside),
    )}
    ring["frame_top"] = from_up, pl.BlockSpec(line, lambda step: (1, 0, second))
    ring["frame_bot"] = from_down, pl.BlockSpec(line, lambda step: (0, 0, second))

    pieces = rows // devices_y
    piece_cols = local_m * piece_x
    shares = (pieces - pieces // 3, pieces // 3)
    moved, start, carry = [], 0, ()
    for piece_y in shares:
        extent = piece_y * devices_y
        sent_shape = jax.ShapeDtypeStruct((devices_y, devices_x, piece_y, piece_cols, width), BF)
        spec = pl.BlockSpec(memory_space=pl.ANY)
        sent, cell_out = conv_step(
            frames, 1, hidden_one, cell_one, ring, weights, bias, (start, extent),
            ("hid_out", "cell_out"), (sent_shape, tile_shapes[1]), (whole(sent_shape), spec), (local_m, piece_x), carry,
            bool(carry),
        )
        carry = (None, cell_out)
        sent = sent.reshape(devices_y * devices_x, piece_y, piece_cols, width)
        moved.append(lax.all_to_all(sent, ("gy", "gx"), split_axis=0, concat_axis=0, tiled=True))
        start += extent
    done, first = None, 0
    for piece_y, value in zip(shares, moved):
        done = block_step(value, done, first, pieces, devices_y, devices_x, w_qkv, w_out, w_up, w_down)
        first += piece_y
    done = done.reshape(devices_y * devices_x, pieces, piece_cols, width)
    landed = lax.all_to_all(done, ("gy", "gx"), split_axis=0, concat_axis=0, tiled=True)
    result = unpack_step(landed.reshape(devices_y, devices_x, *landed.shape[1:]), shares, cols, local_m, piece_x)
    return result, cell_out


def solution(mesh):
    tiled = P("gy", "gx", None)
    in_specs = (tiled, tiled, tiled, P(), P(), P(), P(), P(), P())
    return jax.shard_map(body, mesh=mesh, in_specs=in_specs, out_specs=(tiled, tiled), check_vma=False)
```

```python
import functools

import jax
import jax.numpy as jnp
from jax import lax
from jax.experimental import pallas as pl
from jax.experimental.pallas import tpu as pltpu
from jax.sharding import PartitionSpec as P

HEADS = 8
HDIM = 32
GRID = 8
BF = jnp.bfloat16
F32 = jnp.float32
LOG2E = 1.4426950408889634
BF_MAX = 3.3895313892515355e38
VMEM_LIMIT = 32 * 1024 * 1024
VMEM_ALL = 60 * 1024 * 1024
LOADS = 9
LANES = 128


def sigmoid(x):
    return 0.5 * jnp.tanh(0.5 * x) + 0.5


def lstm(gates, cell_prev):
    width = cell_prev.shape[-1]
    in_gate = sigmoid(gates[:, 0:width])
    forget_gate = sigmoid(gates[:, width : 2 * width])
    candidate = jnp.tanh(gates[:, 2 * width : 3 * width])
    out_gate = sigmoid(gates[:, 3 * width :])
    cell = forget_gate * cell_prev + in_gate * candidate
    return cell, out_gate * jnp.tanh(cell)


def layer_norm(values):
    center = values - jnp.mean(values, axis=-1, keepdims=True)
    spread = jnp.mean(center * center, axis=-1, keepdims=True)
    return center * lax.rsqrt(spread + 1e-05)


def three_columns(wide, left, right):
    count = wide.shape[0]
    place = lax.broadcasted_iota(jnp.int32, wide.shape, 0)
    before = jnp.where(place == 0, left, pltpu.roll(wide, 1, axis=0))
    after = jnp.where(place == count - 1, right, pltpu.roll(wide, count - 1, axis=0))
    return before.astype(BF), wide.astype(BF), after.astype(BF)


def conv_kernel(start, rows, part, refs, packed, *args):
    ref = dict(zip(refs, args))
    spread, hid_out, cell_out = ref["spread"], ref["hid_out"], ref["cell_out"]
    ring = "strips_hid" in ref
    extent = spread.shape[0] - 2
    cols, width = ref["hid"].shape[1:]
    chans = spread.shape[2] // 3
    latent = chans - width
    top, bot = start == 0, start + extent == rows

    def row_of(name, row):
        channels = slice(part * latent, (part + 1) * latent) if name == "frame" else slice(None)
        if ref[name].shape[0] == rows:
            return ref[name][row, :, channels]
        if row == start - 1:
            return ref[name + "_prev"][0]
        if row == start + extent:
            return ref[name + "_next"][0]
        return ref[name][row - start]

    loads = []
    if "weights" in ref:
        size = ref["weights"].shape[0] // LOADS
        for place in range(LOADS):
            run = pl.ds(place * size, size)
            loads.append(pltpu.make_async_copy(ref["weights"].at[run], ref["held"].at[run], ref["sem"].at[place]))
    for load in loads:
        load.start()

    def beside(row):
        if not ring:
            return jnp.zeros((1, chans), F32), jnp.zeros((1, chans), F32)
        at = row + 2
        return tuple(
            jnp.concatenate(
                [ref["beside"][place, at : at + 1, :], ref["strips_hid"][3 * place, at : at + 1, :]], axis=1
            )
            for place in range(2)
        )

    def build(pos):
        row = start + pos - 1
        raw = None
        if 0 <= row < rows:
            raw = row_of("frame", row), row_of("hid", row)
            x, h = raw[0].astype(F32), raw[1].astype(F32)
        elif ring:
            x, h = ref["frame_top" if row < 0 else "frame_bot"][0, :cols].astype(F32), ref["lines_hid"][3 * (row > 0)]
        else:
            spread[pos] = jnp.zeros(spread.shape[1:], BF)
            return
        low, high = beside(row)
        if ring:
            at = row + 2
            place = lax.broadcasted_iota(jnp.int32, h.shape, 0)
            h = jnp.where(place == 0, ref["strips_hid"][1, at : at + 1, :], h)
            h = jnp.where(place == cols - 1, ref["strips_hid"][2, at : at + 1, :], h)
            for spot, line in ((-1, 0), (0, 1), (rows - 1, 2), (rows, 3)):
                if row == spot:
                    h = ref["lines_hid"][line]
        for side, (value, first) in enumerate(((x, 0), (h, latent))):
            size = value.shape[1]
            pieces = three_columns(value, low[:, first : first + size], high[:, first : first + size])
            if raw is not None and (side == 0 or not ring):
                pieces = pieces[0], raw[side], pieces[2]
            for tap in range(3):
                spread[pos, :, tap * chans + first : tap * chans + first + size] = pieces[tap]

    def multiply(first, depth):
        lhs = jnp.concatenate(
            [spread[first + tap : first + tap + depth].reshape(depth * cols, 3 * chans) for tap in range(3)], axis=1
        )
        return jnp.dot(lhs, ref["held"][...], preferred_element_type=F32)

    def activate(first, depth, gates):
        for line in range(first, first + depth):
            row = start + line
            cell_prev = row_of("cell", row)
            if ring:
                at = row + 2
                place = lax.broadcasted_iota(jnp.int32, cell_prev.shape, 0)
                cell_prev = jnp.where(place == 0, ref["strips_cell"][1, at : at + 1, :], cell_prev)
                cell_prev = jnp.where(place == cols - 1, ref["strips_cell"][2, at : at + 1, :], cell_prev)
                if row == 0:
                    cell_prev = ref["lines_cell"][1]
                if row == rows - 1:
                    cell_prev = ref["lines_cell"][2]
            own = gates[(line - first) * cols : (line - first + 1) * cols] + ref["bias"][...]
            new_cell, new_hidden = lstm(own, cell_prev)
            if not packed:
                cell_out[row] = new_cell
                hid_out[row] = new_hidden.astype(BF)
                continue
            ref["cell_rows"][line] = new_cell
            owners_x, piece_y = hid_out.shape[1:3]
            local_m, piece_x = packed
            for owner in range(owners_x):
                picked = [
                    new_hidden[(m * owners_x + owner) * piece_x : (m * owners_x + owner + 1) * piece_x]
                    for m in range(local_m)
                ]
                hid_out[line // piece_y, owner, line % piece_y] = jnp.concatenate(picked, axis=0).astype(BF)

        if packed:
            done = pl.ds(first, depth)
            leave = pltpu.make_async_copy(
                ref["cell_rows"].at[done], cell_out.at[pl.ds(start + first, depth)], ref["left"].at[first // depth]
            )
            leave.start()
            leaving.append(leave)

    leaving = []
    depth = step_rows(0, extent, 24)
    for pos in range(depth + 2):
        build(pos)
    for load in loads:
        load.wait()
    waiting = None
    for first in range(0, extent, depth):
        for pos in range(first + depth + 2, min(first + 2 * depth, extent) + 2):
            build(pos)
        gates = multiply(first, depth)
        if waiting:
            activate(*waiting)
        waiting = first, depth, gates
    activate(*waiting)
    for leave in leaving:
        leave.wait()


def whole(array):
    return pl.BlockSpec(array.shape, lambda *step: (0,) * array.ndim)


def conv_step(frames, part, hid, cell, ring, weights, bias, rows_of, names, out_shapes, out_specs, packed, carry, load):
    rows, cols, width = hid.shape
    latent = weights.shape[0] // 9 - width
    start, extent = rows_of

    def rowed(size, channels, channel, row):
        return pl.BlockSpec((size, cols, channels), lambda step: (row // size, 0, channel))

    before, after = max(start - 1, 0), min(start + extent, rows - 1)
    near = pl.BlockSpec(memory_space=pltpu.VMEM)
    if load:
        inputs = {
            "frame": (frames, rowed(extent, latent, part, start)),
            "frame_prev": (frames, rowed(1, latent, part, before)),
            "frame_next": (frames, rowed(1, latent, part, after)),
            "hid": (hid, rowed(extent, width, 0, start)),
            "hid_prev": (hid, rowed(1, width, 0, before)),
            "hid_next": (hid, rowed(1, width, 0, after)),
            "cell": (cell, rowed(extent, width, 0, start)),
        }
    else:
        inputs = {"frame": (frames, near), "hid": (hid, near), "cell": (cell, near)}
    inputs["bias"] = bias, whole(bias)
    if load:
        inputs["weights"] = weights, pl.BlockSpec(memory_space=pl.ANY)
    else:
        inputs["held"] = weights, near
    inputs |= ring
    aliases = {}
    for place, array in enumerate(carry):
        if array is not None:
            aliases[len(inputs)] = place
            inputs[f"carry{place}"] = (array, pl.BlockSpec(memory_space=pl.ANY) if packed else near)
    refs = [*inputs, *names, "spread"]
    scratch = [pltpu.VMEM((extent + 2, cols, 3 * (latent + width)), BF)]
    if load:
        refs += ["held", "sem"]
        scratch += [pltpu.VMEM(weights.shape, BF), pltpu.SemaphoreType.DMA((LOADS,))]
    if packed:
        refs += ["cell_rows", "left"]
        scratch += [pltpu.VMEM((extent, cols, width), F32), pltpu.SemaphoreType.DMA((extent,))]
    cells = extent * cols
    return pl.pallas_call(
        functools.partial(conv_kernel, start, rows, part, refs, packed),
        grid=(1,),
        in_specs=[spec for _, spec in inputs.values()],
        out_specs=out_specs,
        out_shape=out_shapes,
        scratch_shapes=scratch,
        input_output_aliases=aliases,
        compiler_params=pltpu.CompilerParams(vmem_limit_bytes=VMEM_ALL if load else VMEM_LIMIT),
        cost_estimate=pl.CostEstimate(
            flops=2 * cells * weights.size, bytes_accessed=2 * weights.size + cells * 2048, transcendentals=cells * width * 5
        ),
    )(*(array for array, _ in inputs.values()))


def pack_kernel(frames, hids, cells, send_low, send_high, side_low, side_high, line_top, line_bot, flat):
    rows, cols, width = hids.shape
    latent = frames.shape[2] // 2
    chans = latent + width
    places = ((0, 0, latent), (chans + width, latent, latent))
    for out, near in ((line_top, slice(0, 2)), (line_bot, slice(rows - 2, rows))):
        for to, start, size in places:
            out[:, :, to : to + size] = frames[near, :, start : start + size]
        out[:, :, latent:chans] = hids[near]
        out[:, :, chans : chans + width] = cells[near].astype(BF)
    for out, send, near, start in (
        (side_low, send_low, slice(0, 8), 0),
        (side_high, send_high, slice(cols - 8, cols), 6),
    ):
        for slab in range(out.shape[2] // LANES):
            to = slab * LANES
            if to < latent or to >= chans + width:
                begin = to if to < latent else to - 2 * width
                part = frames[:, near, begin : begin + LANES].astype(F32)
            elif to < chans:
                part = hids[:, near, to - latent : to - latent + LANES].astype(F32)
            else:
                part = cells[:, near, to - chans : to - chans + LANES]
            send[:, :, to : to + LANES] = part[:, start : start + 2].astype(BF)
            flat[...] = part.reshape(rows * 8, LANES)
            for place in range(2):
                out[place, :, to : to + LANES] = flat[pl.ds(start + place, rows, stride=8), :].astype(BF)


def pack_step(frames, hid, cell):
    rows, cols, width = hid.shape
    span = frames.shape[2]
    deep = span + 2 * width
    shapes = [jax.ShapeDtypeStruct((rows, 2, deep), BF)] * 2 + [jax.ShapeDtypeStruct((2, rows, deep), BF)] * 2
    shapes += [jax.ShapeDtypeStruct((2, cols, deep), BF)] * 2
    return pl.pallas_call(
        pack_kernel,
        grid=(1,),
        in_specs=[pl.BlockSpec(memory_space=pltpu.VMEM)] * 3,
        out_specs=[whole(shape) for shape in shapes],
        out_shape=shapes,
        scratch_shapes=[pltpu.VMEM((rows * 8, LANES), F32)],
        compiler_params=pltpu.CompilerParams(vmem_limit_bytes=VMEM_LIMIT),
        cost_estimate=pl.CostEstimate(flops=0, bytes_accessed=4_000_000, transcendentals=0),
    )(frames, hid, cell)


def ring_kernel(
    above, below, line_top, line_bot, from_left, from_right, side_left, side_right, weights, bias,
    line_hid, line_cell, strip_hid, strip_cell, beside, strips,
):
    width = line_hid.shape[2]
    chans = weights.shape[0] // 9
    cols, length = line_top.shape[1], strip_hid.shape[1]
    rows = from_left.shape[1]
    columns = (
        (from_left, 0, cols), (from_left, 1, cols + 1), (side_left, 0, 0), (side_left, 1, 1),
        (side_right, 0, cols - 2), (side_right, 1, cols - 1), (from_right, 0, cols + 2), (from_right, 1, cols + 3),
    )
    ends = [(ref[row].astype(F32), at + row) for ref, at in ((above, 0), (below, rows + 2)) for row in range(2)]
    strips[:, rows + 4 :, :] = jnp.zeros((8, length - rows - 4, strips.shape[2]), F32)
    for place, (source, at, end) in enumerate(columns):
        strips[place, 2 : rows + 2, :] = source[at].astype(F32)
        for value, spot in ends:
            strips[place, spot : spot + 1, :] = value[end : end + 1]
    beside[0] = strips[1, :, chans + width :]
    beside[1] = strips[6, :, chans + width :]
    low, high = strips[1, :, :chans], strips[6, :, :chans]

    def line(ref, row):
        held = ref[row, :cols].astype(F32)
        return held[:, :chans], held[:, chans : chans + width]

    tops = [line(above, 0), line(above, 1), line(line_top, 0), line(line_top, 1)]
    bots = [line(line_bot, 0), line(line_bot, 1), line(below, 0), line(below, 1)]
    parts, held = [], []
    for lead, lines in ((0, tops), (rows, bots)):
        pieces = []
        for row in range(4):
            at = lead + row
            pieces.append(three_columns(lines[row][0], low[at : at + 1], high[at : at + 1]))
        for row in range(2):
            parts.append(jnp.concatenate([pieces[row + tap][col] for tap in range(3) for col in range(3)], axis=1))
            held.append(lines[row + 1][1])
    for side in range(2):
        rolled = []
        for col in range(4):
            wide = strips[4 * side + col, :, :chans]
            rolled.append((pltpu.roll(wide, 1, axis=0), wide, pltpu.roll(wide, length - 1, axis=0)))
        for col in range(2):
            parts.append(
                jnp.concatenate([rolled[col + tap][row].astype(BF) for row in range(3) for tap in range(3)], axis=1)
            )
            held.append(strips[4 * side + col + 1, :, chans : chans + width])
    row_at, col_at = lax.axis_index("gy"), lax.axis_index("gx")
    upper = (row_at > 0).astype(F32)
    lower = (row_at < lax.axis_size("gy") - 1).astype(F32)
    before = (col_at > 0).astype(F32)
    after = (col_at < lax.axis_size("gx") - 1).astype(F32)
    spot = lax.broadcasted_iota(jnp.int32, (length, width), 0)
    inside = jnp.where(spot == 1, upper, jnp.where(spot == rows + 2, lower, 1.0))
    keep = [upper, 1.0, 1.0, lower, inside * before, inside, inside, inside * after]
    lhs = jnp.concatenate(parts, axis=0)
    gates = jnp.dot(lhs, weights[...], preferred_element_type=F32) + bias[...]
    start = 0
    for place in range(8):
        hid, cell = (line_hid, line_cell) if place < 4 else (strip_hid, strip_cell)
        size = hid.shape[1]
        new_cell, hidden = lstm(gates[start : start + size], held[place])
        hid[place % 4] = hidden.astype(BF).astype(F32) * keep[place]
        cell[place % 4] = new_cell
        start += size


def block_kernel(x, w_qkv, w_out, w_up, w_down, *rest):
    out, flat, back, keys_t, own_low, own_high, own_values, ones = rest[-8:]
    group = GRID * GRID
    embed = w_out.shape[0]
    tile = embed // 2

    @pl.when((pl.program_id(0) == 0) & (pl.program_id(1) == 0))
    def _():
        def fill(target, down, across, add):
            above = lax.broadcasted_iota(jnp.int32, target.shape, 0) // down
            along = lax.broadcasted_iota(jnp.int32, target.shape, 1) // across
            target[...] = (above == along + add).astype(F32).astype(BF)

        fill(own_low, HDIM, group, 0)
        fill(own_high, HDIM, group, HEADS // 4)
        fill(own_values, group, HDIM, 0)
        fill(ones, group, group, 0)
        keys_t[...] = w_qkv[:, embed : 2 * embed].astype(F32).T.astype(BF)

    flat[...] = x[...].astype(F32).reshape(flat.shape)
    groups = flat.shape[0] // group
    cells = jnp.concatenate([flat[pl.ds(g, group, stride=groups), :] for g in range(groups)], axis=0)
    normed = layer_norm(cells).astype(BF)
    queries = jnp.dot(normed, w_qkv[:, :embed], preferred_element_type=F32).astype(BF)
    values = jnp.dot(normed, w_qkv[:, 2 * embed :], preferred_element_type=F32).astype(BF)
    keys = lax.dot_general(keys_t[...], normed, (((1,), (1,)), ((), ())), preferred_element_type=F32)
    side = lax.broadcasted_iota(jnp.int32, (embed, 2 * group), 1) < group
    raised = [[], []]
    for pair in range(groups // 2):
        both = keys[:, pair * 2 * group : (pair + 1) * 2 * group]
        turned = pltpu.roll(both, group, axis=1)
        for place, twice in enumerate((jnp.where(side, both, turned), jnp.where(side, turned, both))):
            twice = twice.astype(BF)
            start = (2 * pair + place) * group
            for half in range(2):
                part = twice[half * tile : (half + 1) * tile]
                spread = jnp.concatenate([part * own_low[...], part * own_high[...]], axis=1)
                scores = jnp.dot(
                    queries[start : start + group, half * tile : (half + 1) * tile], spread, preferred_element_type=F32
                )
                raised[half].append(jnp.minimum(jnp.exp2(scores * (LOG2E * HDIM**-0.5)), BF_MAX).astype(BF))
    heads = []
    for half in range(2):
        part = jnp.concatenate(raised[half], axis=0)
        total = jnp.dot(part, ones[...], preferred_element_type=F32)
        guess = pl.reciprocal(total, approx=True)
        attn = (part.astype(F32) * (guess * (2.0 - total * guess))).astype(BF)
        column = []
        for g in range(groups):
            held = values[g * group : (g + 1) * group, half * tile : (half + 1) * tile]
            spread = jnp.concatenate([held] * (HEADS // 2), axis=0) * own_values[...]
            column.append(
                jnp.dot(attn[g * group : (g + 1) * group], spread, preferred_element_type=F32).astype(BF)
            )
        heads.append(jnp.concatenate(column, axis=0))
    heads = jnp.concatenate(heads, axis=1)
    attended = jnp.dot(heads, w_out[...], preferred_element_type=F32).astype(BF)
    mixed = cells + attended.astype(F32)
    normed_two = layer_norm(mixed).astype(BF)
    up = jnp.dot(normed_two, w_up[...], preferred_element_type=F32)
    bent = jnp.tanh(up * (0.7978845608 + (0.7978845608 * 0.044715) * (up * up)))
    half_up = 0.5 * up
    expanded = (half_up + half_up * bent).astype(BF)
    result = mixed + jnp.dot(expanded, w_down[...], preferred_element_type=F32)
    for g in range(groups):
        back[pl.ds(g, group, stride=groups), :] = result[g * group : (g + 1) * group]
    out[...] = back[...].reshape(x.shape).astype(BF)


def block_step(moved, carry, first, pieces, devices_y, devices_x, w_qkv, w_out, w_up, w_down):
    _, piece_y, piece_cols, width = moved.shape
    lanes = devices_y // GRID
    view = moved.reshape(GRID, lanes, devices_x, piece_y, piece_cols, width)
    tokens = GRID * devices_x * piece_cols
    block = (GRID, None, devices_x, None, piece_cols, width)
    operands = [view, w_qkv, w_out, w_up, w_down]
    in_specs = [pl.BlockSpec(block, lambda i, j: (0, i, 0, j, 0, 0)), *(whole(array) for array in operands[1:])]
    aliases = {}
    if carry is not None:
        aliases = {len(operands): 0}
        operands.append(carry)
        in_specs.append(pl.BlockSpec(memory_space=pl.ANY))
    total = lanes * piece_y * tokens
    return pl.pallas_call(
        block_kernel,
        grid=(lanes, piece_y),
        in_specs=in_specs,
        out_specs=pl.BlockSpec(block, lambda i, j: (0, i, 0, first + j, 0, 0)),
        out_shape=jax.ShapeDtypeStruct((GRID, lanes, devices_x, pieces, piece_cols, width), BF),
        scratch_shapes=[
            pltpu.VMEM((tokens, width), F32),
            pltpu.VMEM((tokens, width), F32),
            pltpu.VMEM((w_out.shape[0], width), BF),
            pltpu.VMEM((HEADS // 2 * HDIM, 2 * GRID * GRID), BF),
            pltpu.VMEM((HEADS // 2 * HDIM, 2 * GRID * GRID), BF),
            pltpu.VMEM((HEADS // 2 * GRID * GRID, HEADS // 2 * HDIM), BF),
            pltpu.VMEM((HEADS // 2 * GRID * GRID, HEADS // 2 * GRID * GRID), BF),
        ],
        input_output_aliases=aliases,
        compiler_params=pltpu.CompilerParams(vmem_limit_bytes=VMEM_LIMIT),
        cost_estimate=pl.CostEstimate(
            flops=total * 3_000_000, bytes_accessed=total * width * 4 + 800_000, transcendentals=total * 1100
        ),
    )(*operands)


def unpack_kernel(shares, local_m, piece_x, src, out):
    owners_y, owners_x = src.shape[:2]
    unit = out.shape[0]
    lines, first = [], 0
    for share in shares:
        lines += [(owner_y, first + piece) for owner_y in range(owners_y) for piece in range(share)]
        first += share
    for step in range(len(lines) // unit):

        @pl.when(pl.program_id(0) == step)
        def _():
            for row, (owner_y, piece) in enumerate(lines[step * unit : (step + 1) * unit]):
                wide = src[owner_y, :, piece].astype(F32)
                parts = [
                    wide[owner, m * piece_x : (m + 1) * piece_x] for m in range(local_m) for owner in range(owners_x)
                ]
                out[row] = jnp.concatenate(parts, axis=0).astype(BF)


def unpack_step(landed, shares, cols, local_m, piece_x):
    owners_y, _, pieces, _, width = landed.shape
    rows = owners_y * pieces
    unit = 16 if rows % 16 == 0 else rows
    return pl.pallas_call(
        functools.partial(unpack_kernel, shares, local_m, piece_x),
        grid=(rows // unit,),
        in_specs=[pl.BlockSpec(memory_space=pltpu.VMEM)],
        out_specs=pl.BlockSpec((unit, cols, width), lambda step: (step, 0, 0)),
        out_shape=jax.ShapeDtypeStruct((rows, cols, width), BF),
        compiler_params=pltpu.CompilerParams(vmem_limit_bytes=VMEM_LIMIT),
        cost_estimate=pl.CostEstimate(flops=0, bytes_accessed=rows * cols * width * 4, transcendentals=0),
    )(landed)


def step_rows(start, extent, most):
    return max(size for size in range(1, most + 1) if extent % size == 0 and start % size == 0)


def body(frames, hidden_state, cell_state, w_gates, gate_bias, w_qkv, w_out, w_up, w_down):
    rows, cols, width = hidden_state.shape
    latent = frames.shape[2] // 2
    chans = latent + width
    held = chans + width
    devices_y, devices_x = lax.axis_size("gy"), lax.axis_size("gx")
    local_m = GRID // devices_x
    piece_x = cols // local_m // devices_x
    weights = w_gates.reshape(-1, w_gates.shape[3])
    bias = gate_bias.reshape(1, -1)

    def shifted(value, axis, step):
        count = lax.axis_size(axis)
        pairs = [(i, i + step) for i in range(count) if 0 <= i + step < count]
        return lax.ppermute(value, axis, pairs)

    send_left, send_right, side_left, side_right, line_top, line_bot = pack_step(frames, hidden_state, cell_state)
    from_left = shifted(send_right, "gx", 1)
    from_right = shifted(send_left, "gx", -1)
    to_down = jnp.concatenate([line_bot, from_left[-2:], from_right[-2:]], axis=1)
    to_up = jnp.concatenate([line_top, from_left[:2], from_right[:2]], axis=1)

    tile_shapes = (jax.ShapeDtypeStruct((rows, cols, width), BF), jax.ShapeDtypeStruct((rows, cols, width), F32))
    carry = ()
    for start, extent in ((0, rows // 2), (rows // 2, rows - rows // 2)):
        spec = pl.BlockSpec(memory_space=pltpu.VMEM)
        if carry:
            *carry, to_down, to_up = lax.optimization_barrier((*carry, to_down, to_up))
            from_up, from_down = shifted(to_down, "gy", 1), shifted(to_up, "gy", -1)
        carry = conv_step(
            frames, 0, hidden_state, cell_state, {}, weights, bias, (start, extent), ("hid_out", "cell_out"),
            tile_shapes, (spec, spec), None, carry, False,
        )
    hidden_one, cell_one = carry

    length = -(-(rows + 4) // 16) * 16
    line_shape = jax.ShapeDtypeStruct((4, cols, width), F32)
    strip_shape = jax.ShapeDtypeStruct((4, length, width), F32)
    beside_shape = jax.ShapeDtypeStruct((2, length, latent), F32)
    shapes = (line_shape, line_shape, strip_shape, strip_shape, beside_shape)
    turned = from_left.transpose(1, 0, 2), from_right.transpose(1, 0, 2)
    around = (from_up, from_down, line_top, line_bot, *turned, side_left, side_right)
    line_hid, line_cell, strip_hid, strip_cell, beside = pl.pallas_call(
        ring_kernel,
        grid=(1,),
        in_specs=[*(whole(array) for array in around), pl.BlockSpec(memory_space=pltpu.VMEM), whole(bias)],
        out_specs=[whole(shape) for shape in shapes],
        out_shape=shapes,
        scratch_shapes=[pltpu.VMEM((8, length, held + latent), F32)],
        compiler_params=pltpu.CompilerParams(vmem_limit_bytes=VMEM_LIMIT),
        cost_estimate=pl.CostEstimate(flops=16 * length * weights.size, bytes_accessed=2 * weights.size, transcendentals=0),
    )(*around, weights, bias)

    second = held // latent
    line = (1, from_up.shape[1], latent)
    ring = {name: (array, whole(array)) for name, array in (
        ("strips_hid", strip_hid), ("strips_cell", strip_cell), ("lines_hid", line_hid), ("lines_cell", line_cell),
        ("beside", beside),
    )}
    ring["frame_top"] = from_up, pl.BlockSpec(line, lambda step: (1, 0, second))
    ring["frame_bot"] = from_down, pl.BlockSpec(line, lambda step: (0, 0, second))

    pieces = rows // devices_y
    piece_cols = local_m * piece_x
    shares = (pieces - pieces // 3, pieces // 3)
    moved, start, carry = [], 0, ()
    for piece_y in shares:
        extent = piece_y * devices_y
        sent_shape = jax.ShapeDtypeStruct((devices_y, devices_x, piece_y, piece_cols, width), BF)
        spec = pl.BlockSpec(memory_space=pl.ANY)
        sent, cell_out = conv_step(
            frames, 1, hidden_one, cell_one, ring, weights, bias, (start, extent),
            ("hid_out", "cell_out"), (sent_shape, tile_shapes[1]), (whole(sent_shape), spec), (local_m, piece_x), carry,
            bool(carry),
        )
        carry = (None, cell_out)
        sent = sent.reshape(devices_y * devices_x, piece_y, piece_cols, width)
        moved.append(lax.all_to_all(sent, ("gy", "gx"), split_axis=0, concat_axis=0, tiled=True))
        start += extent
    done, first = None, 0
    for piece_y, value in zip(shares, moved):
        done = block_step(value, done, first, pieces, devices_y, devices_x, w_qkv, w_out, w_up, w_down)
        first += piece_y
    done = done.reshape(devices_y * devices_x, pieces, piece_cols, width)
    landed = lax.all_to_all(done, ("gy", "gx"), split_axis=0, concat_axis=0, tiled=True)
    result = unpack_step(landed.reshape(devices_y, devices_x, *landed.shape[1:]), shares, cols, local_m, piece_x)
    return result, cell_out


def solution(mesh):
    tiled = P("gy", "gx", None)
    in_specs = (tiled, tiled, tiled, P(), P(), P(), P(), P(), P())
    return jax.shard_map(body, mesh=mesh, in_specs=in_specs, out_specs=(tiled, tiled), check_vma=False)
```

```python
import functools

import jax
import jax.numpy as jnp
from jax import lax
from jax.experimental import pallas as pl
from jax.experimental.pallas import tpu as pltpu
from jax.sharding import PartitionSpec as P

HEADS = 8
HDIM = 32
GRID = 8
BF = jnp.bfloat16
F32 = jnp.float32
LOG2E = 1.4426950408889634
BF_MAX = 3.3895313892515355e38
VMEM_LIMIT = 32 * 1024 * 1024
VMEM_ALL = 60 * 1024 * 1024
LOADS = 9
LANES = 128


def sigmoid(x):
    return 0.5 * jnp.tanh(0.5 * x) + 0.5


def lstm(gates, cell_prev):
    width = cell_prev.shape[-1]
    in_gate = sigmoid(gates[:, 0:width])
    forget_gate = sigmoid(gates[:, width : 2 * width])
    candidate = jnp.tanh(gates[:, 2 * width : 3 * width])
    out_gate = sigmoid(gates[:, 3 * width :])
    cell = forget_gate * cell_prev + in_gate * candidate
    return cell, out_gate * jnp.tanh(cell)


def layer_norm(values):
    center = values - jnp.mean(values, axis=-1, keepdims=True)
    spread = jnp.mean(center * center, axis=-1, keepdims=True)
    return center * lax.rsqrt(spread + 1e-05)


def with_first(wide, row):
    place = lax.broadcasted_iota(jnp.int32, (8, wide.shape[1]), 0)
    return jnp.concatenate([jnp.where(place == 0, row, wide[:8]), wide[8:]], axis=0)


def with_last(wide, row):
    place = lax.broadcasted_iota(jnp.int32, (8, wide.shape[1]), 0)
    return jnp.concatenate([wide[:-8], jnp.where(place == 7, row, wide[-8:])], axis=0)


def three_columns(wide, left, right):
    count = wide.shape[0]
    before = with_first(pltpu.roll(wide, 1, axis=0), left)
    after = with_last(pltpu.roll(wide, count - 1, axis=0), right)
    return before.astype(BF), wide.astype(BF), after.astype(BF)


def conv_kernel(start, rows, part, refs, packed, *args):
    ref = dict(zip(refs, args))
    spread, hid_out, cell_out = ref["spread"], ref["hid_out"], ref["cell_out"]
    ring = "strips_hid" in ref
    extent = spread.shape[0] - 2
    cols, width = ref["hid"].shape[1:]
    chans = spread.shape[2] // 3
    latent = chans - width
    top, bot = start == 0, start + extent == rows

    def row_of(name, row):
        channels = slice(part * latent, (part + 1) * latent) if name == "frame" else slice(None)
        if ref[name].shape[0] == rows:
            return ref[name][row, :, channels]
        if row == start - 1:
            return ref[name + "_prev"][0]
        if row == start + extent:
            return ref[name + "_next"][0]
        return ref[name][row - start]

    loads = []
    if "weights" in ref:
        size = ref["weights"].shape[0] // LOADS
        for place in range(LOADS):
            run = pl.ds(place * size, size)
            loads.append(pltpu.make_async_copy(ref["weights"].at[run], ref["held"].at[run], ref["sem"].at[place]))
    for load in loads:
        load.start()

    def beside(row):
        if not ring:
            return jnp.zeros((1, chans), F32), jnp.zeros((1, chans), F32)
        at = row + 2
        return tuple(
            jnp.concatenate(
                [ref["beside"][place, at : at + 1, :], ref["strips_hid"][3 * place, at : at + 1, :]], axis=1
            )
            for place in range(2)
        )

    def build(pos):
        row = start + pos - 1
        raw = None
        if 0 <= row < rows:
            raw = row_of("frame", row), row_of("hid", row)
            x, h = raw[0].astype(F32), raw[1].astype(F32)
        elif ring:
            x, h = ref["frame_top" if row < 0 else "frame_bot"][0, :cols].astype(F32), ref["lines_hid"][3 * (row > 0)]
        else:
            spread[pos] = jnp.zeros(spread.shape[1:], BF)
            return
        low, high = beside(row)
        if ring:
            at = row + 2
            h = with_first(h, ref["strips_hid"][1, at : at + 1, :])
            h = with_last(h, ref["strips_hid"][2, at : at + 1, :])
            for spot, line in ((-1, 0), (0, 1), (rows - 1, 2), (rows, 3)):
                if row == spot:
                    h = ref["lines_hid"][line]
        for side, (value, first) in enumerate(((x, 0), (h, latent))):
            size = value.shape[1]
            pieces = three_columns(value, low[:, first : first + size], high[:, first : first + size])
            if raw is not None and (side == 0 or not ring):
                pieces = pieces[0], raw[side], pieces[2]
            for tap in range(3):
                spread[pos, :, tap * chans + first : tap * chans + first + size] = pieces[tap]

    def multiply(first, depth):
        lhs = jnp.concatenate(
            [spread[first + tap : first + tap + depth].reshape(depth * cols, 3 * chans) for tap in range(3)], axis=1
        )
        return jnp.dot(lhs, ref["held"][...], preferred_element_type=F32)

    def activate(first, depth, gates):
        for line in range(first, first + depth):
            row = start + line
            cell_prev = row_of("cell", row)
            if ring:
                at = row + 2
                cell_prev = with_first(cell_prev, ref["strips_cell"][1, at : at + 1, :])
                cell_prev = with_last(cell_prev, ref["strips_cell"][2, at : at + 1, :])
                if row == 0:
                    cell_prev = ref["lines_cell"][1]
                if row == rows - 1:
                    cell_prev = ref["lines_cell"][2]
            own = gates[(line - first) * cols : (line - first + 1) * cols] + ref["bias"][...]
            new_cell, new_hidden = lstm(own, cell_prev)
            if not packed:
                cell_out[row] = new_cell
                hid_out[row] = new_hidden.astype(BF)
                continue
            ref["cell_rows"][line] = new_cell
            owners_x, piece_y = hid_out.shape[1:3]
            local_m, piece_x = packed
            for owner in range(owners_x):
                picked = [
                    new_hidden[(m * owners_x + owner) * piece_x : (m * owners_x + owner + 1) * piece_x]
                    for m in range(local_m)
                ]
                hid_out[line // piece_y, owner, line % piece_y] = jnp.concatenate(picked, axis=0).astype(BF)

        if packed:
            done = pl.ds(first, depth)
            leave = pltpu.make_async_copy(
                ref["cell_rows"].at[done], cell_out.at[pl.ds(start + first, depth)], ref["left"].at[first // depth]
            )
            leave.start()
            leaving.append(leave)

    leaving = []
    depth = step_rows(0, extent, 12)
    for pos in range(depth + 2):
        build(pos)
    for load in loads:
        load.wait()
    waiting = None
    for first in range(0, extent, depth):
        for pos in range(first + depth + 2, min(first + 2 * depth, extent) + 2):
            build(pos)
        gates = multiply(first, depth)
        if waiting:
            activate(*waiting)
        waiting = first, depth, gates
    activate(*waiting)
    for leave in leaving:
        leave.wait()


def whole(array):
    return pl.BlockSpec(array.shape, lambda *step: (0,) * array.ndim)


def conv_step(frames, part, hid, cell, ring, weights, bias, rows_of, names, out_shapes, out_specs, packed, carry, load):
    rows, cols, width = hid.shape
    latent = weights.shape[0] // 9 - width
    start, extent = rows_of

    def rowed(size, channels, channel, row):
        return pl.BlockSpec((size, cols, channels), lambda step: (row // size, 0, channel))

    before, after = max(start - 1, 0), min(start + extent, rows - 1)
    near = pl.BlockSpec(memory_space=pltpu.VMEM)
    if load:
        inputs = {
            "frame": (frames, rowed(extent, latent, part, start)),
            "frame_prev": (frames, rowed(1, latent, part, before)),
            "frame_next": (frames, rowed(1, latent, part, after)),
            "hid": (hid, rowed(extent, width, 0, start)),
            "hid_prev": (hid, rowed(1, width, 0, before)),
            "hid_next": (hid, rowed(1, width, 0, after)),
            "cell": (cell, rowed(extent, width, 0, start)),
        }
    else:
        inputs = {"frame": (frames, near), "hid": (hid, near), "cell": (cell, near)}
    inputs["bias"] = bias, whole(bias)
    if load:
        inputs["weights"] = weights, pl.BlockSpec(memory_space=pl.ANY)
    else:
        inputs["held"] = weights, near
    inputs |= ring
    aliases = {}
    for place, array in enumerate(carry):
        if array is not None:
            aliases[len(inputs)] = place
            inputs[f"carry{place}"] = (array, pl.BlockSpec(memory_space=pl.ANY) if packed else near)
    refs = [*inputs, *names, "spread"]
    scratch = [pltpu.VMEM((extent + 2, cols, 3 * (latent + width)), BF)]
    if load:
        refs += ["held", "sem"]
        scratch += [pltpu.VMEM(weights.shape, BF), pltpu.SemaphoreType.DMA((LOADS,))]
    if packed:
        refs += ["cell_rows", "left"]
        scratch += [pltpu.VMEM((extent, cols, width), F32), pltpu.SemaphoreType.DMA((extent,))]
    cells = extent * cols
    return pl.pallas_call(
        functools.partial(conv_kernel, start, rows, part, refs, packed),
        grid=(1,),
        in_specs=[spec for _, spec in inputs.values()],
        out_specs=out_specs,
        out_shape=out_shapes,
        scratch_shapes=scratch,
        input_output_aliases=aliases,
        compiler_params=pltpu.CompilerParams(vmem_limit_bytes=VMEM_ALL if load else VMEM_LIMIT),
        cost_estimate=pl.CostEstimate(
            flops=2 * cells * weights.size, bytes_accessed=2 * weights.size + cells * 2048, transcendentals=cells * width * 5
        ),
    )(*(array for array, _ in inputs.values()))


def pack_kernel(frames, hids, cells, send_low, send_high, side_low, side_high, line_top, line_bot, flat):
    rows, cols, width = hids.shape
    latent = frames.shape[2] // 2
    chans = latent + width
    places = ((0, 0, latent), (chans + width, latent, latent))
    for out, near in ((line_top, slice(0, 2)), (line_bot, slice(rows - 2, rows))):
        for to, start, size in places:
            out[:, :, to : to + size] = frames[near, :, start : start + size]
        out[:, :, latent:chans] = hids[near]
        out[:, :, chans : chans + width] = cells[near].astype(BF)
    for out, send, near, start in (
        (side_low, send_low, slice(0, 8), 0),
        (side_high, send_high, slice(cols - 8, cols), 6),
    ):
        for slab in range(out.shape[2] // LANES):
            to = slab * LANES
            if to < latent or to >= chans + width:
                begin = to if to < latent else to - 2 * width
                part = frames[:, near, begin : begin + LANES].astype(F32)
            elif to < chans:
                part = hids[:, near, to - latent : to - latent + LANES].astype(F32)
            else:
                part = cells[:, near, to - chans : to - chans + LANES]
            send[:, :, to : to + LANES] = part[:, start : start + 2].astype(BF)
            flat[...] = part.reshape(rows * 8, LANES)
            for place in range(2):
                out[place, :, to : to + LANES] = flat[pl.ds(start + place, rows, stride=8), :].astype(BF)


def pack_step(frames, hid, cell):
    rows, cols, width = hid.shape
    span = frames.shape[2]
    deep = span + 2 * width
    shapes = [jax.ShapeDtypeStruct((rows, 2, deep), BF)] * 2 + [jax.ShapeDtypeStruct((2, rows, deep), BF)] * 2
    shapes += [jax.ShapeDtypeStruct((2, cols, deep), BF)] * 2
    return pl.pallas_call(
        pack_kernel,
        grid=(1,),
        in_specs=[pl.BlockSpec(memory_space=pltpu.VMEM)] * 3,
        out_specs=[whole(shape) for shape in shapes],
        out_shape=shapes,
        scratch_shapes=[pltpu.VMEM((rows * 8, LANES), F32)],
        compiler_params=pltpu.CompilerParams(vmem_limit_bytes=VMEM_LIMIT),
        cost_estimate=pl.CostEstimate(flops=0, bytes_accessed=4_000_000, transcendentals=0),
    )(frames, hid, cell)


def ring_kernel(
    above, below, line_top, line_bot, from_left, from_right, side_left, side_right, weights, bias,
    line_hid, line_cell, strip_hid, strip_cell, beside, strips,
):
    width = line_hid.shape[2]
    chans = weights.shape[0] // 9
    cols, length = line_top.shape[1], strip_hid.shape[1]
    rows = from_left.shape[1]
    columns = (
        (from_left, 0, cols), (from_left, 1, cols + 1), (side_left, 0, 0), (side_left, 1, 1),
        (side_right, 0, cols - 2), (side_right, 1, cols - 1), (from_right, 0, cols + 2), (from_right, 1, cols + 3),
    )
    ends = [(ref[row].astype(F32), at + row) for ref, at in ((above, 0), (below, rows + 2)) for row in range(2)]
    strips[:, rows + 4 :, :] = jnp.zeros((8, length - rows - 4, strips.shape[2]), F32)
    for place, (source, at, end) in enumerate(columns):
        strips[place, 2 : rows + 2, :] = source[at].astype(F32)
        for value, spot in ends:
            strips[place, spot : spot + 1, :] = value[end : end + 1]
    beside[0] = strips[1, :, chans + width :]
    beside[1] = strips[6, :, chans + width :]
    low, high = strips[1, :, :chans], strips[6, :, :chans]

    def line(ref, row):
        held = ref[row, :cols].astype(F32)
        return held[:, :chans], held[:, chans : chans + width]

    tops = [line(above, 0), line(above, 1), line(line_top, 0), line(line_top, 1)]
    bots = [line(line_bot, 0), line(line_bot, 1), line(below, 0), line(below, 1)]
    parts, held = [], []
    for lead, lines in ((0, tops), (rows, bots)):
        pieces = []
        for row in range(4):
            at = lead + row
            pieces.append(three_columns(lines[row][0], low[at : at + 1], high[at : at + 1]))
        for row in range(2):
            parts.append(jnp.concatenate([pieces[row + tap][col] for tap in range(3) for col in range(3)], axis=1))
            held.append(lines[row + 1][1])
    for side in range(2):
        rolled = []
        for col in range(4):
            wide = strips[4 * side + col, :, :chans]
            rolled.append((pltpu.roll(wide, 1, axis=0), wide, pltpu.roll(wide, length - 1, axis=0)))
        for col in range(2):
            parts.append(
                jnp.concatenate([rolled[col + tap][row].astype(BF) for row in range(3) for tap in range(3)], axis=1)
            )
            held.append(strips[4 * side + col + 1, :, chans : chans + width])
    row_at, col_at = lax.axis_index("gy"), lax.axis_index("gx")
    upper = (row_at > 0).astype(F32)
    lower = (row_at < lax.axis_size("gy") - 1).astype(F32)
    before = (col_at > 0).astype(F32)
    after = (col_at < lax.axis_size("gx") - 1).astype(F32)
    spot = lax.broadcasted_iota(jnp.int32, (length, width), 0)
    inside = jnp.where(spot == 1, upper, jnp.where(spot == rows + 2, lower, 1.0))
    keep = [upper, 1.0, 1.0, lower, inside * before, inside, inside, inside * after]
    lhs = jnp.concatenate(parts, axis=0)
    gates = jnp.dot(lhs, weights[...], preferred_element_type=F32) + bias[...]
    start = 0
    for place in range(8):
        hid, cell = (line_hid, line_cell) if place < 4 else (strip_hid, strip_cell)
        size = hid.shape[1]
        new_cell, hidden = lstm(gates[start : start + size], held[place])
        hid[place % 4] = hidden.astype(BF).astype(F32) * keep[place]
        cell[place % 4] = new_cell
        start += size


def block_kernel(x, w_qkv, w_out, w_up, w_down, *rest):
    out, flat, back, keys_t, own_low, own_high, own_values, ones = rest[-8:]
    group = GRID * GRID
    embed = w_out.shape[0]
    tile = embed // 2

    @pl.when((pl.program_id(0) == 0) & (pl.program_id(1) == 0))
    def _():
        def fill(target, down, across, add):
            above = lax.broadcasted_iota(jnp.int32, target.shape, 0) // down
            along = lax.broadcasted_iota(jnp.int32, target.shape, 1) // across
            target[...] = (above == along + add).astype(F32).astype(BF)

        fill(own_low, HDIM, group, 0)
        fill(own_high, HDIM, group, HEADS // 4)
        fill(own_values, group, HDIM, 0)
        fill(ones, group, group, 0)
        keys_t[...] = w_qkv[:, embed : 2 * embed].astype(F32).T.astype(BF)

    flat[...] = x[...].astype(F32).reshape(flat.shape)
    groups = flat.shape[0] // group
    cells = jnp.concatenate([flat[pl.ds(g, group, stride=groups), :] for g in range(groups)], axis=0)
    normed = layer_norm(cells).astype(BF)
    queries = jnp.dot(normed, w_qkv[:, :embed], preferred_element_type=F32).astype(BF)
    values = jnp.dot(normed, w_qkv[:, 2 * embed :], preferred_element_type=F32).astype(BF)
    keys = lax.dot_general(keys_t[...], normed, (((1,), (1,)), ((), ())), preferred_element_type=F32)
    side = lax.broadcasted_iota(jnp.int32, (embed, 2 * group), 1) < group
    raised = [[], []]
    for pair in range(groups // 2):
        both = keys[:, pair * 2 * group : (pair + 1) * 2 * group]
        turned = pltpu.roll(both, group, axis=1)
        for place, twice in enumerate((jnp.where(side, both, turned), jnp.where(side, turned, both))):
            twice = twice.astype(BF)
            start = (2 * pair + place) * group
            for half in range(2):
                part = twice[half * tile : (half + 1) * tile]
                spread = jnp.concatenate([part * own_low[...], part * own_high[...]], axis=1)
                scores = jnp.dot(
                    queries[start : start + group, half * tile : (half + 1) * tile], spread, preferred_element_type=F32
                )
                raised[half].append(jnp.minimum(jnp.exp2(scores * (LOG2E * HDIM**-0.5)), BF_MAX).astype(BF))
    heads = []
    for half in range(2):
        part = jnp.concatenate(raised[half], axis=0)
        total = jnp.dot(part, ones[...], preferred_element_type=F32)
        guess = pl.reciprocal(total, approx=True)
        attn = (part.astype(F32) * (guess * (2.0 - total * guess))).astype(BF)
        column = []
        for g in range(groups):
            held = values[g * group : (g + 1) * group, half * tile : (half + 1) * tile]
            spread = jnp.concatenate([held] * (HEADS // 2), axis=0) * own_values[...]
            column.append(
                jnp.dot(attn[g * group : (g + 1) * group], spread, preferred_element_type=F32).astype(BF)
            )
        heads.append(jnp.concatenate(column, axis=0))
    heads = jnp.concatenate(heads, axis=1)
    attended = jnp.dot(heads, w_out[...], preferred_element_type=F32).astype(BF)
    mixed = cells + attended.astype(F32)
    normed_two = layer_norm(mixed).astype(BF)
    up = jnp.dot(normed_two, w_up[...], preferred_element_type=F32)
    bent = jnp.tanh(up * (0.7978845608 + (0.7978845608 * 0.044715) * (up * up)))
    half_up = 0.5 * up
    expanded = (half_up + half_up * bent).astype(BF)
    result = mixed + jnp.dot(expanded, w_down[...], preferred_element_type=F32)
    for g in range(groups):
        back[pl.ds(g, group, stride=groups), :] = result[g * group : (g + 1) * group]
    out[...] = back[...].reshape(x.shape).astype(BF)


def block_step(moved, carry, first, pieces, devices_y, devices_x, w_qkv, w_out, w_up, w_down):
    _, piece_y, piece_cols, width = moved.shape
    lanes = devices_y // GRID
    view = moved.reshape(GRID, lanes, devices_x, piece_y, piece_cols, width)
    tokens = GRID * devices_x * piece_cols
    block = (GRID, None, devices_x, None, piece_cols, width)
    operands = [view, w_qkv, w_out, w_up, w_down]
    in_specs = [pl.BlockSpec(block, lambda i, j: (0, i, 0, j, 0, 0)), *(whole(array) for array in operands[1:])]
    aliases = {}
    if carry is not None:
        aliases = {len(operands): 0}
        operands.append(carry)
        in_specs.append(pl.BlockSpec(memory_space=pl.ANY))
    total = lanes * piece_y * tokens
    return pl.pallas_call(
        block_kernel,
        grid=(lanes, piece_y),
        in_specs=in_specs,
        out_specs=pl.BlockSpec(block, lambda i, j: (0, i, 0, first + j, 0, 0)),
        out_shape=jax.ShapeDtypeStruct((GRID, lanes, devices_x, pieces, piece_cols, width), BF),
        scratch_shapes=[
            pltpu.VMEM((tokens, width), F32),
            pltpu.VMEM((tokens, width), F32),
            pltpu.VMEM((w_out.shape[0], width), BF),
            pltpu.VMEM((HEADS // 2 * HDIM, 2 * GRID * GRID), BF),
            pltpu.VMEM((HEADS // 2 * HDIM, 2 * GRID * GRID), BF),
            pltpu.VMEM((HEADS // 2 * GRID * GRID, HEADS // 2 * HDIM), BF),
            pltpu.VMEM((HEADS // 2 * GRID * GRID, HEADS // 2 * GRID * GRID), BF),
        ],
        input_output_aliases=aliases,
        compiler_params=pltpu.CompilerParams(vmem_limit_bytes=VMEM_LIMIT),
        cost_estimate=pl.CostEstimate(
            flops=total * 3_000_000, bytes_accessed=total * width * 4 + 800_000, transcendentals=total * 1100
        ),
    )(*operands)


def unpack_kernel(shares, local_m, piece_x, src, out):
    owners_y, owners_x = src.shape[:2]
    unit = out.shape[0]
    lines, first = [], 0
    for share in shares:
        lines += [(owner_y, first + piece) for owner_y in range(owners_y) for piece in range(share)]
        first += share
    for step in range(len(lines) // unit):

        @pl.when(pl.program_id(0) == step)
        def _():
            for row, (owner_y, piece) in enumerate(lines[step * unit : (step + 1) * unit]):
                wide = src[owner_y, :, piece].astype(F32)
                parts = [
                    wide[owner, m * piece_x : (m + 1) * piece_x] for m in range(local_m) for owner in range(owners_x)
                ]
                out[row] = jnp.concatenate(parts, axis=0).astype(BF)


def unpack_step(landed, shares, cols, local_m, piece_x):
    owners_y, _, pieces, _, width = landed.shape
    rows = owners_y * pieces
    unit = 16 if rows % 16 == 0 else rows
    return pl.pallas_call(
        functools.partial(unpack_kernel, shares, local_m, piece_x),
        grid=(rows // unit,),
        in_specs=[pl.BlockSpec(memory_space=pltpu.VMEM)],
        out_specs=pl.BlockSpec((unit, cols, width), lambda step: (step, 0, 0)),
        out_shape=jax.ShapeDtypeStruct((rows, cols, width), BF),
        compiler_params=pltpu.CompilerParams(vmem_limit_bytes=VMEM_LIMIT),
        cost_estimate=pl.CostEstimate(flops=0, bytes_accessed=rows * cols * width * 4, transcendentals=0),
    )(landed)


def step_rows(start, extent, most=16):
    return max(size for size in range(1, most + 1) if extent % size == 0 and start % size == 0)


def body(frames, hidden_state, cell_state, w_gates, gate_bias, w_qkv, w_out, w_up, w_down):
    rows, cols, width = hidden_state.shape
    latent = frames.shape[2] // 2
    chans = latent + width
    held = chans + width
    devices_y, devices_x = lax.axis_size("gy"), lax.axis_size("gx")
    local_m = GRID // devices_x
    piece_x = cols // local_m // devices_x
    weights = w_gates.reshape(-1, w_gates.shape[3])
    bias = gate_bias.reshape(1, -1)

    def shifted(value, axis, step):
        count = lax.axis_size(axis)
        pairs = [(i, i + step) for i in range(count) if 0 <= i + step < count]
        return lax.ppermute(value, axis, pairs)

    send_left, send_right, side_left, side_right, line_top, line_bot = pack_step(frames, hidden_state, cell_state)
    tile_shapes = (jax.ShapeDtypeStruct((rows, cols, width), BF), jax.ShapeDtypeStruct((rows, cols, width), F32))
    near = pl.BlockSpec(memory_space=pltpu.VMEM)
    carry = ()

    def first_conv(start, extent, *others):
        done = conv_step(
            frames, 0, hidden_state, cell_state, {}, weights, bias, (start, extent), ("hid_out", "cell_out"),
            tile_shapes, (near, near), None, carry, False,
        )
        return lax.optimization_barrier((tuple(done), others))

    quarter = rows // 4
    from_left = shifted(send_right, "gx", 1)
    carry, (send_left,) = first_conv(0, quarter, send_left)
    from_right = shifted(send_left, "gx", -1)
    carry, (line_top, line_bot) = first_conv(quarter, quarter, line_top, line_bot)
    to_down = jnp.concatenate([line_bot, from_left[-2:], from_right[-2:]], axis=1)
    to_up = jnp.concatenate([line_top, from_left[:2], from_right[:2]], axis=1)
    from_up = shifted(to_down, "gy", 1)
    carry, (to_up,) = first_conv(2 * quarter, quarter, to_up)
    from_down = shifted(to_up, "gy", -1)
    carry, _ = first_conv(3 * quarter, rows - 3 * quarter)
    hidden_one, cell_one = carry

    length = -(-(rows + 4) // 16) * 16
    line_shape = jax.ShapeDtypeStruct((4, cols, width), F32)
    strip_shape = jax.ShapeDtypeStruct((4, length, width), F32)
    beside_shape = jax.ShapeDtypeStruct((2, length, latent), F32)
    shapes = (line_shape, line_shape, strip_shape, strip_shape, beside_shape)
    turned = from_left.transpose(1, 0, 2), from_right.transpose(1, 0, 2)
    around = (from_up, from_down, line_top, line_bot, *turned, side_left, side_right)
    line_hid, line_cell, strip_hid, strip_cell, beside = pl.pallas_call(
        ring_kernel,
        grid=(1,),
        in_specs=[*(whole(array) for array in around), pl.BlockSpec(memory_space=pltpu.VMEM), whole(bias)],
        out_specs=[whole(shape) for shape in shapes],
        out_shape=shapes,
        scratch_shapes=[pltpu.VMEM((8, length, held + latent), F32)],
        compiler_params=pltpu.CompilerParams(vmem_limit_bytes=VMEM_LIMIT),
        cost_estimate=pl.CostEstimate(flops=16 * length * weights.size, bytes_accessed=2 * weights.size, transcendentals=0),
    )(*around, weights, bias)

    second = held // latent
    line = (1, from_up.shape[1], latent)
    ring = {name: (array, whole(array)) for name, array in (
        ("strips_hid", strip_hid), ("strips_cell", strip_cell), ("lines_hid", line_hid), ("lines_cell", line_cell),
        ("beside", beside),
    )}
    ring["frame_top"] = from_up, pl.BlockSpec(line, lambda step: (1, 0, second))
    ring["frame_bot"] = from_down, pl.BlockSpec(line, lambda step: (0, 0, second))

    pieces = rows // devices_y
    piece_cols = local_m * piece_x
    shares = (pieces - pieces // 3, pieces // 3)
    moved, start, carry = [], 0, ()
    for piece_y in shares:
        extent = piece_y * devices_y
        sent_shape = jax.ShapeDtypeStruct((devices_y, devices_x, piece_y, piece_cols, width), BF)
        spec = pl.BlockSpec(memory_space=pl.ANY)
        sent, cell_out = conv_step(
            frames, 1, hidden_one, cell_one, ring, weights, bias, (start, extent),
            ("hid_out", "cell_out"), (sent_shape, tile_shapes[1]), (whole(sent_shape), spec), (local_m, piece_x), carry,
            bool(carry),
        )
        carry = (None, cell_out)
        sent = sent.reshape(devices_y * devices_x, piece_y, piece_cols, width)
        moved.append(lax.all_to_all(sent, ("gy", "gx"), split_axis=0, concat_axis=0, tiled=True))
        start += extent
    done, first = None, 0
    for piece_y, value in zip(shares, moved):
        done = block_step(value, done, first, pieces, devices_y, devices_x, w_qkv, w_out, w_up, w_down)
        first += piece_y
    done = done.reshape(devices_y * devices_x, pieces, piece_cols, width)
    landed = lax.all_to_all(done, ("gy", "gx"), split_axis=0, concat_axis=0, tiled=True)
    result = unpack_step(landed.reshape(devices_y, devices_x, *landed.shape[1:]), shares, cols, local_m, piece_x)
    return result, cell_out


def solution(mesh):
    tiled = P("gy", "gx", None)
    in_specs = (tiled, tiled, tiled, P(), P(), P(), P(), P(), P())
    return jax.shard_map(body, mesh=mesh, in_specs=in_specs, out_specs=(tiled, tiled), check_vma=False)
```

```python
import functools

import jax
import jax.numpy as jnp
from jax import lax
from jax.experimental import pallas as pl
from jax.experimental.pallas import tpu as pltpu
from jax.sharding import PartitionSpec as P

HEADS = 8
HDIM = 32
GRID = 8
BF = jnp.bfloat16
F32 = jnp.float32
LOG2E = 1.4426950408889634
BF_MAX = 3.3895313892515355e38
VMEM_LIMIT = 32 * 1024 * 1024
VMEM_ALL = 60 * 1024 * 1024
LOADS = 9
LANES = 128


def sigmoid(x):
    return 0.5 * jnp.tanh(0.5 * x) + 0.5


def lstm(gates, cell_prev):
    width = cell_prev.shape[-1]
    in_gate = sigmoid(gates[:, 0:width])
    forget_gate = sigmoid(gates[:, width : 2 * width])
    candidate = jnp.tanh(gates[:, 2 * width : 3 * width])
    out_gate = sigmoid(gates[:, 3 * width :])
    cell = forget_gate * cell_prev + in_gate * candidate
    return cell, out_gate * jnp.tanh(cell)


def layer_norm(values):
    center = values - jnp.mean(values, axis=-1, keepdims=True)
    spread = jnp.mean(center * center, axis=-1, keepdims=True)
    return center * lax.rsqrt(spread + 1e-05)


def three_columns(wide, left, right):
    count = wide.shape[0]
    place = lax.broadcasted_iota(jnp.int32, wide.shape, 0)
    before = jnp.where(place == 0, left, pltpu.roll(wide, 1, axis=0))
    after = jnp.where(place == count - 1, right, pltpu.roll(wide, count - 1, axis=0))
    return before.astype(BF), wide.astype(BF), after.astype(BF)


def conv_kernel(start, rows, part, tail, refs, packed, *args):
    ref = dict(zip(refs, args))
    hid_out, cell_out = ref["hid_out"], ref["cell_out"]
    extent = ref["spread"].shape[0] - 2
    cols, width = ref["hid"].shape[1:]
    chans = ref["spread"].shape[2] // 3
    latent = chans - width
    loads, leaving = [], []
    if "weights" in ref:
        size = ref["weights"].shape[0] // LOADS
        for place in range(LOADS):
            run = pl.ds(place * size, size)
            loads.append(pltpu.make_async_copy(ref["weights"].at[run], ref["held"].at[run], ref["sem"].at[place]))
    for load in loads:
        load.start()

    def reader(prefix, first, count):
        def row_of(name, row):
            array = ref[prefix + name]
            if array.shape[0] == rows:
                channels = slice(part * latent, (part + 1) * latent) if name == "frame" else slice(None)
                return array[row, :, channels]
            if prefix != "tail_" and tail and row >= tail and name != "frame":
                return ref["late_" + name][row - tail]
            if row == first - 1:
                return ref[prefix + name + "_prev"][0]
            if row == first + count:
                return ref[prefix + name + "_next"][0]
            return array[row - first]

        return row_of

    def convolve(spread, start, extent, row_of, ring, write, leave):
        def beside(row):
            if not ring:
                return jnp.zeros((1, chans), F32), jnp.zeros((1, chans), F32)
            at = row + 2
            return tuple(
                jnp.concatenate(
                    [ref["beside"][place, at : at + 1, :], ref["strips_hid"][3 * place, at : at + 1, :]], axis=1
                )
                for place in range(2)
            )

        def build(pos):
            row = start + pos - 1
            raw = None
            if 0 <= row < rows:
                raw = row_of("frame", row), row_of("hid", row)
                x, h = raw[0].astype(F32), raw[1].astype(F32)
            elif ring:
                x = ref["frame_top" if row < 0 else "frame_bot"][0, :cols].astype(F32)
                h = ref["lines_hid"][3 * (row > 0)]
            else:
                spread[pos] = jnp.zeros(spread.shape[1:], BF)
                return
            low, high = beside(row)
            if ring:
                at = row + 2
                place = lax.broadcasted_iota(jnp.int32, h.shape, 0)
                h = jnp.where(place == 0, ref["strips_hid"][1, at : at + 1, :], h)
                h = jnp.where(place == cols - 1, ref["strips_hid"][2, at : at + 1, :], h)
                for spot, line in ((0, 1), (rows - 1, 2)):
                    if row == spot:
                        h = ref["lines_hid"][line]
            for side, (value, first) in enumerate(((x, 0), (h, latent))):
                size = value.shape[1]
                pieces = three_columns(value, low[:, first : first + size], high[:, first : first + size])
                if raw is not None and (side == 0 or not ring):
                    pieces = pieces[0], raw[side], pieces[2]
                for tap in range(3):
                    spread[pos, :, tap * chans + first : tap * chans + first + size] = pieces[tap]

        def multiply(first, depth):
            lhs = jnp.concatenate(
                [spread[first + tap : first + tap + depth].reshape(depth * cols, 3 * chans) for tap in range(3)], axis=1
            )
            return jnp.dot(lhs, ref["held"][...], preferred_element_type=F32)

        def activate(first, depth, gates):
            for line in range(first, first + depth):
                row = start + line
                cell_prev = row_of("cell", row)
                if ring:
                    at = row + 2
                    place = lax.broadcasted_iota(jnp.int32, cell_prev.shape, 0)
                    cell_prev = jnp.where(place == 0, ref["strips_cell"][1, at : at + 1, :], cell_prev)
                    cell_prev = jnp.where(place == cols - 1, ref["strips_cell"][2, at : at + 1, :], cell_prev)
                    if row == 0:
                        cell_prev = ref["lines_cell"][1]
                    if row == rows - 1:
                        cell_prev = ref["lines_cell"][2]
                own = gates[(line - first) * cols : (line - first + 1) * cols] + ref["bias"][...]
                new_cell, new_hidden = lstm(own, cell_prev)
                write(row, new_cell, new_hidden)
            leave(first, depth)

        depth = step_rows(0, extent, 12)
        for pos in range(depth + 2):
            build(pos)
        while loads:
            loads.pop().wait()
        waiting = None
        for first in range(0, extent, depth):
            for pos in range(first + depth + 2, min(first + 2 * depth, extent) + 2):
                build(pos)
            gates = multiply(first, depth)
            if waiting:
                activate(*waiting)
            waiting = first, depth, gates
        activate(*waiting)

    def keep(row, new_cell, new_hidden):
        cell_out[row] = new_cell
        hid_out[row] = new_hidden.astype(BF)

    def keep_late(row, new_cell, new_hidden):
        ref["late_cell"][row - tail] = new_cell
        ref["late_hid"][row - tail] = new_hidden.astype(BF)

    def send(row, new_cell, new_hidden):
        line = row - start
        ref["cell_rows"][line] = new_cell
        owners_x, piece_y = hid_out.shape[1:3]
        local_m, piece_x = packed
        for owner in range(owners_x):
            picked = [
                new_hidden[(m * owners_x + owner) * piece_x : (m * owners_x + owner + 1) * piece_x]
                for m in range(local_m)
            ]
            hid_out[line // piece_y, owner, line % piece_y] = jnp.concatenate(picked, axis=0).astype(BF)

    def leave(first, depth):
        copy = pltpu.make_async_copy(
            ref["cell_rows"].at[pl.ds(first, depth)], cell_out.at[pl.ds(start + first, depth)],
            ref["left"].at[first // depth],
        )
        copy.start()
        leaving.append(copy)

    def stay(first, depth):
        pass

    if not packed:
        convolve(ref["spread"], start, extent, reader("", start, extent), False, keep, stay)
        return
    if tail:
        convolve(ref["late_spread"], tail, rows - tail, reader("tail_", tail, rows - tail), False, keep_late, stay)
    convolve(ref["spread"], start, extent, reader("", start, extent), True, send, leave)
    for copy in leaving:
        copy.wait()


def whole(array):
    return pl.BlockSpec(array.shape, lambda *step: (0,) * array.ndim)


def conv_step(frames, part, hid, cell, ring, weights, bias, rows_of, names, out_shapes, out_specs, packed, carry, late):
    rows, cols, width = hid.shape
    latent = weights.shape[0] // 9 - width
    start, extent = rows_of

    def rowed(size, channels, channel, row):
        return pl.BlockSpec((size, cols, channels), lambda step: (row // size, 0, channel))

    def windows(prefix, hid, cell, channel, start, extent):
        before, after = max(start - 1, 0), min(start + extent, rows - 1)
        return {
            prefix + "frame": (frames, rowed(extent, latent, channel, start)),
            prefix + "frame_prev": (frames, rowed(1, latent, channel, before)),
            prefix + "frame_next": (frames, rowed(1, latent, channel, after)),
            prefix + "hid": (hid, rowed(extent, width, 0, start)),
            prefix + "hid_prev": (hid, rowed(1, width, 0, before)),
            prefix + "hid_next": (hid, rowed(1, width, 0, after)),
            prefix + "cell": (cell, rowed(extent, width, 0, start)),
        }

    near = pl.BlockSpec(memory_space=pltpu.VMEM)
    tail = 0
    if late:
        tail, *first = late
        inputs = windows("", hid, cell, part, start, extent)
        inputs |= windows("tail_", *first, 0, tail, rows - tail)
    else:
        inputs = {"frame": (frames, near), "hid": (hid, near), "cell": (cell, near)}
    inputs["bias"] = bias, whole(bias)
    if late:
        inputs["weights"] = weights, pl.BlockSpec(memory_space=pl.ANY)
    else:
        inputs["held"] = weights, near
    inputs |= ring
    aliases = {}
    for place, array in enumerate(carry):
        if array is not None:
            aliases[len(inputs)] = place
            inputs[f"carry{place}"] = (array, pl.BlockSpec(memory_space=pl.ANY) if packed else near)
    refs = [*inputs, *names, "spread"]
    scratch = [pltpu.VMEM((extent + 2, cols, 3 * (latent + width)), BF)]
    if late:
        refs += ["held", "sem", "late_spread", "late_hid", "late_cell"]
        scratch += [
            pltpu.VMEM(weights.shape, BF),
            pltpu.SemaphoreType.DMA((LOADS,)),
            pltpu.VMEM((rows - tail + 2, cols, 3 * (latent + width)), BF),
            pltpu.VMEM((rows - tail, cols, width), BF),
            pltpu.VMEM((rows - tail, cols, width), F32),
        ]
    if packed:
        refs += ["cell_rows", "left"]
        scratch += [pltpu.VMEM((extent, cols, width), F32), pltpu.SemaphoreType.DMA((extent,))]
    cells = extent * cols
    return pl.pallas_call(
        functools.partial(conv_kernel, start, rows, part, tail, refs, packed),
        grid=(1,),
        in_specs=[spec for _, spec in inputs.values()],
        out_specs=out_specs,
        out_shape=out_shapes,
        scratch_shapes=scratch,
        input_output_aliases=aliases,
        compiler_params=pltpu.CompilerParams(vmem_limit_bytes=VMEM_ALL if late else VMEM_LIMIT),
        cost_estimate=pl.CostEstimate(
            flops=2 * cells * weights.size, bytes_accessed=2 * weights.size + cells * 2048, transcendentals=cells * width * 5
        ),
    )(*(array for array, _ in inputs.values()))


def pack_kernel(frames, hids, cells, send_low, send_high, side_low, side_high, line_top, line_bot, flat):
    rows, cols, width = hids.shape
    latent = frames.shape[2] // 2
    chans = latent + width
    places = ((0, 0, latent), (chans + width, latent, latent))
    for out, near in ((line_top, slice(0, 2)), (line_bot, slice(rows - 2, rows))):
        for to, start, size in places:
            out[:, :, to : to + size] = frames[near, :, start : start + size]
        out[:, :, latent:chans] = hids[near]
        out[:, :, chans : chans + width] = cells[near].astype(BF)
    for out, send, near, start in (
        (side_low, send_low, slice(0, 8), 0),
        (side_high, send_high, slice(cols - 8, cols), 6),
    ):
        for slab in range(out.shape[2] // LANES):
            to = slab * LANES
            if to < latent or to >= chans + width:
                begin = to if to < latent else to - 2 * width
                part = frames[:, near, begin : begin + LANES].astype(F32)
            elif to < chans:
                part = hids[:, near, to - latent : to - latent + LANES].astype(F32)
            else:
                part = cells[:, near, to - chans : to - chans + LANES]
            send[:, :, to : to + LANES] = part[:, start : start + 2].astype(BF)
            flat[...] = part.reshape(rows * 8, LANES)
            for place in range(2):
                out[place, :, to : to + LANES] = flat[pl.ds(start + place, rows, stride=8), :].astype(BF)


def pack_step(frames, hid, cell):
    rows, cols, width = hid.shape
    span = frames.shape[2]
    deep = span + 2 * width
    shapes = [jax.ShapeDtypeStruct((rows, 2, deep), BF)] * 2 + [jax.ShapeDtypeStruct((2, rows, deep), BF)] * 2
    shapes += [jax.ShapeDtypeStruct((2, cols, deep), BF)] * 2
    return pl.pallas_call(
        pack_kernel,
        grid=(1,),
        in_specs=[pl.BlockSpec(memory_space=pltpu.VMEM)] * 3,
        out_specs=[whole(shape) for shape in shapes],
        out_shape=shapes,
        scratch_shapes=[pltpu.VMEM((rows * 8, LANES), F32)],
        compiler_params=pltpu.CompilerParams(vmem_limit_bytes=VMEM_LIMIT),
        cost_estimate=pl.CostEstimate(flops=0, bytes_accessed=4_000_000, transcendentals=0),
    )(frames, hid, cell)


def ring_kernel(
    above, below, line_top, line_bot, from_left, from_right, side_left, side_right, weights, bias,
    line_hid, line_cell, strip_hid, strip_cell, beside, strips,
):
    width = line_hid.shape[2]
    chans = weights.shape[0] // 9
    cols, length = line_top.shape[1], strip_hid.shape[1]
    rows = from_left.shape[1]
    columns = (
        (from_left, 0, cols), (from_left, 1, cols + 1), (side_left, 0, 0), (side_left, 1, 1),
        (side_right, 0, cols - 2), (side_right, 1, cols - 1), (from_right, 0, cols + 2), (from_right, 1, cols + 3),
    )
    ends = [(ref[row].astype(F32), at + row) for ref, at in ((above, 0), (below, rows + 2)) for row in range(2)]
    strips[:, rows + 4 :, :] = jnp.zeros((8, length - rows - 4, strips.shape[2]), F32)
    for place, (source, at, end) in enumerate(columns):
        strips[place, 2 : rows + 2, :] = source[at].astype(F32)
        for value, spot in ends:
            strips[place, spot : spot + 1, :] = value[end : end + 1]
    beside[0] = strips[1, :, chans + width :]
    beside[1] = strips[6, :, chans + width :]
    low, high = strips[1, :, :chans], strips[6, :, :chans]

    def line(ref, row):
        held = ref[row, :cols].astype(F32)
        return held[:, :chans], held[:, chans : chans + width]

    tops = [line(above, 0), line(above, 1), line(line_top, 0), line(line_top, 1)]
    bots = [line(line_bot, 0), line(line_bot, 1), line(below, 0), line(below, 1)]
    parts, held = [], []
    for lead, lines in ((0, tops), (rows, bots)):
        pieces = []
        for row in range(4):
            at = lead + row
            pieces.append(three_columns(lines[row][0], low[at : at + 1], high[at : at + 1]))
        for row in range(2):
            parts.append(jnp.concatenate([pieces[row + tap][col] for tap in range(3) for col in range(3)], axis=1))
            held.append(lines[row + 1][1])
    for side in range(2):
        rolled = []
        for col in range(4):
            wide = strips[4 * side + col, :, :chans]
            rolled.append((pltpu.roll(wide, 1, axis=0), wide, pltpu.roll(wide, length - 1, axis=0)))
        for col in range(2):
            parts.append(
                jnp.concatenate([rolled[col + tap][row].astype(BF) for row in range(3) for tap in range(3)], axis=1)
            )
            held.append(strips[4 * side + col + 1, :, chans : chans + width])
    row_at, col_at = lax.axis_index("gy"), lax.axis_index("gx")
    upper = (row_at > 0).astype(F32)
    lower = (row_at < lax.axis_size("gy") - 1).astype(F32)
    before = (col_at > 0).astype(F32)
    after = (col_at < lax.axis_size("gx") - 1).astype(F32)
    spot = lax.broadcasted_iota(jnp.int32, (length, width), 0)
    inside = jnp.where(spot == 1, upper, jnp.where(spot == rows + 2, lower, 1.0))
    keep = [upper, 1.0, 1.0, lower, inside * before, inside, inside, inside * after]
    lhs = jnp.concatenate(parts, axis=0)
    gates = jnp.dot(lhs, weights[...], preferred_element_type=F32) + bias[...]
    start = 0
    for place in range(8):
        hid, cell = (line_hid, line_cell) if place < 4 else (strip_hid, strip_cell)
        size = hid.shape[1]
        new_cell, hidden = lstm(gates[start : start + size], held[place])
        hid[place % 4] = hidden.astype(BF).astype(F32) * keep[place]
        cell[place % 4] = new_cell
        start += size


def block_kernel(x, w_qkv, w_out, w_up, w_down, *rest):
    out, flat, back, keys_t, own_low, own_high, own_values, ones = rest[-8:]
    group = GRID * GRID
    embed = w_out.shape[0]
    tile = embed // 2

    @pl.when((pl.program_id(0) == 0) & (pl.program_id(1) == 0))
    def _():
        def fill(target, down, across, add):
            above = lax.broadcasted_iota(jnp.int32, target.shape, 0) // down
            along = lax.broadcasted_iota(jnp.int32, target.shape, 1) // across
            target[...] = (above == along + add).astype(F32).astype(BF)

        fill(own_low, HDIM, group, 0)
        fill(own_high, HDIM, group, HEADS // 4)
        fill(own_values, group, HDIM, 0)
        fill(ones, group, group, 0)
        keys_t[...] = w_qkv[:, embed : 2 * embed].astype(F32).T.astype(BF)

    flat[...] = x[...].astype(F32).reshape(flat.shape)
    groups = flat.shape[0] // group
    cells = jnp.concatenate([flat[pl.ds(g, group, stride=groups), :] for g in range(groups)], axis=0)
    normed = layer_norm(cells).astype(BF)
    queries = jnp.dot(normed, w_qkv[:, :embed], preferred_element_type=F32).astype(BF)
    values = jnp.dot(normed, w_qkv[:, 2 * embed :], preferred_element_type=F32).astype(BF)
    keys = lax.dot_general(keys_t[...], normed, (((1,), (1,)), ((), ())), preferred_element_type=F32)
    side = lax.broadcasted_iota(jnp.int32, (embed, 2 * group), 1) < group
    raised = [[], []]
    for pair in range(groups // 2):
        both = keys[:, pair * 2 * group : (pair + 1) * 2 * group]
        turned = pltpu.roll(both, group, axis=1)
        for place, twice in enumerate((jnp.where(side, both, turned), jnp.where(side, turned, both))):
            twice = twice.astype(BF)
            start = (2 * pair + place) * group
            for half in range(2):
                part = twice[half * tile : (half + 1) * tile]
                spread = jnp.concatenate([part * own_low[...], part * own_high[...]], axis=1)
                scores = jnp.dot(
                    queries[start : start + group, half * tile : (half + 1) * tile], spread, preferred_element_type=F32
                )
                raised[half].append(jnp.minimum(jnp.exp2(scores * (LOG2E * HDIM**-0.5)), BF_MAX).astype(BF))
    heads = []
    for half in range(2):
        part = jnp.concatenate(raised[half], axis=0)
        total = jnp.dot(part, ones[...], preferred_element_type=F32)
        guess = pl.reciprocal(total, approx=True)
        attn = (part.astype(F32) * (guess * (2.0 - total * guess))).astype(BF)
        column = []
        for g in range(groups):
            held = values[g * group : (g + 1) * group, half * tile : (half + 1) * tile]
            spread = jnp.concatenate([held] * (HEADS // 2), axis=0) * own_values[...]
            column.append(
                jnp.dot(attn[g * group : (g + 1) * group], spread, preferred_element_type=F32).astype(BF)
            )
        heads.append(jnp.concatenate(column, axis=0))
    heads = jnp.concatenate(heads, axis=1)
    attended = jnp.dot(heads, w_out[...], preferred_element_type=F32).astype(BF)
    mixed = cells + attended.astype(F32)
    normed_two = layer_norm(mixed).astype(BF)
    up = jnp.dot(normed_two, w_up[...], preferred_element_type=F32)
    bent = jnp.tanh(up * (0.7978845608 + (0.7978845608 * 0.044715) * (up * up)))
    half_up = 0.5 * up
    expanded = (half_up + half_up * bent).astype(BF)
    result = mixed + jnp.dot(expanded, w_down[...], preferred_element_type=F32)
    for g in range(groups):
        back[pl.ds(g, group, stride=groups), :] = result[g * group : (g + 1) * group]
    out[...] = back[...].reshape(x.shape).astype(BF)


def block_step(moved, carry, first, pieces, devices_y, devices_x, w_qkv, w_out, w_up, w_down):
    _, piece_y, piece_cols, width = moved.shape
    lanes = devices_y // GRID
    view = moved.reshape(GRID, lanes, devices_x, piece_y, piece_cols, width)
    tokens = GRID * devices_x * piece_cols
    block = (GRID, None, devices_x, None, piece_cols, width)
    operands = [view, w_qkv, w_out, w_up, w_down]
    in_specs = [pl.BlockSpec(block, lambda i, j: (0, i, 0, j, 0, 0)), *(whole(array) for array in operands[1:])]
    aliases = {}
    if carry is not None:
        aliases = {len(operands): 0}
        operands.append(carry)
        in_specs.append(pl.BlockSpec(memory_space=pl.ANY))
    total = lanes * piece_y * tokens
    return pl.pallas_call(
        block_kernel,
        grid=(lanes, piece_y),
        in_specs=in_specs,
        out_specs=pl.BlockSpec(block, lambda i, j: (0, i, 0, first + j, 0, 0)),
        out_shape=jax.ShapeDtypeStruct((GRID, lanes, devices_x, pieces, piece_cols, width), BF),
        scratch_shapes=[
            pltpu.VMEM((tokens, width), F32),
            pltpu.VMEM((tokens, width), F32),
            pltpu.VMEM((w_out.shape[0], width), BF),
            pltpu.VMEM((HEADS // 2 * HDIM, 2 * GRID * GRID), BF),
            pltpu.VMEM((HEADS // 2 * HDIM, 2 * GRID * GRID), BF),
            pltpu.VMEM((HEADS // 2 * GRID * GRID, HEADS // 2 * HDIM), BF),
            pltpu.VMEM((HEADS // 2 * GRID * GRID, HEADS // 2 * GRID * GRID), BF),
        ],
        input_output_aliases=aliases,
        compiler_params=pltpu.CompilerParams(vmem_limit_bytes=VMEM_LIMIT),
        cost_estimate=pl.CostEstimate(
            flops=total * 3_000_000, bytes_accessed=total * width * 4 + 800_000, transcendentals=total * 1100
        ),
    )(*operands)


def unpack_kernel(shares, local_m, piece_x, src, out):
    owners_y, owners_x = src.shape[:2]
    unit = out.shape[0]
    lines, first = [], 0
    for share in shares:
        lines += [(owner_y, first + piece) for owner_y in range(owners_y) for piece in range(share)]
        first += share
    for step in range(len(lines) // unit):

        @pl.when(pl.program_id(0) == step)
        def _():
            for row, (owner_y, piece) in enumerate(lines[step * unit : (step + 1) * unit]):
                wide = src[owner_y, :, piece].astype(F32)
                parts = [
                    wide[owner, m * piece_x : (m + 1) * piece_x] for m in range(local_m) for owner in range(owners_x)
                ]
                out[row] = jnp.concatenate(parts, axis=0).astype(BF)


def unpack_step(landed, shares, cols, local_m, piece_x):
    owners_y, _, pieces, _, width = landed.shape
    rows = owners_y * pieces
    unit = 16 if rows % 16 == 0 else rows
    return pl.pallas_call(
        functools.partial(unpack_kernel, shares, local_m, piece_x),
        grid=(rows // unit,),
        in_specs=[pl.BlockSpec(memory_space=pltpu.VMEM)],
        out_specs=pl.BlockSpec((unit, cols, width), lambda step: (step, 0, 0)),
        out_shape=jax.ShapeDtypeStruct((rows, cols, width), BF),
        compiler_params=pltpu.CompilerParams(vmem_limit_bytes=VMEM_LIMIT),
        cost_estimate=pl.CostEstimate(flops=0, bytes_accessed=rows * cols * width * 4, transcendentals=0),
    )(landed)


def step_rows(start, extent, most=16):
    return max(size for size in range(1, most + 1) if extent % size == 0 and start % size == 0)


def body(frames, hidden_state, cell_state, w_gates, gate_bias, w_qkv, w_out, w_up, w_down):
    rows, cols, width = hidden_state.shape
    latent = frames.shape[2] // 2
    chans = latent + width
    held = chans + width
    devices_y, devices_x = lax.axis_size("gy"), lax.axis_size("gx")
    local_m = GRID // devices_x
    piece_x = cols // local_m // devices_x
    weights = w_gates.reshape(-1, w_gates.shape[3])
    bias = gate_bias.reshape(1, -1)

    def shifted(value, axis, step):
        count = lax.axis_size(axis)
        pairs = [(i, i + step) for i in range(count) if 0 <= i + step < count]
        return lax.ppermute(value, axis, pairs)

    send_left, send_right, side_left, side_right, line_top, line_bot = pack_step(frames, hidden_state, cell_state)
    from_left = shifted(send_right, "gx", 1)
    from_right = shifted(send_left, "gx", -1)
    to_down = jnp.concatenate([line_bot, from_left[-2:], from_right[-2:]], axis=1)
    to_up = jnp.concatenate([line_top, from_left[:2], from_right[:2]], axis=1)

    pieces = rows // devices_y
    piece_cols = local_m * piece_x
    shares = (pieces - pieces // 3, pieces // 3)
    ahead = rows - max(size for size in range(1, 13) if rows % size == 0 and rows - size > shares[0] * devices_y)
    tile_shapes = (jax.ShapeDtypeStruct((rows, cols, width), BF), jax.ShapeDtypeStruct((rows, cols, width), F32))
    carry = ()
    half = -(-ahead // 8) * 4
    for start, extent in ((0, half), (half, ahead - half)):
        spec = pl.BlockSpec(memory_space=pltpu.VMEM)
        if carry:
            *carry, to_down, to_up = lax.optimization_barrier((*carry, to_down, to_up))
            from_up, from_down = shifted(to_down, "gy", 1), shifted(to_up, "gy", -1)
        carry = conv_step(
            frames, 0, hidden_state, cell_state, {}, weights, bias, (start, extent), ("hid_out", "cell_out"),
            tile_shapes, (spec, spec), None, carry, None,
        )
    hidden_one, cell_one = carry

    length = -(-(rows + 4) // 16) * 16
    line_shape = jax.ShapeDtypeStruct((4, cols, width), F32)
    strip_shape = jax.ShapeDtypeStruct((4, length, width), F32)
    beside_shape = jax.ShapeDtypeStruct((2, length, latent), F32)
    shapes = (line_shape, line_shape, strip_shape, strip_shape, beside_shape)
    turned = from_left.transpose(1, 0, 2), from_right.transpose(1, 0, 2)
    around = (from_up, from_down, line_top, line_bot, *turned, side_left, side_right)
    line_hid, line_cell, strip_hid, strip_cell, beside = pl.pallas_call(
        ring_kernel,
        grid=(1,),
        in_specs=[*(whole(array) for array in around), pl.BlockSpec(memory_space=pltpu.VMEM), whole(bias)],
        out_specs=[whole(shape) for shape in shapes],
        out_shape=shapes,
        scratch_shapes=[pltpu.VMEM((8, length, held + latent), F32)],
        compiler_params=pltpu.CompilerParams(vmem_limit_bytes=VMEM_LIMIT),
        cost_estimate=pl.CostEstimate(flops=16 * length * weights.size, bytes_accessed=2 * weights.size, transcendentals=0),
    )(*around, weights, bias)

    second = held // latent
    line = (1, from_up.shape[1], latent)
    ring = {name: (array, whole(array)) for name, array in (
        ("strips_hid", strip_hid), ("strips_cell", strip_cell), ("lines_hid", line_hid), ("lines_cell", line_cell),
        ("beside", beside),
    )}
    ring["frame_top"] = from_up, pl.BlockSpec(line, lambda step: (1, 0, second))
    ring["frame_bot"] = from_down, pl.BlockSpec(line, lambda step: (0, 0, second))

    moved, start, carry = [], 0, ()
    for piece_y in shares:
        extent = piece_y * devices_y
        sent_shape = jax.ShapeDtypeStruct((devices_y, devices_x, piece_y, piece_cols, width), BF)
        spec = pl.BlockSpec(memory_space=pl.ANY)
        sent, cell_out = conv_step(
            frames, 1, hidden_one, cell_one, ring, weights, bias, (start, extent),
            ("hid_out", "cell_out"), (sent_shape, tile_shapes[1]), (whole(sent_shape), spec), (local_m, piece_x), carry,
            (ahead, hidden_state, cell_state) if carry else None,
        )
        carry = (None, cell_out)
        sent = sent.reshape(devices_y * devices_x, piece_y, piece_cols, width)
        moved.append(lax.all_to_all(sent, ("gy", "gx"), split_axis=0, concat_axis=0, tiled=True))
        start += extent
    done, first = None, 0
    for piece_y, value in zip(shares, moved):
        done = block_step(value, done, first, pieces, devices_y, devices_x, w_qkv, w_out, w_up, w_down)
        first += piece_y
    done = done.reshape(devices_y * devices_x, pieces, piece_cols, width)
    landed = lax.all_to_all(done, ("gy", "gx"), split_axis=0, concat_axis=0, tiled=True)
    result = unpack_step(landed.reshape(devices_y, devices_x, *landed.shape[1:]), shares, cols, local_m, piece_x)
    return result, cell_out


def solution(mesh):
    tiled = P("gy", "gx", None)
    in_specs = (tiled, tiled, tiled, P(), P(), P(), P(), P(), P())
    return jax.shard_map(body, mesh=mesh, in_specs=in_specs, out_specs=(tiled, tiled), check_vma=False)
```

```python
import functools

import jax
import jax.numpy as jnp
from jax import lax
from jax.experimental import pallas as pl
from jax.experimental.pallas import tpu as pltpu
from jax.sharding import PartitionSpec as P

HEADS = 8
HDIM = 32
GRID = 8
BF = jnp.bfloat16
F32 = jnp.float32
LOG2E = 1.4426950408889634
BF_MAX = 3.3895313892515355e38
VMEM_LIMIT = 32 * 1024 * 1024
VMEM_ALL = 60 * 1024 * 1024
LOADS = 9
LANES = 128


def sigmoid(x):
    return 0.5 * jnp.tanh(0.5 * x) + 0.5


def lstm(gates, cell_prev):
    width = cell_prev.shape[-1]
    in_gate = sigmoid(gates[:, 0:width])
    forget_gate = sigmoid(gates[:, width : 2 * width])
    candidate = jnp.tanh(gates[:, 2 * width : 3 * width])
    out_gate = sigmoid(gates[:, 3 * width :])
    cell = forget_gate * cell_prev + in_gate * candidate
    return cell, out_gate * jnp.tanh(cell)


def layer_norm(values):
    center = values - jnp.mean(values, axis=-1, keepdims=True)
    spread = jnp.mean(center * center, axis=-1, keepdims=True)
    return center * lax.rsqrt(spread + 1e-05)


def three_columns(wide, left, right):
    count = wide.shape[0]
    place = lax.broadcasted_iota(jnp.int32, wide.shape, 0)
    before = jnp.where(place == 0, left, pltpu.roll(wide, 1, axis=0))
    after = jnp.where(place == count - 1, right, pltpu.roll(wide, count - 1, axis=0))
    return before.astype(BF), wide.astype(BF), after.astype(BF)


def conv_kernel(start, rows, part, tail, refs, packed, *args):
    ref = dict(zip(refs, args))
    hid_out, cell_out = ref["hid_out"], ref["cell_out"]
    extent = ref["spread"].shape[0] - 2
    cols, width = ref["hid"].shape[1:]
    chans = ref["spread"].shape[2] // 3
    latent = chans - width
    loads, leaving = [], []
    if "weights" in ref:
        size = ref["weights"].shape[0] // LOADS
        for place in range(LOADS):
            run = pl.ds(place * size, size)
            loads.append(pltpu.make_async_copy(ref["weights"].at[run], ref["held"].at[run], ref["sem"].at[place]))
    for load in loads:
        load.start()

    def reader(prefix, first, count):
        def row_of(name, row):
            array = ref[prefix + name]
            if array.shape[0] == rows:
                channels = slice(part * latent, (part + 1) * latent) if name == "frame" else slice(None)
                return array[row, :, channels]
            if prefix != "tail_" and tail and row >= tail and name != "frame":
                return ref["late_" + name][row - tail]
            if row == first - 1:
                return ref[prefix + name + "_prev"][0]
            if row == first + count:
                return ref[prefix + name + "_next"][0]
            return array[row - first]

        return row_of

    def convolve(spread, start, extent, row_of, ring, write, leave):
        def beside(row):
            if not ring:
                return jnp.zeros((1, chans), F32), jnp.zeros((1, chans), F32)
            at = row + 2
            return tuple(
                jnp.concatenate(
                    [ref["beside"][place, at : at + 1, :], ref["strips_hid"][3 * place, at : at + 1, :]], axis=1
                )
                for place in range(2)
            )

        def build(pos):
            row = start + pos - 1
            raw = None
            if 0 <= row < rows:
                raw = row_of("frame", row), row_of("hid", row)
                x, h = raw[0].astype(F32), raw[1].astype(F32)
            elif ring:
                x = ref["frame_top" if row < 0 else "frame_bot"][0, :cols].astype(F32)
                h = ref["lines_hid"][3 * (row > 0)]
            else:
                spread[pos] = jnp.zeros(spread.shape[1:], BF)
                return
            low, high = beside(row)
            if ring:
                at = row + 2
                place = lax.broadcasted_iota(jnp.int32, h.shape, 0)
                h = jnp.where(place == 0, ref["strips_hid"][1, at : at + 1, :], h)
                h = jnp.where(place == cols - 1, ref["strips_hid"][2, at : at + 1, :], h)
                for spot, line in ((0, 1), (rows - 1, 2)):
                    if row == spot:
                        h = ref["lines_hid"][line]
            for side, (value, first) in enumerate(((x, 0), (h, latent))):
                size = value.shape[1]
                pieces = three_columns(value, low[:, first : first + size], high[:, first : first + size])
                if raw is not None and (side == 0 or not ring):
                    pieces = pieces[0], raw[side], pieces[2]
                for tap in range(3):
                    spread[pos, :, tap * chans + first : tap * chans + first + size] = pieces[tap]

        def multiply(first, depth):
            lhs = jnp.concatenate(
                [spread[first + tap : first + tap + depth].reshape(depth * cols, 3 * chans) for tap in range(3)], axis=1
            )
            return jnp.dot(lhs, ref["held"][...], preferred_element_type=F32)

        def activate(first, depth, gates):
            for line in range(first, first + depth):
                row = start + line
                cell_prev = row_of("cell", row)
                if ring:
                    at = row + 2
                    place = lax.broadcasted_iota(jnp.int32, cell_prev.shape, 0)
                    cell_prev = jnp.where(place == 0, ref["strips_cell"][1, at : at + 1, :], cell_prev)
                    cell_prev = jnp.where(place == cols - 1, ref["strips_cell"][2, at : at + 1, :], cell_prev)
                    if row == 0:
                        cell_prev = ref["lines_cell"][1]
                    if row == rows - 1:
                        cell_prev = ref["lines_cell"][2]
                own = gates[(line - first) * cols : (line - first + 1) * cols] + ref["bias"][...]
                new_cell, new_hidden = lstm(own, cell_prev)
                write(row, new_cell, new_hidden)
            leave(first, depth)

        depth = step_rows(0, extent, 12)
        for pos in range(depth + 2):
            build(pos)
        while loads:
            loads.pop().wait()
        waiting = None
        for first in range(0, extent, depth):
            for pos in range(first + depth + 2, min(first + 2 * depth, extent) + 2):
                build(pos)
            gates = multiply(first, depth)
            if waiting:
                activate(*waiting)
            waiting = first, depth, gates
        activate(*waiting)

    def keep(row, new_cell, new_hidden):
        cell_out[row] = new_cell
        hid_out[row] = new_hidden.astype(BF)

    def keep_late(row, new_cell, new_hidden):
        ref["late_cell"][row - tail] = new_cell
        ref["late_hid"][row - tail] = new_hidden.astype(BF)

    def send(row, new_cell, new_hidden):
        line = row - start
        ref["cell_rows"][line] = new_cell
        owners_x, piece_y = hid_out.shape[1:3]
        local_m, piece_x = packed
        for owner in range(owners_x):
            picked = [
                new_hidden[(m * owners_x + owner) * piece_x : (m * owners_x + owner + 1) * piece_x]
                for m in range(local_m)
            ]
            hid_out[line // piece_y, owner, line % piece_y] = jnp.concatenate(picked, axis=0).astype(BF)

    def leave(first, depth):
        copy = pltpu.make_async_copy(
            ref["cell_rows"].at[pl.ds(first, depth)], cell_out.at[pl.ds(start + first, depth)],
            ref["left"].at[first // depth],
        )
        copy.start()
        leaving.append(copy)

    def stay(first, depth):
        pass

    if not packed:
        convolve(ref["spread"], start, extent, reader("", start, extent), False, keep, stay)
        return
    if tail:
        convolve(ref["late_spread"], tail, rows - tail, reader("tail_", tail, rows - tail), False, keep_late, stay)
    convolve(ref["spread"], start, extent, reader("", start, extent), True, send, leave)
    for copy in leaving:
        copy.wait()


def whole(array):
    return pl.BlockSpec(array.shape, lambda *step: (0,) * array.ndim)


def conv_step(frames, part, hid, cell, ring, weights, bias, rows_of, names, out_shapes, out_specs, packed, carry, late):
    rows, cols, width = hid.shape
    latent = weights.shape[0] // 9 - width
    start, extent = rows_of

    def rowed(size, channels, channel, row):
        return pl.BlockSpec((size, cols, channels), lambda step: (row // size, 0, channel))

    def windows(prefix, hid, cell, channel, start, extent):
        before, after = max(start - 1, 0), min(start + extent, rows - 1)
        return {
            prefix + "frame": (frames, rowed(extent, latent, channel, start)),
            prefix + "frame_prev": (frames, rowed(1, latent, channel, before)),
            prefix + "frame_next": (frames, rowed(1, latent, channel, after)),
            prefix + "hid": (hid, rowed(extent, width, 0, start)),
            prefix + "hid_prev": (hid, rowed(1, width, 0, before)),
            prefix + "hid_next": (hid, rowed(1, width, 0, after)),
            prefix + "cell": (cell, rowed(extent, width, 0, start)),
        }

    near = pl.BlockSpec(memory_space=pltpu.VMEM)
    tail = 0
    if late:
        tail, *first = late
        inputs = windows("", hid, cell, part, start, extent)
        inputs |= windows("tail_", *first, 0, tail, rows - tail)
    else:
        inputs = {"frame": (frames, near), "hid": (hid, near), "cell": (cell, near)}
    inputs["bias"] = bias, whole(bias)
    if late:
        inputs["weights"] = weights, pl.BlockSpec(memory_space=pl.ANY)
    else:
        inputs["held"] = weights, near
    inputs |= ring
    aliases = {}
    for place, array in enumerate(carry):
        if array is not None:
            aliases[len(inputs)] = place
            inputs[f"carry{place}"] = (array, pl.BlockSpec(memory_space=pl.ANY) if packed else near)
    refs = [*inputs, *names, "spread"]
    scratch = [pltpu.VMEM((extent + 2, cols, 3 * (latent + width)), BF)]
    if late:
        refs += ["held", "sem", "late_spread", "late_hid", "late_cell"]
        scratch += [
            pltpu.VMEM(weights.shape, BF),
            pltpu.SemaphoreType.DMA((LOADS,)),
            pltpu.VMEM((rows - tail + 2, cols, 3 * (latent + width)), BF),
            pltpu.VMEM((rows - tail, cols, width), BF),
            pltpu.VMEM((rows - tail, cols, width), F32),
        ]
    if packed:
        refs += ["cell_rows", "left"]
        scratch += [pltpu.VMEM((extent, cols, width), F32), pltpu.SemaphoreType.DMA((extent,))]
    cells = extent * cols
    return pl.pallas_call(
        functools.partial(conv_kernel, start, rows, part, tail, refs, packed),
        grid=(1,),
        in_specs=[spec for _, spec in inputs.values()],
        out_specs=out_specs,
        out_shape=out_shapes,
        scratch_shapes=scratch,
        input_output_aliases=aliases,
        compiler_params=pltpu.CompilerParams(vmem_limit_bytes=VMEM_ALL if late else VMEM_LIMIT),
        cost_estimate=pl.CostEstimate(
            flops=2 * cells * weights.size, bytes_accessed=2 * weights.size + cells * 2048, transcendentals=cells * width * 5
        ),
    )(*(array for array, _ in inputs.values()))


def pack_kernel(frames, hids, cells, send_low, send_high, side_low, side_high, line_top, line_bot, flat):
    rows, cols, width = hids.shape
    latent = frames.shape[2] // 2
    chans = latent + width
    places = ((0, 0, latent), (chans + width, latent, latent))
    for out, near in ((line_top, slice(0, 2)), (line_bot, slice(rows - 2, rows))):
        for to, start, size in places:
            out[:, :, to : to + size] = frames[near, :, start : start + size]
        out[:, :, latent:chans] = hids[near]
        out[:, :, chans : chans + width] = cells[near].astype(BF)
    for out, send, near, start in (
        (side_low, send_low, slice(0, 8), 0),
        (side_high, send_high, slice(cols - 8, cols), 6),
    ):
        for slab in range(out.shape[2] // LANES):
            to = slab * LANES
            if to < latent or to >= chans + width:
                begin = to if to < latent else to - 2 * width
                part = frames[:, near, begin : begin + LANES].astype(F32)
            elif to < chans:
                part = hids[:, near, to - latent : to - latent + LANES].astype(F32)
            else:
                part = cells[:, near, to - chans : to - chans + LANES]
            send[:, :, to : to + LANES] = part[:, start : start + 2].astype(BF)
            flat[...] = part.reshape(rows * 8, LANES)
            for place in range(2):
                out[place, :, to : to + LANES] = flat[pl.ds(start + place, rows, stride=8), :].astype(BF)


def pack_step(frames, hid, cell):
    rows, cols, width = hid.shape
    span = frames.shape[2]
    deep = span + 2 * width
    shapes = [jax.ShapeDtypeStruct((rows, 2, deep), BF)] * 2 + [jax.ShapeDtypeStruct((2, rows, deep), BF)] * 2
    shapes += [jax.ShapeDtypeStruct((2, cols, deep), BF)] * 2
    return pl.pallas_call(
        pack_kernel,
        grid=(1,),
        in_specs=[pl.BlockSpec(memory_space=pltpu.VMEM)] * 3,
        out_specs=[whole(shape) for shape in shapes],
        out_shape=shapes,
        scratch_shapes=[pltpu.VMEM((rows * 8, LANES), F32)],
        compiler_params=pltpu.CompilerParams(vmem_limit_bytes=VMEM_LIMIT),
        cost_estimate=pl.CostEstimate(flops=0, bytes_accessed=4_000_000, transcendentals=0),
    )(frames, hid, cell)


def ring_kernel(
    above, below, line_top, line_bot, from_left, from_right, side_left, side_right, weights, bias,
    line_hid, line_cell, strip_hid, strip_cell, beside, strips,
):
    width = line_hid.shape[2]
    chans = weights.shape[0] // 9
    cols, length = line_top.shape[1], strip_hid.shape[1]
    rows = from_left.shape[1]
    columns = (
        (from_left, 0, cols), (from_left, 1, cols + 1), (side_left, 0, 0), (side_left, 1, 1),
        (side_right, 0, cols - 2), (side_right, 1, cols - 1), (from_right, 0, cols + 2), (from_right, 1, cols + 3),
    )
    ends = [(ref[row].astype(F32), at + row) for ref, at in ((above, 0), (below, rows + 2)) for row in range(2)]
    strips[:, rows + 4 :, :] = jnp.zeros((8, length - rows - 4, strips.shape[2]), F32)
    for place, (source, at, end) in enumerate(columns):
        strips[place, 2 : rows + 2, :] = source[at].astype(F32)
        for value, spot in ends:
            strips[place, spot : spot + 1, :] = value[end : end + 1]
    beside[0] = strips[1, :, chans + width :]
    beside[1] = strips[6, :, chans + width :]
    low, high = strips[1, :, :chans], strips[6, :, :chans]

    def line(ref, row):
        held = ref[row, :cols].astype(F32)
        return held[:, :chans], held[:, chans : chans + width]

    tops = [line(above, 0), line(above, 1), line(line_top, 0), line(line_top, 1)]
    bots = [line(line_bot, 0), line(line_bot, 1), line(below, 0), line(below, 1)]
    parts, held = [], []
    for lead, lines in ((0, tops), (rows, bots)):
        pieces = []
        for row in range(4):
            at = lead + row
            pieces.append(three_columns(lines[row][0], low[at : at + 1], high[at : at + 1]))
        for row in range(2):
            parts.append(jnp.concatenate([pieces[row + tap][col] for tap in range(3) for col in range(3)], axis=1))
            held.append(lines[row + 1][1])
    for side in range(2):
        rolled = []
        for col in range(4):
            wide = strips[4 * side + col, :, :chans]
            rolled.append((pltpu.roll(wide, 1, axis=0), wide, pltpu.roll(wide, length - 1, axis=0)))
        for col in range(2):
            parts.append(
                jnp.concatenate([rolled[col + tap][row].astype(BF) for row in range(3) for tap in range(3)], axis=1)
            )
            held.append(strips[4 * side + col + 1, :, chans : chans + width])
    row_at, col_at = lax.axis_index("gy"), lax.axis_index("gx")
    upper = (row_at > 0).astype(F32)
    lower = (row_at < lax.axis_size("gy") - 1).astype(F32)
    before = (col_at > 0).astype(F32)
    after = (col_at < lax.axis_size("gx") - 1).astype(F32)
    spot = lax.broadcasted_iota(jnp.int32, (length, width), 0)
    inside = jnp.where(spot == 1, upper, jnp.where(spot == rows + 2, lower, 1.0))
    keep = [upper, 1.0, 1.0, lower, inside * before, inside, inside, inside * after]
    lhs = jnp.concatenate(parts, axis=0)
    gates = jnp.dot(lhs, weights[...], preferred_element_type=F32) + bias[...]
    start = 0
    for place in range(8):
        hid, cell = (line_hid, line_cell) if place < 4 else (strip_hid, strip_cell)
        size = hid.shape[1]
        new_cell, hidden = lstm(gates[start : start + size], held[place])
        hid[place % 4] = hidden.astype(BF).astype(F32) * keep[place]
        cell[place % 4] = new_cell
        start += size


def block_kernel(x, w_qkv, w_out, w_up, w_down, *rest):
    out, flat, back, keys_t, own_low, own_high, own_values, ones = rest[-8:]
    group = GRID * GRID
    embed = w_out.shape[0]
    tile = embed // 2

    @pl.when((pl.program_id(0) == 0) & (pl.program_id(1) == 0))
    def _():
        def fill(target, down, across, add):
            above = lax.broadcasted_iota(jnp.int32, target.shape, 0) // down
            along = lax.broadcasted_iota(jnp.int32, target.shape, 1) // across
            target[...] = (above == along + add).astype(F32).astype(BF)

        fill(own_low, HDIM, group, 0)
        fill(own_high, HDIM, group, HEADS // 4)
        fill(own_values, group, HDIM, 0)
        fill(ones, group, group, 0)
        keys_t[...] = w_qkv[:, embed : 2 * embed].astype(F32).T.astype(BF)

    def work(sub):
        flat[sub] = x[:, :, sub].astype(F32).reshape(flat.shape[1:])
        groups = flat.shape[1] // group
        cells = jnp.concatenate([flat[sub, pl.ds(g, group, stride=groups), :] for g in range(groups)], axis=0)
        normed = layer_norm(cells).astype(BF)
        yield
        queries = jnp.dot(normed, w_qkv[:, :embed], preferred_element_type=F32).astype(BF)
        values = jnp.dot(normed, w_qkv[:, 2 * embed :], preferred_element_type=F32).astype(BF)
        keys = lax.dot_general(keys_t[...], normed, (((1,), (1,)), ((), ())), preferred_element_type=F32)
        yield
        side = lax.broadcasted_iota(jnp.int32, (embed, 2 * group), 1) < group
        raised = [[], []]
        for pair in range(groups // 2):
            both = keys[:, pair * 2 * group : (pair + 1) * 2 * group]
            turned = pltpu.roll(both, group, axis=1)
            for place, twice in enumerate((jnp.where(side, both, turned), jnp.where(side, turned, both))):
                twice = twice.astype(BF)
                start = (2 * pair + place) * group
                for half in range(2):
                    part = twice[half * tile : (half + 1) * tile]
                    spread = jnp.concatenate([part * own_low[...], part * own_high[...]], axis=1)
                    scores = jnp.dot(
                        queries[start : start + group, half * tile : (half + 1) * tile],
                        spread,
                        preferred_element_type=F32,
                    )
                    raised[half].append(jnp.minimum(jnp.exp2(scores * (LOG2E * HDIM**-0.5)), BF_MAX).astype(BF))
            if pair % 2:
                yield
        attn = []
        for half in range(2):
            part = jnp.concatenate(raised[half], axis=0)
            total = jnp.dot(part, ones[...], preferred_element_type=F32)
            guess = pl.reciprocal(total, approx=True)
            attn.append((part.astype(F32) * (guess * (2.0 - total * guess))).astype(BF))
        yield
        heads = []
        for half in range(2):
            column = []
            for g in range(groups):
                held = values[g * group : (g + 1) * group, half * tile : (half + 1) * tile]
                spread = jnp.concatenate([held] * (HEADS // 2), axis=0) * own_values[...]
                column.append(
                    jnp.dot(attn[half][g * group : (g + 1) * group], spread, preferred_element_type=F32).astype(BF)
                )
            heads.append(jnp.concatenate(column, axis=0))
        heads = jnp.concatenate(heads, axis=1)
        yield
        attended = jnp.dot(heads, w_out[...], preferred_element_type=F32).astype(BF)
        mixed = cells + attended.astype(F32)
        normed_two = layer_norm(mixed).astype(BF)
        yield
        up = jnp.dot(normed_two, w_up[...], preferred_element_type=F32)
        bent = jnp.tanh(up * (0.7978845608 + (0.7978845608 * 0.044715) * (up * up)))
        half_up = 0.5 * up
        expanded = (half_up + half_up * bent).astype(BF)
        yield
        result = mixed + jnp.dot(expanded, w_down[...], preferred_element_type=F32)
        for g in range(groups):
            back[sub, pl.ds(g, group, stride=groups), :] = result[g * group : (g + 1) * group]
        out[:, :, sub] = back[sub].reshape(x.shape[:2] + x.shape[3:]).astype(BF)

    waiting = [work(sub) for sub in range(x.shape[2])]
    running = []
    while waiting or running:
        if waiting:
            running.append(waiting.pop(0))
        for one in list(running):
            if next(one, running) is running:
                running.remove(one)


def block_step(moved, carry, first, pieces, devices_y, devices_x, w_qkv, w_out, w_up, w_down):
    _, piece_y, piece_cols, width = moved.shape
    lanes = devices_y // GRID
    view = moved.reshape(GRID, lanes, devices_x, piece_y, piece_cols, width)
    tokens = GRID * devices_x * piece_cols
    subs = 2 if piece_y % 2 == 0 and first % 2 == 0 else 1
    block = (GRID, None, devices_x, subs, piece_cols, width)
    operands = [view, w_qkv, w_out, w_up, w_down]
    in_specs = [pl.BlockSpec(block, lambda i, j: (0, i, 0, j, 0, 0)), *(whole(array) for array in operands[1:])]
    aliases = {}
    if carry is not None:
        aliases = {len(operands): 0}
        operands.append(carry)
        in_specs.append(pl.BlockSpec(memory_space=pl.ANY))
    total = lanes * piece_y * tokens
    return pl.pallas_call(
        block_kernel,
        grid=(lanes, piece_y // subs),
        in_specs=in_specs,
        out_specs=pl.BlockSpec(block, lambda i, j: (0, i, 0, first // subs + j, 0, 0)),
        out_shape=jax.ShapeDtypeStruct((GRID, lanes, devices_x, pieces, piece_cols, width), BF),
        scratch_shapes=[
            pltpu.VMEM((subs, tokens, width), F32),
            pltpu.VMEM((subs, tokens, width), F32),
            pltpu.VMEM((w_out.shape[0], width), BF),
            pltpu.VMEM((HEADS // 2 * HDIM, 2 * GRID * GRID), BF),
            pltpu.VMEM((HEADS // 2 * HDIM, 2 * GRID * GRID), BF),
            pltpu.VMEM((HEADS // 2 * GRID * GRID, HEADS // 2 * HDIM), BF),
            pltpu.VMEM((HEADS // 2 * GRID * GRID, HEADS // 2 * GRID * GRID), BF),
        ],
        input_output_aliases=aliases,
        compiler_params=pltpu.CompilerParams(vmem_limit_bytes=VMEM_LIMIT),
        cost_estimate=pl.CostEstimate(
            flops=total * 3_000_000, bytes_accessed=total * width * 4 + 800_000, transcendentals=total * 1100
        ),
    )(*operands)


def unpack_kernel(shares, local_m, piece_x, src, out):
    owners_y, owners_x = src.shape[:2]
    unit = out.shape[0]
    lines, first = [], 0
    for share in shares:
        lines += [(owner_y, first + piece) for owner_y in range(owners_y) for piece in range(share)]
        first += share
    for step in range(len(lines) // unit):

        @pl.when(pl.program_id(0) == step)
        def _():
            for row, (owner_y, piece) in enumerate(lines[step * unit : (step + 1) * unit]):
                wide = src[owner_y, :, piece].astype(F32)
                parts = [
                    wide[owner, m * piece_x : (m + 1) * piece_x] for m in range(local_m) for owner in range(owners_x)
                ]
                out[row] = jnp.concatenate(parts, axis=0).astype(BF)


def unpack_step(landed, shares, cols, local_m, piece_x):
    owners_y, _, pieces, _, width = landed.shape
    rows = owners_y * pieces
    unit = 16 if rows % 16 == 0 else rows
    return pl.pallas_call(
        functools.partial(unpack_kernel, shares, local_m, piece_x),
        grid=(rows // unit,),
        in_specs=[pl.BlockSpec(memory_space=pltpu.VMEM)],
        out_specs=pl.BlockSpec((unit, cols, width), lambda step: (step, 0, 0)),
        out_shape=jax.ShapeDtypeStruct((rows, cols, width), BF),
        compiler_params=pltpu.CompilerParams(vmem_limit_bytes=VMEM_LIMIT),
        cost_estimate=pl.CostEstimate(flops=0, bytes_accessed=rows * cols * width * 4, transcendentals=0),
    )(landed)


def step_rows(start, extent, most=16):
    return max(size for size in range(1, most + 1) if extent % size == 0 and start % size == 0)


def body(frames, hidden_state, cell_state, w_gates, gate_bias, w_qkv, w_out, w_up, w_down):
    rows, cols, width = hidden_state.shape
    latent = frames.shape[2] // 2
    chans = latent + width
    held = chans + width
    devices_y, devices_x = lax.axis_size("gy"), lax.axis_size("gx")
    local_m = GRID // devices_x
    piece_x = cols // local_m // devices_x
    weights = w_gates.reshape(-1, w_gates.shape[3])
    bias = gate_bias.reshape(1, -1)

    def shifted(value, axis, step):
        count = lax.axis_size(axis)
        pairs = [(i, i + step) for i in range(count) if 0 <= i + step < count]
        return lax.ppermute(value, axis, pairs)

    send_left, send_right, side_left, side_right, line_top, line_bot = pack_step(frames, hidden_state, cell_state)
    from_left = shifted(send_right, "gx", 1)
    from_right = shifted(send_left, "gx", -1)
    to_down = jnp.concatenate([line_bot, from_left[-2:], from_right[-2:]], axis=1)
    to_up = jnp.concatenate([line_top, from_left[:2], from_right[:2]], axis=1)

    pieces = rows // devices_y
    piece_cols = local_m * piece_x
    shares = (pieces - pieces // 3, pieces // 3)
    ahead = rows - max(size for size in range(1, 13) if rows % size == 0 and rows - size > shares[0] * devices_y)
    tile_shapes = (jax.ShapeDtypeStruct((rows, cols, width), BF), jax.ShapeDtypeStruct((rows, cols, width), F32))
    carry = ()
    half = -(-ahead // 8) * 4
    for start, extent in ((0, half), (half, ahead - half)):
        spec = pl.BlockSpec(memory_space=pltpu.VMEM)
        if carry:
            *carry, to_down, to_up = lax.optimization_barrier((*carry, to_down, to_up))
            from_up, from_down = shifted(to_down, "gy", 1), shifted(to_up, "gy", -1)
        carry = conv_step(
            frames, 0, hidden_state, cell_state, {}, weights, bias, (start, extent), ("hid_out", "cell_out"),
            tile_shapes, (spec, spec), None, carry, None,
        )
    hidden_one, cell_one = carry

    length = -(-(rows + 4) // 16) * 16
    line_shape = jax.ShapeDtypeStruct((4, cols, width), F32)
    strip_shape = jax.ShapeDtypeStruct((4, length, width), F32)
    beside_shape = jax.ShapeDtypeStruct((2, length, latent), F32)
    shapes = (line_shape, line_shape, strip_shape, strip_shape, beside_shape)
    turned = from_left.transpose(1, 0, 2), from_right.transpose(1, 0, 2)
    around = (from_up, from_down, line_top, line_bot, *turned, side_left, side_right)
    line_hid, line_cell, strip_hid, strip_cell, beside = pl.pallas_call(
        ring_kernel,
        grid=(1,),
        in_specs=[*(whole(array) for array in around), pl.BlockSpec(memory_space=pltpu.VMEM), whole(bias)],
        out_specs=[whole(shape) for shape in shapes],
        out_shape=shapes,
        scratch_shapes=[pltpu.VMEM((8, length, held + latent), F32)],
        compiler_params=pltpu.CompilerParams(vmem_limit_bytes=VMEM_LIMIT),
        cost_estimate=pl.CostEstimate(flops=16 * length * weights.size, bytes_accessed=2 * weights.size, transcendentals=0),
    )(*around, weights, bias)

    second = held // latent
    line = (1, from_up.shape[1], latent)
    ring = {name: (array, whole(array)) for name, array in (
        ("strips_hid", strip_hid), ("strips_cell", strip_cell), ("lines_hid", line_hid), ("lines_cell", line_cell),
        ("beside", beside),
    )}
    ring["frame_top"] = from_up, pl.BlockSpec(line, lambda step: (1, 0, second))
    ring["frame_bot"] = from_down, pl.BlockSpec(line, lambda step: (0, 0, second))

    moved, start, carry = [], 0, ()
    for piece_y in shares:
        extent = piece_y * devices_y
        sent_shape = jax.ShapeDtypeStruct((devices_y, devices_x, piece_y, piece_cols, width), BF)
        spec = pl.BlockSpec(memory_space=pl.ANY)
        sent, cell_out = conv_step(
            frames, 1, hidden_one, cell_one, ring, weights, bias, (start, extent),
            ("hid_out", "cell_out"), (sent_shape, tile_shapes[1]), (whole(sent_shape), spec), (local_m, piece_x), carry,
            (ahead, hidden_state, cell_state) if carry else None,
        )
        carry = (None, cell_out)
        sent = sent.reshape(devices_y * devices_x, piece_y, piece_cols, width)
        moved.append(lax.all_to_all(sent, ("gy", "gx"), split_axis=0, concat_axis=0, tiled=True))
        start += extent
    done, first = None, 0
    for piece_y, value in zip(shares, moved):
        done = block_step(value, done, first, pieces, devices_y, devices_x, w_qkv, w_out, w_up, w_down)
        first += piece_y
    done = done.reshape(devices_y * devices_x, pieces, piece_cols, width)
    landed = lax.all_to_all(done, ("gy", "gx"), split_axis=0, concat_axis=0, tiled=True)
    result = unpack_step(landed.reshape(devices_y, devices_x, *landed.shape[1:]), shares, cols, local_m, piece_x)
    return result, cell_out


def solution(mesh):
    tiled = P("gy", "gx", None)
    in_specs = (tiled, tiled, tiled, P(), P(), P(), P(), P(), P())
    return jax.shard_map(body, mesh=mesh, in_specs=in_specs, out_specs=(tiled, tiled), check_vma=False)
```

```python
import functools

import jax
import jax.numpy as jnp
from jax import lax
from jax.experimental import pallas as pl
from jax.experimental.pallas import tpu as pltpu
from jax.sharding import PartitionSpec as P

HEADS = 8
HDIM = 32
GRID = 8
BF = jnp.bfloat16
F32 = jnp.float32
LOG2E = 1.4426950408889634
BF_MAX = 3.3895313892515355e38
VMEM_LIMIT = 32 * 1024 * 1024
VMEM_ALL = 60 * 1024 * 1024
LOADS = 9
LANES = 128


def sigmoid(x):
    return 0.5 * jnp.tanh(0.5 * x) + 0.5


def lstm(gates, cell_prev):
    width = cell_prev.shape[-1]
    in_gate = sigmoid(gates[:, 0:width])
    forget_gate = sigmoid(gates[:, width : 2 * width])
    candidate = jnp.tanh(gates[:, 2 * width : 3 * width])
    out_gate = sigmoid(gates[:, 3 * width :])
    cell = forget_gate * cell_prev + in_gate * candidate
    return cell, out_gate * jnp.tanh(cell)


def layer_norm(values):
    center = values - jnp.mean(values, axis=-1, keepdims=True)
    spread = jnp.mean(center * center, axis=-1, keepdims=True)
    return center * lax.rsqrt(spread + 1e-05)


def three_columns(wide, left, right):
    count = wide.shape[0]
    place = lax.broadcasted_iota(jnp.int32, wide.shape, 0)
    before = jnp.where(place == 0, left, pltpu.roll(wide, 1, axis=0))
    after = jnp.where(place == count - 1, right, pltpu.roll(wide, count - 1, axis=0))
    return before.astype(BF), wide.astype(BF), after.astype(BF)


def conv_kernel(start, rows, part, tail, refs, packed, *args):
    ref = dict(zip(refs, args))
    hid_out, cell_out = ref["hid_out"], ref["cell_out"]
    extent = ref["spread"].shape[0] - 2
    cols, width = ref["hid"].shape[1:]
    chans = ref["spread"].shape[2] // 3
    latent = chans - width
    loads, leaving = [], []
    if "weights" in ref:
        size = ref["weights"].shape[0] // LOADS
        for place in range(LOADS):
            run = pl.ds(place * size, size)
            loads.append(pltpu.make_async_copy(ref["weights"].at[run], ref["held"].at[run], ref["sem"].at[place]))
    for load in loads:
        load.start()

    def reader(prefix, first, count):
        def row_of(name, row):
            array = ref[prefix + name]
            if array.shape[0] == rows:
                channels = slice(part * latent, (part + 1) * latent) if name == "frame" else slice(None)
                return array[row, :, channels]
            if prefix != "tail_" and tail and row >= tail and name != "frame":
                return ref["late_" + name][row - tail]
            if row == first - 1:
                return ref[prefix + name + "_prev"][0]
            if row == first + count:
                return ref[prefix + name + "_next"][0]
            return array[row - first]

        return row_of

    def convolve(spread, start, extent, row_of, ring, write, leave):
        def beside(row):
            if not ring:
                return jnp.zeros((1, chans), F32), jnp.zeros((1, chans), F32)
            at = row + 2
            return tuple(
                jnp.concatenate(
                    [ref["beside"][place, at : at + 1, :], ref["strips_hid"][3 * place, at : at + 1, :]], axis=1
                )
                for place in range(2)
            )

        def build(pos):
            row = start + pos - 1
            raw = None
            if 0 <= row < rows:
                raw = row_of("frame", row), row_of("hid", row)
                x, h = raw[0].astype(F32), raw[1].astype(F32)
            elif ring:
                x = ref["frame_top" if row < 0 else "frame_bot"][0, :cols].astype(F32)
                h = ref["lines_hid"][3 * (row > 0)]
            else:
                spread[pos] = jnp.zeros(spread.shape[1:], BF)
                return
            low, high = beside(row)
            if ring:
                at = row + 2
                place = lax.broadcasted_iota(jnp.int32, h.shape, 0)
                h = jnp.where(place == 0, ref["strips_hid"][1, at : at + 1, :], h)
                h = jnp.where(place == cols - 1, ref["strips_hid"][2, at : at + 1, :], h)
                for spot, line in ((0, 1), (rows - 1, 2)):
                    if row == spot:
                        h = ref["lines_hid"][line]
            for side, (value, first) in enumerate(((x, 0), (h, latent))):
                size = value.shape[1]
                pieces = three_columns(value, low[:, first : first + size], high[:, first : first + size])
                if raw is not None and (side == 0 or not ring):
                    pieces = pieces[0], raw[side], pieces[2]
                for tap in range(3):
                    spread[pos, :, tap * chans + first : tap * chans + first + size] = pieces[tap]

        def multiply(first, depth):
            lhs = jnp.concatenate(
                [spread[first + tap : first + tap + depth].reshape(depth * cols, 3 * chans) for tap in range(3)], axis=1
            )
            return jnp.dot(lhs, ref["held"][...], preferred_element_type=F32)

        def activate(first, depth, gates):
            for line in range(first, first + depth):
                row = start + line
                cell_prev = row_of("cell", row)
                if ring:
                    at = row + 2
                    place = lax.broadcasted_iota(jnp.int32, cell_prev.shape, 0)
                    cell_prev = jnp.where(place == 0, ref["strips_cell"][1, at : at + 1, :], cell_prev)
                    cell_prev = jnp.where(place == cols - 1, ref["strips_cell"][2, at : at + 1, :], cell_prev)
                    if row == 0:
                        cell_prev = ref["lines_cell"][1]
                    if row == rows - 1:
                        cell_prev = ref["lines_cell"][2]
                own = gates[(line - first) * cols : (line - first + 1) * cols] + ref["bias"][...]
                new_cell, new_hidden = lstm(own, cell_prev)
                write(row, new_cell, new_hidden)
            leave(first, depth)

        depth = step_rows(0, extent, 4)
        for pos in range(depth + 2):
            build(pos)
        while loads:
            loads.pop().wait()
        waiting = None
        for first in range(0, extent, depth):
            for pos in range(first + depth + 2, min(first + 2 * depth, extent) + 2):
                build(pos)
            gates = multiply(first, depth)
            if waiting:
                activate(*waiting)
            waiting = first, depth, gates
        activate(*waiting)

    def keep(row, new_cell, new_hidden):
        cell_out[row] = new_cell
        hid_out[row] = new_hidden.astype(BF)

    def keep_late(row, new_cell, new_hidden):
        ref["late_cell"][row - tail] = new_cell
        ref["late_hid"][row - tail] = new_hidden.astype(BF)

    def send(row, new_cell, new_hidden):
        line = row - start
        ref["cell_rows"][line] = new_cell
        owners_x, piece_y = hid_out.shape[1:3]
        local_m, piece_x = packed
        for owner in range(owners_x):
            picked = [
                new_hidden[(m * owners_x + owner) * piece_x : (m * owners_x + owner + 1) * piece_x]
                for m in range(local_m)
            ]
            hid_out[line // piece_y, owner, line % piece_y] = jnp.concatenate(picked, axis=0).astype(BF)

    def leave(first, depth):
        copy = pltpu.make_async_copy(
            ref["cell_rows"].at[pl.ds(first, depth)], cell_out.at[pl.ds(start + first, depth)],
            ref["left"].at[first // depth],
        )
        copy.start()
        leaving.append(copy)

    def stay(first, depth):
        pass

    if not packed:
        convolve(ref["spread"], start, extent, reader("", start, extent), False, keep, stay)
        return
    if tail:
        convolve(ref["late_spread"], tail, rows - tail, reader("tail_", tail, rows - tail), False, keep_late, stay)
    convolve(ref["spread"], start, extent, reader("", start, extent), True, send, leave)
    for copy in leaving:
        copy.wait()


def whole(array):
    return pl.BlockSpec(array.shape, lambda *step: (0,) * array.ndim)


def conv_step(frames, part, hid, cell, ring, weights, bias, rows_of, names, out_shapes, out_specs, packed, carry, late):
    rows, cols, width = hid.shape
    latent = weights.shape[0] // 9 - width
    start, extent = rows_of

    def rowed(size, channels, channel, row):
        return pl.BlockSpec((size, cols, channels), lambda step: (row // size, 0, channel))

    def windows(prefix, hid, cell, channel, start, extent):
        before, after = max(start - 1, 0), min(start + extent, rows - 1)
        return {
            prefix + "frame": (frames, rowed(extent, latent, channel, start)),
            prefix + "frame_prev": (frames, rowed(1, latent, channel, before)),
            prefix + "frame_next": (frames, rowed(1, latent, channel, after)),
            prefix + "hid": (hid, rowed(extent, width, 0, start)),
            prefix + "hid_prev": (hid, rowed(1, width, 0, before)),
            prefix + "hid_next": (hid, rowed(1, width, 0, after)),
            prefix + "cell": (cell, rowed(extent, width, 0, start)),
        }

    near = pl.BlockSpec(memory_space=pltpu.VMEM)
    tail = 0
    if late:
        tail, *first = late
        inputs = windows("", hid, cell, part, start, extent)
        inputs |= windows("tail_", *first, 0, tail, rows - tail)
    else:
        inputs = {"frame": (frames, near), "hid": (hid, near), "cell": (cell, near)}
    inputs["bias"] = bias, whole(bias)
    if late:
        inputs["weights"] = weights, pl.BlockSpec(memory_space=pl.ANY)
    else:
        inputs["held"] = weights, near
    inputs |= ring
    aliases = {}
    for place, array in enumerate(carry):
        if array is not None:
            aliases[len(inputs)] = place
            inputs[f"carry{place}"] = (array, pl.BlockSpec(memory_space=pl.ANY) if packed else near)
    refs = [*inputs, *names, "spread"]
    scratch = [pltpu.VMEM((extent + 2, cols, 3 * (latent + width)), BF)]
    if late:
        refs += ["held", "sem", "late_spread", "late_hid", "late_cell"]
        scratch += [
            pltpu.VMEM(weights.shape, BF),
            pltpu.SemaphoreType.DMA((LOADS,)),
            pltpu.VMEM((rows - tail + 2, cols, 3 * (latent + width)), BF),
            pltpu.VMEM((rows - tail, cols, width), BF),
            pltpu.VMEM((rows - tail, cols, width), F32),
        ]
    if packed:
        refs += ["cell_rows", "left"]
        scratch += [pltpu.VMEM((extent, cols, width), F32), pltpu.SemaphoreType.DMA((extent,))]
    cells = extent * cols
    return pl.pallas_call(
        functools.partial(conv_kernel, start, rows, part, tail, refs, packed),
        grid=(1,),
        in_specs=[spec for _, spec in inputs.values()],
        out_specs=out_specs,
        out_shape=out_shapes,
        scratch_shapes=scratch,
        input_output_aliases=aliases,
        compiler_params=pltpu.CompilerParams(vmem_limit_bytes=VMEM_ALL if late else VMEM_LIMIT),
        cost_estimate=pl.CostEstimate(
            flops=2 * cells * weights.size, bytes_accessed=2 * weights.size + cells * 2048, transcendentals=cells * width * 5
        ),
    )(*(array for array, _ in inputs.values()))


def pack_kernel(frames, hids, cells, send_low, send_high, side_low, side_high, line_top, line_bot, flat):
    rows, cols, width = hids.shape
    latent = frames.shape[2] // 2
    chans = latent + width
    places = ((0, 0, latent), (chans + width, latent, latent))
    for out, near in ((line_top, slice(0, 2)), (line_bot, slice(rows - 2, rows))):
        for to, start, size in places:
            out[:, :, to : to + size] = frames[near, :, start : start + size]
        out[:, :, latent:chans] = hids[near]
        out[:, :, chans : chans + width] = cells[near].astype(BF)
    for out, send, near, start in (
        (side_low, send_low, slice(0, 8), 0),
        (side_high, send_high, slice(cols - 8, cols), 6),
    ):
        for slab in range(out.shape[2] // LANES):
            to = slab * LANES
            if to < latent or to >= chans + width:
                begin = to if to < latent else to - 2 * width
                part = frames[:, near, begin : begin + LANES].astype(F32)
            elif to < chans:
                part = hids[:, near, to - latent : to - latent + LANES].astype(F32)
            else:
                part = cells[:, near, to - chans : to - chans + LANES]
            send[:, :, to : to + LANES] = part[:, start : start + 2].astype(BF)
            flat[...] = part.reshape(rows * 8, LANES)
            for place in range(2):
                out[place, :, to : to + LANES] = flat[pl.ds(start + place, rows, stride=8), :].astype(BF)


def pack_step(frames, hid, cell):
    rows, cols, width = hid.shape
    span = frames.shape[2]
    deep = span + 2 * width
    shapes = [jax.ShapeDtypeStruct((rows, 2, deep), BF)] * 2 + [jax.ShapeDtypeStruct((2, rows, deep), BF)] * 2
    shapes += [jax.ShapeDtypeStruct((2, cols, deep), BF)] * 2
    return pl.pallas_call(
        pack_kernel,
        grid=(1,),
        in_specs=[pl.BlockSpec(memory_space=pltpu.VMEM)] * 3,
        out_specs=[whole(shape) for shape in shapes],
        out_shape=shapes,
        scratch_shapes=[pltpu.VMEM((rows * 8, LANES), F32)],
        compiler_params=pltpu.CompilerParams(vmem_limit_bytes=VMEM_LIMIT),
        cost_estimate=pl.CostEstimate(flops=0, bytes_accessed=4_000_000, transcendentals=0),
    )(frames, hid, cell)


def ring_kernel(
    above, below, line_top, line_bot, from_left, from_right, side_left, side_right, weights, bias,
    line_hid, line_cell, strip_hid, strip_cell, beside, strips,
):
    width = line_hid.shape[2]
    chans = weights.shape[0] // 9
    cols, length = line_top.shape[1], strip_hid.shape[1]
    rows = from_left.shape[1]
    columns = (
        (from_left, 0, cols), (from_left, 1, cols + 1), (side_left, 0, 0), (side_left, 1, 1),
        (side_right, 0, cols - 2), (side_right, 1, cols - 1), (from_right, 0, cols + 2), (from_right, 1, cols + 3),
    )
    ends = [(ref[row].astype(F32), at + row) for ref, at in ((above, 0), (below, rows + 2)) for row in range(2)]
    strips[:, rows + 4 :, :] = jnp.zeros((8, length - rows - 4, strips.shape[2]), F32)
    for place, (source, at, end) in enumerate(columns):
        strips[place, 2 : rows + 2, :] = source[at].astype(F32)
        for value, spot in ends:
            strips[place, spot : spot + 1, :] = value[end : end + 1]
    beside[0] = strips[1, :, chans + width :]
    beside[1] = strips[6, :, chans + width :]
    low, high = strips[1, :, :chans], strips[6, :, :chans]

    def line(ref, row):
        held = ref[row, :cols].astype(F32)
        return held[:, :chans], held[:, chans : chans + width]

    tops = [line(above, 0), line(above, 1), line(line_top, 0), line(line_top, 1)]
    bots = [line(line_bot, 0), line(line_bot, 1), line(below, 0), line(below, 1)]
    parts, held = [], []
    for lead, lines in ((0, tops), (rows, bots)):
        pieces = []
        for row in range(4):
            at = lead + row
            pieces.append(three_columns(lines[row][0], low[at : at + 1], high[at : at + 1]))
        for row in range(2):
            parts.append(jnp.concatenate([pieces[row + tap][col] for tap in range(3) for col in range(3)], axis=1))
            held.append(lines[row + 1][1])
    for side in range(2):
        rolled = []
        for col in range(4):
            wide = strips[4 * side + col, :, :chans]
            rolled.append((pltpu.roll(wide, 1, axis=0), wide, pltpu.roll(wide, length - 1, axis=0)))
        for col in range(2):
            parts.append(
                jnp.concatenate([rolled[col + tap][row].astype(BF) for row in range(3) for tap in range(3)], axis=1)
            )
            held.append(strips[4 * side + col + 1, :, chans : chans + width])
    row_at, col_at = lax.axis_index("gy"), lax.axis_index("gx")
    upper = (row_at > 0).astype(F32)
    lower = (row_at < lax.axis_size("gy") - 1).astype(F32)
    before = (col_at > 0).astype(F32)
    after = (col_at < lax.axis_size("gx") - 1).astype(F32)
    spot = lax.broadcasted_iota(jnp.int32, (length, width), 0)
    inside = jnp.where(spot == 1, upper, jnp.where(spot == rows + 2, lower, 1.0))
    keep = [upper, 1.0, 1.0, lower, inside * before, inside, inside, inside * after]
    lhs = jnp.concatenate(parts, axis=0)
    gates = jnp.dot(lhs, weights[...], preferred_element_type=F32) + bias[...]
    start = 0
    for place in range(8):
        hid, cell = (line_hid, line_cell) if place < 4 else (strip_hid, strip_cell)
        size = hid.shape[1]
        new_cell, hidden = lstm(gates[start : start + size], held[place])
        hid[place % 4] = hidden.astype(BF).astype(F32) * keep[place]
        cell[place % 4] = new_cell
        start += size


def block_kernel(x, w_qkv, w_out, w_up, w_down, *rest):
    out, flat, back, keys_t, own_low, own_high, own_values, ones = rest[-8:]
    group = GRID * GRID
    embed = w_out.shape[0]
    tile = embed // 2

    @pl.when((pl.program_id(0) == 0) & (pl.program_id(1) == 0))
    def _():
        def fill(target, down, across, add):
            above = lax.broadcasted_iota(jnp.int32, target.shape, 0) // down
            along = lax.broadcasted_iota(jnp.int32, target.shape, 1) // across
            target[...] = (above == along + add).astype(F32).astype(BF)

        fill(own_low, HDIM, group, 0)
        fill(own_high, HDIM, group, HEADS // 4)
        fill(own_values, group, HDIM, 0)
        fill(ones, group, group, 0)
        keys_t[...] = w_qkv[:, embed : 2 * embed].astype(F32).T.astype(BF)

    def work(sub):
        flat[sub] = x[:, :, sub].astype(F32).reshape(flat.shape[1:])
        groups = flat.shape[1] // group
        cells = jnp.concatenate([flat[sub, pl.ds(g, group, stride=groups), :] for g in range(groups)], axis=0)
        normed = layer_norm(cells).astype(BF)
        yield
        queries = jnp.dot(normed, w_qkv[:, :embed], preferred_element_type=F32).astype(BF)
        values = jnp.dot(normed, w_qkv[:, 2 * embed :], preferred_element_type=F32).astype(BF)
        keys = lax.dot_general(keys_t[...], normed, (((1,), (1,)), ((), ())), preferred_element_type=F32)
        yield
        side = lax.broadcasted_iota(jnp.int32, (embed, 2 * group), 1) < group
        raised = [[], []]
        for pair in range(groups // 2):
            both = keys[:, pair * 2 * group : (pair + 1) * 2 * group]
            turned = pltpu.roll(both, group, axis=1)
            for place, twice in enumerate((jnp.where(side, both, turned), jnp.where(side, turned, both))):
                twice = twice.astype(BF)
                start = (2 * pair + place) * group
                for half in range(2):
                    part = twice[half * tile : (half + 1) * tile]
                    spread = jnp.concatenate([part * own_low[...], part * own_high[...]], axis=1)
                    scores = jnp.dot(
                        queries[start : start + group, half * tile : (half + 1) * tile],
                        spread,
                        preferred_element_type=F32,
                    )
                    raised[half].append(jnp.minimum(jnp.exp2(scores * (LOG2E * HDIM**-0.5)), BF_MAX).astype(BF))
            if pair % 2:
                yield
        attn = []
        for half in range(2):
            part = jnp.concatenate(raised[half], axis=0)
            total = jnp.dot(part, ones[...], preferred_element_type=F32)
            guess = pl.reciprocal(total, approx=True)
            attn.append((part.astype(F32) * (guess * (2.0 - total * guess))).astype(BF))
        yield
        heads = []
        for half in range(2):
            column = []
            for g in range(groups):
                held = values[g * group : (g + 1) * group, half * tile : (half + 1) * tile]
                spread = jnp.concatenate([held] * (HEADS // 2), axis=0) * own_values[...]
                column.append(
                    jnp.dot(attn[half][g * group : (g + 1) * group], spread, preferred_element_type=F32).astype(BF)
                )
            heads.append(jnp.concatenate(column, axis=0))
        heads = jnp.concatenate(heads, axis=1)
        yield
        attended = jnp.dot(heads, w_out[...], preferred_element_type=F32).astype(BF)
        mixed = cells + attended.astype(F32)
        normed_two = layer_norm(mixed).astype(BF)
        yield
        up = jnp.dot(normed_two, w_up[...], preferred_element_type=F32)
        bent = jnp.tanh(up * (0.7978845608 + (0.7978845608 * 0.044715) * (up * up)))
        half_up = 0.5 * up
        expanded = (half_up + half_up * bent).astype(BF)
        yield
        result = mixed + jnp.dot(expanded, w_down[...], preferred_element_type=F32)
        for g in range(groups):
            back[sub, pl.ds(g, group, stride=groups), :] = result[g * group : (g + 1) * group]
        out[:, :, sub] = back[sub].reshape(x.shape[:2] + x.shape[3:]).astype(BF)

    waiting = [work(sub) for sub in range(x.shape[2])]
    running = []
    while waiting or running:
        if waiting:
            running.append(waiting.pop(0))
        for one in list(running):
            if next(one, running) is running:
                running.remove(one)


def block_step(moved, carry, first, pieces, devices_y, devices_x, w_qkv, w_out, w_up, w_down):
    _, piece_y, piece_cols, width = moved.shape
    lanes = devices_y // GRID
    view = moved.reshape(GRID, lanes, devices_x, piece_y, piece_cols, width)
    tokens = GRID * devices_x * piece_cols
    subs = max(size for size in (1, 2, 4) if piece_y % size == 0 and first % size == 0)
    block = (GRID, None, devices_x, subs, piece_cols, width)
    operands = [view, w_qkv, w_out, w_up, w_down]
    in_specs = [pl.BlockSpec(block, lambda i, j: (0, i, 0, j, 0, 0)), *(whole(array) for array in operands[1:])]
    aliases = {}
    if carry is not None:
        aliases = {len(operands): 0}
        operands.append(carry)
        in_specs.append(pl.BlockSpec(memory_space=pl.ANY))
    total = lanes * piece_y * tokens
    return pl.pallas_call(
        block_kernel,
        grid=(lanes, piece_y // subs),
        in_specs=in_specs,
        out_specs=pl.BlockSpec(block, lambda i, j: (0, i, 0, first // subs + j, 0, 0)),
        out_shape=jax.ShapeDtypeStruct((GRID, lanes, devices_x, pieces, piece_cols, width), BF),
        scratch_shapes=[
            pltpu.VMEM((subs, tokens, width), F32),
            pltpu.VMEM((subs, tokens, width), F32),
            pltpu.VMEM((w_out.shape[0], width), BF),
            pltpu.VMEM((HEADS // 2 * HDIM, 2 * GRID * GRID), BF),
            pltpu.VMEM((HEADS // 2 * HDIM, 2 * GRID * GRID), BF),
            pltpu.VMEM((HEADS // 2 * GRID * GRID, HEADS // 2 * HDIM), BF),
            pltpu.VMEM((HEADS // 2 * GRID * GRID, HEADS // 2 * GRID * GRID), BF),
        ],
        input_output_aliases=aliases,
        compiler_params=pltpu.CompilerParams(vmem_limit_bytes=VMEM_LIMIT),
        cost_estimate=pl.CostEstimate(
            flops=total * 3_000_000, bytes_accessed=total * width * 4 + 800_000, transcendentals=total * 1100
        ),
    )(*operands)


def unpack_kernel(shares, local_m, piece_x, src, out):
    owners_y, owners_x = src.shape[:2]
    unit = out.shape[0]
    lines, first = [], 0
    for share in shares:
        lines += [(owner_y, first + piece) for owner_y in range(owners_y) for piece in range(share)]
        first += share
    for step in range(len(lines) // unit):

        @pl.when(pl.program_id(0) == step)
        def _():
            for row, (owner_y, piece) in enumerate(lines[step * unit : (step + 1) * unit]):
                wide = src[owner_y, :, piece].astype(F32)
                parts = [
                    wide[owner, m * piece_x : (m + 1) * piece_x] for m in range(local_m) for owner in range(owners_x)
                ]
                out[row] = jnp.concatenate(parts, axis=0).astype(BF)


def unpack_step(landed, shares, cols, local_m, piece_x):
    owners_y, _, pieces, _, width = landed.shape
    rows = owners_y * pieces
    unit = 16 if rows % 16 == 0 else rows
    return pl.pallas_call(
        functools.partial(unpack_kernel, shares, local_m, piece_x),
        grid=(rows // unit,),
        in_specs=[pl.BlockSpec(memory_space=pltpu.VMEM)],
        out_specs=pl.BlockSpec((unit, cols, width), lambda step: (step, 0, 0)),
        out_shape=jax.ShapeDtypeStruct((rows, cols, width), BF),
        compiler_params=pltpu.CompilerParams(vmem_limit_bytes=VMEM_LIMIT),
        cost_estimate=pl.CostEstimate(flops=0, bytes_accessed=rows * cols * width * 4, transcendentals=0),
    )(landed)


def step_rows(start, extent, most=16):
    return max(size for size in range(1, most + 1) if extent % size == 0 and start % size == 0)


def body(frames, hidden_state, cell_state, w_gates, gate_bias, w_qkv, w_out, w_up, w_down):
    rows, cols, width = hidden_state.shape
    latent = frames.shape[2] // 2
    chans = latent + width
    held = chans + width
    devices_y, devices_x = lax.axis_size("gy"), lax.axis_size("gx")
    local_m = GRID // devices_x
    piece_x = cols // local_m // devices_x
    weights = w_gates.reshape(-1, w_gates.shape[3])
    bias = gate_bias.reshape(1, -1)

    def shifted(value, axis, step):
        count = lax.axis_size(axis)
        pairs = [(i, i + step) for i in range(count) if 0 <= i + step < count]
        return lax.ppermute(value, axis, pairs)

    send_left, send_right, side_left, side_right, line_top, line_bot = pack_step(frames, hidden_state, cell_state)
    from_left = shifted(send_right, "gx", 1)
    from_right = shifted(send_left, "gx", -1)
    to_down = jnp.concatenate([line_bot, from_left[-2:], from_right[-2:]], axis=1)
    to_up = jnp.concatenate([line_top, from_left[:2], from_right[:2]], axis=1)

    pieces = rows // devices_y
    piece_cols = local_m * piece_x
    shares = (pieces - pieces // 3, pieces // 3)
    ahead = rows - max(size for size in range(1, 13) if rows % size == 0 and rows - size > shares[0] * devices_y)
    tile_shapes = (jax.ShapeDtypeStruct((rows, cols, width), BF), jax.ShapeDtypeStruct((rows, cols, width), F32))
    carry = ()
    half = -(-ahead // 8) * 4
    for start, extent in ((0, half), (half, ahead - half)):
        spec = pl.BlockSpec(memory_space=pltpu.VMEM)
        if carry:
            *carry, to_down, to_up = lax.optimization_barrier((*carry, to_down, to_up))
            from_up, from_down = shifted(to_down, "gy", 1), shifted(to_up, "gy", -1)
        carry = conv_step(
            frames, 0, hidden_state, cell_state, {}, weights, bias, (start, extent), ("hid_out", "cell_out"),
            tile_shapes, (spec, spec), None, carry, None,
        )
    hidden_one, cell_one = carry

    length = -(-(rows + 4) // 16) * 16
    line_shape = jax.ShapeDtypeStruct((4, cols, width), F32)
    strip_shape = jax.ShapeDtypeStruct((4, length, width), F32)
    beside_shape = jax.ShapeDtypeStruct((2, length, latent), F32)
    shapes = (line_shape, line_shape, strip_shape, strip_shape, beside_shape)
    turned = from_left.transpose(1, 0, 2), from_right.transpose(1, 0, 2)
    around = (from_up, from_down, line_top, line_bot, *turned, side_left, side_right)
    line_hid, line_cell, strip_hid, strip_cell, beside = pl.pallas_call(
        ring_kernel,
        grid=(1,),
        in_specs=[*(whole(array) for array in around), pl.BlockSpec(memory_space=pltpu.VMEM), whole(bias)],
        out_specs=[whole(shape) for shape in shapes],
        out_shape=shapes,
        scratch_shapes=[pltpu.VMEM((8, length, held + latent), F32)],
        compiler_params=pltpu.CompilerParams(vmem_limit_bytes=VMEM_LIMIT),
        cost_estimate=pl.CostEstimate(flops=16 * length * weights.size, bytes_accessed=2 * weights.size, transcendentals=0),
    )(*around, weights, bias)

    second = held // latent
    line = (1, from_up.shape[1], latent)
    ring = {name: (array, whole(array)) for name, array in (
        ("strips_hid", strip_hid), ("strips_cell", strip_cell), ("lines_hid", line_hid), ("lines_cell", line_cell),
        ("beside", beside),
    )}
    ring["frame_top"] = from_up, pl.BlockSpec(line, lambda step: (1, 0, second))
    ring["frame_bot"] = from_down, pl.BlockSpec(line, lambda step: (0, 0, second))

    moved, start, carry = [], 0, ()
    for piece_y in shares:
        extent = piece_y * devices_y
        sent_shape = jax.ShapeDtypeStruct((devices_y, devices_x, piece_y, piece_cols, width), BF)
        spec = pl.BlockSpec(memory_space=pl.ANY)
        sent, cell_out = conv_step(
            frames, 1, hidden_one, cell_one, ring, weights, bias, (start, extent),
            ("hid_out", "cell_out"), (sent_shape, tile_shapes[1]), (whole(sent_shape), spec), (local_m, piece_x), carry,
            (ahead, hidden_state, cell_state) if carry else None,
        )
        carry = (None, cell_out)
        sent = sent.reshape(devices_y * devices_x, piece_y, piece_cols, width)
        moved.append(lax.all_to_all(sent, ("gy", "gx"), split_axis=0, concat_axis=0, tiled=True))
        start += extent
    done, first = None, 0
    for piece_y, value in zip(shares, moved):
        done = block_step(value, done, first, pieces, devices_y, devices_x, w_qkv, w_out, w_up, w_down)
        first += piece_y
    done = done.reshape(devices_y * devices_x, pieces, piece_cols, width)
    landed = lax.all_to_all(done, ("gy", "gx"), split_axis=0, concat_axis=0, tiled=True)
    result = unpack_step(landed.reshape(devices_y, devices_x, *landed.shape[1:]), shares, cols, local_m, piece_x)
    return result, cell_out


def solution(mesh):
    tiled = P("gy", "gx", None)
    in_specs = (tiled, tiled, tiled, P(), P(), P(), P(), P(), P())
    return jax.shard_map(body, mesh=mesh, in_specs=in_specs, out_specs=(tiled, tiled), check_vma=False)
```

```python
import functools

import jax
import jax.numpy as jnp
from jax import lax
from jax.experimental import pallas as pl
from jax.experimental.pallas import tpu as pltpu
from jax.sharding import PartitionSpec as P

HEADS = 8
HDIM = 32
GRID = 8
BF = jnp.bfloat16
F32 = jnp.float32
LOG2E = 1.4426950408889634
BF_MAX = 3.3895313892515355e38
VMEM_LIMIT = 32 * 1024 * 1024
VMEM_ALL = 60 * 1024 * 1024
LOADS = 9
LANES = 128


def sigmoid(x):
    return 0.5 * jnp.tanh(0.5 * x) + 0.5


def lstm(gates, cell_prev):
    width = cell_prev.shape[-1]
    in_gate = sigmoid(gates[:, 0:width])
    forget_gate = sigmoid(gates[:, width : 2 * width])
    candidate = jnp.tanh(gates[:, 2 * width : 3 * width])
    out_gate = sigmoid(gates[:, 3 * width :])
    cell = forget_gate * cell_prev + in_gate * candidate
    return cell, out_gate * jnp.tanh(cell)


def layer_norm(values):
    center = values - jnp.mean(values, axis=-1, keepdims=True)
    spread = jnp.mean(center * center, axis=-1, keepdims=True)
    return center * lax.rsqrt(spread + 1e-05)


def three_columns(wide, left, right):
    count = wide.shape[0]
    place = lax.broadcasted_iota(jnp.int32, wide.shape, 0)
    before = jnp.where(place == 0, left, pltpu.roll(wide, 1, axis=0))
    after = jnp.where(place == count - 1, right, pltpu.roll(wide, count - 1, axis=0))
    return before.astype(BF), wide.astype(BF), after.astype(BF)


def conv_kernel(start, rows, part, tail, refs, packed, *args):
    ref = dict(zip(refs, args))
    hid_out, cell_out = ref["hid_out"], ref["cell_out"]
    extent = ref["spread"].shape[0] - 2
    cols, width = ref["hid"].shape[1:]
    chans = ref["spread"].shape[2] // 3
    latent = chans - width
    loads, leaving = [], []
    if "weights" in ref:
        size = ref["weights"].shape[0] // LOADS
        for place in range(LOADS):
            run = pl.ds(place * size, size)
            loads.append(pltpu.make_async_copy(ref["weights"].at[run], ref["held"].at[run], ref["sem"].at[place]))
    for load in loads:
        load.start()

    def reader(prefix, first, count):
        def row_of(name, row):
            array = ref[prefix + name]
            if array.shape[0] == rows:
                channels = slice(part * latent, (part + 1) * latent) if name == "frame" else slice(None)
                return array[row, :, channels]
            if prefix != "tail_" and tail and row >= tail and name != "frame":
                return ref["late_" + name][row - tail]
            if row == first - 1:
                return ref[prefix + name + "_prev"][0]
            if row == first + count:
                return ref[prefix + name + "_next"][0]
            return array[row - first]

        return row_of

    def convolve(spread, start, extent, row_of, ring, write, leave):
        def beside(row):
            if not ring:
                return jnp.zeros((1, chans), F32), jnp.zeros((1, chans), F32)
            at = row + 2
            return tuple(
                jnp.concatenate(
                    [ref["beside"][place, at : at + 1, :], ref["strips_hid"][3 * place, at : at + 1, :]], axis=1
                )
                for place in range(2)
            )

        def build(pos):
            row = start + pos - 1
            raw = None
            if 0 <= row < rows:
                raw = row_of("frame", row), row_of("hid", row)
                x, h = raw[0].astype(F32), raw[1].astype(F32)
            elif ring:
                x = ref["frame_top" if row < 0 else "frame_bot"][0, :cols].astype(F32)
                h = ref["lines_hid"][3 * (row > 0)]
            else:
                spread[pos] = jnp.zeros(spread.shape[1:], BF)
                return
            low, high = beside(row)
            if ring:
                at = row + 2
                place = lax.broadcasted_iota(jnp.int32, h.shape, 0)
                h = jnp.where(place == 0, ref["strips_hid"][1, at : at + 1, :], h)
                h = jnp.where(place == cols - 1, ref["strips_hid"][2, at : at + 1, :], h)
                for spot, line in ((0, 1), (rows - 1, 2)):
                    if row == spot:
                        h = ref["lines_hid"][line]
            for side, (value, first) in enumerate(((x, 0), (h, latent))):
                size = value.shape[1]
                pieces = three_columns(value, low[:, first : first + size], high[:, first : first + size])
                if raw is not None and (side == 0 or not ring):
                    pieces = pieces[0], raw[side], pieces[2]
                for tap in range(3):
                    spread[pos, :, tap * chans + first : tap * chans + first + size] = pieces[tap]

        def multiply(first, depth):
            lhs = jnp.concatenate(
                [spread[first + tap : first + tap + depth].reshape(depth * cols, 3 * chans) for tap in range(3)], axis=1
            )
            return jnp.dot(lhs, ref["held"][...], preferred_element_type=F32)

        def activate(first, depth, gates):
            for line in range(first, first + depth):
                row = start + line
                cell_prev = row_of("cell", row)
                if ring:
                    at = row + 2
                    place = lax.broadcasted_iota(jnp.int32, cell_prev.shape, 0)
                    cell_prev = jnp.where(place == 0, ref["strips_cell"][1, at : at + 1, :], cell_prev)
                    cell_prev = jnp.where(place == cols - 1, ref["strips_cell"][2, at : at + 1, :], cell_prev)
                    if row == 0:
                        cell_prev = ref["lines_cell"][1]
                    if row == rows - 1:
                        cell_prev = ref["lines_cell"][2]
                own = gates[(line - first) * cols : (line - first + 1) * cols] + ref["bias"][...]
                new_cell, new_hidden = lstm(own, cell_prev)
                write(row, new_cell, new_hidden)
            leave(first, depth)

        depth = step_rows(0, extent, 4)
        for pos in range(depth + 2):
            build(pos)
        while loads:
            loads.pop().wait()
        waiting = None
        for first in range(0, extent, depth):
            for pos in range(first + depth + 2, min(first + 2 * depth, extent) + 2):
                build(pos)
            gates = multiply(first, depth)
            if waiting:
                activate(*waiting)
            waiting = first, depth, gates
        activate(*waiting)

    def keep(row, new_cell, new_hidden):
        cell_out[row] = new_cell
        hid_out[row] = new_hidden.astype(BF)

    def keep_late(row, new_cell, new_hidden):
        ref["late_cell"][row - tail] = new_cell
        ref["late_hid"][row - tail] = new_hidden.astype(BF)

    def send(row, new_cell, new_hidden):
        line = row - start
        ref["cell_rows"][line] = new_cell
        owners_x, piece_y = hid_out.shape[1:3]
        local_m, piece_x = packed
        for owner in range(owners_x):
            picked = [
                new_hidden[(m * owners_x + owner) * piece_x : (m * owners_x + owner + 1) * piece_x]
                for m in range(local_m)
            ]
            hid_out[line // piece_y, owner, line % piece_y] = jnp.concatenate(picked, axis=0).astype(BF)

    def leave(first, depth):
        copy = pltpu.make_async_copy(
            ref["cell_rows"].at[pl.ds(first, depth)], cell_out.at[pl.ds(start + first, depth)],
            ref["left"].at[first // depth],
        )
        copy.start()
        leaving.append(copy)

    def stay(first, depth):
        pass

    if not packed:
        convolve(ref["spread"], start, extent, reader("", start, extent), False, keep, stay)
        return
    if tail:
        convolve(ref["late_spread"], tail, rows - tail, reader("tail_", tail, rows - tail), False, keep_late, stay)
    convolve(ref["spread"], start, extent, reader("", start, extent), True, send, leave)
    for copy in leaving:
        copy.wait()


def whole(array):
    return pl.BlockSpec(array.shape, lambda *step: (0,) * array.ndim)


def conv_step(frames, part, hid, cell, ring, weights, bias, rows_of, names, out_shapes, out_specs, packed, carry, late):
    rows, cols, width = hid.shape
    latent = weights.shape[0] // 9 - width
    start, extent = rows_of

    def rowed(size, channels, channel, row):
        return pl.BlockSpec((size, cols, channels), lambda step: (row // size, 0, channel))

    def windows(prefix, hid, cell, channel, start, extent):
        before, after = max(start - 1, 0), min(start + extent, rows - 1)
        return {
            prefix + "frame": (frames, rowed(extent, latent, channel, start)),
            prefix + "frame_prev": (frames, rowed(1, latent, channel, before)),
            prefix + "frame_next": (frames, rowed(1, latent, channel, after)),
            prefix + "hid": (hid, rowed(extent, width, 0, start)),
            prefix + "hid_prev": (hid, rowed(1, width, 0, before)),
            prefix + "hid_next": (hid, rowed(1, width, 0, after)),
            prefix + "cell": (cell, rowed(extent, width, 0, start)),
        }

    near = pl.BlockSpec(memory_space=pltpu.VMEM)
    tail = 0
    if late:
        tail, *first = late
        inputs = windows("", hid, cell, part, start, extent)
        inputs |= windows("tail_", *first, 0, tail, rows - tail)
    else:
        inputs = {"frame": (frames, near), "hid": (hid, near), "cell": (cell, near)}
    inputs["bias"] = bias, whole(bias)
    if late:
        inputs["weights"] = weights, pl.BlockSpec(memory_space=pl.ANY)
    else:
        inputs["held"] = weights, near
    inputs |= ring
    aliases = {}
    for place, array in enumerate(carry):
        if array is not None:
            aliases[len(inputs)] = place
            inputs[f"carry{place}"] = (array, pl.BlockSpec(memory_space=pl.ANY) if packed else near)
    refs = [*inputs, *names, "spread"]
    scratch = [pltpu.VMEM((extent + 2, cols, 3 * (latent + width)), BF)]
    if late:
        refs += ["held", "sem", "late_spread", "late_hid", "late_cell"]
        scratch += [
            pltpu.VMEM(weights.shape, BF),
            pltpu.SemaphoreType.DMA((LOADS,)),
            pltpu.VMEM((rows - tail + 2, cols, 3 * (latent + width)), BF),
            pltpu.VMEM((rows - tail, cols, width), BF),
            pltpu.VMEM((rows - tail, cols, width), F32),
        ]
    if packed:
        refs += ["cell_rows", "left"]
        scratch += [pltpu.VMEM((extent, cols, width), F32), pltpu.SemaphoreType.DMA((extent,))]
    cells = extent * cols
    return pl.pallas_call(
        functools.partial(conv_kernel, start, rows, part, tail, refs, packed),
        grid=(1,),
        in_specs=[spec for _, spec in inputs.values()],
        out_specs=out_specs,
        out_shape=out_shapes,
        scratch_shapes=scratch,
        input_output_aliases=aliases,
        compiler_params=pltpu.CompilerParams(vmem_limit_bytes=VMEM_ALL if late else VMEM_LIMIT),
        cost_estimate=pl.CostEstimate(
            flops=2 * cells * weights.size, bytes_accessed=2 * weights.size + cells * 2048, transcendentals=cells * width * 5
        ),
    )(*(array for array, _ in inputs.values()))


def pack_kernel(frames, hids, cells, send_low, send_high, side_low, side_high, line_top, line_bot, flat):
    rows, cols, width = hids.shape
    latent = frames.shape[2] // 2
    chans = latent + width
    places = ((0, 0, latent), (chans + width, latent, latent))
    for out, near in ((line_top, slice(0, 2)), (line_bot, slice(rows - 2, rows))):
        for to, start, size in places:
            out[:, :, to : to + size] = frames[near, :, start : start + size]
        out[:, :, latent:chans] = hids[near]
        out[:, :, chans : chans + width] = cells[near].astype(BF)
    for out, send, near, start in (
        (side_low, send_low, slice(0, 8), 0),
        (side_high, send_high, slice(cols - 8, cols), 6),
    ):
        for slab in range(out.shape[2] // LANES):
            to = slab * LANES
            if to < latent or to >= chans + width:
                begin = to if to < latent else to - 2 * width
                part = frames[:, near, begin : begin + LANES].astype(F32)
            elif to < chans:
                part = hids[:, near, to - latent : to - latent + LANES].astype(F32)
            else:
                part = cells[:, near, to - chans : to - chans + LANES]
            send[:, :, to : to + LANES] = part[:, start : start + 2].astype(BF)
            flat[...] = part.reshape(rows * 8, LANES)
            for place in range(2):
                out[place, :, to : to + LANES] = flat[pl.ds(start + place, rows, stride=8), :].astype(BF)


def pack_step(frames, hid, cell):
    rows, cols, width = hid.shape
    span = frames.shape[2]
    deep = span + 2 * width
    shapes = [jax.ShapeDtypeStruct((rows, 2, deep), BF)] * 2 + [jax.ShapeDtypeStruct((2, rows, deep), BF)] * 2
    shapes += [jax.ShapeDtypeStruct((2, cols, deep), BF)] * 2
    return pl.pallas_call(
        pack_kernel,
        grid=(1,),
        in_specs=[pl.BlockSpec(memory_space=pltpu.VMEM)] * 3,
        out_specs=[whole(shape) for shape in shapes],
        out_shape=shapes,
        scratch_shapes=[pltpu.VMEM((rows * 8, LANES), F32)],
        compiler_params=pltpu.CompilerParams(vmem_limit_bytes=VMEM_LIMIT),
        cost_estimate=pl.CostEstimate(flops=0, bytes_accessed=4_000_000, transcendentals=0),
    )(frames, hid, cell)


def ring_kernel(
    above, below, line_top, line_bot, from_left, from_right, side_left, side_right, weights, bias,
    line_hid, line_cell, strip_hid, strip_cell, beside, strips,
):
    width = line_hid.shape[2]
    chans = weights.shape[0] // 9
    cols, length = line_top.shape[1], strip_hid.shape[1]
    rows = from_left.shape[1]
    columns = (
        (from_left, 0, cols), (from_left, 1, cols + 1), (side_left, 0, 0), (side_left, 1, 1),
        (side_right, 0, cols - 2), (side_right, 1, cols - 1), (from_right, 0, cols + 2), (from_right, 1, cols + 3),
    )
    ends = [(ref[row].astype(F32), at + row) for ref, at in ((above, 0), (below, rows + 2)) for row in range(2)]
    strips[:, rows + 4 :, :] = jnp.zeros((8, length - rows - 4, strips.shape[2]), F32)
    for place, (source, at, end) in enumerate(columns):
        strips[place, 2 : rows + 2, :] = source[at].astype(F32)
        for value, spot in ends:
            strips[place, spot : spot + 1, :] = value[end : end + 1]
    beside[0] = strips[1, :, chans + width :]
    beside[1] = strips[6, :, chans + width :]
    low, high = strips[1, :, :chans], strips[6, :, :chans]

    def line(ref, row):
        held = ref[row, :cols].astype(F32)
        return held[:, :chans], held[:, chans : chans + width]

    tops = [line(above, 0), line(above, 1), line(line_top, 0), line(line_top, 1)]
    bots = [line(line_bot, 0), line(line_bot, 1), line(below, 0), line(below, 1)]
    parts, held = [], []
    for lead, lines in ((0, tops), (rows, bots)):
        pieces = []
        for row in range(4):
            at = lead + row
            pieces.append(three_columns(lines[row][0], low[at : at + 1], high[at : at + 1]))
        for row in range(2):
            parts.append(jnp.concatenate([pieces[row + tap][col] for tap in range(3) for col in range(3)], axis=1))
            held.append(lines[row + 1][1])
    for side in range(2):
        rolled = []
        for col in range(4):
            wide = strips[4 * side + col, :, :chans]
            rolled.append((pltpu.roll(wide, 1, axis=0), wide, pltpu.roll(wide, length - 1, axis=0)))
        for col in range(2):
            parts.append(
                jnp.concatenate([rolled[col + tap][row].astype(BF) for row in range(3) for tap in range(3)], axis=1)
            )
            held.append(strips[4 * side + col + 1, :, chans : chans + width])
    row_at, col_at = lax.axis_index("gy"), lax.axis_index("gx")
    upper = (row_at > 0).astype(F32)
    lower = (row_at < lax.axis_size("gy") - 1).astype(F32)
    before = (col_at > 0).astype(F32)
    after = (col_at < lax.axis_size("gx") - 1).astype(F32)
    spot = lax.broadcasted_iota(jnp.int32, (length, width), 0)
    inside = jnp.where(spot == 1, upper, jnp.where(spot == rows + 2, lower, 1.0))
    keep = [upper, 1.0, 1.0, lower, inside * before, inside, inside, inside * after]
    lhs = jnp.concatenate(parts, axis=0)
    gates = jnp.dot(lhs, weights[...], preferred_element_type=F32) + bias[...]
    start = 0
    for place in range(8):
        hid, cell = (line_hid, line_cell) if place < 4 else (strip_hid, strip_cell)
        size = hid.shape[1]
        new_cell, hidden = lstm(gates[start : start + size], held[place])
        hid[place % 4] = hidden.astype(BF).astype(F32) * keep[place]
        cell[place % 4] = new_cell
        start += size


def block_kernel(x, w_qkv, w_out, w_up, w_down, *rest):
    out, flat, back, keys_t, own_low, own_high, own_values, ones = rest[-8:]
    group = GRID * GRID
    embed = w_out.shape[0]
    tile = embed // 2

    @pl.when((pl.program_id(0) == 0) & (pl.program_id(1) == 0))
    def _():
        def fill(target, down, across, add):
            above = lax.broadcasted_iota(jnp.int32, target.shape, 0) // down
            along = lax.broadcasted_iota(jnp.int32, target.shape, 1) // across
            target[...] = (above == along + add).astype(F32).astype(BF)

        fill(own_low, HDIM, group, 0)
        fill(own_high, HDIM, group, HEADS // 4)
        fill(own_values, group, HDIM, 0)
        fill(ones, group, group, 0)
        keys_t[...] = w_qkv[:, embed : 2 * embed].astype(F32).T.astype(BF)

    def work(sub):
        flat[sub] = x[:, :, sub].astype(F32).reshape(flat.shape[1:])
        groups = flat.shape[1] // group
        cells = jnp.concatenate([flat[sub, pl.ds(g, group, stride=groups), :] for g in range(groups)], axis=0)
        normed = layer_norm(cells).astype(BF)
        yield
        queries = jnp.dot(normed, w_qkv[:, :embed], preferred_element_type=F32).astype(BF)
        yield
        values = jnp.dot(normed, w_qkv[:, 2 * embed :], preferred_element_type=F32).astype(BF)
        keys = lax.dot_general(keys_t[...], normed, (((1,), (1,)), ((), ())), preferred_element_type=F32)
        yield
        side = lax.broadcasted_iota(jnp.int32, (embed, 2 * group), 1) < group
        raised = [[], []]
        for pair in range(groups // 2):
            both = keys[:, pair * 2 * group : (pair + 1) * 2 * group]
            turned = pltpu.roll(both, group, axis=1)
            for place, twice in enumerate((jnp.where(side, both, turned), jnp.where(side, turned, both))):
                twice = twice.astype(BF)
                start = (2 * pair + place) * group
                for half in range(2):
                    part = twice[half * tile : (half + 1) * tile]
                    spread = jnp.concatenate([part * own_low[...], part * own_high[...]], axis=1)
                    scores = jnp.dot(
                        queries[start : start + group, half * tile : (half + 1) * tile],
                        spread,
                        preferred_element_type=F32,
                    )
                    raised[half].append(jnp.minimum(jnp.exp2(scores * (LOG2E * HDIM**-0.5)), BF_MAX).astype(BF))
            yield
        attn = []
        for half in range(2):
            part = jnp.concatenate(raised[half], axis=0)
            total = jnp.dot(part, ones[...], preferred_element_type=F32)
            guess = pl.reciprocal(total, approx=True)
            attn.append((part.astype(F32) * (guess * (2.0 - total * guess))).astype(BF))
            yield
        heads = []
        for half in range(2):
            column = []
            for g in range(groups):
                held = values[g * group : (g + 1) * group, half * tile : (half + 1) * tile]
                spread = jnp.concatenate([held] * (HEADS // 2), axis=0) * own_values[...]
                column.append(
                    jnp.dot(attn[half][g * group : (g + 1) * group], spread, preferred_element_type=F32).astype(BF)
                )
            heads.append(jnp.concatenate(column, axis=0))
            yield
        heads = jnp.concatenate(heads, axis=1)
        attended = jnp.dot(heads, w_out[...], preferred_element_type=F32).astype(BF)
        mixed = cells + attended.astype(F32)
        yield
        normed_two = layer_norm(mixed).astype(BF)
        yield
        up = jnp.dot(normed_two, w_up[...], preferred_element_type=F32)
        bent = jnp.tanh(up * (0.7978845608 + (0.7978845608 * 0.044715) * (up * up)))
        half_up = 0.5 * up
        expanded = (half_up + half_up * bent).astype(BF)
        yield
        result = mixed + jnp.dot(expanded, w_down[...], preferred_element_type=F32)
        for g in range(groups):
            back[sub, pl.ds(g, group, stride=groups), :] = result[g * group : (g + 1) * group]
        out[:, :, sub] = back[sub].reshape(x.shape[:2] + x.shape[3:]).astype(BF)

    waiting = [work(sub) for sub in range(x.shape[2])]
    running = []
    while waiting or running:
        if waiting:
            running.append(waiting.pop(0))
        for one in list(running):
            if next(one, running) is running:
                running.remove(one)


def block_step(moved, carry, first, pieces, devices_y, devices_x, w_qkv, w_out, w_up, w_down):
    _, piece_y, piece_cols, width = moved.shape
    lanes = devices_y // GRID
    view = moved.reshape(GRID, lanes, devices_x, piece_y, piece_cols, width)
    tokens = GRID * devices_x * piece_cols
    subs = max(size for size in (1, 2, 4) if piece_y % size == 0 and first % size == 0)
    block = (GRID, None, devices_x, subs, piece_cols, width)
    operands = [view, w_qkv, w_out, w_up, w_down]
    in_specs = [pl.BlockSpec(block, lambda i, j: (0, i, 0, j, 0, 0)), *(whole(array) for array in operands[1:])]
    aliases = {}
    if carry is not None:
        aliases = {len(operands): 0}
        operands.append(carry)
        in_specs.append(pl.BlockSpec(memory_space=pl.ANY))
    total = lanes * piece_y * tokens
    return pl.pallas_call(
        block_kernel,
        grid=(lanes, piece_y // subs),
        in_specs=in_specs,
        out_specs=pl.BlockSpec(block, lambda i, j: (0, i, 0, first // subs + j, 0, 0)),
        out_shape=jax.ShapeDtypeStruct((GRID, lanes, devices_x, pieces, piece_cols, width), BF),
        scratch_shapes=[
            pltpu.VMEM((subs, tokens, width), F32),
            pltpu.VMEM((subs, tokens, width), F32),
            pltpu.VMEM((w_out.shape[0], width), BF),
            pltpu.VMEM((HEADS // 2 * HDIM, 2 * GRID * GRID), BF),
            pltpu.VMEM((HEADS // 2 * HDIM, 2 * GRID * GRID), BF),
            pltpu.VMEM((HEADS // 2 * GRID * GRID, HEADS // 2 * HDIM), BF),
            pltpu.VMEM((HEADS // 2 * GRID * GRID, HEADS // 2 * GRID * GRID), BF),
        ],
        input_output_aliases=aliases,
        compiler_params=pltpu.CompilerParams(vmem_limit_bytes=VMEM_LIMIT),
        cost_estimate=pl.CostEstimate(
            flops=total * 3_000_000, bytes_accessed=total * width * 4 + 800_000, transcendentals=total * 1100
        ),
    )(*operands)


def unpack_kernel(shares, local_m, piece_x, src, out):
    owners_y, owners_x = src.shape[:2]
    unit = out.shape[0]
    lines, first = [], 0
    for share in shares:
        lines += [(owner_y, first + piece) for owner_y in range(owners_y) for piece in range(share)]
        first += share
    for step in range(len(lines) // unit):

        @pl.when(pl.program_id(0) == step)
        def _():
            for row, (owner_y, piece) in enumerate(lines[step * unit : (step + 1) * unit]):
                wide = src[owner_y, :, piece].astype(F32)
                parts = [
                    wide[owner, m * piece_x : (m + 1) * piece_x] for m in range(local_m) for owner in range(owners_x)
                ]
                out[row] = jnp.concatenate(parts, axis=0).astype(BF)


def unpack_step(landed, shares, cols, local_m, piece_x):
    owners_y, _, pieces, _, width = landed.shape
    rows = owners_y * pieces
    unit = 16 if rows % 16 == 0 else rows
    return pl.pallas_call(
        functools.partial(unpack_kernel, shares, local_m, piece_x),
        grid=(rows // unit,),
        in_specs=[pl.BlockSpec(memory_space=pltpu.VMEM)],
        out_specs=pl.BlockSpec((unit, cols, width), lambda step: (step, 0, 0)),
        out_shape=jax.ShapeDtypeStruct((rows, cols, width), BF),
        compiler_params=pltpu.CompilerParams(vmem_limit_bytes=VMEM_LIMIT),
        cost_estimate=pl.CostEstimate(flops=0, bytes_accessed=rows * cols * width * 4, transcendentals=0),
    )(landed)


def step_rows(start, extent, most=16):
    return max(size for size in range(1, most + 1) if extent % size == 0 and start % size == 0)


def body(frames, hidden_state, cell_state, w_gates, gate_bias, w_qkv, w_out, w_up, w_down):
    rows, cols, width = hidden_state.shape
    latent = frames.shape[2] // 2
    chans = latent + width
    held = chans + width
    devices_y, devices_x = lax.axis_size("gy"), lax.axis_size("gx")
    local_m = GRID // devices_x
    piece_x = cols // local_m // devices_x
    weights = w_gates.reshape(-1, w_gates.shape[3])
    bias = gate_bias.reshape(1, -1)

    def shifted(value, axis, step):
        count = lax.axis_size(axis)
        pairs = [(i, i + step) for i in range(count) if 0 <= i + step < count]
        return lax.ppermute(value, axis, pairs)

    send_left, send_right, side_left, side_right, line_top, line_bot = pack_step(frames, hidden_state, cell_state)
    from_left = shifted(send_right, "gx", 1)
    from_right = shifted(send_left, "gx", -1)
    to_down = jnp.concatenate([line_bot, from_left[-2:], from_right[-2:]], axis=1)
    to_up = jnp.concatenate([line_top, from_left[:2], from_right[:2]], axis=1)

    pieces = rows // devices_y
    piece_cols = local_m * piece_x
    shares = (pieces - pieces // 3, pieces // 3)
    ahead = rows - max(size for size in range(1, 13) if rows % size == 0 and rows - size > shares[0] * devices_y)
    tile_shapes = (jax.ShapeDtypeStruct((rows, cols, width), BF), jax.ShapeDtypeStruct((rows, cols, width), F32))
    carry = ()
    half = -(-ahead // 8) * 4
    for start, extent in ((0, half), (half, ahead - half)):
        spec = pl.BlockSpec(memory_space=pltpu.VMEM)
        if carry:
            *carry, to_down, to_up = lax.optimization_barrier((*carry, to_down, to_up))
            from_up, from_down = shifted(to_down, "gy", 1), shifted(to_up, "gy", -1)
        carry = conv_step(
            frames, 0, hidden_state, cell_state, {}, weights, bias, (start, extent), ("hid_out", "cell_out"),
            tile_shapes, (spec, spec), None, carry, None,
        )
    hidden_one, cell_one = carry

    length = -(-(rows + 4) // 16) * 16
    line_shape = jax.ShapeDtypeStruct((4, cols, width), F32)
    strip_shape = jax.ShapeDtypeStruct((4, length, width), F32)
    beside_shape = jax.ShapeDtypeStruct((2, length, latent), F32)
    shapes = (line_shape, line_shape, strip_shape, strip_shape, beside_shape)
    turned = from_left.transpose(1, 0, 2), from_right.transpose(1, 0, 2)
    around = (from_up, from_down, line_top, line_bot, *turned, side_left, side_right)
    line_hid, line_cell, strip_hid, strip_cell, beside = pl.pallas_call(
        ring_kernel,
        grid=(1,),
        in_specs=[*(whole(array) for array in around), pl.BlockSpec(memory_space=pltpu.VMEM), whole(bias)],
        out_specs=[whole(shape) for shape in shapes],
        out_shape=shapes,
        scratch_shapes=[pltpu.VMEM((8, length, held + latent), F32)],
        compiler_params=pltpu.CompilerParams(vmem_limit_bytes=VMEM_LIMIT),
        cost_estimate=pl.CostEstimate(flops=16 * length * weights.size, bytes_accessed=2 * weights.size, transcendentals=0),
    )(*around, weights, bias)

    second = held // latent
    line = (1, from_up.shape[1], latent)
    ring = {name: (array, whole(array)) for name, array in (
        ("strips_hid", strip_hid), ("strips_cell", strip_cell), ("lines_hid", line_hid), ("lines_cell", line_cell),
        ("beside", beside),
    )}
    ring["frame_top"] = from_up, pl.BlockSpec(line, lambda step: (1, 0, second))
    ring["frame_bot"] = from_down, pl.BlockSpec(line, lambda step: (0, 0, second))

    moved, start, carry = [], 0, ()
    for piece_y in shares:
        extent = piece_y * devices_y
        sent_shape = jax.ShapeDtypeStruct((devices_y, devices_x, piece_y, piece_cols, width), BF)
        spec = pl.BlockSpec(memory_space=pl.ANY)
        sent, cell_out = conv_step(
            frames, 1, hidden_one, cell_one, ring, weights, bias, (start, extent),
            ("hid_out", "cell_out"), (sent_shape, tile_shapes[1]), (whole(sent_shape), spec), (local_m, piece_x), carry,
            (ahead, hidden_state, cell_state) if carry else None,
        )
        carry = (None, cell_out)
        sent = sent.reshape(devices_y * devices_x, piece_y, piece_cols, width)
        moved.append(lax.all_to_all(sent, ("gy", "gx"), split_axis=0, concat_axis=0, tiled=True))
        start += extent
    done, first = None, 0
    for piece_y, value in zip(shares, moved):
        done = block_step(value, done, first, pieces, devices_y, devices_x, w_qkv, w_out, w_up, w_down)
        first += piece_y
    done = done.reshape(devices_y * devices_x, pieces, piece_cols, width)
    landed = lax.all_to_all(done, ("gy", "gx"), split_axis=0, concat_axis=0, tiled=True)
    result = unpack_step(landed.reshape(devices_y, devices_x, *landed.shape[1:]), shares, cols, local_m, piece_x)
    return result, cell_out


def solution(mesh):
    tiled = P("gy", "gx", None)
    in_specs = (tiled, tiled, tiled, P(), P(), P(), P(), P(), P())
    return jax.shard_map(body, mesh=mesh, in_specs=in_specs, out_specs=(tiled, tiled), check_vma=False)
```

```python
import functools

import jax
import jax.numpy as jnp
from jax import lax
from jax.experimental import pallas as pl
from jax.experimental.pallas import tpu as pltpu
from jax.sharding import PartitionSpec as P

HEADS = 8
HDIM = 32
GRID = 8
BF = jnp.bfloat16
F32 = jnp.float32
LOG2E = 1.4426950408889634
BF_MAX = 3.3895313892515355e38
VMEM_LIMIT = 32 * 1024 * 1024
VMEM_ALL = 60 * 1024 * 1024
LOADS = 9
LANES = 128


def sigmoid(x):
    return 0.5 * jnp.tanh(0.5 * x) + 0.5


def lstm(gates, cell_prev):
    width = cell_prev.shape[-1]
    in_gate = sigmoid(gates[:, 0:width])
    forget_gate = sigmoid(gates[:, width : 2 * width])
    candidate = jnp.tanh(gates[:, 2 * width : 3 * width])
    out_gate = sigmoid(gates[:, 3 * width :])
    cell = forget_gate * cell_prev + in_gate * candidate
    return cell, out_gate * jnp.tanh(cell)


def layer_norm(values):
    center = values - jnp.mean(values, axis=-1, keepdims=True)
    spread = jnp.mean(center * center, axis=-1, keepdims=True)
    return center * lax.rsqrt(spread + 1e-05)


def three_columns(wide, left, right):
    count = wide.shape[0]
    place = lax.broadcasted_iota(jnp.int32, wide.shape, 0)
    before = jnp.where(place == 0, left, pltpu.roll(wide, 1, axis=0))
    after = jnp.where(place == count - 1, right, pltpu.roll(wide, count - 1, axis=0))
    return before.astype(BF), wide.astype(BF), after.astype(BF)


def conv_kernel(start, rows, part, tail, refs, packed, *args):
    ref = dict(zip(refs, args))
    hid_out, cell_out = ref["hid_out"], ref["cell_out"]
    extent = ref["spread"].shape[0] - 2
    cols, width = ref["hid"].shape[1:]
    chans = ref["spread"].shape[2] // 3
    latent = chans - width
    loads, leaving = [], []
    if "weights" in ref:
        size = ref["weights"].shape[0] // LOADS
        for place in range(LOADS):
            run = pl.ds(place * size, size)
            loads.append(pltpu.make_async_copy(ref["weights"].at[run], ref["held"].at[run], ref["sem"].at[place]))
    for load in loads:
        load.start()

    def reader(prefix, first, count):
        def row_of(name, row):
            array = ref[prefix + name]
            if array.shape[0] == rows:
                channels = slice(part * latent, (part + 1) * latent) if name == "frame" else slice(None)
                return array[row, :, channels]
            if prefix != "tail_" and tail and row >= tail and name != "frame":
                return ref["late_" + name][row - tail]
            if row == first - 1:
                return ref[prefix + name + "_prev"][0]
            if row == first + count:
                return ref[prefix + name + "_next"][0]
            return array[row - first]

        return row_of

    def convolve(spread, start, extent, row_of, ring, write, leave):
        def beside(row):
            if not ring:
                return jnp.zeros((1, chans), F32), jnp.zeros((1, chans), F32)
            at = row + 2
            return tuple(
                jnp.concatenate(
                    [ref["beside"][place, at : at + 1, :], ref["strips_hid"][3 * place, at : at + 1, :]], axis=1
                )
                for place in range(2)
            )

        def build(pos):
            row = start + pos - 1
            raw = None
            if 0 <= row < rows:
                raw = row_of("frame", row), row_of("hid", row)
                x, h = raw[0].astype(F32), raw[1].astype(F32)
            elif ring:
                x = ref["frame_top" if row < 0 else "frame_bot"][0, :cols].astype(F32)
                h = ref["lines_hid"][3 * (row > 0)]
            else:
                spread[pos] = jnp.zeros(spread.shape[1:], BF)
                return
            low, high = beside(row)
            if ring:
                at = row + 2
                place = lax.broadcasted_iota(jnp.int32, h.shape, 0)
                h = jnp.where(place == 0, ref["strips_hid"][1, at : at + 1, :], h)
                h = jnp.where(place == cols - 1, ref["strips_hid"][2, at : at + 1, :], h)
                for spot, line in ((0, 1), (rows - 1, 2)):
                    if row == spot:
                        h = ref["lines_hid"][line]
            for side, (value, first) in enumerate(((x, 0), (h, latent))):
                size = value.shape[1]
                pieces = three_columns(value, low[:, first : first + size], high[:, first : first + size])
                if raw is not None and (side == 0 or not ring):
                    pieces = pieces[0], raw[side], pieces[2]
                for tap in range(3):
                    spread[pos, :, tap * chans + first : tap * chans + first + size] = pieces[tap]

        def multiply(first, depth):
            lhs = jnp.concatenate(
                [spread[first + tap : first + tap + depth].reshape(depth * cols, 3 * chans) for tap in range(3)], axis=1
            )
            return jnp.dot(lhs, ref["held"][...], preferred_element_type=F32)

        def activate(first, depth, gates):
            for line in range(first, first + depth):
                row = start + line
                cell_prev = row_of("cell", row)
                if ring:
                    at = row + 2
                    place = lax.broadcasted_iota(jnp.int32, cell_prev.shape, 0)
                    cell_prev = jnp.where(place == 0, ref["strips_cell"][1, at : at + 1, :], cell_prev)
                    cell_prev = jnp.where(place == cols - 1, ref["strips_cell"][2, at : at + 1, :], cell_prev)
                    if row == 0:
                        cell_prev = ref["lines_cell"][1]
                    if row == rows - 1:
                        cell_prev = ref["lines_cell"][2]
                own = gates[(line - first) * cols : (line - first + 1) * cols] + ref["bias"][...]
                new_cell, new_hidden = lstm(own, cell_prev)
                write(row, new_cell, new_hidden)
            leave(first, depth)

        depth = step_rows(0, extent, 4)
        for pos in range(depth + 2):
            build(pos)
        while loads:
            loads.pop().wait()
        waiting = None
        for first in range(0, extent, depth):
            for pos in range(first + depth + 2, min(first + 2 * depth, extent) + 2):
                build(pos)
            gates = multiply(first, depth)
            if waiting:
                activate(*waiting)
            waiting = first, depth, gates
        activate(*waiting)

    def keep(row, new_cell, new_hidden):
        cell_out[row] = new_cell
        hid_out[row] = new_hidden.astype(BF)

    def keep_late(row, new_cell, new_hidden):
        ref["late_cell"][row - tail] = new_cell
        ref["late_hid"][row - tail] = new_hidden.astype(BF)

    def send(row, new_cell, new_hidden):
        line = row - start
        ref["cell_rows"][line] = new_cell
        owners_x, piece_y = hid_out.shape[1:3]
        local_m, piece_x = packed
        for owner in range(owners_x):
            picked = [
                new_hidden[(m * owners_x + owner) * piece_x : (m * owners_x + owner + 1) * piece_x]
                for m in range(local_m)
            ]
            hid_out[line // piece_y, owner, line % piece_y] = jnp.concatenate(picked, axis=0).astype(BF)

    def leave(first, depth):
        copy = pltpu.make_async_copy(
            ref["cell_rows"].at[pl.ds(first, depth)], cell_out.at[pl.ds(start + first, depth)],
            ref["left"].at[first // depth],
        )
        copy.start()
        leaving.append(copy)

    def stay(first, depth):
        pass

    if not packed:
        convolve(ref["spread"], start, extent, reader("", start, extent), False, keep, stay)
        return
    if tail:
        convolve(ref["late_spread"], tail, rows - tail, reader("tail_", tail, rows - tail), False, keep_late, stay)
    convolve(ref["spread"], start, extent, reader("", start, extent), True, send, leave)
    for copy in leaving:
        copy.wait()


def whole(array):
    return pl.BlockSpec(array.shape, lambda *step: (0,) * array.ndim)


def conv_step(frames, part, hid, cell, ring, weights, bias, rows_of, names, out_shapes, out_specs, packed, carry, late):
    rows, cols, width = hid.shape
    latent = weights.shape[0] // 9 - width
    start, extent = rows_of

    def rowed(size, channels, channel, row):
        return pl.BlockSpec((size, cols, channels), lambda step: (row // size, 0, channel))

    def windows(prefix, hid, cell, channel, start, extent):
        before, after = max(start - 1, 0), min(start + extent, rows - 1)
        return {
            prefix + "frame": (frames, rowed(extent, latent, channel, start)),
            prefix + "frame_prev": (frames, rowed(1, latent, channel, before)),
            prefix + "frame_next": (frames, rowed(1, latent, channel, after)),
            prefix + "hid": (hid, rowed(extent, width, 0, start)),
            prefix + "hid_prev": (hid, rowed(1, width, 0, before)),
            prefix + "hid_next": (hid, rowed(1, width, 0, after)),
            prefix + "cell": (cell, rowed(extent, width, 0, start)),
        }

    near = pl.BlockSpec(memory_space=pltpu.VMEM)
    tail = 0
    if late:
        tail, *first = late
        inputs = windows("", hid, cell, part, start, extent)
        inputs |= windows("tail_", *first, 0, tail, rows - tail)
    else:
        inputs = {"frame": (frames, near), "hid": (hid, near), "cell": (cell, near)}
    inputs["bias"] = bias, whole(bias)
    if late:
        inputs["weights"] = weights, pl.BlockSpec(memory_space=pl.ANY)
    else:
        inputs["held"] = weights, near
    inputs |= ring
    aliases = {}
    for place, array in enumerate(carry):
        if array is not None:
            aliases[len(inputs)] = place
            inputs[f"carry{place}"] = (array, pl.BlockSpec(memory_space=pl.ANY) if packed else near)
    refs = [*inputs, *names, "spread"]
    scratch = [pltpu.VMEM((extent + 2, cols, 3 * (latent + width)), BF)]
    if late:
        refs += ["held", "sem", "late_spread", "late_hid", "late_cell"]
        scratch += [
            pltpu.VMEM(weights.shape, BF),
            pltpu.SemaphoreType.DMA((LOADS,)),
            pltpu.VMEM((rows - tail + 2, cols, 3 * (latent + width)), BF),
            pltpu.VMEM((rows - tail, cols, width), BF),
            pltpu.VMEM((rows - tail, cols, width), F32),
        ]
    if packed:
        refs += ["cell_rows", "left"]
        scratch += [pltpu.VMEM((extent, cols, width), F32), pltpu.SemaphoreType.DMA((extent,))]
    cells = extent * cols
    return pl.pallas_call(
        functools.partial(conv_kernel, start, rows, part, tail, refs, packed),
        grid=(1,),
        in_specs=[spec for _, spec in inputs.values()],
        out_specs=out_specs,
        out_shape=out_shapes,
        scratch_shapes=scratch,
        input_output_aliases=aliases,
        compiler_params=pltpu.CompilerParams(vmem_limit_bytes=VMEM_ALL if late else VMEM_LIMIT),
        cost_estimate=pl.CostEstimate(
            flops=2 * cells * weights.size, bytes_accessed=2 * weights.size + cells * 2048, transcendentals=cells * width * 5
        ),
    )(*(array for array, _ in inputs.values()))


def pack_kernel(frames, hids, cells, send_low, send_high, side_low, side_high, line_top, line_bot, flat):
    rows, cols, width = hids.shape
    latent = frames.shape[2] // 2
    chans = latent + width
    places = ((0, 0, latent), (chans + width, latent, latent))
    for out, near in ((line_top, slice(0, 2)), (line_bot, slice(rows - 2, rows))):
        for to, start, size in places:
            out[:, :, to : to + size] = frames[near, :, start : start + size]
        out[:, :, latent:chans] = hids[near]
        out[:, :, chans : chans + width] = cells[near].astype(BF)
    for out, send, near, start in (
        (side_low, send_low, slice(0, 8), 0),
        (side_high, send_high, slice(cols - 8, cols), 6),
    ):
        for slab in range(out.shape[2] // LANES):
            to = slab * LANES
            if to < latent or to >= chans + width:
                begin = to if to < latent else to - 2 * width
                part = frames[:, near, begin : begin + LANES].astype(F32)
            elif to < chans:
                part = hids[:, near, to - latent : to - latent + LANES].astype(F32)
            else:
                part = cells[:, near, to - chans : to - chans + LANES]
            send[:, :, to : to + LANES] = part[:, start : start + 2].astype(BF)
            flat[...] = part.reshape(rows * 8, LANES)
            for place in range(2):
                out[place, :, to : to + LANES] = flat[pl.ds(start + place, rows, stride=8), :].astype(BF)


def pack_step(frames, hid, cell):
    rows, cols, width = hid.shape
    span = frames.shape[2]
    deep = span + 2 * width
    shapes = [jax.ShapeDtypeStruct((rows, 2, deep), BF)] * 2 + [jax.ShapeDtypeStruct((2, rows, deep), BF)] * 2
    shapes += [jax.ShapeDtypeStruct((2, cols, deep), BF)] * 2
    return pl.pallas_call(
        pack_kernel,
        grid=(1,),
        in_specs=[pl.BlockSpec(memory_space=pltpu.VMEM)] * 3,
        out_specs=[whole(shape) for shape in shapes],
        out_shape=shapes,
        scratch_shapes=[pltpu.VMEM((rows * 8, LANES), F32)],
        compiler_params=pltpu.CompilerParams(vmem_limit_bytes=VMEM_LIMIT),
        cost_estimate=pl.CostEstimate(flops=0, bytes_accessed=4_000_000, transcendentals=0),
    )(frames, hid, cell)


def ring_kernel(
    above, below, line_top, line_bot, from_left, from_right, side_left, side_right, weights, bias,
    line_hid, line_cell, strip_hid, strip_cell, beside, strips,
):
    width = line_hid.shape[2]
    chans = weights.shape[0] // 9
    cols, length = line_top.shape[1], strip_hid.shape[1]
    rows = from_left.shape[1]
    columns = (
        (from_left, 0, cols), (from_left, 1, cols + 1), (side_left, 0, 0), (side_left, 1, 1),
        (side_right, 0, cols - 2), (side_right, 1, cols - 1), (from_right, 0, cols + 2), (from_right, 1, cols + 3),
    )
    ends = [(ref[row].astype(F32), at + row) for ref, at in ((above, 0), (below, rows + 2)) for row in range(2)]
    strips[:, rows + 4 :, :] = jnp.zeros((8, length - rows - 4, strips.shape[2]), F32)
    for place, (source, at, end) in enumerate(columns):
        strips[place, 2 : rows + 2, :] = source[at].astype(F32)
        for value, spot in ends:
            strips[place, spot : spot + 1, :] = value[end : end + 1]
    beside[0] = strips[1, :, chans + width :]
    beside[1] = strips[6, :, chans + width :]
    low, high = strips[1, :, :chans], strips[6, :, :chans]

    def line(ref, row):
        held = ref[row, :cols].astype(F32)
        return held[:, :chans], held[:, chans : chans + width]

    tops = [line(above, 0), line(above, 1), line(line_top, 0), line(line_top, 1)]
    bots = [line(line_bot, 0), line(line_bot, 1), line(below, 0), line(below, 1)]
    parts, held = [], []
    for lead, lines in ((0, tops), (rows, bots)):
        pieces = []
        for row in range(4):
            at = lead + row
            pieces.append(three_columns(lines[row][0], low[at : at + 1], high[at : at + 1]))
        for row in range(2):
            parts.append(jnp.concatenate([pieces[row + tap][col] for tap in range(3) for col in range(3)], axis=1))
            held.append(lines[row + 1][1])
    for side in range(2):
        rolled = []
        for col in range(4):
            wide = strips[4 * side + col, :, :chans]
            rolled.append((pltpu.roll(wide, 1, axis=0), wide, pltpu.roll(wide, length - 1, axis=0)))
        for col in range(2):
            parts.append(
                jnp.concatenate([rolled[col + tap][row].astype(BF) for row in range(3) for tap in range(3)], axis=1)
            )
            held.append(strips[4 * side + col + 1, :, chans : chans + width])
    row_at, col_at = lax.axis_index("gy"), lax.axis_index("gx")
    upper = (row_at > 0).astype(F32)
    lower = (row_at < lax.axis_size("gy") - 1).astype(F32)
    before = (col_at > 0).astype(F32)
    after = (col_at < lax.axis_size("gx") - 1).astype(F32)
    spot = lax.broadcasted_iota(jnp.int32, (length, width), 0)
    inside = jnp.where(spot == 1, upper, jnp.where(spot == rows + 2, lower, 1.0))
    keep = [upper, 1.0, 1.0, lower, inside * before, inside, inside, inside * after]
    lhs = jnp.concatenate(parts, axis=0)
    gates = jnp.dot(lhs, weights[...], preferred_element_type=F32) + bias[...]
    start = 0
    for place in range(8):
        hid, cell = (line_hid, line_cell) if place < 4 else (strip_hid, strip_cell)
        size = hid.shape[1]
        new_cell, hidden = lstm(gates[start : start + size], held[place])
        hid[place % 4] = hidden.astype(BF).astype(F32) * keep[place]
        cell[place % 4] = new_cell
        start += size


def block_kernel(x, w_qkv, w_out, w_up, w_down, *rest):
    out, flat, back, keys_t, own_low, own_high, own_values, ones = rest[-8:]
    group = GRID * GRID
    embed = w_out.shape[0]
    tile = embed // 2

    @pl.when((pl.program_id(0) == 0) & (pl.program_id(1) == 0))
    def _():
        def fill(target, down, across, add):
            above = lax.broadcasted_iota(jnp.int32, target.shape, 0) // down
            along = lax.broadcasted_iota(jnp.int32, target.shape, 1) // across
            target[...] = (above == along + add).astype(F32).astype(BF)

        fill(own_low, HDIM, group, 0)
        fill(own_high, HDIM, group, HEADS // 4)
        fill(own_values, group, HDIM, 0)
        fill(ones, group, group, 0)
        keys_t[...] = w_qkv[:, embed : 2 * embed].astype(F32).T.astype(BF)

    def work(sub):
        flat[sub] = x[:, :, sub].astype(F32).reshape(flat.shape[1:])
        groups = flat.shape[1] // group
        cells = jnp.concatenate([flat[sub, pl.ds(g, group, stride=groups), :] for g in range(groups)], axis=0)
        normed = layer_norm(cells).astype(BF)
        yield
        queries = jnp.dot(normed, w_qkv[:, :embed], preferred_element_type=F32).astype(BF)
        yield
        values = jnp.dot(normed, w_qkv[:, 2 * embed :], preferred_element_type=F32).astype(BF)
        keys = lax.dot_general(keys_t[...], normed, (((1,), (1,)), ((), ())), preferred_element_type=F32)
        yield
        side = lax.broadcasted_iota(jnp.int32, (embed, 2 * group), 1) < group
        raised = [[], []]
        for pair in range(groups // 2):
            both = keys[:, pair * 2 * group : (pair + 1) * 2 * group]
            turned = pltpu.roll(both, group, axis=1)
            for place, twice in enumerate((jnp.where(side, both, turned), jnp.where(side, turned, both))):
                twice = twice.astype(BF)
                start = (2 * pair + place) * group
                for half in range(2):
                    part = twice[half * tile : (half + 1) * tile]
                    spread = jnp.concatenate([part * own_low[...], part * own_high[...]], axis=1)
                    scores = jnp.dot(
                        queries[start : start + group, half * tile : (half + 1) * tile],
                        spread,
                        preferred_element_type=F32,
                    )
                    raised[half].append(jnp.minimum(jnp.exp2(scores * (LOG2E * HDIM**-0.5)), BF_MAX).astype(BF))
            yield
        attn = []
        for half in range(2):
            part = jnp.concatenate(raised[half], axis=0)
            total = jnp.dot(part, ones[...], preferred_element_type=F32)
            guess = pl.reciprocal(total, approx=True)
            attn.append((part.astype(F32) * (guess * (2.0 - total * guess))).astype(BF))
            yield
        heads = []
        for half in range(2):
            column = []
            for g in range(groups):
                held = values[g * group : (g + 1) * group, half * tile : (half + 1) * tile]
                spread = jnp.concatenate([held] * (HEADS // 2), axis=0) * own_values[...]
                column.append(
                    jnp.dot(attn[half][g * group : (g + 1) * group], spread, preferred_element_type=F32).astype(BF)
                )
            heads.append(jnp.concatenate(column, axis=0))
            yield
        heads = jnp.concatenate(heads, axis=1)
        attended = jnp.dot(heads, w_out[...], preferred_element_type=F32).astype(BF)
        mixed = cells + attended.astype(F32)
        yield
        normed_two = layer_norm(mixed).astype(BF)
        yield
        up = jnp.dot(normed_two, w_up[...], preferred_element_type=F32)
        bent = jnp.tanh(up * (0.7978845608 + (0.7978845608 * 0.044715) * (up * up)))
        half_up = 0.5 * up
        expanded = (half_up + half_up * bent).astype(BF)
        yield
        result = mixed + jnp.dot(expanded, w_down[...], preferred_element_type=F32)
        for g in range(groups):
            back[sub, pl.ds(g, group, stride=groups), :] = result[g * group : (g + 1) * group]
        out[:, :, sub] = back[sub].reshape(x.shape[:2] + x.shape[3:]).astype(BF)

    waiting = [work(sub) for sub in range(x.shape[2])]
    running = []
    while waiting or running:
        if waiting:
            running.append(waiting.pop(0))
        for one in list(running):
            if next(one, running) is running:
                running.remove(one)


def block_step(moved, carry, first, pieces, devices_y, devices_x, w_qkv, w_out, w_up, w_down):
    _, piece_y, piece_cols, width = moved.shape
    lanes = devices_y // GRID
    view = moved.reshape(GRID, lanes, devices_x, piece_y, piece_cols, width)
    tokens = GRID * devices_x * piece_cols
    subs = max(size for size in (1, 2, 4) if piece_y % size == 0 and first % size == 0)
    block = (GRID, None, devices_x, subs, piece_cols, width)
    operands = [view, w_qkv, w_out, w_up, w_down]
    in_specs = [pl.BlockSpec(block, lambda i, j: (0, i, 0, j, 0, 0)), *(whole(array) for array in operands[1:])]
    aliases = {}
    if carry is not None:
        aliases = {len(operands): 0}
        operands.append(carry)
        in_specs.append(pl.BlockSpec(memory_space=pl.ANY))
    total = lanes * piece_y * tokens
    return pl.pallas_call(
        block_kernel,
        grid=(lanes, piece_y // subs),
        in_specs=in_specs,
        out_specs=pl.BlockSpec(block, lambda i, j: (0, i, 0, first // subs + j, 0, 0)),
        out_shape=jax.ShapeDtypeStruct((GRID, lanes, devices_x, pieces, piece_cols, width), BF),
        scratch_shapes=[
            pltpu.VMEM((subs, tokens, width), F32),
            pltpu.VMEM((subs, tokens, width), F32),
            pltpu.VMEM((w_out.shape[0], width), BF),
            pltpu.VMEM((HEADS // 2 * HDIM, 2 * GRID * GRID), BF),
            pltpu.VMEM((HEADS // 2 * HDIM, 2 * GRID * GRID), BF),
            pltpu.VMEM((HEADS // 2 * GRID * GRID, HEADS // 2 * HDIM), BF),
            pltpu.VMEM((HEADS // 2 * GRID * GRID, HEADS // 2 * GRID * GRID), BF),
        ],
        input_output_aliases=aliases,
        compiler_params=pltpu.CompilerParams(vmem_limit_bytes=VMEM_LIMIT),
        cost_estimate=pl.CostEstimate(
            flops=total * 3_000_000, bytes_accessed=total * width * 4 + 800_000, transcendentals=total * 1100
        ),
    )(*operands)


def unpack_kernel(shares, local_m, piece_x, src, out):
    owners_y, owners_x = src.shape[:2]
    unit = out.shape[0]
    lines, first = [], 0
    for share in shares:
        lines += [(owner_y, first + piece) for owner_y in range(owners_y) for piece in range(share)]
        first += share
    for step in range(len(lines) // unit):

        @pl.when(pl.program_id(0) == step)
        def _():
            for row, (owner_y, piece) in enumerate(lines[step * unit : (step + 1) * unit]):
                wide = src[owner_y, :, piece].astype(F32)
                parts = [
                    wide[owner, m * piece_x : (m + 1) * piece_x] for m in range(local_m) for owner in range(owners_x)
                ]
                out[row] = jnp.concatenate(parts, axis=0).astype(BF)


def unpack_step(landed, shares, cols, local_m, piece_x):
    owners_y, _, pieces, _, width = landed.shape
    rows = owners_y * pieces
    unit = 16 if rows % 16 == 0 else rows
    return pl.pallas_call(
        functools.partial(unpack_kernel, shares, local_m, piece_x),
        grid=(rows // unit,),
        in_specs=[pl.BlockSpec(memory_space=pltpu.VMEM)],
        out_specs=pl.BlockSpec((unit, cols, width), lambda step: (step, 0, 0)),
        out_shape=jax.ShapeDtypeStruct((rows, cols, width), BF),
        compiler_params=pltpu.CompilerParams(vmem_limit_bytes=VMEM_LIMIT),
        cost_estimate=pl.CostEstimate(flops=0, bytes_accessed=rows * cols * width * 4, transcendentals=0),
    )(landed)


def step_rows(start, extent, most=16):
    return max(size for size in range(1, most + 1) if extent % size == 0 and start % size == 0)


def body(frames, hidden_state, cell_state, w_gates, gate_bias, w_qkv, w_out, w_up, w_down):
    rows, cols, width = hidden_state.shape
    latent = frames.shape[2] // 2
    chans = latent + width
    held = chans + width
    devices_y, devices_x = lax.axis_size("gy"), lax.axis_size("gx")
    local_m = GRID // devices_x
    piece_x = cols // local_m // devices_x
    weights = w_gates.reshape(-1, w_gates.shape[3])
    bias = gate_bias.reshape(1, -1)

    def shifted(value, axis, step):
        count = lax.axis_size(axis)
        pairs = [(i, i + step) for i in range(count) if 0 <= i + step < count]
        return lax.ppermute(value, axis, pairs)

    send_left, send_right, side_left, side_right, line_top, line_bot = pack_step(frames, hidden_state, cell_state)
    from_left = shifted(send_right, "gx", 1)
    from_right = shifted(send_left, "gx", -1)
    to_down = jnp.concatenate([line_bot, from_left[-2:], from_right[-2:]], axis=1)
    to_up = jnp.concatenate([line_top, from_left[:2], from_right[:2]], axis=1)

    pieces = rows // devices_y
    piece_cols = local_m * piece_x
    shares = (pieces - pieces // 3, pieces // 3)
    ahead = rows - max(size for size in range(1, 13) if rows % size == 0 and rows - size > shares[0] * devices_y)
    tile_shapes = (jax.ShapeDtypeStruct((rows, cols, width), BF), jax.ShapeDtypeStruct((rows, cols, width), F32))
    carry = ()
    half = -(-ahead // 6) * 4
    for start, extent in ((0, half), (half, ahead - half)):
        spec = pl.BlockSpec(memory_space=pltpu.VMEM)
        if carry:
            *carry, to_down, to_up = lax.optimization_barrier((*carry, to_down, to_up))
            from_up, from_down = shifted(to_down, "gy", 1), shifted(to_up, "gy", -1)
        carry = conv_step(
            frames, 0, hidden_state, cell_state, {}, weights, bias, (start, extent), ("hid_out", "cell_out"),
            tile_shapes, (spec, spec), None, carry, None,
        )
    hidden_one, cell_one = carry

    length = -(-(rows + 4) // 16) * 16
    line_shape = jax.ShapeDtypeStruct((4, cols, width), F32)
    strip_shape = jax.ShapeDtypeStruct((4, length, width), F32)
    beside_shape = jax.ShapeDtypeStruct((2, length, latent), F32)
    shapes = (line_shape, line_shape, strip_shape, strip_shape, beside_shape)
    turned = from_left.transpose(1, 0, 2), from_right.transpose(1, 0, 2)
    around = (from_up, from_down, line_top, line_bot, *turned, side_left, side_right)
    line_hid, line_cell, strip_hid, strip_cell, beside = pl.pallas_call(
        ring_kernel,
        grid=(1,),
        in_specs=[*(whole(array) for array in around), pl.BlockSpec(memory_space=pltpu.VMEM), whole(bias)],
        out_specs=[whole(shape) for shape in shapes],
        out_shape=shapes,
        scratch_shapes=[pltpu.VMEM((8, length, held + latent), F32)],
        compiler_params=pltpu.CompilerParams(vmem_limit_bytes=VMEM_LIMIT),
        cost_estimate=pl.CostEstimate(flops=16 * length * weights.size, bytes_accessed=2 * weights.size, transcendentals=0),
    )(*around, weights, bias)

    second = held // latent
    line = (1, from_up.shape[1], latent)
    ring = {name: (array, whole(array)) for name, array in (
        ("strips_hid", strip_hid), ("strips_cell", strip_cell), ("lines_hid", line_hid), ("lines_cell", line_cell),
        ("beside", beside),
    )}
    ring["frame_top"] = from_up, pl.BlockSpec(line, lambda step: (1, 0, second))
    ring["frame_bot"] = from_down, pl.BlockSpec(line, lambda step: (0, 0, second))

    moved, start, carry = [], 0, ()
    for piece_y in shares:
        extent = piece_y * devices_y
        sent_shape = jax.ShapeDtypeStruct((devices_y, devices_x, piece_y, piece_cols, width), BF)
        spec = pl.BlockSpec(memory_space=pl.ANY)
        sent, cell_out = conv_step(
            frames, 1, hidden_one, cell_one, ring, weights, bias, (start, extent),
            ("hid_out", "cell_out"), (sent_shape, tile_shapes[1]), (whole(sent_shape), spec), (local_m, piece_x), carry,
            (ahead, hidden_state, cell_state) if carry else None,
        )
        carry = (None, cell_out)
        sent = sent.reshape(devices_y * devices_x, piece_y, piece_cols, width)
        moved.append(lax.all_to_all(sent, ("gy", "gx"), split_axis=0, concat_axis=0, tiled=True))
        start += extent
    done, first = None, 0
    for piece_y, value in zip(shares, moved):
        done = block_step(value, done, first, pieces, devices_y, devices_x, w_qkv, w_out, w_up, w_down)
        first += piece_y
    done = done.reshape(devices_y * devices_x, pieces, piece_cols, width)
    landed = lax.all_to_all(done, ("gy", "gx"), split_axis=0, concat_axis=0, tiled=True)
    result = unpack_step(landed.reshape(devices_y, devices_x, *landed.shape[1:]), shares, cols, local_m, piece_x)
    return result, cell_out


def solution(mesh):
    tiled = P("gy", "gx", None)
    in_specs = (tiled, tiled, tiled, P(), P(), P(), P(), P(), P())
    return jax.shard_map(body, mesh=mesh, in_specs=in_specs, out_specs=(tiled, tiled), check_vma=False)
```

```python
import functools

import jax
import jax.numpy as jnp
from jax import lax
from jax.experimental import pallas as pl
from jax.experimental.pallas import tpu as pltpu
from jax.sharding import PartitionSpec as P

HEADS = 8
HDIM = 32
GRID = 8
BF = jnp.bfloat16
F32 = jnp.float32
LOG2E = 1.4426950408889634
BF_MAX = 3.3895313892515355e38
VMEM_LIMIT = 32 * 1024 * 1024
VMEM_ALL = 60 * 1024 * 1024
LOADS = 9
LANES = 128


def sigmoid(x):
    return 0.5 * jnp.tanh(0.5 * x) + 0.5


def lstm(gates, cell_prev):
    width = cell_prev.shape[-1]
    in_gate = sigmoid(gates[:, 0:width])
    forget_gate = sigmoid(gates[:, width : 2 * width])
    candidate = jnp.tanh(gates[:, 2 * width : 3 * width])
    out_gate = sigmoid(gates[:, 3 * width :])
    cell = forget_gate * cell_prev + in_gate * candidate
    return cell, out_gate * jnp.tanh(cell)


def layer_norm(values):
    center = values - jnp.mean(values, axis=-1, keepdims=True)
    spread = jnp.mean(center * center, axis=-1, keepdims=True)
    return center * lax.rsqrt(spread + 1e-05)


def three_columns(wide, left, right):
    count = wide.shape[0]
    place = lax.broadcasted_iota(jnp.int32, wide.shape, 0)
    before = jnp.where(place == 0, left, pltpu.roll(wide, 1, axis=0))
    after = jnp.where(place == count - 1, right, pltpu.roll(wide, count - 1, axis=0))
    return before.astype(BF), wide.astype(BF), after.astype(BF)


def conv_kernel(start, rows, part, tail, refs, packed, *args):
    ref = dict(zip(refs, args))
    hid_out, cell_out = ref["hid_out"], ref["cell_out"]
    extent = ref["spread"].shape[0] - 2
    cols, width = ref["hid"].shape[1:]
    chans = ref["spread"].shape[2] // 3
    latent = chans - width
    loads, leaving = [], []
    if "weights" in ref:
        size = ref["weights"].shape[0] // LOADS
        for place in range(LOADS):
            run = pl.ds(place * size, size)
            loads.append(pltpu.make_async_copy(ref["weights"].at[run], ref["held"].at[run], ref["sem"].at[place]))
    for load in loads:
        load.start()

    def reader(prefix, first, count):
        def row_of(name, row):
            array = ref[prefix + name]
            if array.shape[0] == rows:
                channels = slice(part * latent, (part + 1) * latent) if name == "frame" else slice(None)
                return array[row, :, channels]
            if prefix != "tail_" and tail and row >= tail and name != "frame":
                return ref["late_" + name][row - tail]
            if row == first - 1:
                return ref[prefix + name + "_prev"][0]
            if row == first + count:
                return ref[prefix + name + "_next"][0]
            return array[row - first]

        return row_of

    def convolve(spread, start, extent, row_of, ring, write, leave):
        def beside(row):
            if not ring:
                return jnp.zeros((1, chans), F32), jnp.zeros((1, chans), F32)
            at = row + 2
            return tuple(
                jnp.concatenate(
                    [ref["beside"][place, at : at + 1, :], ref["strips_hid"][3 * place, at : at + 1, :]], axis=1
                )
                for place in range(2)
            )

        def build(pos):
            row = start + pos - 1
            raw = None
            if 0 <= row < rows:
                raw = row_of("frame", row), row_of("hid", row)
                x, h = raw[0].astype(F32), raw[1].astype(F32)
            elif ring:
                x = ref["frame_top" if row < 0 else "frame_bot"][0, :cols].astype(F32)
                h = ref["lines_hid"][3 * (row > 0)]
            else:
                spread[pos] = jnp.zeros(spread.shape[1:], BF)
                return
            low, high = beside(row)
            if ring:
                at = row + 2
                place = lax.broadcasted_iota(jnp.int32, h.shape, 0)
                h = jnp.where(place == 0, ref["strips_hid"][1, at : at + 1, :], h)
                h = jnp.where(place == cols - 1, ref["strips_hid"][2, at : at + 1, :], h)
                for spot, line in ((0, 1), (rows - 1, 2)):
                    if row == spot:
                        h = ref["lines_hid"][line]
            for side, (value, first) in enumerate(((x, 0), (h, latent))):
                size = value.shape[1]
                pieces = three_columns(value, low[:, first : first + size], high[:, first : first + size])
                if raw is not None and (side == 0 or not ring):
                    pieces = pieces[0], raw[side], pieces[2]
                for tap in range(3):
                    spread[pos, :, tap * chans + first : tap * chans + first + size] = pieces[tap]

        def multiply(first, depth):
            lhs = jnp.concatenate(
                [spread[first + tap : first + tap + depth].reshape(depth * cols, 3 * chans) for tap in range(3)], axis=1
            )
            return jnp.dot(lhs, ref["held"][...], preferred_element_type=F32)

        def activate(first, depth, gates):
            for line in range(first, first + depth):
                row = start + line
                cell_prev = row_of("cell", row)
                if ring:
                    at = row + 2
                    place = lax.broadcasted_iota(jnp.int32, cell_prev.shape, 0)
                    cell_prev = jnp.where(place == 0, ref["strips_cell"][1, at : at + 1, :], cell_prev)
                    cell_prev = jnp.where(place == cols - 1, ref["strips_cell"][2, at : at + 1, :], cell_prev)
                    if row == 0:
                        cell_prev = ref["lines_cell"][1]
                    if row == rows - 1:
                        cell_prev = ref["lines_cell"][2]
                own = gates[(line - first) * cols : (line - first + 1) * cols] + ref["bias"][...]
                new_cell, new_hidden = lstm(own, cell_prev)
                write(row, new_cell, new_hidden)
            leave(first, depth)

        depth = step_rows(0, extent, 4)
        for pos in range(depth + 2):
            build(pos)
        while loads:
            loads.pop().wait()
        waiting = None
        for first in range(0, extent, depth):
            for pos in range(first + depth + 2, min(first + 2 * depth, extent) + 2):
                build(pos)
            gates = multiply(first, depth)
            if waiting:
                activate(*waiting)
            waiting = first, depth, gates
        activate(*waiting)

    def keep(row, new_cell, new_hidden):
        cell_out[row] = new_cell
        hid_out[row] = new_hidden.astype(BF)

    def keep_late(row, new_cell, new_hidden):
        ref["late_cell"][row - tail] = new_cell
        ref["late_hid"][row - tail] = new_hidden.astype(BF)

    def send(row, new_cell, new_hidden):
        line = row - start
        ref["cell_rows"][line] = new_cell
        owners_x, piece_y = hid_out.shape[1:3]
        local_m, piece_x = packed
        for owner in range(owners_x):
            picked = [
                new_hidden[(m * owners_x + owner) * piece_x : (m * owners_x + owner + 1) * piece_x]
                for m in range(local_m)
            ]
            hid_out[line // piece_y, owner, line % piece_y] = jnp.concatenate(picked, axis=0).astype(BF)

    def leave(first, depth):
        copy = pltpu.make_async_copy(
            ref["cell_rows"].at[pl.ds(first, depth)], cell_out.at[pl.ds(start + first, depth)],
            ref["left"].at[first // depth],
        )
        copy.start()
        leaving.append(copy)

    def stay(first, depth):
        pass

    if not packed:
        convolve(ref["spread"], start, extent, reader("", start, extent), False, keep, stay)
        return
    if tail:
        convolve(ref["late_spread"], tail, rows - tail, reader("tail_", tail, rows - tail), False, keep_late, stay)
    convolve(ref["spread"], start, extent, reader("", start, extent), True, send, leave)
    for copy in leaving:
        copy.wait()


def whole(array):
    return pl.BlockSpec(array.shape, lambda *step: (0,) * array.ndim)


def conv_step(frames, part, hid, cell, ring, weights, bias, rows_of, names, out_shapes, out_specs, packed, carry, late):
    rows, cols, width = hid.shape
    latent = weights.shape[0] // 9 - width
    start, extent = rows_of

    def rowed(size, channels, channel, row):
        return pl.BlockSpec((size, cols, channels), lambda step: (row // size, 0, channel))

    def windows(prefix, hid, cell, channel, start, extent):
        before, after = max(start - 1, 0), min(start + extent, rows - 1)
        return {
            prefix + "frame": (frames, rowed(extent, latent, channel, start)),
            prefix + "frame_prev": (frames, rowed(1, latent, channel, before)),
            prefix + "frame_next": (frames, rowed(1, latent, channel, after)),
            prefix + "hid": (hid, rowed(extent, width, 0, start)),
            prefix + "hid_prev": (hid, rowed(1, width, 0, before)),
            prefix + "hid_next": (hid, rowed(1, width, 0, after)),
            prefix + "cell": (cell, rowed(extent, width, 0, start)),
        }

    near = pl.BlockSpec(memory_space=pltpu.VMEM)
    tail = 0
    if late:
        tail, *first = late
        inputs = windows("", hid, cell, part, start, extent)
        inputs |= windows("tail_", *first, 0, tail, rows - tail)
    else:
        inputs = {"frame": (frames, near), "hid": (hid, near), "cell": (cell, near)}
    inputs["bias"] = bias, whole(bias)
    if late:
        inputs["weights"] = weights, pl.BlockSpec(memory_space=pl.ANY)
    else:
        inputs["held"] = weights, near
    inputs |= ring
    aliases = {}
    for place, array in enumerate(carry):
        if array is not None:
            aliases[len(inputs)] = place
            inputs[f"carry{place}"] = (array, pl.BlockSpec(memory_space=pl.ANY) if packed else near)
    refs = [*inputs, *names, "spread"]
    scratch = [pltpu.VMEM((extent + 2, cols, 3 * (latent + width)), BF)]
    if late:
        refs += ["held", "sem", "late_spread", "late_hid", "late_cell"]
        scratch += [
            pltpu.VMEM(weights.shape, BF),
            pltpu.SemaphoreType.DMA((LOADS,)),
            pltpu.VMEM((rows - tail + 2, cols, 3 * (latent + width)), BF),
            pltpu.VMEM((rows - tail, cols, width), BF),
            pltpu.VMEM((rows - tail, cols, width), F32),
        ]
    if packed:
        refs += ["cell_rows", "left"]
        scratch += [pltpu.VMEM((extent, cols, width), F32), pltpu.SemaphoreType.DMA((extent,))]
    cells = extent * cols
    return pl.pallas_call(
        functools.partial(conv_kernel, start, rows, part, tail, refs, packed),
        grid=(1,),
        in_specs=[spec for _, spec in inputs.values()],
        out_specs=out_specs,
        out_shape=out_shapes,
        scratch_shapes=scratch,
        input_output_aliases=aliases,
        compiler_params=pltpu.CompilerParams(vmem_limit_bytes=VMEM_ALL if late else VMEM_LIMIT),
        cost_estimate=pl.CostEstimate(
            flops=2 * cells * weights.size, bytes_accessed=2 * weights.size + cells * 2048, transcendentals=cells * width * 5
        ),
    )(*(array for array, _ in inputs.values()))


def pack_kernel(frames, hids, cells, send_low, send_high, side_low, side_high, line_top, line_bot, flat):
    rows, cols, width = hids.shape
    latent = frames.shape[2] // 2
    chans = latent + width
    places = ((0, 0, latent), (chans + width, latent, latent))
    for out, near in ((line_top, slice(0, 2)), (line_bot, slice(rows - 2, rows))):
        for to, start, size in places:
            out[:, :, to : to + size] = frames[near, :, start : start + size]
        out[:, :, latent:chans] = hids[near]
        out[:, :, chans : chans + width] = cells[near].astype(BF)
    for out, send, near, start in (
        (side_low, send_low, slice(0, 8), 0),
        (side_high, send_high, slice(cols - 8, cols), 6),
    ):
        for slab in range(out.shape[2] // LANES):
            to = slab * LANES
            if to < latent or to >= chans + width:
                begin = to if to < latent else to - 2 * width
                part = frames[:, near, begin : begin + LANES].astype(F32)
            elif to < chans:
                part = hids[:, near, to - latent : to - latent + LANES].astype(F32)
            else:
                part = cells[:, near, to - chans : to - chans + LANES]
            send[:, :, to : to + LANES] = part[:, start : start + 2].astype(BF)
            flat[...] = part.reshape(rows * 8, LANES)
            for place in range(2):
                out[place, :, to : to + LANES] = flat[pl.ds(start + place, rows, stride=8), :].astype(BF)


def pack_step(frames, hid, cell):
    rows, cols, width = hid.shape
    span = frames.shape[2]
    deep = span + 2 * width
    shapes = [jax.ShapeDtypeStruct((rows, 2, deep), BF)] * 2 + [jax.ShapeDtypeStruct((2, rows, deep), BF)] * 2
    shapes += [jax.ShapeDtypeStruct((2, cols, deep), BF)] * 2
    return pl.pallas_call(
        pack_kernel,
        grid=(1,),
        in_specs=[pl.BlockSpec(memory_space=pltpu.VMEM)] * 3,
        out_specs=[whole(shape) for shape in shapes],
        out_shape=shapes,
        scratch_shapes=[pltpu.VMEM((rows * 8, LANES), F32)],
        compiler_params=pltpu.CompilerParams(vmem_limit_bytes=VMEM_LIMIT),
        cost_estimate=pl.CostEstimate(flops=0, bytes_accessed=4_000_000, transcendentals=0),
    )(frames, hid, cell)


def ring_kernel(
    above, below, line_top, line_bot, from_left, from_right, side_left, side_right, weights, bias,
    line_hid, line_cell, strip_hid, strip_cell, beside, strips,
):
    width = line_hid.shape[2]
    chans = weights.shape[0] // 9
    cols, length = line_top.shape[1], strip_hid.shape[1]
    rows = from_left.shape[1]
    columns = (
        (from_left, 0, cols), (from_left, 1, cols + 1), (side_left, 0, 0), (side_left, 1, 1),
        (side_right, 0, cols - 2), (side_right, 1, cols - 1), (from_right, 0, cols + 2), (from_right, 1, cols + 3),
    )
    ends = [(ref[row].astype(F32), at + row) for ref, at in ((above, 0), (below, rows + 2)) for row in range(2)]
    strips[:, rows + 4 :, :] = jnp.zeros((8, length - rows - 4, strips.shape[2]), F32)
    for place, (source, at, end) in enumerate(columns):
        strips[place, 2 : rows + 2, :] = source[at].astype(F32)
        for value, spot in ends:
            strips[place, spot : spot + 1, :] = value[end : end + 1]
    beside[0] = strips[1, :, chans + width :]
    beside[1] = strips[6, :, chans + width :]
    low, high = strips[1, :, :chans], strips[6, :, :chans]

    def line(ref, row):
        held = ref[row, :cols].astype(F32)
        return held[:, :chans], held[:, chans : chans + width]

    tops = [line(above, 0), line(above, 1), line(line_top, 0), line(line_top, 1)]
    bots = [line(line_bot, 0), line(line_bot, 1), line(below, 0), line(below, 1)]
    parts, held = [], []
    for lead, lines in ((0, tops), (rows, bots)):
        pieces = []
        for row in range(4):
            at = lead + row
            pieces.append(three_columns(lines[row][0], low[at : at + 1], high[at : at + 1]))
        for row in range(2):
            parts.append(jnp.concatenate([pieces[row + tap][col] for tap in range(3) for col in range(3)], axis=1))
            held.append(lines[row + 1][1])
    for side in range(2):
        rolled = []
        for col in range(4):
            wide = strips[4 * side + col, :, :chans]
            rolled.append((pltpu.roll(wide, 1, axis=0), wide, pltpu.roll(wide, length - 1, axis=0)))
        for col in range(2):
            parts.append(
                jnp.concatenate([rolled[col + tap][row].astype(BF) for row in range(3) for tap in range(3)], axis=1)
            )
            held.append(strips[4 * side + col + 1, :, chans : chans + width])
    row_at, col_at = lax.axis_index("gy"), lax.axis_index("gx")
    upper = (row_at > 0).astype(F32)
    lower = (row_at < lax.axis_size("gy") - 1).astype(F32)
    before = (col_at > 0).astype(F32)
    after = (col_at < lax.axis_size("gx") - 1).astype(F32)
    spot = lax.broadcasted_iota(jnp.int32, (length, width), 0)
    inside = jnp.where(spot == 1, upper, jnp.where(spot == rows + 2, lower, 1.0))
    keep = [upper, 1.0, 1.0, lower, inside * before, inside, inside, inside * after]
    lhs = jnp.concatenate(parts, axis=0)
    gates = jnp.dot(lhs, weights[...], preferred_element_type=F32) + bias[...]
    start = 0
    for place in range(8):
        hid, cell = (line_hid, line_cell) if place < 4 else (strip_hid, strip_cell)
        size = hid.shape[1]
        new_cell, hidden = lstm(gates[start : start + size], held[place])
        hid[place % 4] = hidden.astype(BF).astype(F32) * keep[place]
        cell[place % 4] = new_cell
        start += size


def block_kernel(x, w_qkv, w_out, w_up, w_down, *rest):
    out, flat, back, keys_t, own_low, own_high, own_values, ones = rest[-8:]
    group = GRID * GRID
    embed = w_out.shape[0]
    tile = embed // 2

    @pl.when((pl.program_id(0) == 0) & (pl.program_id(1) == 0))
    def _():
        def fill(target, down, across, add):
            above = lax.broadcasted_iota(jnp.int32, target.shape, 0) // down
            along = lax.broadcasted_iota(jnp.int32, target.shape, 1) // across
            target[...] = (above == along + add).astype(F32).astype(BF)

        fill(own_low, HDIM, group, 0)
        fill(own_high, HDIM, group, HEADS // 4)
        fill(own_values, group, HDIM, 0)
        fill(ones, group, group, 0)
        keys_t[...] = w_qkv[:, embed : 2 * embed].astype(F32).T.astype(BF)

    def work(sub):
        flat[sub] = x[:, :, sub].astype(F32).reshape(flat.shape[1:])
        groups = flat.shape[1] // group
        cells = jnp.concatenate([flat[sub, pl.ds(g, group, stride=groups), :] for g in range(groups)], axis=0)
        normed = layer_norm(cells).astype(BF)
        yield
        queries = jnp.dot(normed, w_qkv[:, :embed], preferred_element_type=F32).astype(BF)
        yield
        values = jnp.dot(normed, w_qkv[:, 2 * embed :], preferred_element_type=F32).astype(BF)
        keys = lax.dot_general(keys_t[...], normed, (((1,), (1,)), ((), ())), preferred_element_type=F32)
        yield
        side = lax.broadcasted_iota(jnp.int32, (embed, 2 * group), 1) < group
        raised = [[], []]
        for pair in range(groups // 2):
            both = keys[:, pair * 2 * group : (pair + 1) * 2 * group]
            turned = pltpu.roll(both, group, axis=1)
            for place, twice in enumerate((jnp.where(side, both, turned), jnp.where(side, turned, both))):
                twice = twice.astype(BF)
                start = (2 * pair + place) * group
                for half in range(2):
                    part = twice[half * tile : (half + 1) * tile]
                    spread = jnp.concatenate([part * own_low[...], part * own_high[...]], axis=1)
                    scores = jnp.dot(
                        queries[start : start + group, half * tile : (half + 1) * tile],
                        spread,
                        preferred_element_type=F32,
                    )
                    raised[half].append(jnp.minimum(jnp.exp2(scores * (LOG2E * HDIM**-0.5)), BF_MAX).astype(BF))
            yield
        attn = []
        for half in range(2):
            part = jnp.concatenate(raised[half], axis=0)
            total = jnp.dot(part, ones[...], preferred_element_type=F32)
            guess = pl.reciprocal(total, approx=True)
            attn.append((part.astype(F32) * (guess * (2.0 - total * guess))).astype(BF))
            yield
        heads = []
        for half in range(2):
            column = []
            for g in range(groups):
                held = values[g * group : (g + 1) * group, half * tile : (half + 1) * tile]
                spread = jnp.concatenate([held] * (HEADS // 2), axis=0) * own_values[...]
                column.append(
                    jnp.dot(attn[half][g * group : (g + 1) * group], spread, preferred_element_type=F32).astype(BF)
                )
            heads.append(jnp.concatenate(column, axis=0))
            yield
        heads = jnp.concatenate(heads, axis=1)
        attended = jnp.dot(heads, w_out[...], preferred_element_type=F32).astype(BF)
        mixed = cells + attended.astype(F32)
        yield
        normed_two = layer_norm(mixed).astype(BF)
        yield
        up = jnp.dot(normed_two, w_up[...], preferred_element_type=F32)
        bent = jnp.tanh(up * (0.7978845608 + (0.7978845608 * 0.044715) * (up * up)))
        half_up = 0.5 * up
        expanded = (half_up + half_up * bent).astype(BF)
        yield
        result = mixed + jnp.dot(expanded, w_down[...], preferred_element_type=F32)
        for g in range(groups):
            back[sub, pl.ds(g, group, stride=groups), :] = result[g * group : (g + 1) * group]
        out[:, :, sub] = back[sub].reshape(x.shape[:2] + x.shape[3:]).astype(BF)

    waiting = [work(sub) for sub in range(x.shape[2])]
    running = []
    while waiting or running:
        if waiting:
            running.append(waiting.pop(0))
        for one in list(running):
            if next(one, running) is running:
                running.remove(one)


def block_step(moved, carry, first, pieces, devices_y, devices_x, w_qkv, w_out, w_up, w_down):
    _, piece_y, piece_cols, width = moved.shape
    lanes = devices_y // GRID
    view = moved.reshape(GRID, lanes, devices_x, piece_y, piece_cols, width)
    tokens = GRID * devices_x * piece_cols
    subs = max(size for size in (1, 2, 4) if piece_y % size == 0 and first % size == 0)
    block = (GRID, None, devices_x, subs, piece_cols, width)
    operands = [view, w_qkv, w_out, w_up, w_down]
    in_specs = [pl.BlockSpec(block, lambda i, j: (0, i, 0, j, 0, 0)), *(whole(array) for array in operands[1:])]
    aliases = {}
    if carry is not None:
        aliases = {len(operands): 0}
        operands.append(carry)
        in_specs.append(pl.BlockSpec(memory_space=pl.ANY))
    total = lanes * piece_y * tokens
    return pl.pallas_call(
        block_kernel,
        grid=(lanes, piece_y // subs),
        in_specs=in_specs,
        out_specs=pl.BlockSpec(block, lambda i, j: (0, i, 0, first // subs + j, 0, 0)),
        out_shape=jax.ShapeDtypeStruct((GRID, lanes, devices_x, pieces, piece_cols, width), BF),
        scratch_shapes=[
            pltpu.VMEM((subs, tokens, width), F32),
            pltpu.VMEM((subs, tokens, width), F32),
            pltpu.VMEM((w_out.shape[0], width), BF),
            pltpu.VMEM((HEADS // 2 * HDIM, 2 * GRID * GRID), BF),
            pltpu.VMEM((HEADS // 2 * HDIM, 2 * GRID * GRID), BF),
            pltpu.VMEM((HEADS // 2 * GRID * GRID, HEADS // 2 * HDIM), BF),
            pltpu.VMEM((HEADS // 2 * GRID * GRID, HEADS // 2 * GRID * GRID), BF),
        ],
        input_output_aliases=aliases,
        compiler_params=pltpu.CompilerParams(vmem_limit_bytes=VMEM_LIMIT),
        cost_estimate=pl.CostEstimate(
            flops=total * 3_000_000, bytes_accessed=total * width * 4 + 800_000, transcendentals=total * 1100
        ),
    )(*operands)


def unpack_kernel(shares, local_m, piece_x, unit, src, out, lines_out, sem):
    owners_y, owners_x = src.shape[:2]
    lines, first = [], 0
    for share in shares:
        lines += [(owner_y, first + piece) for owner_y in range(owners_y) for piece in range(share)]
        first += share
    leaving = []
    for step in range(len(lines) // unit):
        for row in range(step * unit, (step + 1) * unit):
            owner_y, piece = lines[row]
            wide = src[owner_y, :, piece].astype(F32)
            parts = [wide[owner, m * piece_x : (m + 1) * piece_x] for m in range(local_m) for owner in range(owners_x)]
            lines_out[row] = jnp.concatenate(parts, axis=0).astype(BF)
        run = pl.ds(step * unit, unit)
        leaving.append(pltpu.make_async_copy(lines_out.at[run], out.at[run], sem.at[step]))
        leaving[-1].start()
    for copy in leaving:
        copy.wait()


def unpack_step(landed, shares, cols, local_m, piece_x):
    owners_y, _, pieces, _, width = landed.shape
    rows = owners_y * pieces
    unit = 16 if rows % 16 == 0 else rows
    return pl.pallas_call(
        functools.partial(unpack_kernel, shares, local_m, piece_x, unit),
        in_specs=[pl.BlockSpec(memory_space=pltpu.VMEM)],
        out_specs=pl.BlockSpec(memory_space=pl.ANY),
        out_shape=jax.ShapeDtypeStruct((rows, cols, width), BF),
        scratch_shapes=[pltpu.VMEM((rows, cols, width), BF), pltpu.SemaphoreType.DMA((rows // unit,))],
        compiler_params=pltpu.CompilerParams(vmem_limit_bytes=VMEM_LIMIT),
        cost_estimate=pl.CostEstimate(flops=0, bytes_accessed=rows * cols * width * 4, transcendentals=0),
    )(landed)


def step_rows(start, extent, most=16):
    return max(size for size in range(1, most + 1) if extent % size == 0 and start % size == 0)


def body(frames, hidden_state, cell_state, w_gates, gate_bias, w_qkv, w_out, w_up, w_down):
    rows, cols, width = hidden_state.shape
    latent = frames.shape[2] // 2
    chans = latent + width
    held = chans + width
    devices_y, devices_x = lax.axis_size("gy"), lax.axis_size("gx")
    local_m = GRID // devices_x
    piece_x = cols // local_m // devices_x
    weights = w_gates.reshape(-1, w_gates.shape[3])
    bias = gate_bias.reshape(1, -1)

    def shifted(value, axis, step):
        count = lax.axis_size(axis)
        pairs = [(i, i + step) for i in range(count) if 0 <= i + step < count]
        return lax.ppermute(value, axis, pairs)

    send_left, send_right, side_left, side_right, line_top, line_bot = pack_step(frames, hidden_state, cell_state)
    from_left = shifted(send_right, "gx", 1)
    from_right = shifted(send_left, "gx", -1)
    to_down = jnp.concatenate([line_bot, from_left[-2:], from_right[-2:]], axis=1)
    to_up = jnp.concatenate([line_top, from_left[:2], from_right[:2]], axis=1)

    pieces = rows // devices_y
    piece_cols = local_m * piece_x
    shares = (pieces - pieces // 3, pieces // 3)
    ahead = rows - max(size for size in range(1, 13) if rows % size == 0 and rows - size > shares[0] * devices_y)
    tile_shapes = (jax.ShapeDtypeStruct((rows, cols, width), BF), jax.ShapeDtypeStruct((rows, cols, width), F32))
    carry = ()
    half = -(-ahead // 8) * 4
    for start, extent in ((0, half), (half, ahead - half)):
        spec = pl.BlockSpec(memory_space=pltpu.VMEM)
        if carry:
            *carry, to_down, to_up = lax.optimization_barrier((*carry, to_down, to_up))
            from_up, from_down = shifted(to_down, "gy", 1), shifted(to_up, "gy", -1)
        carry = conv_step(
            frames, 0, hidden_state, cell_state, {}, weights, bias, (start, extent), ("hid_out", "cell_out"),
            tile_shapes, (spec, spec), None, carry, None,
        )
    hidden_one, cell_one = carry

    length = -(-(rows + 4) // 16) * 16
    line_shape = jax.ShapeDtypeStruct((4, cols, width), F32)
    strip_shape = jax.ShapeDtypeStruct((4, length, width), F32)
    beside_shape = jax.ShapeDtypeStruct((2, length, latent), F32)
    shapes = (line_shape, line_shape, strip_shape, strip_shape, beside_shape)
    turned = from_left.transpose(1, 0, 2), from_right.transpose(1, 0, 2)
    around = (from_up, from_down, line_top, line_bot, *turned, side_left, side_right)
    line_hid, line_cell, strip_hid, strip_cell, beside = pl.pallas_call(
        ring_kernel,
        grid=(1,),
        in_specs=[*(whole(array) for array in around), pl.BlockSpec(memory_space=pltpu.VMEM), whole(bias)],
        out_specs=[whole(shape) for shape in shapes],
        out_shape=shapes,
        scratch_shapes=[pltpu.VMEM((8, length, held + latent), F32)],
        compiler_params=pltpu.CompilerParams(vmem_limit_bytes=VMEM_LIMIT),
        cost_estimate=pl.CostEstimate(flops=16 * length * weights.size, bytes_accessed=2 * weights.size, transcendentals=0),
    )(*around, weights, bias)

    second = held // latent
    line = (1, from_up.shape[1], latent)
    ring = {name: (array, whole(array)) for name, array in (
        ("strips_hid", strip_hid), ("strips_cell", strip_cell), ("lines_hid", line_hid), ("lines_cell", line_cell),
        ("beside", beside),
    )}
    ring["frame_top"] = from_up, pl.BlockSpec(line, lambda step: (1, 0, second))
    ring["frame_bot"] = from_down, pl.BlockSpec(line, lambda step: (0, 0, second))

    moved, start, carry = [], 0, ()
    for piece_y in shares:
        extent = piece_y * devices_y
        sent_shape = jax.ShapeDtypeStruct((devices_y, devices_x, piece_y, piece_cols, width), BF)
        spec = pl.BlockSpec(memory_space=pl.ANY)
        sent, cell_out = conv_step(
            frames, 1, hidden_one, cell_one, ring, weights, bias, (start, extent),
            ("hid_out", "cell_out"), (sent_shape, tile_shapes[1]), (whole(sent_shape), spec), (local_m, piece_x), carry,
            (ahead, hidden_state, cell_state) if carry else None,
        )
        carry = (None, cell_out)
        sent = sent.reshape(devices_y * devices_x, piece_y, piece_cols, width)
        moved.append(lax.all_to_all(sent, ("gy", "gx"), split_axis=0, concat_axis=0, tiled=True))
        start += extent
    done, first = None, 0
    for piece_y, value in zip(shares, moved):
        done = block_step(value, done, first, pieces, devices_y, devices_x, w_qkv, w_out, w_up, w_down)
        first += piece_y
    done = done.reshape(devices_y * devices_x, pieces, piece_cols, width)
    landed = lax.all_to_all(done, ("gy", "gx"), split_axis=0, concat_axis=0, tiled=True)
    result = unpack_step(landed.reshape(devices_y, devices_x, *landed.shape[1:]), shares, cols, local_m, piece_x)
    return result, cell_out


def solution(mesh):
    tiled = P("gy", "gx", None)
    in_specs = (tiled, tiled, tiled, P(), P(), P(), P(), P(), P())
    return jax.shard_map(body, mesh=mesh, in_specs=in_specs, out_specs=(tiled, tiled), check_vma=False)
```
